32 devices in a mesh: rep: 4 (over x, core), fsdp: 8 (over z, y).
Axes of the slice: x: 2, y: 2, z: 4, core: 2. Of those that a mesh axis runs over, the one named last changes fastest.
Arguments:
- tokens: bfloat16 [256, 196, 768], P(('rep', 'fsdp')), may hold values from -6 to 6
- teacher: bfloat16 [256, 196, 768], P(('rep', 'fsdp')), may hold values from -6 to 6
- valid_mask: int32 [256, 196], P(('rep', 'fsdp')), may hold values from 0 to 1, as said below
- attn_gain: bfloat16 [768], P('fsdp'), may hold values from 0.099609375 to 1.8984375
- attn_shift: bfloat16 [768], P('fsdp'), may hold values from -1.75 to 1.75
- qkv_weight: bfloat16 [768, 2304], P('fsdp'), may hold values from -0.21875 to 0.21875
- query_bias: bfloat16 [768], P('fsdp'), may hold values from -3 to 3
- value_bias: bfloat16 [768], P('fsdp'), may hold values from -3 to 3
- rel_pos_h: bfloat16 [27, 64], P(None, 'fsdp'), may hold values from -0.375 to 0.375
- rel_pos_w: bfloat16 [27, 64], P(None, 'fsdp'), may hold values from -0.375 to 0.375
- proj_weight: bfloat16 [768, 768], P('fsdp'), may hold values from -0.625 to 0.625
- proj_bias: bfloat16 [768], P('fsdp'), may hold values from -1.75 to 1.75
- mlp_gain: bfloat16 [768], P('fsdp'), may hold values from 0.099609375 to 1.8984375
- mlp_shift: bfloat16 [768], P('fsdp'), may hold values from -1.75 to 1.75
- up_weight: bfloat16 [768, 3072], P('fsdp'), may hold values from -0.21875 to 0.21875
- up_bias: bfloat16 [3072], P('fsdp'), may hold values from -1.75 to 1.75
- down_weight: bfloat16 [3072, 768], P('fsdp'), may hold values from -0.15625 to 0.15625
- down_bias: bfloat16 [768], P('fsdp'), may hold values from -1.75 to 1.75
Outputs:
- block_output: bfloat16 [256, 196, 768], P(('rep', 'fsdp'))
- loss: float32 [], replicated
- input_grad: float32 [256, 196, 768], P(('rep', 'fsdp'))
- attn_gain_grad: float32 [768], P('fsdp')
- attn_shift_grad: float32 [768], P('fsdp')
- qkv_weight_grad: float32 [768, 2304], P('fsdp')
- query_bias_grad: float32 [768], P('fsdp')
- value_bias_grad: float32 [768], P('fsdp')
- rel_pos_h_grad: float32 [27, 64], P(None, 'fsdp')
- rel_pos_w_grad: float32 [27, 64], P(None, 'fsdp')
- proj_weight_grad: float32 [768, 768], P('fsdp')
- proj_bias_grad: float32 [768], P('fsdp')
- mlp_gain_grad: float32 [768], P('fsdp')
- mlp_shift_grad: float32 [768], P('fsdp')
- up_weight_grad: float32 [768, 3072], P('fsdp')
- up_bias_grad: float32 [3072], P('fsdp')
- down_weight_grad: float32 [3072, 768], P('fsdp')
- down_bias_grad: float32 [768], P('fsdp')
The draws below stay inside these ranges and needn't reach their ends.
Inputs may be any that keep to these rules, and one draw needn't show every extreme that they name: `valid_mask`: the first slot of every window is 1.
All inputs are finite; a program needn't handle non-finite values.
Results may differ from the reference program's by a relative error of at most 0.01.
Values may be sent and summed in bfloat16 or wider, within the bound.
No kernel may reach another device: no remote copies, remote signals or barrier semaphores. Data moves between devices by JAX's collectives and lax.ppermute only.
A program may use at most 384 MiB of HBM per device.

```python
import math
import jax
import jax.numpy as jnp
from jax import lax

D = 768
HEADS = 12
HEAD_DIM = 64
MLP = 3072
WIN = 14
MAP = 64
WINDOWS = 256


def draw_teacher(key, part):
    base = jax.random.normal(key, (WINDOWS, WIN * WIN, D), jnp.float32)
    return jnp.clip(base, -6.0, 6.0).astype(jnp.bfloat16)


def draw_valid_mask(key, part):
    dice_rolls = jax.random.randint(key, (WINDOWS, WIN * WIN), 0, 16, dtype=jnp.int32)
    threshold = 5 + 11 * jnp.arange(WINDOWS, dtype=jnp.int32) // WINDOWS
    counted = (dice_rolls < threshold[:, None]).astype(jnp.int32)
    first_slot = jnp.arange(WIN * WIN, dtype=jnp.int32) == 0
    return jnp.where(first_slot[None, :], 1, counted).astype(jnp.int32)


def strengthened(entries, key, source, target, blocks, factor):
    def block_of(axis_at):
        return (jnp.arange(entries.shape[axis_at]) // (entries.shape[axis_at] // blocks)).reshape((-1,) + (1,) * (entries.ndim - 1 - axis_at))

    one_side = jax.random.permutation(key, blocks)[block_of(target)]
    second = (block_of(target) + blocks // 2) % blocks
    return jnp.where((block_of(source) == one_side) | (block_of(source) == second), factor * entries, entries)


def block_scale(rng, extent, split, low, high):
    level, own = 1.0, jax.random.fold_in(rng, 6)
    for position, shards_of in split:
        steps = jnp.exp(jax.random.uniform(jax.random.fold_in(own, position), (shards_of,), jnp.float32, low / len(split), high / len(split)))
        level = level * jnp.repeat(steps, extent[position] // shards_of).reshape([-1 if axis == position else 1 for axis in range(len(extent))])
    return level


def noise(rng, dims, deviation, limit, shards=(), kind=jnp.bfloat16):
    level = block_scale(rng, dims, shards, -0.22, 0.18) if shards else 1.0
    array = jax.random.normal(rng, dims, jnp.float32) * deviation * level
    return jnp.minimum(jnp.maximum(array, -limit), limit).astype(kind)


def heavy_noise(stream_key, extent, spread, reach, cuts, heavy, kind=jnp.bfloat16):
    array = spread * jax.random.normal(stream_key, extent, jnp.float32)
    if cuts:
        array = array * block_scale(stream_key, extent, cuts, -0.22, 0.18)
    return jnp.clip(strengthened(array, jax.random.fold_in(stream_key, 3), *heavy), -reach, reach).astype(kind)


def setup_inputs(seed: int = 0) -> dict:
    key_list = jax.random.split(jax.random.key(seed), 19)
    tokens = heavy_noise(key_list[0], (WINDOWS, WIN * WIN, D), 1.0, 6.0, ((0, 32),), (0, 2, 32, 2.75))
    teacher = draw_teacher(jax.random.fold_in(key_list[18], 71), 0)
    valid_mask = draw_valid_mask(jax.random.fold_in(key_list[18], 71), 0)
    attn_gain = jnp.clip(1.0 + 0.18 * jax.random.normal(key_list[3], (D,), jnp.float32), 0.099609375, 1.8984375).astype(jnp.bfloat16)
    attn_shift = noise(key_list[4], (D,), 0.3, 1.75, ((0, 8),))
    qkv_weight = noise(key_list[5], (D, 3 * D), D ** -0.5, 0.21875, ((0, 8),))
    query_bias = noise(key_list[6], (D,), 0.5, 3.0, ((0, 8),))
    value_bias = noise(key_list[7], (D,), 0.5, 3.0, ((0, 8),))
    rel_pos_h = noise(key_list[8], (2 * WIN - 1, HEAD_DIM), (4 * HEAD_DIM) ** -0.5, 0.375, ((1, 8),))
    rel_pos_w = noise(key_list[9], (2 * WIN - 1, HEAD_DIM), (4 * HEAD_DIM) ** -0.5, 0.375, ((1, 8),))
    proj_weight = noise(key_list[10], (D, D), (D // 8) ** -0.5, 0.625, ((0, 8),))
    proj_bias = noise(key_list[11], (D,), 0.3, 1.75, ((0, 8),))
    mlp_gain = jnp.clip(1.0 + 0.18 * jax.random.normal(key_list[12], (D,), jnp.float32), 0.099609375, 1.8984375).astype(jnp.bfloat16)
    mlp_shift = noise(key_list[13], (D,), 0.3, 1.75, ((0, 8),))
    up_weight = noise(key_list[14], (D, MLP), D ** -0.5, 0.21875, ((0, 8),))
    up_bias = noise(key_list[15], (MLP,), 0.3, 1.75, ((0, 8),))
    down_weight = noise(key_list[16], (MLP, D), (MLP // 2) ** -0.5, 0.15625, ((0, 8),))
    down_bias = noise(key_list[17], (D,), 0.3, 1.75, ((0, 8),))
    return dict(tokens=tokens, teacher=teacher, valid_mask=valid_mask, attn_gain=attn_gain, attn_shift=attn_shift, qkv_weight=qkv_weight, query_bias=query_bias, value_bias=value_bias, rel_pos_h=rel_pos_h, rel_pos_w=rel_pos_w, proj_weight=proj_weight, proj_bias=proj_bias, mlp_gain=mlp_gain, mlp_shift=mlp_shift, up_weight=up_weight, up_bias=up_bias, down_weight=down_weight, down_bias=down_bias)


@jax.custom_vjp
def low(v):
    return lax.optimization_barrier(v.astype(jnp.bfloat16)).astype(jnp.float32)

@jax.custom_vjp
def low_back(v):
    return v

def low_keep(v):
    return (low(v), None)

def low_pass(kept, grad):
    return (grad,)

def back_keep(v):
    return (v, None)

def back_low(kept, grad):
    return (low(grad),)
low.defvjp(low_keep, low_pass)
low_back.defvjp(back_keep, back_low)
LN_EPS = 1e-06
HIGH = lax.Precision.HIGHEST

def layer_norm(values, gain, shift):
    row_mean = lax.optimization_barrier(jnp.mean(values, axis=-1, keepdims=True))
    centred = values - row_mean
    return centred * lax.rsqrt(lax.optimization_barrier(jnp.mean(centred * centred, axis=-1, keepdims=True)) + LN_EPS) * gain + shift

def inside_mask(count_windows):
    grid_side = (MAP + WIN - 1) // WIN
    map_place = jnp.arange(count_windows, dtype=jnp.int32) % (grid_side * grid_side)
    cell_ids = jnp.arange(WIN * WIN, dtype=jnp.int32)
    row_pos = (map_place // grid_side)[:, None] * WIN + (cell_ids // WIN)[None, :]
    col_pos = (map_place % grid_side)[:, None] * WIN + (cell_ids % WIN)[None, :]
    return ((row_pos < MAP) & (col_pos < MAP)).astype(jnp.float32)

def window_block(params, pieces):
    inputs, inside = pieces
    attn_gain, attn_shift, qkv_weight, query_bias, value_bias, rel_pos_h, rel_pos_w, proj_weight, proj_bias, mlp_gain, mlp_shift, up_weight, up_bias, down_weight, down_bias = params
    group_size = inputs.shape[0]
    keep_rows = inside[..., None]
    first_in = low(layer_norm(inputs, attn_gain, attn_shift) * keep_rows)
    bias_row = jnp.concatenate([query_bias, jnp.zeros_like(query_bias), value_bias])
    qkv_out = jnp.einsum('gsd,de->gse', first_in, qkv_weight, precision=HIGH) + bias_row
    heads_shape = (group_size, WIN * WIN, HEADS, HEAD_DIM)
    query = low(low_back(qkv_out[..., :D])).reshape(heads_shape)
    keys = low(low_back(qkv_out[..., D:2 * D])).reshape(heads_shape)
    values = low(low_back(qkv_out[..., 2 * D:])).reshape(heads_shape)
    positions = jnp.arange(WIN, dtype=jnp.int32)
    offsets = positions[:, None] - positions[None, :] + WIN - 1
    table_h = rel_pos_h[offsets]
    table_w = rel_pos_w[offsets]
    plain = jnp.einsum('gihd,gjhd->ghij', query, keys, precision=HIGH) * HEAD_DIM ** (-0.5)
    grid_query = query.reshape(group_size, WIN, WIN, HEADS, HEAD_DIM)
    along_h = jnp.einsum('grchd,rkd->ghrck', grid_query, table_h, precision=HIGH)
    along_w = jnp.einsum('grchd,ckd->ghrck', grid_query, table_w, precision=HIGH)
    scores = plain.reshape(group_size, HEADS, WIN, WIN, WIN, WIN) + along_h[..., :, None] + along_w[..., None, :]
    scores = low_back(scores.reshape(group_size, HEADS, WIN * WIN, WIN * WIN))
    attn_prob = jax.nn.softmax(scores, axis=-1)
    mixed = jnp.einsum('ghij,gjhd->gihd', low(attn_prob), values, precision=HIGH).reshape(group_size, WIN * WIN, D)
    mixed = low(low_back(mixed))
    attn_out = low_back(jnp.einsum('gsd,de->gse', mixed, proj_weight, precision=HIGH) + proj_bias)
    hidden = keep_rows * (inputs + attn_out)
    second_in = low(layer_norm(hidden, mlp_gain, mlp_shift))
    up_pre = low_back(jnp.einsum('gsd,df->gsf', second_in, up_weight, precision=HIGH) + up_bias)
    up_act = low(jax.nn.gelu(up_pre, approximate=False))
    down_out = low_back(jnp.einsum('gsf,fd->gsd', up_act, down_weight, precision=HIGH) + down_bias)
    return keep_rows * (hidden + down_out)

def reference(tokens, teacher, valid_mask, attn_gain, attn_shift, qkv_weight, query_bias, value_bias, rel_pos_h, rel_pos_w, proj_weight, proj_bias, mlp_gain, mlp_shift, up_weight, up_bias, down_weight, down_bias):
    count_windows = tokens.shape[0]
    loss_scale = 64.0 * D * count_windows
    group_size = math.gcd(count_windows, 16)
    inside = inside_mask(count_windows)
    valid = valid_mask.astype(jnp.float32) * inside
    valid_total = jnp.sum(valid)
    target = teacher.astype(jnp.float32)
    weights = tuple((weight_arg.astype(jnp.float32) for weight_arg in (attn_gain, attn_shift, qkv_weight, query_bias, value_bias, rel_pos_h, rel_pos_w, proj_weight, proj_bias, mlp_gain, mlp_shift, up_weight, up_bias, down_weight, down_bias)))
    block_step = jax.checkpoint(window_block)

    def forward(inputs, params):

        def per_block(pieces):
            return block_step(params, pieces)
        blocks = (inputs.reshape(-1, group_size, WIN * WIN, D), inside.reshape(-1, group_size, WIN * WIN))
        output = lax.map(per_block, blocks).reshape(count_windows, WIN * WIN, D)
        error_term = output - target
        loss = jnp.sum(valid[..., None] * error_term * error_term) / (valid_total * D)
        return (loss_scale * loss, (output, loss))
    scaled, pull_back, aux = jax.vjp(forward, tokens.astype(jnp.float32), weights, has_aux=True)
    output, loss = aux
    grad_input, grads = pull_back(jnp.ones_like(scaled))
    return (output.astype(jnp.bfloat16), loss, grad_input, grads[0], grads[1], grads[2], grads[3], grads[4], grads[5], grads[6], grads[7], grads[8], grads[9], grads[10], grads[11], grads[12], grads[13], grads[14])
```

```python
import functools
import math

import jax
import jax.numpy as jnp
import numpy as np
from jax import lax
from jax.experimental import pallas as pl
from jax.experimental.pallas import tpu as pltpu
from jax.sharding import PartitionSpec as P

D = 768
HEADS = 12
HEAD_DIM = 64
MLP = 3072
WIN = 14
MAP = 64
SLOTS = WIN * WIN
ROWS = 208
LANES = 256
PAIRS = HEADS // 2
PAIR = 2 * HEAD_DIM
SIDE = (MAP + WIN - 1) // WIN
LN_EPS = 1e-06
F32 = jnp.float32
BF16 = jnp.bfloat16
VMEM_LIMIT = 60 * 1024 * 1024


def nn(left, right):
    return jnp.dot(left, right, preferred_element_type=F32)


def nt(left, right):
    return lax.dot_general(left, right, (((1,), (1,)), ((), ())), preferred_element_type=F32)


def tn(left, right):
    return lax.dot_general(left, right, (((0,), (0,)), ((), ())), preferred_element_type=F32)


def key_places():
    table = np.zeros((ROWS, HEAD_DIM), np.float32)
    for slot in range(SLOTS):
        for base in (0, 32):
            table[slot, base + WIN - 1 - slot // WIN] = 1.0
            table[slot, base + 16 + WIN - 1 - slot % WIN] = 1.0
    return table


def keep_column(base_ref, window):
    slot = lax.broadcasted_iota(jnp.int32, (ROWS, 1), 0)
    row = lax.shift_right_logical(slot * 4682, 16)
    col = slot - row * WIN
    place = lax.rem(base_ref[0] + window, SIDE * SIDE)
    place_row = lax.div(place, SIDE)
    place_col = place - place_row * SIDE
    inside = (slot < SLOTS) & (row + place_row * WIN < MAP) & (col + place_col * WIN < MAP)
    return inside.astype(F32)


def lane_places():
    slot = lax.broadcasted_iota(jnp.int32, (1, LANES), 1)
    row = lax.shift_right_logical(slot * 4682, 16)
    return row, slot - row * WIN


def norm_parts(values):
    mean = jnp.mean(values, axis=-1, keepdims=True)
    centred = values - mean
    inv_std = lax.rsqrt(jnp.mean(centred * centred, axis=-1, keepdims=True) + LN_EPS)
    return centred * inv_std, inv_std


def norm_grad(grad, scaled, inv_std, gain):
    grad_scaled = grad * gain
    first = jnp.mean(grad_scaled, axis=-1, keepdims=True)
    second = jnp.mean(grad_scaled * scaled, axis=-1, keepdims=True)
    return inv_std * (grad_scaled - first - scaled * second)


def up_by(values, amount):
    take = lambda bit: (amount & bit) != 0
    part = jnp.where(take(8), values[8:32], values[0:24])
    part = jnp.where(take(4), pltpu.roll(part, 20, 0), part)
    part = jnp.where(take(2), pltpu.roll(part, 22, 0), part)
    part = jnp.where(take(1), pltpu.roll(part, 23, 0), part)
    return part[0:16]


def down_by(values, amount):
    take = lambda bit: (amount & bit) != 0
    zeros = jnp.zeros((8, values.shape[1]), values.dtype)
    part = jnp.concatenate([values, zeros], axis=0)
    part = jnp.where(take(1), pltpu.roll(part, 1, 0), part)
    part = jnp.where(take(2), pltpu.roll(part, 2, 0), part)
    part = jnp.where(take(4), pltpu.roll(part, 4, 0), part)
    return jnp.where(
        take(8),
        jnp.concatenate([zeros, part], axis=0),
        jnp.concatenate([part, zeros], axis=0),
    )


def fill_rows(values):
    return jnp.concatenate(
        [values, jnp.zeros((LANES - ROWS,) + values.shape[1:], values.dtype)], axis=0
    )


def attend_kernel(
    base_ref, tok_ref, w_ref, bias_ref, gain_ref, shift_ref, rel_ref, place_ref, wp_ref, pb_ref,
    hid_ref, qkv_ref, prob_ref, mix_ref, fin_ref, x_ref,
):
    keep = keep_column(base_ref, pl.program_id(0))
    x_ref[pl.ds(192, 16), :] = jnp.zeros((16, D), F32)
    x_ref[pl.ds(0, SLOTS), :] = tok_ref[0].astype(F32)
    scaled, _ = norm_parts(x_ref[...])
    first_in = (keep * (scaled * gain_ref[...] + shift_ref[...])).astype(BF16)
    fin_ref[0] = first_in
    for part in range(3):
        cols = pl.ds(part * D, D)
        qkv_ref[0, :, cols] = (nn(first_in, w_ref[:, cols]) + bias_ref[:, cols]).astype(BF16)
    lane_row, lane_col = lane_places()
    low_half = lax.broadcasted_iota(jnp.int32, (ROWS, PAIR), 1) < HEAD_DIM
    tail_rows = lax.broadcasted_iota(jnp.int32, (16, LANES), 0) + 192
    places = place_ref[...]
    place_pair = jnp.concatenate([places, places], axis=1)

    def one_pair(pair, carry):
        at = pl.multiple_of(pair * PAIR, PAIR)
        query = qkv_ref[0, :, pl.ds(at, PAIR)]
        keys = qkv_ref[0, :, pl.ds(pl.multiple_of(D + at, PAIR), PAIR)]
        values = qkv_ref[0, :, pl.ds(pl.multiple_of(2 * D + at, PAIR), PAIR)]
        query_t = fill_rows(query).T
        values_t = fill_rows(values).T
        offsets = nn(rel_ref[...], query_t)
        mixed = []
        for head in range(2):
            mine = offsets[head * HEAD_DIM : (head + 1) * HEAD_DIM]
            along = jnp.concatenate(
                [up_by(mine[0:32], lane_row), up_by(mine[32:64], lane_col)], axis=0
            )
            high = along.astype(BF16)
            rest = (along - high.astype(F32)).astype(BF16)
            scaled_q = query_t[head * HEAD_DIM : (head + 1) * HEAD_DIM] * jnp.asarray(
                HEAD_DIM ** (-0.5), BF16
            )
            if head == 0:
                query_ext = jnp.concatenate([scaled_q, high, rest], axis=0)
                keys_ext = jnp.where(low_half, keys, place_pair)
            else:
                query_ext = jnp.concatenate([high, rest, scaled_q], axis=0)
                keys_ext = jnp.where(low_half, place_pair, keys)
            scores = nn(keys_ext, query_ext)
            scores = jnp.concatenate(
                [scores[0:192], jnp.where(tail_rows < SLOTS, scores[192:208], -1e30)], axis=0
            )
            peak = jnp.max(scores, axis=0, keepdims=True)
            expo = jnp.exp(scores - peak)
            total = jnp.sum(expo, axis=0, keepdims=True)
            probs = (expo * (1.0 / total)).astype(BF16)
            prob_ref[0, 2 * pair + head] = probs
            mixed.append(
                nn(values_t[head * HEAD_DIM : (head + 1) * HEAD_DIM], fill_rows(probs)).astype(BF16)
            )
        mix_ref[0, :, pl.ds(at, PAIR)] = jnp.concatenate(mixed, axis=0).T[0:ROWS]
        return carry

    lax.fori_loop(0, PAIRS, one_pair, 0)
    attn_out = nn(mix_ref[0], wp_ref[...]) + pb_ref[...]
    hid_ref[0] = keep * (x_ref[...] + attn_out)


def gelu_parts(pre):
    bell = jnp.exp(pre * pre * (-0.5))
    steps = 1.0 / (1.0 + (0.3275911 * math.sqrt(0.5)) * jnp.abs(pre))
    poly = steps * (
        0.5 * 0.254829592
        + steps
        * (
            0.5 * -0.284496736
            + steps * (0.5 * 1.421413741 + steps * (0.5 * -1.453152027 + steps * (0.5 * 1.061405429)))
        )
    )
    tail = poly * bell
    cumulative = jnp.where(pre > 0, 1.0 - tail, tail)
    return pre * cumulative, cumulative + pre * (bell * 0.3989422804014327)


def mlp_kernel(
    coef_ref, hid_ref, teach_ref, aux_ref, gain_ref, shift_ref, up_ref, ub_ref, down_ref, db_ref,
    out_ref, gh_ref, si_ref, act_ref, gd_ref, gu_ref, sums_ref, usum_ref, slope_ref, t_ref, *, group
):
    step = pl.program_id(0)
    rows = group * ROWS

    @pl.when(step == 0)
    def _():
        sums_ref[...] = jnp.zeros_like(sums_ref)
        usum_ref[...] = jnp.zeros_like(usum_ref)

    hidden = hid_ref[...].reshape(rows, D)
    aux = aux_ref[...].reshape(rows, 2)
    keep, valid = aux[:, 0:1], aux[:, 1:2]
    scaled, inv_std = norm_parts(hidden)
    second_in = (scaled * gain_ref[...] + shift_ref[...]).astype(BF16)
    si_ref[...] = second_in.reshape(group, ROWS, D)
    chunk = D

    def forward(part, total):
        cols = pl.ds(pl.multiple_of(part * chunk, chunk), chunk)
        pre = nn(second_in, up_ref[:, cols]) + ub_ref[:, cols]
        act, slope = gelu_parts(pre)
        slope_ref[:, cols] = slope
        low = act.astype(BF16)
        act_ref[:, :, cols] = low.reshape(group, ROWS, chunk)
        return total + nn(low, down_ref[cols, :])

    down = lax.fori_loop(0, MLP // chunk, forward, jnp.zeros((rows, D), F32))
    final = keep * (hidden + (down + db_ref[...]))
    for at in range(group):
        out_ref[at] = final[at * ROWS : at * ROWS + SLOTS].astype(BF16)
        t_ref[at, pl.ds(192, 16), :] = jnp.zeros((16, D), F32)
        t_ref[at, pl.ds(0, SLOTS), :] = teach_ref[at].astype(F32)
    error = final - t_ref[...].reshape(rows, D)
    weighted = valid * error
    grad_final = coef_ref[0] * weighted
    grad_down = grad_final.astype(BF16)
    gd_ref[...] = grad_down.reshape(group, ROWS, D)
    sums_ref[0:1, :] += jnp.sum(weighted * error, axis=0, keepdims=True)
    sums_ref[1:2, :] += jnp.sum(grad_down.astype(F32), axis=0, keepdims=True)

    def backward(part, total):
        cols = pl.ds(pl.multiple_of(part * chunk, chunk), chunk)
        grad_up = (nt(grad_down, down_ref[cols, :]) * slope_ref[:, cols]).astype(BF16)
        gu_ref[:, :, cols] = grad_up.reshape(group, ROWS, chunk)
        usum_ref[:, cols] += jnp.sum(grad_up.astype(F32), axis=0, keepdims=True)
        return total + nt(grad_up, up_ref[:, cols])

    grad_second = lax.fori_loop(0, MLP // chunk, backward, jnp.zeros((rows, D), F32))
    sums_ref[2:3, :] += jnp.sum(grad_second * scaled, axis=0, keepdims=True)
    sums_ref[3:4, :] += jnp.sum(grad_second, axis=0, keepdims=True)
    grad_hidden = grad_final + norm_grad(grad_second, scaled, inv_std, gain_ref[...])
    gh_ref[...] = (keep * grad_hidden).reshape(group, ROWS, D)


def attend_back_kernel(
    gh_ref, wp_ref, qkv_ref, prob_ref, rel_ref, relt_ref, place_ref, placet_ref,
    dqkv_ref, ga_ref, rg_ref, sums_ref, qsum_ref, gm_ref,
):
    @pl.when(pl.program_id(0) == 0)
    def _():
        rg_ref[...] = jnp.zeros_like(rg_ref)
        sums_ref[...] = jnp.zeros_like(sums_ref)
        qsum_ref[...] = jnp.zeros_like(qsum_ref)
        gm_ref[pl.ds(ROWS, LANES - ROWS), :] = jnp.zeros((LANES - ROWS, D), BF16)

    grad_attn = gh_ref[0].astype(BF16)
    ga_ref[0] = grad_attn
    sums_ref[...] += jnp.sum(grad_attn.astype(F32), axis=0, keepdims=True)
    gm_ref[pl.ds(0, ROWS), :] = nt(grad_attn, wp_ref[...]).astype(BF16)
    lane_row, lane_col = lane_places()
    low_half = lax.broadcasted_iota(jnp.int32, (ROWS, PAIR), 1) < HEAD_DIM
    low_full = lax.broadcasted_iota(jnp.int32, (LANES, PAIR), 1) < HEAD_DIM
    blank = jnp.zeros((), BF16)
    scale = HEAD_DIM ** (-0.5)

    def one_pair(pair, carry):
        at = pl.multiple_of(pair * PAIR, PAIR)
        q_at = pl.ds(at, PAIR)
        k_at = pl.ds(pl.multiple_of(D + at, PAIR), PAIR)
        v_at = pl.ds(pl.multiple_of(2 * D + at, PAIR), PAIR)
        query = fill_rows(qkv_ref[0, :, q_at])
        keys_t = fill_rows(qkv_ref[0, :, k_at]).T
        values = qkv_ref[0, :, v_at]
        grad_out = gm_ref[:, q_at]
        stacked = jnp.concatenate(
            [jnp.where(low_half, values, blank), jnp.where(low_half, blank, values)], axis=0
        )
        grad_probs = nt(stacked, grad_out)
        grad_values = jnp.zeros((ROWS, PAIR), F32)
        grad_keys = jnp.zeros((ROWS, PAIR), F32)
        spread, plain = [], []
        for head in range(2):
            own = (lambda full: jnp.where(low_full, full, blank)) if head == 0 else (
                lambda full: jnp.where(low_full, blank, full)
            )
            low = prob_ref[0, 2 * pair + head]
            probs = low.astype(F32)
            grad_p = grad_probs[head * ROWS : (head + 1) * ROWS]
            row_dot = jnp.sum(probs * grad_p, axis=0, keepdims=True)
            grad_score = (probs * (grad_p - row_dot)).astype(BF16)
            grad_values = grad_values + nn(low, own(grad_out))
            grad_keys = grad_keys + nn(grad_score, own(query))
            keys_ext = jnp.concatenate(
                [keys_t[head * HEAD_DIM : (head + 1) * HEAD_DIM], placet_ref[...]], axis=0
            )
            grad_ext = nn(keys_ext, fill_rows(grad_score))
            plain.append(grad_ext[0:64])
            spread.append(down_by(grad_ext[64:80], lane_row))
            spread.append(down_by(grad_ext[80:96], lane_col))
        spread = jnp.concatenate(spread, axis=0).astype(BF16)
        grad_query = jnp.concatenate(plain, axis=0) * scale + nn(relt_ref[...], spread)
        rg_ref[...] += nn(spread, query)
        grad_query = grad_query.astype(BF16).T[0:ROWS]
        grad_keys = (grad_keys * scale).astype(BF16)
        grad_values = grad_values.astype(BF16)
        dqkv_ref[0, :, q_at] = grad_query
        dqkv_ref[0, :, k_at] = grad_keys
        dqkv_ref[0, :, v_at] = grad_values
        qsum_ref[0:1, q_at] += jnp.sum(grad_query.astype(F32), axis=0, keepdims=True)
        qsum_ref[1:2, q_at] += jnp.sum(grad_values.astype(F32), axis=0, keepdims=True)
        return carry

    lax.fori_loop(0, PAIRS, one_pair, 0)


def input_kernel(
    base_ref, dqkv_ref, w_ref, tok_ref, gh_ref, gain_ref, out_ref, sums_ref, x_ref, *, group
):
    step = pl.program_id(0)

    @pl.when(step == 0)
    def _():
        sums_ref[...] = jnp.zeros_like(sums_ref)

    for at in range(group):
        keep = keep_column(base_ref, step * group + at)
        grad_first = keep * nt(dqkv_ref[at], w_ref[...])
        x_ref[pl.ds(192, 16), :] = jnp.zeros((16, D), F32)
        x_ref[pl.ds(0, SLOTS), :] = tok_ref[at].astype(F32)
        scaled, inv_std = norm_parts(x_ref[...])
        sums_ref[0:1, :] += jnp.sum(grad_first * scaled, axis=0, keepdims=True)
        sums_ref[1:2, :] += jnp.sum(grad_first, axis=0, keepdims=True)
        total = gh_ref[at] + norm_grad(grad_first, scaled, inv_std, gain_ref[...])
        out_ref[at] = total[0:SLOTS]


def whole(shape):
    zeros = (0,) * len(shape)
    return pl.BlockSpec(shape, lambda *_: zeros)


def per_window(shape):
    tail = (0,) * (len(shape) - 1)
    return pl.BlockSpec(shape, lambda step, *_: (step,) + tail)


SMEM = pl.BlockSpec(memory_space=pltpu.SMEM)


def params():
    return pltpu.CompilerParams(
        vmem_limit_bytes=VMEM_LIMIT, dimension_semantics=("arbitrary",)
    )


def shape_of(shape, dtype):
    return jax.ShapeDtypeStruct(shape, dtype)


def attend(base, tokens, weight, bias, gain, shift, rel, places, proj, proj_bias):
    count = tokens.shape[0]
    return pl.pallas_call(
        attend_kernel,
        grid=(count,),
        in_specs=[
            SMEM, per_window((1, SLOTS, D)), whole((D, 3 * D)), whole((1, 3 * D)), whole((1, D)),
            whole((1, D)), whole((PAIR, PAIR)), whole((ROWS, HEAD_DIM)), whole((D, D)), whole((1, D)),
        ],
        out_specs=[
            per_window((1, ROWS, D)), per_window((1, ROWS, 3 * D)),
            per_window((1, HEADS, ROWS, LANES)), per_window((1, ROWS, D)), per_window((1, ROWS, D)),
        ],
        out_shape=[
            shape_of((count, ROWS, D), F32), shape_of((count, ROWS, 3 * D), BF16),
            shape_of((count, HEADS, ROWS, LANES), BF16), shape_of((count, ROWS, D), BF16),
            shape_of((count, ROWS, D), BF16),
        ],
        scratch_shapes=[pltpu.VMEM((ROWS, D), F32)],
        compiler_params=params(),
        cost_estimate=pl.CostEstimate(
            flops=count * 3_500_000_000 // 2, bytes_accessed=40_000_000, transcendentals=0
        ),
        name="attend",
    )(base, tokens, weight, bias, gain, shift, rel, places, proj, proj_bias)


def mlp(coef, hidden, teacher, aux, gain, shift, up, up_bias, down, down_bias):
    count = hidden.shape[0]
    group = math.gcd(count, 2)
    win = lambda width: per_window((group, ROWS, width))
    arr = lambda width, dtype: shape_of((count, ROWS, width), dtype)
    return pl.pallas_call(
        functools.partial(mlp_kernel, group=group),
        grid=(count // group,),
        in_specs=[
            SMEM, win(D), per_window((group, SLOTS, D)), win(2), whole((1, D)), whole((1, D)),
            whole((D, MLP)), whole((1, MLP)), whole((MLP, D)), whole((1, D)),
        ],
        out_specs=[
            per_window((group, SLOTS, D)), win(D), win(D), win(MLP), win(D), win(MLP),
            whole((4, D)), whole((1, MLP)),
        ],
        out_shape=[
            shape_of((count, SLOTS, D), BF16), arr(D, F32), arr(D, BF16), arr(MLP, BF16),
            arr(D, BF16), arr(MLP, BF16), shape_of((4, D), F32), shape_of((1, MLP), F32),
        ],
        scratch_shapes=[pltpu.VMEM((group * ROWS, MLP), F32), pltpu.VMEM((group, ROWS, D), F32)],
        compiler_params=params(),
        cost_estimate=pl.CostEstimate(
            flops=count * 8 * ROWS * D * MLP, bytes_accessed=60_000_000, transcendentals=0
        ),
        name="mlp",
    )(coef, hidden, teacher, aux, gain, shift, up, up_bias, down, down_bias)


def attend_back(grad_hidden, proj, qkv, probs, rel, rel_t, places, places_t):
    count = grad_hidden.shape[0]
    return pl.pallas_call(
        attend_back_kernel,
        grid=(count,),
        in_specs=[
            per_window((1, ROWS, D)), whole((D, D)), per_window((1, ROWS, 3 * D)),
            per_window((1, HEADS, ROWS, LANES)), whole((PAIR, PAIR)), whole((PAIR, PAIR)),
            whole((ROWS, HEAD_DIM)), whole((32, LANES)),
        ],
        out_specs=[
            per_window((1, ROWS, 3 * D)), per_window((1, ROWS, D)), whole((PAIR, PAIR)),
            whole((1, D)), whole((2, D)),
        ],
        out_shape=[
            shape_of((count, ROWS, 3 * D), BF16), shape_of((count, ROWS, D), BF16),
            shape_of((PAIR, PAIR), F32), shape_of((1, D), F32), shape_of((2, D), F32),
        ],
        scratch_shapes=[pltpu.VMEM((LANES, D), BF16)],
        compiler_params=params(),
        cost_estimate=pl.CostEstimate(
            flops=count * 5_000_000_000 // 2, bytes_accessed=40_000_000, transcendentals=0
        ),
        name="attend_back",
    )(grad_hidden, proj, qkv, probs, rel, rel_t, places, places_t)


def input_back(base, dqkv, weight, tokens, grad_hidden, gain):
    count = tokens.shape[0]
    group = math.gcd(count, 2)
    return pl.pallas_call(
        functools.partial(input_kernel, group=group),
        grid=(count // group,),
        in_specs=[
            SMEM, per_window((group, ROWS, 3 * D)), whole((D, 3 * D)),
            per_window((group, SLOTS, D)), per_window((group, ROWS, D)), whole((1, D)),
        ],
        out_specs=[per_window((group, SLOTS, D)), whole((2, D))],
        out_shape=[shape_of((count, SLOTS, D), F32), shape_of((2, D), F32)],
        scratch_shapes=[pltpu.VMEM((ROWS, D), F32)],
        compiler_params=params(),
        cost_estimate=pl.CostEstimate(
            flops=count * 6 * ROWS * D * D, bytes_accessed=25_000_000, transcendentals=0
        ),
        name="input_back",
    )(base, dqkv, weight, tokens, grad_hidden, gain)


def split_small(packed, parts, width):
    pieces, at = [], 0
    for size in width:
        pieces.append(packed[:, at : at + size])
        at += size
    return pieces


def body(
    tokens, teacher, valid_mask, attn_gain, attn_shift, qkv_weight, query_bias, value_bias,
    rel_pos_h, rel_pos_w, proj_weight, proj_bias, mlp_gain, mlp_shift, up_weight, up_bias,
    down_weight, down_bias,
):
    count = tokens.shape[0]
    parts = lax.axis_size("fsdp")
    copies = lax.axis_size("rep")
    device = lax.axis_index("rep") * parts + lax.axis_index("fsdp")
    base = (device * count).astype(jnp.int32).reshape(1)
    window_ids = device * count + jnp.arange(count, dtype=jnp.int32)
    place = window_ids % (SIDE * SIDE)
    cells = jnp.arange(SLOTS, dtype=jnp.int32)
    inside = ((place // SIDE)[:, None] * WIN + (cells // WIN)[None, :] < MAP) & (
        (place % SIDE)[:, None] * WIN + (cells % WIN)[None, :] < MAP
    )
    keep = inside.astype(F32)
    valid = valid_mask.astype(F32) * keep
    valid_total = lax.psum(jnp.sum(valid), ("rep", "fsdp"))
    aux = jnp.pad(jnp.stack([keep, valid], axis=-1), ((0, 0), (0, ROWS - SLOTS), (0, 0)))

    small = [attn_gain, attn_shift, query_bias, value_bias, proj_bias, mlp_gain, mlp_shift,
             down_bias, up_bias, rel_pos_h, rel_pos_w]
    packed = lax.all_gather(jnp.concatenate([v.reshape(-1) for v in small]), "fsdp")
    pieces = split_small(packed, parts, [v.size for v in small])
    rows = [p.reshape(1, -1).astype(F32) for p in pieces[:9]]
    gain1, shift1, qb, vb, pb, gain2, shift2, db, ub = rows
    offsets = rel_pos_h.shape[0]
    tables = [
        p.reshape(parts, offsets, -1).transpose(1, 0, 2).reshape(offsets, HEAD_DIM)
        for p in pieces[9:]
    ]
    gap = jnp.zeros((32 - offsets, HEAD_DIM), BF16)
    table = jnp.concatenate([tables[0], gap, tables[1], gap], axis=0)
    hole = jnp.zeros((HEAD_DIM, HEAD_DIM), BF16)
    rel = jnp.concatenate(
        [jnp.concatenate([table, hole], axis=1), jnp.concatenate([hole, table], axis=1)], axis=0
    )
    rel_t = rel.T
    bias = jnp.concatenate([qb, jnp.zeros((1, D), F32), vb], axis=1)
    places = jnp.asarray(key_places(), BF16)
    places_t = jnp.asarray(np.pad(key_places().T[0:32], ((0, 0), (0, LANES - ROWS))), BF16)

    gather = lambda v: lax.all_gather(v, "fsdp", axis=0, tiled=True)
    w_qkv, w_proj, w_up, w_down = (
        gather(qkv_weight), gather(proj_weight), gather(up_weight), gather(down_weight)
    )
    hidden, qkv, probs, mixed, first_in = attend(
        base, tokens, w_qkv, bias, gain1, shift1, rel, places, w_proj, pb
    )
    loss_scale = 64.0 * D * count * copies * parts
    coef = (loss_scale * 2.0 / (valid_total * D)).reshape(1)
    out, grad_hidden, second_in, act, grad_down, grad_up, sums2, up_sum = mlp(
        coef, hidden, teacher, aux, gain2, shift2, w_up, ub, w_down, db
    )
    flat = lambda v: v.reshape(count * ROWS, v.shape[-1])
    scatter = lambda v: lax.psum(
        lax.psum_scatter(v.astype(BF16), "fsdp", scatter_dimension=0, tiled=True), "rep"
    ).astype(F32)
    d_down = scatter(tn(flat(act), flat(grad_down)))
    d_up = scatter(tn(flat(second_in), flat(grad_up)))
    dqkv, grad_attn, rel_grad, proj_sum, qv_sum = attend_back(
        grad_hidden, w_proj, qkv, probs, rel, rel_t, places, places_t
    )
    d_proj = scatter(tn(flat(mixed), flat(grad_attn)))
    d_qkv = scatter(tn(flat(first_in), flat(dqkv)))
    input_grad, sums1 = input_back(base, dqkv, w_qkv, tokens, grad_hidden, gain1)
    rel_sum = rel_grad[0:64, 0:64] + rel_grad[64:128, 64:128]
    loss_part = jnp.sum(sums2[0])
    vectors = [sums1[0], sums1[1], qv_sum[0], qv_sum[1], proj_sum[0], sums2[2], sums2[3], sums2[1],
               up_sum[0]]
    own = [
        jnp.concatenate([v.reshape(parts, -1) for v in vectors], axis=1),
        rel_sum[0:offsets].reshape(offsets, parts, -1).transpose(1, 0, 2).reshape(parts, -1),
        rel_sum[32 : 32 + offsets].reshape(offsets, parts, -1).transpose(1, 0, 2).reshape(parts, -1),
        jnp.broadcast_to(loss_part, (parts, 1)),
    ]
    totals = lax.psum(jnp.concatenate(own, axis=1), ("rep", "fsdp"))
    mine = lax.dynamic_index_in_dim(totals, lax.axis_index("fsdp"), 0, keepdims=False)
    outs, at = [], 0
    for v in [v for v in small]:
        outs.append(mine[at : at + v.size].reshape(v.shape))
        at += v.size
    (g_gain1, g_shift1, g_qb, g_vb, g_pb, g_gain2, g_shift2, g_db, g_ub, g_rh, g_rw) = outs
    loss = mine[at] / (valid_total * D)
    return (
        out, loss, input_grad, g_gain1, g_shift1, d_qkv, g_qb, g_vb, g_rh, g_rw, d_proj, g_pb,
        g_gain2, g_shift2, d_up, g_ub, d_down, g_db,
    )


def solution(mesh):
    windows = P(("rep", "fsdp"), None, None)
    vector = P("fsdp")
    matrix = P("fsdp", None)
    table = P(None, "fsdp")
    in_specs = (
        windows, windows, P(("rep", "fsdp"), None), vector, vector, matrix, vector, vector, table,
        table, matrix, vector, vector, vector, matrix, vector, matrix, vector,
    )
    out_specs = (windows, P(), windows) + in_specs[3:]
    return jax.shard_map(body, mesh=mesh, in_specs=in_specs, out_specs=out_specs, check_vma=False)
```

```python
import functools
import math

import jax
import jax.numpy as jnp
import numpy as np
from jax import lax
from jax.experimental import pallas as pl
from jax.experimental.pallas import tpu as pltpu
from jax.sharding import PartitionSpec as P

D = 768
HEADS = 12
HEAD_DIM = 64
MLP = 3072
WIN = 14
MAP = 64
SLOTS = WIN * WIN
ROWS = 208
LANES = 256
PAIRS = HEADS // 2
PAIR = 2 * HEAD_DIM
SIDE = (MAP + WIN - 1) // WIN
LN_EPS = 1e-06
F32 = jnp.float32
BF16 = jnp.bfloat16
VMEM_LIMIT = 60 * 1024 * 1024
QKV_HALF = 3 * D // 2
NOTES = 128
STEPS = (1, 2, 4, 1)
BACK_STEPS = (1, 5, 2)


def nn(left, right):
    return jnp.dot(left, right, preferred_element_type=F32)


def nt(left, right):
    return lax.dot_general(left, right, (((1,), (1,)), ((), ())), preferred_element_type=F32)


def tn(left, right):
    return lax.dot_general(left, right, (((0,), (0,)), ((), ())), preferred_element_type=F32)


def key_places():
    table = np.zeros((ROWS, HEAD_DIM), np.float32)
    for slot in range(SLOTS):
        for base in (0, 32):
            table[slot, base + WIN - 1 - slot // WIN] = 1.0
            table[slot, base + 16 + WIN - 1 - slot % WIN] = 1.0
    return table


def keep_column(base_ref, window):
    slot = lax.broadcasted_iota(jnp.int32, (ROWS, 1), 0)
    row = lax.shift_right_logical(slot * 4682, 16)
    col = slot - row * WIN
    place = lax.rem(base_ref[2] + window, SIDE * SIDE)
    place_row = lax.div(place, SIDE)
    place_col = place - place_row * SIDE
    inside = (slot < SLOTS) & (row + place_row * WIN < MAP) & (col + place_col * WIN < MAP)
    return inside.astype(F32)


def lane_places():
    slot = lax.broadcasted_iota(jnp.int32, (1, LANES), 1)
    row = lax.shift_right_logical(slot * 4682, 16)
    return row, slot - row * WIN


def norm_parts(values):
    mean = jnp.mean(values, axis=-1, keepdims=True)
    centred = values - mean
    inv_std = lax.rsqrt(jnp.mean(centred * centred, axis=-1, keepdims=True) + LN_EPS)
    return centred * inv_std, inv_std


def norm_grad(grad, scaled, inv_std, gain):
    grad_scaled = grad * gain
    first = jnp.mean(grad_scaled, axis=-1, keepdims=True)
    second = jnp.mean(grad_scaled * scaled, axis=-1, keepdims=True)
    return inv_std * (grad_scaled - first - scaled * second)


def up_by(values, amount):
    take = lambda bit: (amount & bit) != 0
    part = jnp.where(take(8), values[8:32], values[0:24])
    part = jnp.where(take(4), pltpu.roll(part, 20, 0), part)
    part = jnp.where(take(2), pltpu.roll(part, 22, 0), part)
    part = jnp.where(take(1), pltpu.roll(part, 23, 0), part)
    return part[0:16]


def down_by(values, amount):
    take = lambda bit: (amount & bit) != 0
    zeros = jnp.zeros((8, values.shape[1]), values.dtype)
    part = jnp.concatenate([values, zeros], axis=0)
    part = jnp.where(take(1), pltpu.roll(part, 1, 0), part)
    part = jnp.where(take(2), pltpu.roll(part, 2, 0), part)
    part = jnp.where(take(4), pltpu.roll(part, 4, 0), part)
    return jnp.where(
        take(8),
        jnp.concatenate([zeros, part], axis=0),
        jnp.concatenate([part, zeros], axis=0),
    )


def fill_rows(values):
    return jnp.concatenate(
        [values, jnp.zeros((LANES - ROWS,) + values.shape[1:], values.dtype)], axis=0
    )


def chunk_place(me_ref, index, far_y, along_y):
    mid, plane = index // 2, index % 2
    dist_x, dist_y = (far_y, mid) if along_y else (mid, far_y)
    plane = plane * 2 + (0 if along_y else 4)
    return (me_ref[0] // 2) ^ dist_x, me_ref[1] ^ (plane + dist_y)


ARRIVED = tuple((half, along_y, other) for other in (0, 1) for along_y in (True, False) for half in (0, 1))


def load_first(me_ref, parts, full, sem):
    core = me_ref[0] % 2
    for ref, (half, along_y, other) in zip(parts, ARRIVED):

        def start(index, carry, ref=ref, half=half, along_y=along_y, other=other):
            far_x, owner = chunk_place(me_ref, index, half, along_y)
            pltpu.make_async_copy(
                ref.at[index, :, pl.ds(0, QKV_HALF)],
                full.at[
                    pl.ds(pl.multiple_of(owner * 96 + far_x * 48, 16), 48),
                    pl.ds(pl.multiple_of((core ^ other) * QKV_HALF, 128), QKV_HALF),
                ],
                sem.at[0],
            ).start()
            return carry

        lax.fori_loop(0, 4, start, 0)
    pltpu.make_async_copy(full, full, sem.at[0]).wait()


def piece_place(me_ref, index):
    group, high, mid, plane = index // 8, (index // 4) % 2, (index // 2) % 2, index % 2
    dist_x = jnp.where(group == 0, high, mid)
    dist_y = jnp.where(group == 0, mid, high)
    return (me_ref[0] // 2) ^ dist_x, me_ref[1] ^ (group * 4 + plane * 2 + dist_y)


def spread_rows(notes_of, owner_of, width, total):
    row = lax.broadcasted_iota(jnp.int32, (128, total), 0)
    col = lax.broadcasted_iota(jnp.int32, (128, total), 1)
    acc = None
    for at in range(8):
        put = ((row < width) & (col == row + owner_of(at) * width)).astype(BF16)
        part = nn(notes_of(at), put)
        acc = part if acc is None else acc + part
    return acc


def notes_kernel(me_ref, a_ref, b_ref, c_ref, vec_ref, rel_ref, relt_ref):
    picks = [(a_ref, at, at % 2 * 2 + at // 2) for at in range(4)]
    picks += [(b_ref, at, 4 + at * 2) for at in range(2)] + [(c_ref, at, 5 + at * 2) for at in range(2)]
    owner_of = lambda at: me_ref[1] ^ picks[at][2]
    lanes = pl.ds(QKV_HALF, NOTES)
    vec_ref[...] = spread_rows(
        lambda at: picks[at][0][picks[at][1], 0:16, lanes], owner_of, 96, D
    )[0:8]
    row = lax.broadcasted_iota(jnp.int32, (128, 128), 0)
    col = lax.broadcasted_iota(jnp.int32, (128, 128), 1)
    halves = []
    for which in range(2):
        acc = jnp.zeros((32, 128), F32)
        for at in range(8):
            lane = row - 8 * which
            place = lane + owner_of(at) * 8
            put = ((lane >= 0) & (lane < 8) & ((col == place) | (col == place + 64))).astype(BF16)
            acc = acc + nn(picks[at][0][picks[at][1], 16:48, lanes], put)
        halves.append(acc)
    table = jnp.concatenate(halves * 2, axis=0)
    table = jnp.where((row < 64) == (col < 64), table, 0.0).astype(BF16)
    rel_ref[...] = table
    relt_ref[...] = table.T


def attend_kernel(*refs, first, pieces, earlier):
    base_ref, tok_ref = refs[0:2]
    at = 2 + max(pieces, 1)
    vec_ref, rel_ref, place_ref = refs[at : at + 3]
    at += 3 + earlier
    qkv_ref, prob_ref, mix_ref, fin_ref = refs[at : at + 4]
    if pieces:
        w_ref, x_ref, sem = refs[at + 4 :]

        @pl.when(pl.program_id(0) == 0)
        def _():
            load_first(base_ref, refs[2 : 2 + pieces], w_ref, sem)
    else:
        w_ref, x_ref = refs[2], refs[at + 4]
    keep = keep_column(base_ref, pl.program_id(0) + first)
    x_ref[pl.ds(192, 16), :] = jnp.zeros((16, D), F32)
    x_ref[pl.ds(0, SLOTS), :] = tok_ref[0].astype(F32)
    scaled, _ = norm_parts(x_ref[...])
    first_in = (keep * (scaled * vec_ref[0:1, :] + vec_ref[1:2, :])).astype(BF16)
    fin_ref[0] = first_in
    for part in range(3):
        cols = pl.ds(part * D, D)
        total = nn(first_in, w_ref[:, cols])
        if part != 1:
            total = total + vec_ref[2 + part // 2 : 3 + part // 2, :]
        qkv_ref[0, :, cols] = total.astype(BF16)
    lane_row, lane_col = lane_places()
    low_half = lax.broadcasted_iota(jnp.int32, (ROWS, PAIR), 1) < HEAD_DIM
    tail_rows = lax.broadcasted_iota(jnp.int32, (16, LANES), 0) + 192
    places = place_ref[...]
    place_pair = jnp.concatenate([places, places], axis=1)

    def one_pair(pair, carry):
        at = pl.multiple_of(pair * PAIR, PAIR)
        query = qkv_ref[0, :, pl.ds(at, PAIR)]
        keys = qkv_ref[0, :, pl.ds(pl.multiple_of(D + at, PAIR), PAIR)]
        values = qkv_ref[0, :, pl.ds(pl.multiple_of(2 * D + at, PAIR), PAIR)]
        query_t = fill_rows(query).T
        values_t = fill_rows(values).T
        offsets = nn(rel_ref[...], query_t)
        mixed = []
        for head in range(2):
            mine = offsets[head * HEAD_DIM : (head + 1) * HEAD_DIM]
            along = jnp.concatenate(
                [up_by(mine[0:32], lane_row), up_by(mine[32:64], lane_col)], axis=0
            )
            high = along.astype(BF16)
            rest = (along - high.astype(F32)).astype(BF16)
            scaled_q = query_t[head * HEAD_DIM : (head + 1) * HEAD_DIM] * jnp.asarray(
                HEAD_DIM ** (-0.5), BF16
            )
            if head == 0:
                query_ext = jnp.concatenate([scaled_q, high, rest], axis=0)
                keys_ext = jnp.where(low_half, keys, place_pair)
            else:
                query_ext = jnp.concatenate([high, rest, scaled_q], axis=0)
                keys_ext = jnp.where(low_half, place_pair, keys)
            scores = nn(keys_ext, query_ext)
            scores = jnp.concatenate(
                [scores[0:192], jnp.where(tail_rows < SLOTS, scores[192:208], -1e30)], axis=0
            )
            peak = jnp.max(scores, axis=0, keepdims=True)
            expo = jnp.exp(scores - peak)
            total = jnp.sum(expo, axis=0, keepdims=True)
            probs = (expo * (1.0 / total)).astype(BF16)
            prob_ref[0, 2 * pair + head] = probs
            mixed.append(
                nn(values_t[head * HEAD_DIM : (head + 1) * HEAD_DIM], fill_rows(probs)).astype(BF16)
            )
        mix_ref[0, :, pl.ds(at, PAIR)] = jnp.concatenate(mixed, axis=0).T[0:ROWS]
        return carry

    lax.fori_loop(0, PAIRS, one_pair, 0)


def gelu_parts(pre):
    bell = jnp.exp(pre * pre * (-0.5))
    steps = 1.0 / (1.0 + (0.3275911 * math.sqrt(0.5)) * jnp.abs(pre))
    poly = steps * (
        0.5 * 0.254829592
        + steps
        * (
            0.5 * -0.284496736
            + steps * (0.5 * 1.421413741 + steps * (0.5 * -1.453152027 + steps * (0.5 * 1.061405429)))
        )
    )
    tail = poly * bell
    cumulative = jnp.where(pre > 0, 1.0 - tail, tail)
    return pre * cumulative, cumulative + pre * (bell * 0.3989422804014327)


def load_mlp(me_ref, pieces, up, down, proj, notes, sem):
    core = me_ref[0] % 2
    for array, (ref, (half, along_y, other)) in enumerate(zip(pieces, ARRIVED)):

        def start(index, carry, ref=ref, half=half, along_y=along_y, far_core=core ^ other, array=array):
            far_x, owner = chunk_place(me_ref, index, half, along_y)
            rows = pl.ds(pl.multiple_of(owner * 96 + far_x * 48, 16), 48)
            for block in range(2):
                cols = pl.ds(pl.multiple_of(far_core * 1536 + block * D, 128), D)
                pltpu.make_async_copy(ref.at[index, block], up.at[rows, cols], sem.at[0]).start()
            place = owner * 8 + far_core * 4 + far_x * 2
            pltpu.make_async_copy(
                ref.at[index, pl.ds(2, 2)], down.at[pl.ds(place, 2)], sem.at[1]
            ).start()
            cols = pl.ds(pl.multiple_of(far_core * 384, 128), 384)
            pltpu.make_async_copy(
                ref.at[index, 4, :, pl.ds(0, 384)], proj.at[rows, cols], sem.at[2]
            ).start()
            pltpu.make_async_copy(
                ref.at[index, 4, pl.ds(0, 16), pl.ds(384, 384)], notes.at[array * 4 + index], sem.at[3]
            ).start()
            return carry

        lax.fori_loop(0, 4, start, 0)
    for at, full in ((3, notes), (2, proj), (0, up), (1, down)):
        pltpu.make_async_copy(full, full, sem.at[at]).wait()


def mlp_kernel(*refs, group, pieces, scale):
    step = pl.program_id(0)
    rows = group * ROWS
    me_ref, tok_ref, mix_ref, teach_ref, aux_ref = refs[0:5]
    at = 5 + (pieces or 6)
    (out_ref, gh_ref, ga_ref, si_ref, act_ref, gd_ref, gu_ref, sums_ref, usum_ref) = refs[at : at + 9]
    at += 9
    if pieces:
        wp_ref, slope_ref, t_ref, up_ref, down3_ref, notes, vec_ref, ub_ref, total_ref, sem = refs[at:]

        @pl.when(step == 0)
        def _():
            load_mlp(me_ref, refs[5 : 5 + pieces], up_ref, down3_ref, wp_ref, notes, sem)
            picks = [(at, at % 2 * 2 + at // 2) for at in range(4)]
            picks += [(8 + at, 4 + at * 2) for at in range(2)] + [(12 + at, 5 + at * 2) for at in range(2)]
            owner_of = lambda at: me_ref[1] ^ picks[at][1]
            vec_ref[...] = spread_rows(lambda at: notes[picks[at][0], :, 0:128], owner_of, 96, D)
            for at in range(8):
                lanes = pl.ds(pl.multiple_of(owner_of(at) * 384, 128), 384)
                ub_ref[:, lanes] = notes[picks[at][0], 0:16, :].astype(F32)[4:5, :]
            counts = notes[0].astype(F32)
            for at in range(1, 32):
                counts = counts + notes[at].astype(F32)
            counts = counts[5:6, 0:128]
            lane = lax.broadcasted_iota(jnp.int32, (1, 128), 1)
            weight = jnp.where(lane == 0, 128.0, jnp.where(lane == 1, 1.0, 0.0))
            total_ref[...] = jnp.sum(counts * weight, axis=1, keepdims=True)

        down_rows = lambda part: down3_ref[pl.ds(part * 16, 16)].reshape(D, D)
    else:
        wp_ref, up_ref, down_ref, vec_ref, ub_ref, total_ref = refs[5:11]
        slope_ref, t_ref = refs[at:]
        down_rows = lambda part: down_ref[pl.ds(pl.multiple_of(part * D, D), D), :]
    pb_row, gain_row, shift_row, db_row = [vec_ref[at : at + 1, :] for at in range(4)]
    coef = scale / total_ref[...]

    @pl.when(step == 0)
    def _():
        sums_ref[...] = jnp.zeros_like(sums_ref)
        sums_ref[5:6, :] = jnp.broadcast_to(total_ref[...], (1, D))
        usum_ref[...] = jnp.zeros_like(usum_ref)

    aux = aux_ref[...].reshape(rows, 2)
    keep, valid = aux[:, 0:1], aux[:, 1:2]
    for at in range(group):
        t_ref[at, pl.ds(192, 16), :] = jnp.zeros((16, D), F32)
        t_ref[at, pl.ds(0, SLOTS), :] = tok_ref[at].astype(F32)
    attn_out = nn(mix_ref[...].reshape(rows, D), wp_ref[...]) + pb_row
    hidden = keep * (t_ref[...].reshape(rows, D) + attn_out)
    scaled, inv_std = norm_parts(hidden)
    second_in = (scaled * gain_row + shift_row).astype(BF16)
    si_ref[...] = second_in.reshape(group, ROWS, D)
    chunk = D

    def forward(part, total):
        cols = pl.ds(pl.multiple_of(part * chunk, chunk), chunk)
        pre = nn(second_in, up_ref[:, cols]) + ub_ref[:, cols]
        act, slope = gelu_parts(pre)
        slope_ref[:, cols] = slope
        low = act.astype(BF16)
        act_ref[:, :, cols] = low.reshape(group, ROWS, chunk)
        return total + nn(low, down_rows(part))

    down = lax.fori_loop(0, MLP // chunk, forward, jnp.zeros((rows, D), F32))
    final = keep * (hidden + (down + db_row))
    for at in range(group):
        out_ref[at] = final[at * ROWS : at * ROWS + SLOTS].astype(BF16)
        t_ref[at, pl.ds(192, 16), :] = jnp.zeros((16, D), F32)
        t_ref[at, pl.ds(0, SLOTS), :] = teach_ref[at].astype(F32)
    error = final - t_ref[...].reshape(rows, D)
    weighted = valid * error
    grad_final = coef * weighted
    grad_down = grad_final.astype(BF16)
    gd_ref[...] = grad_down.reshape(group, ROWS, D)
    sums_ref[0:1, :] += jnp.sum(weighted * error, axis=0, keepdims=True)
    sums_ref[1:2, :] += jnp.sum(grad_down.astype(F32), axis=0, keepdims=True)

    def backward(part, total):
        cols = pl.ds(pl.multiple_of(part * chunk, chunk), chunk)
        grad_up = (nt(grad_down, down_rows(part)) * slope_ref[:, cols]).astype(BF16)
        gu_ref[:, :, cols] = grad_up.reshape(group, ROWS, chunk)
        usum_ref[:, cols] += jnp.sum(grad_up.astype(F32), axis=0, keepdims=True)
        return total + nt(grad_up, up_ref[:, cols])

    grad_second = lax.fori_loop(0, MLP // chunk, backward, jnp.zeros((rows, D), F32))
    sums_ref[2:3, :] += jnp.sum(grad_second * scaled, axis=0, keepdims=True)
    sums_ref[3:4, :] += jnp.sum(grad_second, axis=0, keepdims=True)
    grad_hidden = grad_final + norm_grad(grad_second, scaled, inv_std, gain_row)
    grad_hidden = keep * grad_hidden
    gh_ref[...] = grad_hidden.reshape(group, ROWS, D)
    grad_attn = grad_hidden.astype(BF16)
    ga_ref[...] = grad_attn.reshape(group, ROWS, D)
    sums_ref[4:5, :] += jnp.sum(grad_attn.astype(F32), axis=0, keepdims=True)


def attend_back_kernel(*refs, earlier):
    ga_ref, wp_ref, qkv_ref, prob_ref, relt_ref, placet_ref = refs[0:6]
    dqkv_ref, rg_ref, qsum_ref, gm_ref = refs[6 + earlier :]

    @pl.when(pl.program_id(0) == 0)
    def _():
        rg_ref[...] = refs[7][...] if earlier else jnp.zeros_like(rg_ref)
        qsum_ref[...] = refs[8][...] if earlier else jnp.zeros_like(qsum_ref)
        gm_ref[pl.ds(ROWS, LANES - ROWS), :] = jnp.zeros((LANES - ROWS, D), BF16)

    gm_ref[pl.ds(0, ROWS), :] = nt(ga_ref[0], wp_ref[...]).astype(BF16)
    lane_row, lane_col = lane_places()
    low_half = lax.broadcasted_iota(jnp.int32, (ROWS, PAIR), 1) < HEAD_DIM
    low_full = lax.broadcasted_iota(jnp.int32, (LANES, PAIR), 1) < HEAD_DIM
    blank = jnp.zeros((), BF16)
    scale = HEAD_DIM ** (-0.5)

    def one_pair(pair, carry):
        at = pl.multiple_of(pair * PAIR, PAIR)
        q_at = pl.ds(at, PAIR)
        k_at = pl.ds(pl.multiple_of(D + at, PAIR), PAIR)
        v_at = pl.ds(pl.multiple_of(2 * D + at, PAIR), PAIR)
        query = fill_rows(qkv_ref[0, :, q_at])
        keys_t = fill_rows(qkv_ref[0, :, k_at]).T
        values = qkv_ref[0, :, v_at]
        grad_out = gm_ref[:, q_at]
        stacked = jnp.concatenate(
            [jnp.where(low_half, values, blank), jnp.where(low_half, blank, values)], axis=0
        )
        grad_probs = nt(stacked, grad_out)
        grad_values = jnp.zeros((ROWS, PAIR), F32)
        grad_keys = jnp.zeros((ROWS, PAIR), F32)
        spread, plain = [], []
        for head in range(2):
            own = (lambda full: jnp.where(low_full, full, blank)) if head == 0 else (
                lambda full: jnp.where(low_full, blank, full)
            )
            low = prob_ref[0, 2 * pair + head]
            probs = low.astype(F32)
            grad_p = grad_probs[head * ROWS : (head + 1) * ROWS]
            row_dot = jnp.sum(probs * grad_p, axis=0, keepdims=True)
            grad_score = (probs * (grad_p - row_dot)).astype(BF16)
            grad_values = grad_values + nn(low, own(grad_out))
            grad_keys = grad_keys + nn(grad_score, own(query))
            keys_ext = jnp.concatenate(
                [keys_t[head * HEAD_DIM : (head + 1) * HEAD_DIM], placet_ref[...]], axis=0
            )
            grad_ext = nn(keys_ext, fill_rows(grad_score))
            plain.append(grad_ext[0:64])
            spread.append(down_by(grad_ext[64:80], lane_row))
            spread.append(down_by(grad_ext[80:96], lane_col))
        spread = jnp.concatenate(spread, axis=0).astype(BF16)
        grad_query = jnp.concatenate(plain, axis=0) * scale + nn(relt_ref[...], spread)
        rg_ref[...] += nn(spread, query)
        grad_query = grad_query.astype(BF16).T[0:ROWS]
        grad_keys = (grad_keys * scale).astype(BF16)
        grad_values = grad_values.astype(BF16)
        dqkv_ref[0, :, q_at] = grad_query
        dqkv_ref[0, :, k_at] = grad_keys
        dqkv_ref[0, :, v_at] = grad_values
        qsum_ref[0:1, q_at] += jnp.sum(grad_query.astype(F32), axis=0, keepdims=True)
        qsum_ref[1:2, q_at] += jnp.sum(grad_values.astype(F32), axis=0, keepdims=True)
        return carry

    lax.fori_loop(0, PAIRS, one_pair, 0)


def input_kernel(
    base_ref, dqkv_ref, w_ref, tok_ref, gh_ref, vec_ref, *refs, group, first, earlier
):
    step = pl.program_id(0)
    out_ref, sums_ref, x_ref = refs[earlier:]

    @pl.when(step == 0)
    def _():
        sums_ref[...] = refs[1][...] if earlier else jnp.zeros_like(sums_ref)

    for at in range(group):
        keep = keep_column(base_ref, first + step * group + at)
        grad_first = keep * nt(dqkv_ref[at], w_ref[...])
        x_ref[pl.ds(192, 16), :] = jnp.zeros((16, D), F32)
        x_ref[pl.ds(0, SLOTS), :] = tok_ref[at].astype(F32)
        scaled, inv_std = norm_parts(x_ref[...])
        sums_ref[0:1, :] += jnp.sum(grad_first * scaled, axis=0, keepdims=True)
        sums_ref[1:2, :] += jnp.sum(grad_first, axis=0, keepdims=True)
        total = gh_ref[at] + norm_grad(grad_first, scaled, inv_std, vec_ref[0:1, :])
        out_ref[at] = total[0:SLOTS]


def weight_grad_kernel(*refs):
    left_ref, right_ref, out_ref = refs
    out_ref[...] = tn(left_ref[...], right_ref[...]).astype(BF16)


def qkv_grad_kernel(me_ref, left_ref, right_ref, keep_ref, send_ref, full, sem):
    step = pl.program_id(0)
    cols = pl.ds(pl.multiple_of(step * D, D), D)
    full[:, cols] = tn(left_ref[...], right_ref[...]).astype(BF16)

    @pl.when(step == pl.num_programs(0) - 1)
    def _():
        core = me_ref[0] % 2
        for at, (ref, far_core) in enumerate(((send_ref, 1 - core), (keep_ref, core))):

            def start(index, carry, ref=ref, far_core=far_core, at=at):
                far_x, owner = piece_place(me_ref, index)
                pltpu.make_async_copy(
                    full.at[
                        pl.ds(pl.multiple_of(owner * 96 + far_x * 48, 16), 48),
                        pl.ds(pl.multiple_of(far_core * QKV_HALF, 128), QKV_HALF),
                    ],
                    ref.at[index],
                    sem.at[at],
                ).start()
                return carry

            lax.fori_loop(0, 16, start, 0)
        for at, ref in enumerate((send_ref, keep_ref)):
            pltpu.make_async_copy(ref, ref, sem.at[at]).wait()


def up_grad_kernel(me_ref, left_ref, right_ref, keep_ref, send_ref, full, sem):
    step = pl.program_id(0)
    full[step] = tn(left_ref[...], right_ref[...]).astype(BF16)
    mine = (step // 2) == me_ref[0] % 2

    def send_to(ref, at):
        def start(index, carry):
            far_x, owner = piece_place(me_ref, index)
            rows = pl.ds(pl.multiple_of(owner * 96 + far_x * 48, 16), 48)
            pltpu.make_async_copy(
                full.at[step, rows], ref.at[index, step % 2], sem.at[at]
            ).start()
            return carry

        lax.fori_loop(0, 16, start, 0)

    @pl.when(mine)
    def _():
        send_to(keep_ref, 0)

    @pl.when(jnp.logical_not(mine))
    def _():
        send_to(send_ref, 1)

    @pl.when(step == pl.num_programs(0) - 1)
    def _():
        pltpu.make_async_copy(keep_ref, keep_ref, sem.at[0]).wait()
        pltpu.make_async_copy(send_ref, send_ref, sem.at[1]).wait()


def down_grad_kernel(
    me_ref, act_ref, gd_ref, mix_ref, ga_ref, keep_ref, send_ref, full, half, sem
):
    step = pl.program_id(0)
    last = pl.num_programs(0) - 1

    @pl.when(step < last)
    def _():
        full[step] = tn(act_ref[...], gd_ref[...]).astype(BF16).reshape(16, 48, D)

    @pl.when(step == last)
    def _():
        total = tn(mix_ref[...], ga_ref[...]).astype(BF16)
        for core in range(2):
            half[core] = total[:, core * 384 : core * 384 + 384]

    core = me_ref[0] % 2
    for ref, far_core, at in ((keep_ref, core, 0), (send_ref, 1 - core, 1)):

        def start_down(index, carry, ref=ref, far_core=far_core, at=at):
            far_x, owner = piece_place(me_ref, index)

            @pl.when(owner // 2 == step)
            def _():
                place = (owner % 2) * 8 + far_core * 4 + far_x * 2
                pltpu.make_async_copy(
                    full.at[step, pl.ds(place, 2)], ref.at[index, pl.ds(0, 2)], sem.at[at]
                ).start()

            return carry

        def start_proj(index, carry, ref=ref, far_core=far_core, at=at):
            far_x, owner = piece_place(me_ref, index)
            rows = pl.ds(pl.multiple_of(owner * 96 + far_x * 48, 16), 48)
            for col in (0, 384):
                pltpu.make_async_copy(
                    half.at[far_core, rows], ref.at[index, 2, :, pl.ds(col, 384)], sem.at[at]
                ).start()
            return carry

        @pl.when(step < last)
        def _(start_down=start_down):
            lax.fori_loop(0, 16, start_down, 0)

        @pl.when(step == last)
        def _(start_proj=start_proj):
            lax.fori_loop(0, 16, start_proj, 0)

    @pl.when(step == last)
    def _():
        pltpu.make_async_copy(keep_ref, keep_ref, sem.at[0]).wait()
        pltpu.make_async_copy(send_ref, send_ref, sem.at[1]).wait()


def whole(shape):
    zeros = (0,) * len(shape)
    return pl.BlockSpec(shape, lambda *_: zeros)


def windows_from(first, shape):
    tail = (0,) * (len(shape) - 1)
    return pl.BlockSpec(shape, lambda step: (step + first,) + tail)


SMEM = pl.BlockSpec(memory_space=pltpu.SMEM)
ANY = pl.BlockSpec(memory_space=pl.ANY)


def params():
    return pltpu.CompilerParams(
        vmem_limit_bytes=VMEM_LIMIT, dimension_semantics=("arbitrary",)
    )


def shape_of(shape, dtype):
    return jax.ShapeDtypeStruct(shape, dtype)


def cost(flops, moved):
    return pl.CostEstimate(flops=int(flops), bytes_accessed=int(moved), transcendentals=0)


def notes_of(me, near, far_x, far_y):
    return pl.pallas_call(
        notes_kernel,
        in_specs=[SMEM] + [whole(v.shape) for v in (near, far_x, far_y)],
        out_specs=[whole((8, D)), whole((PAIR, PAIR)), whole((PAIR, PAIR))],
        out_shape=[shape_of((8, D), F32)] + [shape_of((PAIR, PAIR), BF16)] * 2,
        grid=(1,),
        compiler_params=params(),
        cost_estimate=cost(1e9, 1e6),
        name="notes",
    )(me, near, far_x, far_y)


def attend(me, tokens, weight, vec, rel, places, first, number, earlier=()):
    count = tokens.shape[0]
    win = lambda shape: windows_from(first, shape)
    pieces = len(weight) if isinstance(weight, tuple) else 0
    weights = weight if pieces else (weight,)
    weight_specs = [ANY] * pieces if pieces else [whole((D, 3 * D))]
    out_specs = [win((1, ROWS, 3 * D)), win((1, HEADS, ROWS, LANES)), win((1, ROWS, D)),
                 win((1, ROWS, D))]
    out_shape = [
        shape_of((count, ROWS, 3 * D), BF16), shape_of((count, HEADS, ROWS, LANES), BF16),
        shape_of((count, ROWS, D), BF16), shape_of((count, ROWS, D), BF16),
    ]
    scratch = [pltpu.VMEM((ROWS, D), F32)]
    if pieces:
        out_specs.append(whole((D, 3 * D)))
        out_shape.append(shape_of((D, 3 * D), BF16))
        scratch.append(pltpu.SemaphoreType.DMA((1,)))
    inputs = 5 + len(weights)
    return pl.pallas_call(
        functools.partial(attend_kernel, first=first, pieces=pieces, earlier=len(earlier)),
        grid=(number,),
        in_specs=[
            SMEM, win((1, SLOTS, D)), *weight_specs, whole((8, D)),
            whole((PAIR, PAIR)), whole((ROWS, HEAD_DIM)), *([ANY] * len(earlier)),
        ],
        out_specs=out_specs,
        out_shape=out_shape,
        scratch_shapes=scratch,
        input_output_aliases={inputs + at: at for at in range(len(earlier))},
        compiler_params=params(),
        cost_estimate=cost(number * 6e9, number * 2e6),
        name="attend",
    )(me, tokens, *weights, vec, rel, places, *earlier)


def mlp(me, tokens, mixed, teacher, aux, weights, scale, chunked):
    count = tokens.shape[0]
    group = math.gcd(count, 2)
    win = lambda width: windows_from(0, (group, ROWS, width))
    plain = windows_from(0, (group, SLOTS, D))
    arr = lambda width, dtype: shape_of((count, ROWS, width), dtype)
    pieces = len(weights) if chunked else 0
    weight_specs = [ANY] * pieces if pieces else [whole(v.shape) for v in weights]
    out_specs = [plain, win(D), win(D), win(D), win(MLP), win(D), win(MLP), whole((6, D)),
                 whole((1, MLP))]
    out_shape = [
        shape_of((count, SLOTS, D), BF16), arr(D, F32), arr(D, BF16), arr(D, BF16), arr(MLP, BF16),
        arr(D, BF16), arr(MLP, BF16), shape_of((6, D), F32), shape_of((1, MLP), F32),
    ]
    scratch = [pltpu.VMEM((group * ROWS, MLP), F32), pltpu.VMEM((group, ROWS, D), F32)]
    if pieces:
        out_specs.append(whole((D, D)))
        out_shape.append(shape_of((D, D), BF16))
        scratch += [pltpu.VMEM((D, MLP), BF16), pltpu.VMEM((MLP // 48, 48, D), BF16),
                    pltpu.VMEM((32, 16, 384), BF16), pltpu.VMEM((16, D), F32),
                    pltpu.VMEM((1, MLP), F32), pltpu.VMEM((1, 1), F32),
                    pltpu.SemaphoreType.DMA((4,))]
    return pl.pallas_call(
        functools.partial(mlp_kernel, group=group, pieces=pieces, scale=scale),
        grid=(count // group,),
        in_specs=[SMEM, plain, win(D), plain, win(2), *weight_specs],
        out_specs=out_specs,
        out_shape=out_shape,
        scratch_shapes=scratch,
        compiler_params=params(),
        cost_estimate=cost(count * 8e9, 60e6),
        name="mlp",
    )(me, tokens, mixed, teacher, aux, *weights)


def attend_back(grad_attn, proj, qkv, probs, rel_t, places_t, first, number, earlier=()):
    count = grad_attn.shape[0]
    win = lambda shape: windows_from(first, shape)
    before = [ANY, whole((PAIR, PAIR)), whole((2, D))] if earlier else []
    return pl.pallas_call(
        functools.partial(attend_back_kernel, earlier=len(earlier)),
        grid=(number,),
        in_specs=[
            win((1, ROWS, D)), whole((D, D)), win((1, ROWS, 3 * D)), win((1, HEADS, ROWS, LANES)),
            whole((PAIR, PAIR)), whole((32, LANES)), *before,
        ],
        out_specs=[win((1, ROWS, 3 * D)), whole((PAIR, PAIR)), whole((2, D))],
        out_shape=[
            shape_of((count, ROWS, 3 * D), BF16), shape_of((PAIR, PAIR), F32),
            shape_of((2, D), F32),
        ],
        scratch_shapes=[pltpu.VMEM((LANES, D), BF16)],
        input_output_aliases={6: 0} if earlier else {},
        compiler_params=params(),
        cost_estimate=cost(number * 6e9, number * 2e6),
        name="attend_back",
    )(grad_attn, proj, qkv, probs, rel_t, places_t, *earlier)


def input_back(me, dqkv, weight, tokens, grad_hidden, vec, first, number, earlier=()):
    count = tokens.shape[0]
    group = math.gcd(math.gcd(first, number), 2)
    win = lambda shape: windows_from(first // group, shape)
    before = [ANY, whole((2, D))] if earlier else []
    return pl.pallas_call(
        functools.partial(input_kernel, group=group, first=first, earlier=len(earlier)),
        grid=(number // group,),
        in_specs=[
            SMEM, win((group, ROWS, 3 * D)), whole((D, 3 * D)), win((group, SLOTS, D)),
            win((group, ROWS, D)), whole((8, D)), *before,
        ],
        out_specs=[win((group, SLOTS, D)), whole((2, D))],
        out_shape=[shape_of((count, SLOTS, D), F32), shape_of((2, D), F32)],
        scratch_shapes=[pltpu.VMEM((ROWS, D), F32)],
        input_output_aliases={6: 0} if earlier else {},
        compiler_params=params(),
        cost_estimate=cost(number * 2e9, 25e6),
        name="input_back",
    )(me, dqkv, weight, tokens, grad_hidden, vec, *earlier)


def pick(left, right):
    return jnp.dot(left, right, preferred_element_type=F32, precision=lax.Precision.HIGHEST)


def pack_kernel(me_ref, one_ref, qv_ref, two_ref, up_ref, rel_ref, out_ref):
    vectors = jnp.concatenate(
        [one_ref[0:2], qv_ref[0:2], two_ref[4:5], two_ref[2:4], two_ref[1:2]], axis=0
    )
    error = jnp.sum(two_ref[0:1, :], axis=1, keepdims=True)
    tables = rel_ref[0:64, 0:64] + rel_ref[64:128, 64:128]
    row = lax.broadcasted_iota(jnp.int32, (D, 128), 0)
    col = lax.broadcasted_iota(jnp.int32, (D, 128), 1)
    small_row = lax.broadcasted_iota(jnp.int32, (64, 128), 0)
    small_col = lax.broadcasted_iota(jnp.int32, (64, 128), 1)
    for at in range(8):
        owner = me_ref[1] ^ ((at % 4) * 2 + at // 4)
        own = pick(vectors, ((col < 96) & (row == col + owner * 96)).astype(F32))
        total = jnp.concatenate([own, jnp.zeros((24, 128), F32)], axis=0)
        for which in range(2):
            lane = small_col - 96 - 8 * which
            put = ((lane >= 0) & (lane < 8) & (small_row == lane + owner * 8)).astype(F32)
            total = total + pick(tables[32 * which : 32 * which + 32], put)
        out_ref[at] = total
        for part in range(3):
            lanes = pl.ds(pl.multiple_of(owner * 384 + part * 128, 128), 128)
            out_ref[at, 27 + part : 28 + part, :] = up_ref[:, lanes]
        out_ref[at, 30:31, :] = jnp.broadcast_to(error, (1, 128))


def pack(me, *sums):
    return pl.pallas_call(
        pack_kernel,
        grid=(1,),
        in_specs=[SMEM] + [whole(v.shape) for v in sums],
        out_specs=whole((8, 32, 128)),
        out_shape=shape_of((8, 32, 128), F32),
        compiler_params=params(),
        cost_estimate=cost(1e9, 1e6),
        name="pack",
    )(me, *sums)


def shard_kernel(me_ref, *refs, split):
    quarters, outs = refs[0:4], refs[4:]
    core, far_x = me_ref[0] % 2, me_ref[0] // 2
    for at, ref in enumerate(quarters):
        this_core, this_x = core ^ (at // 2), far_x ^ (at % 2)
        rows = pl.ds(pl.multiple_of(this_x * 48, 16), 48)
        if not split:
            cols = pl.ds(pl.multiple_of(this_core * QKV_HALF, 128), QKV_HALF)
            outs[0][rows, cols] = ref[...].astype(F32)
            continue
        up_ref, down_ref, proj_ref = outs
        for block in range(2):
            cols = pl.ds(pl.multiple_of(this_core * 1536 + block * D, 128), D)
            up_ref[rows, cols] = ref[block].astype(F32)
            at_row = this_core * 192 + this_x * 96 + block * 48
            down_ref[pl.ds(pl.multiple_of(at_row, 16), 48), :] = ref[2 + block].astype(F32)
        cols = pl.ds(pl.multiple_of(this_core * 384, 128), 384)
        proj_ref[rows, cols] = ref[4, :, 0:384].astype(F32)


def shard(me, quarters, split):
    shapes = [(96, MLP), (384, D), (96, D)] if split else [(96, 3 * D)]
    return pl.pallas_call(
        functools.partial(shard_kernel, split=split),
        grid=(1,),
        in_specs=[SMEM] + [whole(v.shape) for v in quarters],
        out_specs=[whole(s) for s in shapes],
        out_shape=[shape_of(s, F32) for s in shapes],
        compiler_params=params(),
        cost_estimate=cost(1e9, 5e6),
        name="shard",
    )(me, *quarters)


def column_blocks(rows):
    return pl.BlockSpec((rows, D), lambda step: (0, step))


def weight_grad(left, right, by_rows=False):
    rows = left.shape[0]
    blocks = (left if by_rows else right).shape[1] // D
    moving, still = column_blocks(rows), whole((rows, D))
    return pl.pallas_call(
        weight_grad_kernel,
        grid=(blocks,),
        in_specs=[moving, still] if by_rows else [still, moving],
        out_specs=pl.BlockSpec((D, D), (lambda s: (s, 0)) if by_rows else (lambda s: (0, s))),
        out_shape=shape_of((left.shape[1], right.shape[1]), BF16),
        compiler_params=params(),
        name="weight_grad",
    )(left, right)


def qkv_grad(me, left, right):
    rows = left.shape[0]
    return pl.pallas_call(
        qkv_grad_kernel,
        grid=(3,),
        in_specs=[SMEM, whole((rows, D)), column_blocks(rows)],
        out_specs=[ANY] * 2,
        out_shape=[shape_of((16, 48, QKV_HALF), BF16)] * 2,
        scratch_shapes=[pltpu.VMEM((D, 3 * D), BF16), pltpu.SemaphoreType.DMA((2,))],
        compiler_params=params(),
        cost_estimate=cost(12e9, 18e6),
        name="qkv_grad",
    )(me, left, right)


def up_grad(me, left, right):
    rows = left.shape[0]
    return pl.pallas_call(
        up_grad_kernel,
        grid=(4,),
        in_specs=[SMEM, whole((rows, D)), column_blocks(rows)],
        out_specs=[ANY] * 2,
        out_shape=[shape_of((16, 2, 48, D), BF16)] * 2,
        scratch_shapes=[pltpu.VMEM((4, D, D), BF16), pltpu.SemaphoreType.DMA((2,))],
        compiler_params=params(),
        cost_estimate=cost(14e9, 18e6),
        name="up_grad",
    )(me, left, right)


def down_grad(me, act, grad_down, mixed, grad_attn):
    rows = act.shape[0]
    return pl.pallas_call(
        down_grad_kernel,
        grid=(5,),
        in_specs=[
            SMEM, pl.BlockSpec((rows, D), lambda step: (0, jnp.minimum(step, 3))),
            whole((rows, D)), whole((rows, D)), whole((rows, D)),
        ],
        out_specs=[ANY] * 2,
        out_shape=[shape_of((16, 3, 48, D), BF16)] * 2,
        scratch_shapes=[
            pltpu.VMEM((4, 16, 48, D), BF16), pltpu.VMEM((2, D, 384), BF16),
            pltpu.SemaphoreType.DMA((2,)),
        ],
        compiler_params=params(),
        cost_estimate=cost(18e9, 22e6),
        name="down_grad",
    )(me, act, grad_down, mixed, grad_attn)


def swap(values, axis, mask):
    size = lax.axis_size(axis)
    return lax.ppermute(values, axis, [(at, at ^ mask) for at in range(size)])


def joined(stack, axis, mask):
    return jnp.concatenate([stack, swap(stack, axis, mask)], axis=0)


def added(one, two):
    return (one.astype(F32) + two.astype(F32)).astype(BF16)


def tied(*values):
    return lax.optimization_barrier(values)


def cut(values, row, col, rows, cols):
    return lax.dynamic_slice(values, (row, col), (rows, cols))


def body(
    tokens, teacher, valid_mask, attn_gain, attn_shift, qkv_weight, query_bias, value_bias,
    rel_pos_h, rel_pos_w, proj_weight, proj_bias, mlp_gain, mlp_shift, up_weight, up_bias,
    down_weight, down_bias,
):
    count = tokens.shape[0]
    parts = lax.axis_size("fsdp")
    copies = lax.axis_size("rep")
    in_pieces = (copies, parts) == (4, 8)
    rep_at, part_at = lax.axis_index("rep"), lax.axis_index("fsdp")
    device = rep_at * parts + part_at
    core, far_x = rep_at % 2, rep_at // 2
    me = jnp.stack([rep_at, part_at, device * count]).astype(jnp.int32)
    window_ids = device * count + jnp.arange(count, dtype=jnp.int32)
    place = window_ids % (SIDE * SIDE)
    cells = jnp.arange(SLOTS, dtype=jnp.int32)
    inside = ((place // SIDE)[:, None] * WIN + (cells // WIN)[None, :] < MAP) & (
        (place % SIDE)[:, None] * WIN + (cells % WIN)[None, :] < MAP
    )
    keep = inside.astype(F32)
    valid = valid_mask.astype(F32) * keep
    counted = jnp.sum(valid_mask * inside.astype(jnp.int32))
    aux = jnp.pad(jnp.stack([keep, valid], axis=-1), ((0, 0), (0, ROWS - SLOTS), (0, 0)))

    small = [attn_gain, attn_shift, query_bias, value_bias, proj_bias, mlp_gain, mlp_shift,
             down_bias, up_bias, rel_pos_h, rel_pos_w]
    places = jnp.asarray(key_places(), BF16)
    places_t = jnp.asarray(np.pad(key_places().T[0:32], ((0, 0), (0, LANES - ROWS))), BF16)
    counted = jnp.stack([counted // 128, counted % 128]).astype(BF16)
    loss_scale = 64.0 * D * count * copies * parts

    def noted(shape, *entries):
        total = jnp.zeros(shape, BF16)
        for values, row, col in entries:
            if values.ndim == 1:
                values = values[None]
            high, wide = values.shape
            total = total + jnp.pad(
                values, ((row, shape[0] - row - high), (col, shape[1] - col - wide))
            )
        return total

    if in_pieces:
        rect = cut(qkv_weight, far_x * 48, core * QKV_HALF, 48, QKV_HALF)
        notes = noted(
            (48, NOTES), *[(v, at, 0) for at, v in enumerate(small[0:4])],
            (rel_pos_h, 16, 0), (rel_pos_w, 16, 8),
        )
        rect = jnp.concatenate([rect, notes], axis=1)
        near = [rect] + [swap(rect, "fsdp", mask) for mask in (2, 4, 6)]
        up_rect = cut(up_weight, far_x * 48, core * 1536, 48, 1536)
        down_rect = cut(down_weight, core * 192 + far_x * 96, 0, 96, D)
        proj_rect = cut(proj_weight, far_x * 48, core * 384, 48, 384)
        notes = noted(
            (48, 384), *[(v, at, 0) for at, v in enumerate(small[4:8])], (up_bias, 4, 0),
            (counted, 5, 0),
        )
        rects = jnp.concatenate(
            [up_rect.reshape(48, 2, D).transpose(1, 0, 2), down_rect.reshape(2, 48, D),
             jnp.concatenate([proj_rect, notes], axis=1)[None]], axis=0,
        )
        *near, rects, aux = tied(*near, rects, aux)
        near_a, near_b = jnp.stack(near[0:2]), jnp.stack(near[2:4])
        from_a, from_b = swap(near_a, "fsdp", 1), swap(near_b, "rep", 2)
        planes = [rects] + [swap(rects, "fsdp", mask) for mask in (2, 4, 6)]
        near_a = jnp.concatenate([near_a, from_a])
        near_b = jnp.concatenate([near_b, from_b])
        far_a, far_b = swap(near_a, "rep", 2), swap(near_b, "fsdp", 1)
        own = (near_a, far_a, near_b, far_b)
        own = tied(*own)
        other = tuple(swap(v, "rep", 1) for v in own)
        vec, rel, rel_t = notes_of(me, own[0], own[2], own[3])
        vec, rel, rel_t, *other = tied(vec, rel, rel_t, *other)
        *state, w_qkv = attend(me, tokens, own + tuple(other), vec, rel, places, 0, STEPS[0])
        *planes, s0 = tied(*planes, state[0])
        state[0] = s0
        near_a, near_b = jnp.stack(planes[0:2]), jnp.stack(planes[2:4])
        near_a, near_b, *state = tied(near_a, near_b, *state)
        from_a, from_b = swap(near_a, "fsdp", 1), swap(near_b, "rep", 2)
        state = attend(me, tokens, w_qkv, vec, rel, places, STEPS[0], STEPS[1], tuple(state))
        from_a, from_b, *state = tied(from_a, from_b, *state)
        near_a = jnp.concatenate([near_a, from_a])
        near_b = jnp.concatenate([near_b, from_b])
        near_a, near_b, *state = tied(near_a, near_b, *state)
        far_a, far_b = swap(near_a, "rep", 2), swap(near_b, "fsdp", 1)
        core_a, core_b = swap(near_a, "rep", 1), swap(near_b, "rep", 1)
        state = attend(
            me, tokens, w_qkv, vec, rel, places, sum(STEPS[:2]), STEPS[2], tuple(state)
        )
        far_a, far_b, core_a, core_b, *state = tied(far_a, far_b, core_a, core_b, *state)
        own = (near_a, far_a, near_b, far_b)
        other = (core_a, swap(far_a, "rep", 1), core_b, swap(far_b, "rep", 1))
        state = attend(
            me, tokens, w_qkv, vec, rel, places, sum(STEPS[:3]), STEPS[3], tuple(state)
        )
        weights = own + other
    else:
        gather = lambda v: lax.all_gather(v, "fsdp", axis=0, tiled=True)
        w_qkv, w_proj = gather(qkv_weight), gather(proj_weight)
        packed = gather(jnp.concatenate([v.reshape(-1) for v in small] + [counted])[None])
        pieces, at = [], 0
        for v in small:
            pieces.append(packed[:, at : at + v.size])
            at += v.size
        rows = [p.reshape(1, -1).astype(F32) for p in pieces[:9]]
        offsets = rel_pos_h.shape[0]
        tables = [
            p.reshape(parts, offsets, -1).transpose(1, 0, 2).reshape(offsets, HEAD_DIM)
            for p in pieces[9:]
        ]
        gap = jnp.zeros((32 - offsets, HEAD_DIM), BF16)
        table = jnp.concatenate([tables[0], gap, tables[1], gap], axis=0)
        hole = jnp.zeros((HEAD_DIM, HEAD_DIM), BF16)
        rel = jnp.concatenate(
            [jnp.concatenate([table, hole], axis=1), jnp.concatenate([hole, table], axis=1)],
            axis=0,
        )
        rel_t = rel.T
        fill = jnp.zeros((4, D), F32)
        vec = jnp.concatenate(rows[0:4] + [fill])
        counts = lax.psum(jnp.sum(valid), ("rep", "fsdp")).reshape(1, 1)
        weights = (w_proj, gather(up_weight), gather(down_weight),
                   jnp.concatenate(rows[4:8] + [fill]), rows[8], counts)
        state = attend(me, tokens, w_qkv, vec, rel, places, 0, count)
    qkv, probs, mixed, first_in = state
    out, grad_hidden, grad_attn, second_in, act, grad_down, grad_up, sums2, up_sum, *rest = mlp(
        me, tokens, mixed, teacher, aux, weights, loss_scale * 2.0 / D, in_pieces
    )
    valid_total = sums2[5, 0]
    w_proj = rest[0] if in_pieces else w_proj
    flat = lambda v: v.reshape(count * ROWS, v.shape[-1])
    if in_pieces:
        keep_d, send_d = down_grad(me, flat(act), flat(grad_down), flat(mixed), flat(grad_attn))
        send_d, second_in = tied(send_d, second_in)
        from_d = swap(send_d, "rep", 1)
        keep_u, send_u = up_grad(me, flat(second_in), flat(grad_up))
        from_d, keep_u, send_u, grad_attn = tied(from_d, keep_u, send_u, grad_attn)
        from_u = swap(send_u, "rep", 1)
        back = (grad_attn, w_proj, qkv, probs, rel_t, places_t)
        ends = (0,) + tuple(sum(BACK_STEPS[: at + 1]) for at in range(3))
        state = attend_back(*back, 0, BACK_STEPS[0])
        both = lambda at, to: jnp.concatenate(
            [added(keep_u[at:to], from_u[at:to]), added(keep_d[at:to], from_d[at:to])], axis=1
        )
        from_u, *state = tied(from_u, *state)
        send_a, send_b = both(4, 8), both(12, 16)
        send_a, send_b, *state = tied(send_a, send_b, *state)
        from_a, from_b = swap(send_a, "rep", 2), swap(send_b, "fsdp", 1)
        state = attend_back(*back, ends[1], BACK_STEPS[1], tuple(state))
        from_a, from_b, *state = tied(from_a, from_b, *state)
        sum_a, sum_b = added(both(0, 4), from_a), added(both(8, 12), from_b)
        send_a, send_b = sum_a[2:4], sum_b[2:4]
        send_a, send_b, *state = tied(send_a, send_b, *state)
        from_a, from_b = swap(send_a, "fsdp", 1), swap(send_b, "rep", 2)
        state = attend_back(*back, ends[2], BACK_STEPS[2], tuple(state))
        from_a, from_b, *state = tied(from_a, from_b, *state)
        sum_a, sum_b = added(sum_a[0:2], from_a), added(sum_b[0:2], from_b)
        sends = (sum_a[0], sum_a[1], sum_b[0], sum_b[1])
        *sends, dqkv, rel_grad, qv_sum = tied(*sends, *state)
        from_z = [swap(v, "fsdp", mask) for v, mask in zip(sends[1:], (2, 4, 6))]
        keep, send = qkv_grad(me, flat(first_in), flat(dqkv))
        half = count // 2
        keep, send, dqkv = tied(keep, send, dqkv)
        from_core = swap(send, "rep", 1)
        state = input_back(me, dqkv, w_qkv, tokens, grad_hidden, vec, 0, half)
        from_core, *state = tied(from_core, *state)
        both = lambda at, to: added(keep[at:to], from_core[at:to])
        send_a, send_b = both(4, 8), both(12, 16)
        send_a, send_b, *state = tied(send_a, send_b, *state)
        from_a, from_b = swap(send_a, "rep", 2), swap(send_b, "fsdp", 1)
        input_grad, sums1 = input_back(
            me, dqkv, w_qkv, tokens, grad_hidden, vec, half, count - half, tuple(state)
        )
        *from_z, from_a, from_b, sums1 = tied(*from_z, from_a, from_b, sums1)
        sum_a, sum_b = added(both(0, 4), from_a), added(both(8, 12), from_b)
        from_a, from_b = swap(sum_a[2:4], "fsdp", 1), swap(sum_b[2:4], "rep", 2)
        own = sends[0].astype(F32)
        for v in from_z:
            own = own + v.astype(F32)
        own = own.astype(BF16)
        from_x = swap(own, "rep", 2)
        notes = pack(me, sums1, qv_sum, sums2, up_sum, rel_grad)
        from_a, from_b, notes = tied(from_a, from_b, notes)
        sum_a, sum_b = added(sum_a[0:2], from_a), added(sum_b[0:2], from_b)
        from_z = [swap(v, "fsdp", mask) for v, mask in
                  ((sum_a[1], 2), (sum_b[0], 4), (sum_b[1], 6))]
        notes = notes + swap(notes, "rep", 1)
        notes = notes + swap(notes, "rep", 2)
        notes = notes[0:4] + swap(notes[4:8], "fsdp", 1)
        d_up, d_down, d_proj = shard(
            me, (own, from_x, swap(own, "rep", 1), swap(from_x, "rep", 1)), True
        )
        mine = notes[0]
        for at, mask in ((1, 2), (2, 4), (3, 6)):
            mine = mine + swap(notes[at], "fsdp", mask)
        own = sum_a[0].astype(F32)
        for v in from_z:
            own = own + v.astype(F32)
        own = own.astype(BF16)
        from_x = swap(own, "rep", 2)
        (d_qkv,) = shard(
            me, (own, from_x, swap(own, "rep", 1), swap(from_x, "rep", 1)), False
        )
        lanes = tokens.shape[2] // parts
        vectors = [mine[at, 0:lanes] for at in range(8)]
        tables = [mine[0:27, 96 + 8 * at : 104 + 8 * at] for at in range(2)]
        outs = vectors + [mine[27:30].reshape(-1)] + tables
        loss = mine[30, 0] / (valid_total * D)
    else:
        scatter = lambda v: lax.psum(
            lax.psum_scatter(v, "fsdp", scatter_dimension=0, tiled=True), "rep"
        ).astype(F32)
        d_down = scatter(weight_grad(flat(act), flat(grad_down), True))
        d_up = scatter(weight_grad(flat(second_in), flat(grad_up)))
        d_proj = scatter(weight_grad(flat(mixed), flat(grad_attn)))
        back = (grad_attn, w_proj, qkv, probs, rel_t, places_t)
        dqkv, rel_grad, qv_sum = attend_back(*back, 0, count)
        d_qkv = scatter(weight_grad(flat(first_in), flat(dqkv)))
        input_grad, sums1 = input_back(me, dqkv, w_qkv, tokens, grad_hidden, vec, 0, count)
        offsets = rel_pos_h.shape[0]
        rel_sum = rel_grad[0:64, 0:64] + rel_grad[64:128, 64:128]
        vectors = [sums1[0], sums1[1], qv_sum[0], qv_sum[1], sums2[4], sums2[2], sums2[3],
                   sums2[1], up_sum[0]]
        own = jnp.concatenate(
            [v.reshape(parts, -1) for v in vectors]
            + [
                rel_sum[at : at + offsets].reshape(offsets, parts, -1).transpose(1, 0, 2)
                .reshape(parts, -1) for at in (0, 32)
            ]
            + [jnp.broadcast_to(jnp.sum(sums2[0]), (parts, 1))],
            axis=1,
        )
        mine = lax.dynamic_index_in_dim(
            lax.psum(own, ("rep", "fsdp")), part_at, 0, keepdims=False
        )
        outs, at = [], 0
        for v in small:
            outs.append(mine[at : at + v.size].reshape(v.shape))
            at += v.size
        loss = mine[at] / (valid_total * D)
    (g_gain1, g_shift1, g_qb, g_vb, g_pb, g_gain2, g_shift2, g_db, g_ub, g_rh, g_rw) = outs
    return (
        out, loss, input_grad, g_gain1, g_shift1, d_qkv, g_qb, g_vb, g_rh, g_rw, d_proj, g_pb,
        g_gain2, g_shift2, d_up, g_ub, d_down, g_db,
    )


def solution(mesh):
    windows = P(("rep", "fsdp"), None, None)
    vector = P("fsdp")
    matrix = P("fsdp", None)
    table = P(None, "fsdp")
    in_specs = (
        windows, windows, P(("rep", "fsdp"), None), vector, vector, matrix, vector, vector, table,
        table, matrix, vector, vector, vector, matrix, vector, matrix, vector,
    )
    out_specs = (windows, P(), windows) + in_specs[3:]
    return jax.shard_map(body, mesh=mesh, in_specs=in_specs, out_specs=out_specs, check_vma=False)
```

```python
import functools
import math

import jax
import jax.numpy as jnp
import numpy as np
from jax import lax
from jax.experimental import pallas as pl
from jax.experimental.pallas import tpu as pltpu
from jax.sharding import PartitionSpec as P

D = 768
HEADS = 12
HEAD_DIM = 64
MLP = 3072
WIN = 14
MAP = 64
SLOTS = WIN * WIN
ROWS = 208
LANES = 256
PAIRS = HEADS // 2
PAIR = 2 * HEAD_DIM
SIDE = (MAP + WIN - 1) // WIN
LN_EPS = 1e-06
SQRT_HALF = 0.7071067811865476
INV_ROOT_TAU = 0.3989422804014327
F32 = jnp.float32
BF16 = jnp.bfloat16
QKV_HALF = 3 * D // 2
NOTES = 128
STEPS = (3, 4, 1)
COST = 1e8
BACK_STEPS = (2, 4, 2)


def nn(left, right):
    return jnp.dot(left, right, preferred_element_type=F32)


def nt(left, right):
    return lax.dot_general(left, right, (((1,), (1,)), ((), ())), preferred_element_type=F32)


def tn(left, right):
    return lax.dot_general(left, right, (((0,), (0,)), ((), ())), preferred_element_type=F32)


def key_places():
    table = np.zeros((ROWS, HEAD_DIM), np.float32)
    for slot in range(SLOTS):
        for base in (0, 32):
            table[slot, base + WIN - 1 - slot // WIN] = 1.0
            table[slot, base + 16 + WIN - 1 - slot % WIN] = 1.0
    return table


def keep_column(base_ref, window):
    slot = lax.broadcasted_iota(jnp.int32, (ROWS, 1), 0)
    row = lax.shift_right_logical(slot * 4682, 16)
    col = slot - row * WIN
    place = lax.rem(base_ref[2] + window, SIDE * SIDE)
    place_row = lax.div(place, SIDE)
    place_col = place - place_row * SIDE
    inside = (slot < SLOTS) & (row + place_row * WIN < MAP) & (col + place_col * WIN < MAP)
    return inside.astype(F32)


def lane_places():
    slot = lax.broadcasted_iota(jnp.int32, (1, LANES), 1)
    row = lax.shift_right_logical(slot * 4682, 16)
    return row, slot - row * WIN


def norm_parts(values):
    mean = jnp.mean(values, axis=-1, keepdims=True)
    centred = values - mean
    inv_std = lax.rsqrt(jnp.mean(centred * centred, axis=-1, keepdims=True) + LN_EPS)
    return centred * inv_std, inv_std


def norm_grad(grad, scaled, inv_std, gain):
    grad_scaled = grad * gain
    first = jnp.mean(grad_scaled, axis=-1, keepdims=True)
    second = jnp.mean(grad_scaled * scaled, axis=-1, keepdims=True)
    return inv_std * (grad_scaled - first - scaled * second)


def up_by(values, amount):
    take = lambda bit: (amount & bit) != 0
    part = jnp.where(take(8), values[8:32], values[0:24])
    part = jnp.where(take(4), pltpu.roll(part, 20, 0), part)
    part = jnp.where(take(2), pltpu.roll(part, 22, 0), part)
    part = jnp.where(take(1), pltpu.roll(part, 23, 0), part)
    return part[0:16]


def down_by(values, amount):
    take = lambda bit: (amount & bit) != 0
    zeros = jnp.zeros((8, values.shape[1]), values.dtype)
    part = jnp.concatenate([values, zeros], axis=0)
    part = jnp.where(take(1), pltpu.roll(part, 1, 0), part)
    part = jnp.where(take(2), pltpu.roll(part, 2, 0), part)
    part = jnp.where(take(4), pltpu.roll(part, 4, 0), part)
    return jnp.where(
        take(8),
        jnp.concatenate([zeros, part], axis=0),
        jnp.concatenate([part, zeros], axis=0),
    )


def fill_rows(values):
    return jnp.concatenate(
        [values, jnp.zeros((LANES - ROWS,) + values.shape[1:], values.dtype)], axis=0
    )


def chunk_place(me_ref, index, far_y, along_y):
    mid, plane = index // 2, index % 2
    dist_x, dist_y = (far_y, mid) if along_y else (mid, far_y)
    plane = plane * 2 + (0 if along_y else 4)
    return (me_ref[0] // 2) ^ dist_x, me_ref[1] ^ (plane + dist_y)


ARRIVED = tuple((half, along_y, other) for other in (0, 1) for along_y in (True, False) for half in (0, 1))


def load_first(me_ref, parts, full, sem):
    core = me_ref[0] % 2
    for at, ref in enumerate(parts):
        along_y, other = at % 2 == 0, at // 2

        def start(index, carry, ref=ref, along_y=along_y, other=other):
            far_x, owner = chunk_place(me_ref, index % 4, index // 4, along_y)
            pltpu.make_async_copy(
                ref.at[index, :, pl.ds(0, QKV_HALF)],
                full.at[
                    pl.ds(pl.multiple_of(owner * 96 + far_x * 48, 16), 48),
                    pl.ds(pl.multiple_of((core ^ other) * QKV_HALF, 128), QKV_HALF),
                ],
                sem.at[0],
            ).start()
            return carry

        lax.fori_loop(0, 8, start, 0)
    pltpu.make_async_copy(full, full, sem.at[0]).wait()


def piece_place(me_ref, index):
    group, high, mid, plane = index // 8, (index // 4) % 2, (index // 2) % 2, index % 2
    dist_x = jnp.where(group == 0, high, mid)
    dist_y = jnp.where(group == 0, mid, high)
    return (me_ref[0] // 2) ^ dist_x, me_ref[1] ^ (group * 4 + plane * 2 + dist_y)


def piece_index(me_ref, far_x, owner):
    dist = me_ref[1] ^ owner
    dist_x = (me_ref[0] // 2) ^ far_x
    dist_y, plane, group = dist % 2, (dist // 2) % 2, dist // 4
    high = jnp.where(group == 0, dist_x, dist_y)
    mid = jnp.where(group == 0, dist_y, dist_x)
    return group * 8 + high * 4 + mid * 2 + plane


def spread_rows(notes_of, owner_of, width, total):
    row = lax.broadcasted_iota(jnp.int32, (128, total), 0)
    col = lax.broadcasted_iota(jnp.int32, (128, total), 1)
    acc = None
    for at in range(8):
        put = ((row < width) & (col == row + owner_of(at) * width)).astype(BF16)
        part = nn(notes_of(at), put)
        acc = part if acc is None else acc + part
    return acc


def notes_kernel(me_ref, a_ref, b_ref, c_ref, vec_ref, rel_ref, relt_ref):
    picks = [(a_ref, at, at % 2 * 2 + at // 2) for at in range(4)]
    picks += [(b_ref, at, 4 + at * 2) for at in range(2)] + [(c_ref, at, 5 + at * 2) for at in range(2)]
    owner_of = lambda at: me_ref[1] ^ picks[at][2]
    lanes = pl.ds(QKV_HALF, NOTES)
    vec_ref[...] = spread_rows(
        lambda at: picks[at][0][picks[at][1], 0:16, lanes], owner_of, 96, D
    )[0:8]
    row = lax.broadcasted_iota(jnp.int32, (128, 128), 0)
    col = lax.broadcasted_iota(jnp.int32, (128, 128), 1)
    halves = []
    for which in range(2):
        acc = jnp.zeros((32, 128), F32)
        for at in range(8):
            lane = row - 8 * which
            place = lane + owner_of(at) * 8
            put = ((lane >= 0) & (lane < 8) & ((col == place) | (col == place + 64))).astype(BF16)
            acc = acc + nn(picks[at][0][picks[at][1], 16:48, lanes], put)
        halves.append(acc)
    table = jnp.concatenate(halves * 2, axis=0)
    table = jnp.where((row < 64) == (col < 64), table, 0.0).astype(BF16)
    rel_ref[...] = table
    relt_ref[...] = table.T


def attend_kernel(*refs, first, pieces, earlier):
    base_ref, tok_ref = refs[0:2]
    at = 2 + max(pieces, 1)
    vec_ref, rel_ref, place_ref = refs[at : at + 3]
    at += 3 + earlier
    qkv_ref, prob_ref, mix_ref, fin_ref = refs[at : at + 4]
    if pieces:
        w_ref, x_ref, sem = refs[at + 4 :]

        @pl.when(pl.program_id(0) == 0)
        def _():
            load_first(base_ref, refs[2 : 2 + pieces], w_ref, sem)
    else:
        w_ref, x_ref = refs[2], refs[at + 4]
    keep = keep_column(base_ref, pl.program_id(0) + first)
    x_ref[pl.ds(192, 16), :] = jnp.zeros((16, D), F32)
    x_ref[pl.ds(0, SLOTS), :] = tok_ref[0].astype(F32)
    scaled, _ = norm_parts(x_ref[...])
    first_in = (keep * (scaled * vec_ref[0:1, :] + vec_ref[1:2, :])).astype(BF16)
    fin_ref[0] = first_in
    for part in range(3):
        cols = pl.ds(part * D, D)
        total = nn(first_in, w_ref[:, cols])
        if part != 1:
            total = total + vec_ref[2 + part // 2 : 3 + part // 2, :]
        qkv_ref[0, :, cols] = total.astype(BF16)
    lane_row, lane_col = lane_places()
    low_half = lax.broadcasted_iota(jnp.int32, (ROWS, PAIR), 1) < HEAD_DIM
    tail_rows = lax.broadcasted_iota(jnp.int32, (16, LANES), 0) + 192
    places = place_ref[...]
    place_pair = jnp.concatenate([places, places], axis=1)

    def one_pair(pair, carry):
        at = pl.multiple_of(pair * PAIR, PAIR)
        query = qkv_ref[0, :, pl.ds(at, PAIR)]
        keys = qkv_ref[0, :, pl.ds(pl.multiple_of(D + at, PAIR), PAIR)]
        values = qkv_ref[0, :, pl.ds(pl.multiple_of(2 * D + at, PAIR), PAIR)]
        query_t = fill_rows(query).T
        offsets = nn(rel_ref[...], query_t)
        mixed = []
        for head in range(2):
            mine = offsets[head * HEAD_DIM : (head + 1) * HEAD_DIM]
            along = jnp.concatenate(
                [up_by(mine[0:32], lane_row), up_by(mine[32:64], lane_col)], axis=0
            )
            high = along.astype(BF16)
            rest = (along - high.astype(F32)).astype(BF16)
            scaled_q = query_t[head * HEAD_DIM : (head + 1) * HEAD_DIM] * jnp.asarray(
                HEAD_DIM ** (-0.5), BF16
            )
            if head == 0:
                query_ext = jnp.concatenate([scaled_q, high, rest], axis=0)
                keys_ext = jnp.where(low_half, keys, place_pair)
            else:
                query_ext = jnp.concatenate([high, rest, scaled_q], axis=0)
                keys_ext = jnp.where(low_half, place_pair, keys)
            scores = nn(keys_ext, query_ext)
            scores = jnp.concatenate(
                [scores[0:192], jnp.where(tail_rows < SLOTS, scores[192:208], -1e30)], axis=0
            )
            peak = jnp.max(scores, axis=0, keepdims=True)
            expo = jnp.exp(scores - peak)
            total = jnp.sum(expo, axis=0, keepdims=True)
            probs = (expo * (1.0 / total)).astype(BF16)
            prob_ref[0, 2 * pair + head] = probs
            mixed.append(tn(probs, values)[0:ROWS].astype(BF16))
        mix_ref[0, :, pl.ds(at, PAIR)] = jnp.where(low_half, mixed[0], mixed[1])
        return carry

    lax.fori_loop(0, PAIRS, one_pair, 0, unroll=PAIRS)


def gelu_parts(pre):
    cumulative = 0.5 + 0.5 * lax.erf(pre * SQRT_HALF)
    bell = jnp.exp(pre * pre * (-0.5))
    return pre * cumulative, cumulative + pre * (bell * INV_ROOT_TAU)


def load_up(me_ref, pieces, up, proj, notes, sem):
    core = me_ref[0] % 2
    for array, (ref, (half, along_y, other)) in enumerate(zip(pieces, ARRIVED)):

        def start(index, carry, ref=ref, half=half, along_y=along_y, far_core=core ^ other, array=array):
            far_x, owner = chunk_place(me_ref, index, half, along_y)
            rows = pl.ds(pl.multiple_of(owner * 96 + far_x * 48, 16), 48)
            cols = pl.ds(pl.multiple_of(far_core * 384, 128), 384)
            pltpu.make_async_copy(
                ref.at[index, 2, :, pl.ds(0, 384)], proj.at[rows, cols], sem.at[1]
            ).start()
            pltpu.make_async_copy(
                ref.at[index, 2, pl.ds(0, 16), pl.ds(384, 384)], notes.at[array * 4 + index], sem.at[2]
            ).start()
            for block in range(2):
                cols = pl.ds(pl.multiple_of(far_core * 1536 + block * D, 128), D)
                pltpu.make_async_copy(ref.at[index, block], up.at[rows, cols], sem.at[0]).start()
            return carry

        lax.fori_loop(0, 4, start, 0)
    for at, full in ((2, notes), (1, proj), (0, up)):
        pltpu.make_async_copy(full, full, sem.at[at]).wait()


def load_down(me_ref, pieces, down, sem):
    core = me_ref[0] % 2
    for ref, (half, along_y, other) in zip(pieces, ARRIVED):

        def start(index, carry, ref=ref, half=half, along_y=along_y, far_core=core ^ other):
            far_x, owner = chunk_place(me_ref, index, half, along_y)
            place = owner * 8 + far_core * 4 + far_x * 2
            pltpu.make_async_copy(ref.at[index], down.at[pl.ds(place, 2)], sem.at[0]).start()
            return carry

        lax.fori_loop(0, 4, start, 0)
    pltpu.make_async_copy(down, down, sem.at[0]).wait()


def up_kernel(*refs, group, pieces):
    rows = group * ROWS
    me_ref, tok_ref, mix_ref, keep_ref = refs[0:4]
    at = 4 + (pieces or 4)
    hid_ref, si_ref, act_ref, slope_ref = refs[at : at + 4]
    at += 4
    if pieces:
        up_ref, wp_ref, vec_ref, ub_ref, total_ref, t_ref, notes, sem = refs[at:]

        @pl.when(pl.program_id(0) == 0)
        def _():
            load_up(me_ref, refs[4 : 4 + pieces], up_ref, wp_ref, notes, sem)
            picks = [(at, at % 2 * 2 + at // 2) for at in range(4)]
            picks += [(8 + at, 4 + at * 2) for at in range(2)] + [(12 + at, 5 + at * 2) for at in range(2)]
            owner_of = lambda at: me_ref[1] ^ picks[at][1]
            vec_ref[...] = spread_rows(
                lambda at: notes[picks[at][0], :, 0:128], owner_of, 96, D
            )[0:8]
            for at in range(8):
                lanes = pl.ds(pl.multiple_of(owner_of(at) * 384, 128), 384)
                ub_ref[:, lanes] = notes[picks[at][0], 0:16, :].astype(F32)[4:5, :]
            counts = notes[0].astype(F32)
            for at in range(1, 32):
                counts = counts + notes[at].astype(F32)
            counts = counts[5:6, 0:128]
            lane = lax.broadcasted_iota(jnp.int32, (1, 128), 1)
            weight = jnp.where(lane == 0, 128.0, jnp.where(lane == 1, 1.0, 0.0))
            total_ref[...] = jnp.broadcast_to(
                jnp.sum(counts * weight, axis=1, keepdims=True), (1, 128)
            )
    else:
        wp_ref, up_ref, vec_ref, ub_ref = refs[4:8]
        t_ref = refs[at]
    pb_row, gain_row, shift_row = [vec_ref[at : at + 1, :] for at in range(3)]
    keep = keep_ref[...].reshape(rows, 2)[:, 0:1]
    for at in range(group):
        t_ref[at, pl.ds(192, 16), :] = jnp.zeros((16, D), F32)
        t_ref[at, pl.ds(0, SLOTS), :] = tok_ref[at].astype(F32)
    attn_out = nn(mix_ref[...].reshape(rows, D), wp_ref[...]) + pb_row
    hidden = keep * (t_ref[...].reshape(rows, D) + attn_out)
    hid_ref[...] = hidden.reshape(group, ROWS, D)
    scaled, _ = norm_parts(hidden)
    second_in = (scaled * gain_row + shift_row).astype(BF16)
    si_ref[...] = second_in.reshape(group, ROWS, D)
    for part in range(MLP // D):
        cols = slice(part * D, part * D + D)
        act, slope = gelu_parts(nn(second_in, up_ref[:, cols]) + ub_ref[:, cols])
        slope_ref[:, :, cols] = slope.astype(BF16).reshape(group, ROWS, D)
        act_ref[:, :, cols] = act.astype(BF16).reshape(group, ROWS, D)


def down_kernel(*refs, group, pieces, scale):
    step = pl.program_id(0)
    rows = group * ROWS
    me_ref, hid_ref, act_ref, slope_ref, teach_ref, aux_ref, up_ref, vec_ref, total_ref = refs[0:9]
    at = 9 + (pieces or 1)
    out_ref, gh_ref, ga_ref, gd_ref, gu_ref, sums_ref, usum_ref, t_ref = refs[at : at + 8]
    if pieces:
        down3_ref, sem = refs[at + 8 :]

        @pl.when(step == 0)
        def _():
            load_down(me_ref, refs[9 : 9 + pieces], down3_ref, sem)

        down_rows = lambda part: down3_ref[pl.ds(part * 16, 16)].reshape(D, D)
    else:
        down_rows = lambda part: refs[9][pl.ds(part * D, D), :]

    @pl.when(step == 0)
    def _():
        sums_ref[...] = jnp.zeros_like(sums_ref)
        usum_ref[...] = jnp.zeros_like(usum_ref)

    gain_row, db_row = vec_ref[1:2, :], vec_ref[3:4, :]
    coef = scale / total_ref[:, 0:1]
    aux = aux_ref[...].reshape(rows, 2)
    keep, valid = aux[:, 0:1], aux[:, 1:2]
    hidden = hid_ref[...].reshape(rows, D)
    down = db_row
    for part in range(MLP // D):
        cols = slice(part * D, part * D + D)
        down = down + nn(act_ref[:, :, cols].reshape(rows, D), down_rows(part))
    final = keep * (hidden + down)
    for at in range(group):
        out_ref[at] = final[at * ROWS : at * ROWS + SLOTS].astype(BF16)
        t_ref[at, pl.ds(192, 16), :] = jnp.zeros((16, D), F32)
        t_ref[at, pl.ds(0, SLOTS), :] = teach_ref[at].astype(F32)
    error = final - t_ref[...].reshape(rows, D)
    weighted = valid * error
    grad_final = coef * weighted
    grad_down = grad_final.astype(BF16)
    gd_ref[...] = grad_down.reshape(group, ROWS, D)
    sums_ref[0:1, :] += jnp.sum(weighted * error, axis=0, keepdims=True)
    sums_ref[1:2, :] += jnp.sum(grad_down.astype(F32), axis=0, keepdims=True)
    for part in range(MLP // D):
        cols = slice(part * D, part * D + D)
        slope = slope_ref[:, :, cols].reshape(rows, D).astype(F32)
        grad_up = (nt(grad_down, down_rows(part)) * slope).astype(BF16)
        gu_ref[:, :, cols] = grad_up.reshape(group, ROWS, D)
        usum_ref[:, cols] += jnp.sum(grad_up.astype(F32), axis=0, keepdims=True)
    grad_second = nt(gu_ref[...].reshape(rows, MLP), up_ref[...])
    scaled, inv_std = norm_parts(hidden)
    sums_ref[2:3, :] += jnp.sum(grad_second * scaled, axis=0, keepdims=True)
    sums_ref[3:4, :] += jnp.sum(grad_second, axis=0, keepdims=True)
    grad_hidden = keep * (grad_final + norm_grad(grad_second, scaled, inv_std, gain_row))
    gh_ref[...] = grad_hidden.reshape(group, ROWS, D)
    grad_attn = grad_hidden.astype(BF16)
    ga_ref[...] = grad_attn.reshape(group, ROWS, D)
    sums_ref[4:5, :] += jnp.sum(grad_attn.astype(F32), axis=0, keepdims=True)


def attend_back_kernel(*refs, earlier):
    ga_ref, wp_ref, qkv_ref, prob_ref, relt_ref, placet_ref = refs[0:6]
    dqkv_ref, rg_ref, qsum_ref, gm_ref = refs[6 + earlier :]

    @pl.when(pl.program_id(0) == 0)
    def _():
        rg_ref[...] = refs[7][...] if earlier else jnp.zeros_like(rg_ref)
        qsum_ref[...] = refs[8][...] if earlier else jnp.zeros_like(qsum_ref)
        gm_ref[pl.ds(ROWS, LANES - ROWS), :] = jnp.zeros((LANES - ROWS, D), BF16)

    gm_ref[pl.ds(0, ROWS), :] = nt(ga_ref[0], wp_ref[...]).astype(BF16)
    lane_row, lane_col = lane_places()
    low_half = lax.broadcasted_iota(jnp.int32, (ROWS, PAIR), 1) < HEAD_DIM
    low_full = lax.broadcasted_iota(jnp.int32, (LANES, PAIR), 1) < HEAD_DIM
    blank = jnp.zeros((), BF16)
    scale = HEAD_DIM ** (-0.5)

    def one_pair(pair, carry):
        at = pl.multiple_of(pair * PAIR, PAIR)
        q_at = pl.ds(at, PAIR)
        k_at = pl.ds(pl.multiple_of(D + at, PAIR), PAIR)
        v_at = pl.ds(pl.multiple_of(2 * D + at, PAIR), PAIR)
        query = fill_rows(qkv_ref[0, :, q_at])
        keys_t = fill_rows(qkv_ref[0, :, k_at]).T
        values = qkv_ref[0, :, v_at]
        grad_out = gm_ref[:, q_at]
        stacked = jnp.concatenate(
            [jnp.where(low_half, values, blank), jnp.where(low_half, blank, values)], axis=0
        )
        grad_probs = nt(stacked, grad_out)
        grad_values = jnp.zeros((ROWS, PAIR), F32)
        grad_keys = jnp.zeros((ROWS, PAIR), F32)
        spread, plain = [], []
        for head in range(2):
            own = (lambda full: jnp.where(low_full, full, blank)) if head == 0 else (
                lambda full: jnp.where(low_full, blank, full)
            )
            low = prob_ref[0, 2 * pair + head]
            probs = low.astype(F32)
            grad_p = grad_probs[head * ROWS : (head + 1) * ROWS]
            row_dot = jnp.sum(probs * grad_p, axis=0, keepdims=True)
            grad_score = (probs * (grad_p - row_dot)).astype(BF16)
            grad_values = grad_values + nn(low, own(grad_out))
            grad_keys = grad_keys + nn(grad_score, own(query))
            keys_ext = jnp.concatenate(
                [keys_t[head * HEAD_DIM : (head + 1) * HEAD_DIM], placet_ref[...]], axis=0
            )
            grad_ext = nn(keys_ext, fill_rows(grad_score))
            plain.append(grad_ext[0:64])
            spread.append(down_by(grad_ext[64:80], lane_row))
            spread.append(down_by(grad_ext[80:96], lane_col))
        spread = jnp.concatenate(spread, axis=0).astype(BF16)
        grad_query = jnp.concatenate(plain, axis=0) * scale + nn(relt_ref[...], spread)
        rg_ref[...] += nn(spread, query)
        grad_query = grad_query.astype(BF16).T[0:ROWS]
        grad_keys = (grad_keys * scale).astype(BF16)
        grad_values = grad_values.astype(BF16)
        dqkv_ref[0, :, q_at] = grad_query
        dqkv_ref[0, :, k_at] = grad_keys
        dqkv_ref[0, :, v_at] = grad_values
        qsum_ref[0:1, q_at] += jnp.sum(grad_query.astype(F32), axis=0, keepdims=True)
        qsum_ref[1:2, q_at] += jnp.sum(grad_values.astype(F32), axis=0, keepdims=True)
        return carry

    lax.fori_loop(0, PAIRS, one_pair, 0, unroll=PAIRS)


def input_kernel(
    base_ref, dqkv_ref, w_ref, tok_ref, gh_ref, vec_ref, *refs, group, first, earlier
):
    step = pl.program_id(0)
    out_ref, sums_ref, x_ref = refs[earlier:]

    @pl.when(step == 0)
    def _():
        sums_ref[...] = refs[1][...] if earlier else jnp.zeros_like(sums_ref)

    for at in range(group):
        keep = keep_column(base_ref, first + step * group + at)
        grad_first = keep * nt(dqkv_ref[at], w_ref[...])
        x_ref[pl.ds(192, 16), :] = jnp.zeros((16, D), F32)
        x_ref[pl.ds(0, SLOTS), :] = tok_ref[at].astype(F32)
        scaled, inv_std = norm_parts(x_ref[...])
        sums_ref[0:1, :] += jnp.sum(grad_first * scaled, axis=0, keepdims=True)
        sums_ref[1:2, :] += jnp.sum(grad_first, axis=0, keepdims=True)
        total = gh_ref[at] + norm_grad(grad_first, scaled, inv_std, vec_ref[0:1, :])
        out_ref[at] = total[0:SLOTS]


def weight_grad_kernel(*refs):
    left_ref, right_ref, out_ref = refs
    out_ref[...] = tn(left_ref[...], right_ref[...]).astype(BF16)


def qkv_grad_kernel(me_ref, left_ref, right_ref, keep_ref, send_ref, full, sem):
    step = pl.program_id(0)
    cols = pl.ds(pl.multiple_of(step * D, D), D)
    full[:, cols] = tn(left_ref[...], right_ref[...]).astype(BF16)

    @pl.when(step == pl.num_programs(0) - 1)
    def _():
        core = me_ref[0] % 2
        for at, (ref, far_core) in enumerate(((send_ref, 1 - core), (keep_ref, core))):

            def start(index, carry, ref=ref, far_core=far_core, at=at):
                far_x, owner = piece_place(me_ref, index)
                pltpu.make_async_copy(
                    full.at[
                        pl.ds(pl.multiple_of(owner * 96 + far_x * 48, 16), 48),
                        pl.ds(pl.multiple_of(far_core * QKV_HALF, 128), QKV_HALF),
                    ],
                    ref.at[index],
                    sem.at[at],
                ).start()
                return carry

            lax.fori_loop(0, 16, start, 0)
        for at, ref in enumerate((send_ref, keep_ref)):
            pltpu.make_async_copy(ref, ref, sem.at[at]).wait()


def up_grad_kernel(me_ref, left_ref, right_ref, out_ref, full, sem):
    step = pl.program_id(0)
    full[step] = tn(left_ref[...], right_ref[...]).astype(BF16)
    cols = pl.ds(pl.multiple_of((step % 2) * 384, 128), 384)

    def start(index, carry):
        far_x, owner = piece_place(me_ref, index)
        rows = pl.ds(pl.multiple_of(owner * 96 + far_x * 48, 16), 48)
        pltpu.make_async_copy(
            full.at[step, rows], out_ref.at[index, step // 2, :, cols], sem.at[0]
        ).start()
        return carry

    lax.fori_loop(0, 16, start, 0)

    @pl.when(step == pl.num_programs(0) - 1)
    def _():
        pltpu.make_async_copy(out_ref, out_ref, sem.at[0]).wait()


def down_grad_kernel(
    me_ref, act_ref, gd_ref, mix_any, ga_any, keep_ref, send_ref, full, half, mix_ref, ga_ref, sem
):
    step = pl.program_id(0)
    last = pl.num_programs(0) - 1
    fetches = [
        pltpu.make_async_copy(mix_any, mix_ref, sem.at[2]),
        pltpu.make_async_copy(ga_any, ga_ref, sem.at[3]),
    ]

    @pl.when(step == 0)
    def _():
        for fetch in fetches:
            fetch.start()

    @pl.when(step < last)
    def _():
        full[step] = tn(act_ref[...], gd_ref[...]).astype(BF16).reshape(8, 48, D)

    @pl.when(step == last)
    def _():
        for fetch in fetches:
            fetch.wait()
        total = tn(mix_ref[...], ga_ref[...]).astype(BF16)
        for core in range(2):
            half[core] = total[:, core * 384 : core * 384 + 384]

    core = me_ref[0] % 2
    for ref, far_core, at in ((keep_ref, core, 0), (send_ref, 1 - core, 1)):

        def start_proj(index, carry, ref=ref, far_core=far_core, at=at):
            far_x, owner = piece_place(me_ref, index)
            rows = pl.ds(pl.multiple_of(owner * 96 + far_x * 48, 16), 48)
            for col in (0, 384):
                pltpu.make_async_copy(
                    half.at[far_core, rows], ref.at[index, 2, :, pl.ds(col, 384)], sem.at[at]
                ).start()
            return carry

        @pl.when(step < last)
        def _(ref=ref, far_core=far_core, at=at):
            for far_x in range(2):
                pltpu.make_async_copy(
                    full.at[step, pl.ds(far_core * 4 + far_x * 2, 2)],
                    ref.at[piece_index(me_ref, far_x, step), pl.ds(0, 2)],
                    sem.at[at],
                ).start()

        @pl.when(step == last)
        def _(start_proj=start_proj):
            lax.fori_loop(0, 16, start_proj, 0)

    @pl.when(step == last)
    def _():
        pltpu.make_async_copy(keep_ref, keep_ref, sem.at[0]).wait()
        pltpu.make_async_copy(send_ref, send_ref, sem.at[1]).wait()


def whole(shape):
    zeros = (0,) * len(shape)
    return pl.BlockSpec(shape, lambda *_: zeros, pipeline_mode=pl.Buffered(1))


def whole_out(shape):
    zeros = (0,) * len(shape)
    return pl.BlockSpec(shape, lambda *_: zeros)


def windows_from(first, shape):
    tail = (0,) * (len(shape) - 1)
    return pl.BlockSpec(shape, lambda step: (step + first,) + tail)


SMEM = pl.BlockSpec(memory_space=pltpu.SMEM)
ANY = pl.BlockSpec(memory_space=pl.ANY)


def params(mebibytes=32):
    return pltpu.CompilerParams(
        vmem_limit_bytes=mebibytes * 1024 * 1024, dimension_semantics=("arbitrary",)
    )


def shape_of(shape, dtype):
    return jax.ShapeDtypeStruct(shape, dtype)


def cost(flops, moved):
    return pl.CostEstimate(flops=int(flops), bytes_accessed=int(moved), transcendentals=0)


def notes_of(me, near, far_x, far_y):
    return pl.pallas_call(
        notes_kernel,
        in_specs=[SMEM] + [whole(v.shape) for v in (near, far_x, far_y)],
        out_specs=[whole_out((8, D)), whole_out((PAIR, PAIR)), whole_out((PAIR, PAIR))],
        out_shape=[shape_of((8, D), F32)] + [shape_of((PAIR, PAIR), BF16)] * 2,
        grid=(1,),
        compiler_params=params(),
        cost_estimate=cost(COST, 1e5),
        name="notes",
    )(me, near, far_x, far_y)


def attend(me, tokens, weight, vec, rel, places, first, number, earlier=()):
    count = tokens.shape[0]
    win = lambda shape: windows_from(first, shape)
    pieces = len(weight) if isinstance(weight, tuple) else 0
    weights = weight if pieces else (weight,)
    weight_specs = [ANY] * pieces if pieces else [whole((D, 3 * D))]
    out_specs = [win((1, ROWS, 3 * D)), win((1, HEADS, ROWS, LANES)), win((1, ROWS, D)),
                 win((1, ROWS, D))]
    out_shape = [
        shape_of((count, ROWS, 3 * D), BF16), shape_of((count, HEADS, ROWS, LANES), BF16),
        shape_of((count, ROWS, D), BF16), shape_of((count, ROWS, D), BF16),
    ]
    scratch = [pltpu.VMEM((ROWS, D), F32)]
    if pieces:
        out_specs.append(whole_out((D, 3 * D)))
        out_shape.append(shape_of((D, 3 * D), BF16))
        scratch.append(pltpu.SemaphoreType.DMA((1,)))
    inputs = 5 + len(weights)
    return pl.pallas_call(
        functools.partial(attend_kernel, first=first, pieces=pieces, earlier=len(earlier)),
        grid=(number,),
        in_specs=[
            SMEM, win((1, SLOTS, D)), *weight_specs, whole((8, D)),
            whole((PAIR, PAIR)), whole((ROWS, HEAD_DIM)), *([ANY] * len(earlier)),
        ],
        out_specs=out_specs,
        out_shape=out_shape,
        scratch_shapes=scratch,
        input_output_aliases={inputs + at: at for at in range(len(earlier))},
        compiler_params=params(),
        cost_estimate=cost(COST, 1e5),
        name="attend",
    )(me, tokens, *weights, vec, rel, places, *earlier)


def mlp_up(me, tokens, mixed, aux, weights, chunked):
    count = tokens.shape[0]
    group = math.gcd(count, 2)
    win = lambda width: windows_from(0, (group, ROWS, width))
    arr = lambda width, dtype: shape_of((count, ROWS, width), dtype)
    pieces = len(weights) if chunked else 0
    out_specs = [win(D), win(D), win(MLP), win(MLP)]
    out_shape = [arr(D, F32), arr(D, BF16), arr(MLP, BF16), arr(MLP, BF16)]
    scratch = [pltpu.VMEM((group, ROWS, D), F32)]
    if pieces:
        shapes = [((D, MLP), BF16), ((D, D), BF16), ((8, D), F32), ((1, MLP), F32), ((1, 128), F32)]
        out_specs += [whole_out(s) for s, _ in shapes]
        out_shape += [shape_of(s, t) for s, t in shapes]
        scratch += [pltpu.VMEM((32, 16, 384), BF16), pltpu.SemaphoreType.DMA((3,))]
    return pl.pallas_call(
        functools.partial(up_kernel, group=group, pieces=pieces),
        grid=(count // group,),
        in_specs=[SMEM, windows_from(0, (group, SLOTS, D)), win(D), win(2)]
        + ([ANY] * pieces if pieces else [whole(v.shape) for v in weights]),
        out_specs=out_specs,
        out_shape=out_shape,
        scratch_shapes=scratch,
        compiler_params=params(44),
        cost_estimate=cost(COST * count, 1e5),
        name="mlp_up",
    )(me, tokens, mixed, aux, *weights)


def mlp_down(me, hidden, act, slope, teacher, aux, up, vec, total, weights, scale, chunked):
    count = hidden.shape[0]
    group = math.gcd(count, 2)
    win = lambda width: windows_from(0, (group, ROWS, width))
    plain = windows_from(0, (group, SLOTS, D))
    arr = lambda width, dtype: shape_of((count, ROWS, width), dtype)
    pieces = len(weights) if chunked else 0
    scratch = [pltpu.VMEM((group, ROWS, D), F32)]
    if pieces:
        scratch += [pltpu.VMEM((MLP // 48, 48, D), BF16), pltpu.SemaphoreType.DMA((1,))]
    return pl.pallas_call(
        functools.partial(down_kernel, group=group, pieces=pieces, scale=scale),
        grid=(count // group,),
        in_specs=[SMEM, win(D), win(MLP), win(MLP), plain, win(2), whole((D, MLP)), whole((8, D)),
                  whole((1, 128))]
        + ([ANY] * pieces if pieces else [whole(v.shape) for v in weights]),
        out_specs=[plain, win(D), win(D), win(D), win(MLP), whole_out((5, D)), whole_out((1, MLP))],
        out_shape=[
            shape_of((count, SLOTS, D), BF16), arr(D, F32), arr(D, BF16), arr(D, BF16),
            arr(MLP, BF16), shape_of((5, D), F32), shape_of((1, MLP), F32),
        ],
        scratch_shapes=scratch,
        compiler_params=params(48),
        cost_estimate=cost(COST * count, 1e5),
        name="mlp_down",
    )(me, hidden, act, slope, teacher, aux, up, vec, total, *weights)


def attend_back(grad_attn, proj, qkv, probs, rel_t, places_t, first, number, earlier=()):
    count = grad_attn.shape[0]
    win = lambda shape: windows_from(first, shape)
    before = [ANY, whole((PAIR, PAIR)), whole((2, D))] if earlier else []
    return pl.pallas_call(
        functools.partial(attend_back_kernel, earlier=len(earlier)),
        grid=(number,),
        in_specs=[
            win((1, ROWS, D)), whole((D, D)), win((1, ROWS, 3 * D)), win((1, HEADS, ROWS, LANES)),
            whole((PAIR, PAIR)), whole((32, LANES)), *before,
        ],
        out_specs=[win((1, ROWS, 3 * D)), whole_out((PAIR, PAIR)), whole_out((2, D))],
        out_shape=[
            shape_of((count, ROWS, 3 * D), BF16), shape_of((PAIR, PAIR), F32),
            shape_of((2, D), F32),
        ],
        scratch_shapes=[pltpu.VMEM((LANES, D), BF16)],
        input_output_aliases={6: 0} if earlier else {},
        compiler_params=params(),
        cost_estimate=cost(COST, 1e5),
        name="attend_back",
    )(grad_attn, proj, qkv, probs, rel_t, places_t, *earlier)


def input_back(me, dqkv, weight, tokens, grad_hidden, vec, first, number, earlier=()):
    count = tokens.shape[0]
    group = math.gcd(math.gcd(first, number), 2)
    win = lambda shape: windows_from(first // group, shape)
    before = [ANY, whole((2, D))] if earlier else []
    return pl.pallas_call(
        functools.partial(input_kernel, group=group, first=first, earlier=len(earlier)),
        grid=(number // group,),
        in_specs=[
            SMEM, win((group, ROWS, 3 * D)), whole((D, 3 * D)), win((group, SLOTS, D)),
            win((group, ROWS, D)), whole((8, D)), *before,
        ],
        out_specs=[win((group, SLOTS, D)), whole_out((2, D))],
        out_shape=[shape_of((count, SLOTS, D), F32), shape_of((2, D), F32)],
        scratch_shapes=[pltpu.VMEM((ROWS, D), F32)],
        input_output_aliases={6: 0} if earlier else {},
        compiler_params=params(),
        cost_estimate=cost(COST, 1e5),
        name="input_back",
    )(me, dqkv, weight, tokens, grad_hidden, vec, *earlier)


def pick(left, right):
    return jnp.dot(left, right, preferred_element_type=F32, precision=lax.Precision.HIGHEST)


def pack_kernel(me_ref, one_ref, qv_ref, two_ref, up_ref, rel_ref, out_ref):
    vectors = jnp.concatenate(
        [one_ref[0:2], qv_ref[0:2], two_ref[4:5], two_ref[2:4], two_ref[1:2]], axis=0
    )
    error = jnp.sum(two_ref[0:1, :], axis=1, keepdims=True)
    tables = rel_ref[0:64, 0:64] + rel_ref[64:128, 64:128]
    row = lax.broadcasted_iota(jnp.int32, (D, 128), 0)
    col = lax.broadcasted_iota(jnp.int32, (D, 128), 1)
    small_row = lax.broadcasted_iota(jnp.int32, (64, 128), 0)
    small_col = lax.broadcasted_iota(jnp.int32, (64, 128), 1)
    for at in range(8):
        owner = me_ref[1] ^ ((at % 4) * 2 + at // 4)
        own = pick(vectors, ((col < 96) & (row == col + owner * 96)).astype(F32))
        total = jnp.concatenate([own, jnp.zeros((24, 128), F32)], axis=0)
        for which in range(2):
            lane = small_col - 96 - 8 * which
            put = ((lane >= 0) & (lane < 8) & (small_row == lane + owner * 8)).astype(F32)
            total = total + pick(tables[32 * which : 32 * which + 32], put)
        out_ref[at] = total
        for part in range(3):
            lanes = pl.ds(pl.multiple_of(owner * 384 + part * 128, 128), 128)
            out_ref[at, 27 + part : 28 + part, :] = up_ref[:, lanes]
        out_ref[at, 30:31, :] = jnp.broadcast_to(error, (1, 128))


def pack(me, *sums):
    return pl.pallas_call(
        pack_kernel,
        grid=(1,),
        in_specs=[SMEM] + [whole(v.shape) for v in sums],
        out_specs=whole_out((8, 32, 128)),
        out_shape=shape_of((8, 32, 128), F32),
        compiler_params=params(),
        cost_estimate=cost(COST, 1e5),
        name="pack",
    )(me, *sums)


def shard_kernel(me_ref, *refs, split):
    quarters, outs = refs[0:4], refs[4:]
    core, far_x = me_ref[0] % 2, me_ref[0] // 2
    for at, ref in enumerate(quarters):
        this_core, this_x = core ^ (at // 2), far_x ^ (at % 2)
        rows = pl.ds(pl.multiple_of(this_x * 48, 16), 48)
        if not split:
            cols = pl.ds(pl.multiple_of(this_core * QKV_HALF, 128), QKV_HALF)
            outs[0][rows, cols] = ref[...].astype(F32)
            continue
        up_ref, down_ref, proj_ref = outs
        for block in range(2):
            cols = pl.ds(pl.multiple_of(this_core * 1536 + block * D, 128), D)
            up_ref[rows, cols] = ref[block].astype(F32)
            at_row = this_core * 192 + this_x * 96 + block * 48
            down_ref[pl.ds(pl.multiple_of(at_row, 16), 48), :] = ref[2 + block].astype(F32)
        cols = pl.ds(pl.multiple_of(this_core * 384, 128), 384)
        proj_ref[rows, cols] = ref[4, :, 0:384].astype(F32)


def shard(me, quarters, split):
    shapes = [(96, MLP), (384, D), (96, D)] if split else [(96, 3 * D)]
    return pl.pallas_call(
        functools.partial(shard_kernel, split=split),
        grid=(1,),
        in_specs=[SMEM] + [whole(v.shape) for v in quarters],
        out_specs=[whole_out(s) for s in shapes],
        out_shape=[shape_of(s, F32) for s in shapes],
        compiler_params=params(),
        cost_estimate=cost(COST, 1e5),
        name="shard",
    )(me, *quarters)


def column_blocks(rows):
    return pl.BlockSpec((rows, D), lambda step: (0, step))


def weight_grad(left, right, by_rows=False):
    rows = left.shape[0]
    blocks = (left if by_rows else right).shape[1] // D
    moving, still = column_blocks(rows), whole((rows, D))
    return pl.pallas_call(
        weight_grad_kernel,
        grid=(blocks,),
        in_specs=[moving, still] if by_rows else [still, moving],
        out_specs=pl.BlockSpec((D, D), (lambda s: (s, 0)) if by_rows else (lambda s: (0, s))),
        out_shape=shape_of((left.shape[1], right.shape[1]), BF16),
        compiler_params=params(44),
        name="weight_grad",
    )(left, right)


def qkv_grad(me, left, right):
    rows = left.shape[0]
    return pl.pallas_call(
        qkv_grad_kernel,
        grid=(3,),
        in_specs=[SMEM, whole((rows, D)), column_blocks(rows)],
        out_specs=[ANY] * 2,
        out_shape=[shape_of((16, 48, QKV_HALF), BF16)] * 2,
        scratch_shapes=[pltpu.VMEM((D, 3 * D), BF16), pltpu.SemaphoreType.DMA((2,))],
        compiler_params=params(),
        cost_estimate=cost(COST, 1e5),
        name="qkv_grad",
    )(me, left, right)


def up_grad(me, left, right, other):
    rows = left.shape[0]
    return pl.pallas_call(
        up_grad_kernel,
        grid_spec=pltpu.PrefetchScalarGridSpec(
            num_scalar_prefetch=1,
            grid=(4,),
            in_specs=[
                whole((rows, D)),
                pl.BlockSpec((rows, 384), lambda step, me: (0, ((me[0] % 2) ^ other) * 4 + step)),
            ],
            out_specs=ANY,
            scratch_shapes=[pltpu.VMEM((4, D, 384), BF16), pltpu.SemaphoreType.DMA((1,))],
        ),
        out_shape=shape_of((16, 2, 48, D), BF16),
        compiler_params=params(),
        cost_estimate=cost(COST, 1e5),
        name="up_grad",
    )(me, left, right)


def down_grad(me, act, grad_down, mixed, grad_attn):
    rows = act.shape[0]
    return pl.pallas_call(
        down_grad_kernel,
        grid=(9,),
        in_specs=[
            SMEM, pl.BlockSpec((rows, 384), lambda step: (0, jnp.minimum(step, 7))),
            whole((rows, D)), ANY, ANY,
        ],
        out_specs=[ANY] * 2,
        out_shape=[shape_of((16, 3, 48, D), BF16)] * 2,
        scratch_shapes=[
            pltpu.VMEM((8, 8, 48, D), BF16), pltpu.VMEM((2, D, 384), BF16),
            pltpu.VMEM((rows, D), BF16), pltpu.VMEM((rows, D), BF16),
            pltpu.SemaphoreType.DMA((4,)),
        ],
        compiler_params=params(),
        cost_estimate=cost(COST, 1e5),
        name="down_grad",
    )(me, act, grad_down, mixed, grad_attn)


def swap(values, axis, mask):
    size = lax.axis_size(axis)
    return lax.ppermute(values, axis, [(at, at ^ mask) for at in range(size)])


def joined(stack, axis, mask):
    return jnp.concatenate([stack, swap(stack, axis, mask)], axis=0)


def added(one, two):
    return (one.astype(F32) + two.astype(F32)).astype(BF16)


def tied(*values):
    return lax.optimization_barrier(values)


def cut(values, row, col, rows, cols):
    return lax.dynamic_slice(values, (row, col), (rows, cols))


def body(
    tokens, teacher, valid_mask, attn_gain, attn_shift, qkv_weight, query_bias, value_bias,
    rel_pos_h, rel_pos_w, proj_weight, proj_bias, mlp_gain, mlp_shift, up_weight, up_bias,
    down_weight, down_bias,
):
    count = tokens.shape[0]
    parts = lax.axis_size("fsdp")
    copies = lax.axis_size("rep")
    in_pieces = (copies, parts) == (4, 8)
    rep_at, part_at = lax.axis_index("rep"), lax.axis_index("fsdp")
    device = rep_at * parts + part_at
    core, far_x = rep_at % 2, rep_at // 2
    me = jnp.stack([rep_at, part_at, device * count]).astype(jnp.int32)
    window_ids = device * count + jnp.arange(count, dtype=jnp.int32)
    place = window_ids % (SIDE * SIDE)
    cells = jnp.arange(SLOTS, dtype=jnp.int32)
    inside = ((place // SIDE)[:, None] * WIN + (cells // WIN)[None, :] < MAP) & (
        (place % SIDE)[:, None] * WIN + (cells % WIN)[None, :] < MAP
    )
    keep = inside.astype(F32)
    valid = valid_mask.astype(F32) * keep
    counted = jnp.sum(valid_mask * inside.astype(jnp.int32))
    aux = jnp.pad(jnp.stack([keep, valid], axis=-1), ((0, 0), (0, ROWS - SLOTS), (0, 0)))

    small = [attn_gain, attn_shift, query_bias, value_bias, proj_bias, mlp_gain, mlp_shift,
             down_bias, up_bias, rel_pos_h, rel_pos_w]
    places = jnp.asarray(key_places(), BF16)
    places_t = jnp.asarray(np.pad(key_places().T[0:32], ((0, 0), (0, LANES - ROWS))), BF16)
    counted = jnp.stack([counted // 128, counted % 128]).astype(BF16)
    loss_scale = 64.0 * D * count * copies * parts

    def noted(shape, *entries):
        total = jnp.zeros(shape, BF16)
        for values, row, col in entries:
            if values.ndim == 1:
                values = values[None]
            high, wide = values.shape
            total = total + jnp.pad(
                values, ((row, shape[0] - row - high), (col, shape[1] - col - wide))
            )
        return total

    if in_pieces:
        rect = cut(qkv_weight, far_x * 48, core * QKV_HALF, 48, QKV_HALF)
        notes = noted(
            (48, NOTES), *[(v, at, 0) for at, v in enumerate(small[0:4])],
            (rel_pos_h, 16, 0), (rel_pos_w, 16, 8),
        )
        rect = jnp.concatenate([rect, notes], axis=1)
        near = [rect] + [swap(rect, "fsdp", mask) for mask in (2, 4, 6)]
        up_rect = cut(up_weight, far_x * 48, core * 1536, 48, 1536)
        down_rect = cut(down_weight, core * 192 + far_x * 96, 0, 96, D)
        proj_rect = cut(proj_weight, far_x * 48, core * 384, 48, 384)
        notes = noted(
            (48, 384), *[(v, at, 0) for at, v in enumerate(small[4:8])], (up_bias, 4, 0),
            (counted, 5, 0),
        )
        rects = jnp.concatenate(
            [up_rect.reshape(48, 2, D).transpose(1, 0, 2),
             jnp.concatenate([proj_rect, notes], axis=1)[None]], axis=0,
        )
        down_rect = down_rect.reshape(2, 48, D)
        *near, rects, down_rect, aux = tied(*near, rects, down_rect, aux)
        planes = [rects] + [swap(rects, "fsdp", mask) for mask in (2, 4, 6)]
        near_a, near_b = jnp.stack(near[0:2]), jnp.stack(near[2:4])
        from_a, from_b = swap(near_a, "fsdp", 1), swap(near_b, "rep", 2)
        from_a, from_b, planes[1] = tied(from_a, from_b, planes[1])
        near_a = jnp.concatenate([near_a, from_a])
        near_b = jnp.concatenate([near_b, from_b])
        far_a, far_b = swap(near_a, "rep", 2), swap(near_b, "fsdp", 1)
        far_a, far_b, planes[2] = tied(far_a, far_b, planes[2])
        all_a, all_b = jnp.concatenate([near_a, far_a]), jnp.concatenate([near_b, far_b])
        other_a, other_b = swap(all_a, "rep", 1), swap(all_b, "rep", 1)
        vec, rel, rel_t = notes_of(me, near_a, near_b, far_b)
        vec, rel, rel_t, other_a, other_b, planes[3] = tied(
            vec, rel, rel_t, other_a, other_b, planes[3]
        )
        up_a, up_b = jnp.stack(planes[0:2]), jnp.stack(planes[2:4])
        up_a, up_b, vec = tied(up_a, up_b, vec)
        from_a, from_b = swap(up_a, "fsdp", 1), swap(up_b, "rep", 2)
        planes = [down_rect] + [swap(down_rect, "fsdp", mask) for mask in (2, 4, 6)]
        *state, w_qkv = attend(
            me, tokens, (all_a, all_b, other_a, other_b), vec, rel, places, 0, STEPS[0]
        )
        from_a, from_b, *rest = tied(from_a, from_b, *planes[1:], *state)
        planes, state = [down_rect] + rest[0:3], rest[3:]
        up_a, up_b = jnp.concatenate([up_a, from_a]), jnp.concatenate([up_b, from_b])
        down_a, down_b = jnp.stack(planes[0:2]), jnp.stack(planes[2:4])
        up_a, up_b, down_a, down_b, *state = tied(up_a, up_b, down_a, down_b, *state)
        far_up_a, far_up_b = swap(up_a, "rep", 2), swap(up_b, "fsdp", 1)
        core_up_a, core_up_b = swap(up_a, "rep", 1), swap(up_b, "rep", 1)
        state = attend(me, tokens, w_qkv, vec, rel, places, STEPS[0], STEPS[1], tuple(state))
        far_up_a, far_up_b, core_up_a, core_up_b, *state = tied(
            far_up_a, far_up_b, core_up_a, core_up_b, *state
        )
        from_a, from_b = swap(down_a, "fsdp", 1), swap(down_b, "rep", 2)
        core_far_a, core_far_b = swap(far_up_a, "rep", 1), swap(far_up_b, "rep", 1)
        state = attend(me, tokens, w_qkv, vec, rel, places, sum(STEPS[:2]), STEPS[2], tuple(state))
        from_a, from_b, core_far_a, core_far_b, *state = tied(
            from_a, from_b, core_far_a, core_far_b, *state
        )
        up_pieces = (up_a, far_up_a, up_b, far_up_b, core_up_a, core_far_a, core_up_b, core_far_b)
        down_a, down_b = jnp.concatenate([down_a, from_a]), jnp.concatenate([down_b, from_b])
        down_a, down_b, *state = tied(down_a, down_b, *state)
        far_a, far_b = swap(down_a, "rep", 2), swap(down_b, "fsdp", 1)
        core_a, core_b = swap(down_a, "rep", 1), swap(down_b, "rep", 1)
        qkv, probs, mixed, first_in = state
        hidden, second_in, act, slope, w_up, w_proj, vec2, _, total = mlp_up(
            me, tokens, mixed, aux, up_pieces, True
        )
        far_a, far_b, core_a, core_b, hidden = tied(far_a, far_b, core_a, core_b, hidden)
        down_pieces = (
            down_a, far_a, down_b, far_b,
            core_a, swap(far_a, "rep", 1), core_b, swap(far_b, "rep", 1),
        )
    else:
        gather = lambda v: lax.all_gather(v, "fsdp", axis=0, tiled=True)
        w_qkv, w_proj = gather(qkv_weight), gather(proj_weight)
        packed = gather(jnp.concatenate([v.reshape(-1) for v in small] + [counted])[None])
        pieces, at = [], 0
        for v in small:
            pieces.append(packed[:, at : at + v.size])
            at += v.size
        rows = [p.reshape(1, -1).astype(F32) for p in pieces[:9]]
        offsets = rel_pos_h.shape[0]
        tables = [
            p.reshape(parts, offsets, -1).transpose(1, 0, 2).reshape(offsets, HEAD_DIM)
            for p in pieces[9:]
        ]
        gap = jnp.zeros((32 - offsets, HEAD_DIM), BF16)
        table = jnp.concatenate([tables[0], gap, tables[1], gap], axis=0)
        hole = jnp.zeros((HEAD_DIM, HEAD_DIM), BF16)
        rel = jnp.concatenate(
            [jnp.concatenate([table, hole], axis=1), jnp.concatenate([hole, table], axis=1)],
            axis=0,
        )
        rel_t = rel.T
        fill = jnp.zeros((4, D), F32)
        vec = jnp.concatenate(rows[0:4] + [fill])
        counts = lax.psum(jnp.sum(valid), ("rep", "fsdp")).reshape(1, 1)
        vec2 = jnp.concatenate(rows[4:8] + [fill])
        total = jnp.broadcast_to(counts, (1, 128))
        w_up, down_pieces = gather(up_weight), (gather(down_weight),)
        qkv, probs, mixed, first_in = attend(me, tokens, w_qkv, vec, rel, places, 0, count)
        hidden, second_in, act, slope = mlp_up(
            me, tokens, mixed, aux, (w_proj, w_up, vec2, rows[8]), False
        )
    out, grad_hidden, grad_attn, grad_down, grad_up, sums2, up_sum = mlp_down(
        me, hidden, act, slope, teacher, aux, w_up, vec2, total, down_pieces,
        loss_scale * 2.0 / D, in_pieces,
    )
    valid_total = total[0, 0]
    flat = lambda v: v.reshape(count * ROWS, v.shape[-1])
    if in_pieces:
        back_ends = (0, BACK_STEPS[0], BACK_STEPS[0] + BACK_STEPS[1])
        parts_of = lambda keep, come: lambda at, to: added(keep[at:to], come[at:to])
        keep_d, send_d = down_grad(me, flat(act), flat(grad_down), flat(mixed), flat(grad_attn))
        send_d, second_in = tied(send_d, flat(second_in))
        from_d = swap(send_d, "rep", 1)
        send_u = up_grad(me, second_in, flat(grad_up), 1)
        from_d, send_u, second_in = tied(from_d, send_u, second_in)
        sum_d = parts_of(keep_d, from_d)
        send_a, send_b = sum_d(4, 8), sum_d(12, 16)
        send_a, send_b, send_u, second_in = tied(send_a, send_b, send_u, second_in)
        from_u = swap(send_u, "rep", 1)
        from_a, from_b = swap(send_a, "rep", 2), swap(send_b, "fsdp", 1)
        keep_u = up_grad(me, second_in, flat(grad_up), 0)
        from_u, keep_u, grad_attn = tied(from_u, keep_u, grad_attn)
        sum_u = parts_of(keep_u, from_u)
        send_ua, send_ub = sum_u(4, 8), sum_u(12, 16)
        send_ua, send_ub, grad_attn = tied(send_ua, send_ub, grad_attn)
        back = (grad_attn, w_proj, qkv, probs, rel_t, places_t)
        state = attend_back(*back, 0, BACK_STEPS[0])
        from_a, from_b, *state = tied(from_a, from_b, *state)
        d_a, d_b = added(sum_d(0, 4), from_a), added(sum_d(8, 12), from_b)
        send_a, send_b = d_a[2:4], d_b[2:4]
        send_a, send_b, *state = tied(send_a, send_b, *state)
        from_a, from_b = swap(send_a, "fsdp", 1), swap(send_b, "rep", 2)
        from_ua, from_ub = swap(send_ua, "rep", 2), swap(send_ub, "fsdp", 1)
        state = attend_back(*back, back_ends[1], BACK_STEPS[1], tuple(state))
        from_a, from_b, from_ua, from_ub, *state = tied(from_a, from_b, from_ua, from_ub, *state)
        d_a, d_b = added(d_a[0:2], from_a), added(d_b[0:2], from_b)
        u_a, u_b = added(sum_u(0, 4), from_ua), added(sum_u(8, 12), from_ub)
        sends_d = (d_a[0], d_a[1], d_b[0], d_b[1])
        send_ua, send_ub = u_a[2:4], u_b[2:4]
        *sends_d, send_ua, send_ub, s0, s1, s2 = tied(*sends_d, send_ua, send_ub, *state)
        from_z = [swap(v, "fsdp", mask) for v, mask in zip(sends_d[1:], (2, 4, 6))]
        from_ua, from_ub = swap(send_ua, "fsdp", 1), swap(send_ub, "rep", 2)
        state = attend_back(*back, back_ends[2], BACK_STEPS[2], (s0, s1, s2))
        from_ua, from_ub, from_z[0], dqkv, rel_grad, qv_sum = tied(
            from_ua, from_ub, from_z[0], *state
        )
        keep, send = qkv_grad(me, flat(first_in), flat(dqkv))
        half = count // 2
        from_z[1], from_z[2], keep, send, dqkv = tied(from_z[1], from_z[2], keep, send, dqkv)
        own_d = sends_d[0].astype(F32)
        for v in from_z:
            own_d = own_d + v.astype(F32)
        u_a, u_b = added(u_a[0:2], from_ua), added(u_b[0:2], from_ub)
        sends_u = (u_a[0], u_a[1], u_b[0], u_b[1])
        *sends_u, send, dqkv = tied(*sends_u, send, dqkv)
        from_core = swap(send, "rep", 1)
        from_z = [swap(v, "fsdp", mask) for v, mask in zip(sends_u[1:], (2, 4, 6))]
        state = input_back(me, dqkv, w_qkv, tokens, grad_hidden, vec, 0, half)
        from_core, *rest = tied(from_core, *from_z, *state)
        from_z, state = rest[0:3], rest[3:]
        both = parts_of(keep, from_core)
        send_a, send_b = both(4, 8), both(12, 16)
        own_u = sends_u[0].astype(F32)
        for v in from_z:
            own_u = own_u + v.astype(F32)
        own = jnp.concatenate([own_u.astype(BF16), own_d.astype(BF16)], axis=0)
        send_a, send_b, own, *state = tied(send_a, send_b, own, *state)
        from_a, from_b = swap(send_a, "rep", 2), swap(send_b, "fsdp", 1)
        from_x = swap(own, "rep", 2)
        input_grad, sums1 = input_back(
            me, dqkv, w_qkv, tokens, grad_hidden, vec, half, count - half, tuple(state)
        )
        from_a, from_b, from_x, sums1 = tied(from_a, from_b, from_x, sums1)
        sum_a, sum_b = added(both(0, 4), from_a), added(both(8, 12), from_b)
        from_a, from_b = swap(sum_a[2:4], "fsdp", 1), swap(sum_b[2:4], "rep", 2)
        core_own, core_x = swap(own, "rep", 1), swap(from_x, "rep", 1)
        notes = pack(me, sums1, qv_sum, sums2, up_sum, rel_grad)
        from_a, from_b, notes, core_own, core_x = tied(from_a, from_b, notes, core_own, core_x)
        sum_a, sum_b = added(sum_a[0:2], from_a), added(sum_b[0:2], from_b)
        from_z = [swap(v, "fsdp", mask) for v, mask in
                  ((sum_a[1], 2), (sum_b[0], 4), (sum_b[1], 6))]
        notes = notes + swap(notes, "rep", 1)
        notes = notes + swap(notes, "rep", 2)
        notes = notes[0:4] + swap(notes[4:8], "fsdp", 1)
        d_up, d_down, d_proj = shard(me, (own, from_x, core_own, core_x), True)
        mine = notes[0]
        for at, mask in ((1, 2), (2, 4), (3, 6)):
            mine = mine + swap(notes[at], "fsdp", mask)
        own = sum_a[0].astype(F32)
        for v in from_z:
            own = own + v.astype(F32)
        own = own.astype(BF16)
        from_x = swap(own, "rep", 2)
        (d_qkv,) = shard(
            me, (own, from_x, swap(own, "rep", 1), swap(from_x, "rep", 1)), False
        )
        lanes = tokens.shape[2] // parts
        vectors = [mine[at, 0:lanes] for at in range(8)]
        tables = [mine[0:27, 96 + 8 * at : 104 + 8 * at] for at in range(2)]
        outs = vectors + [mine[27:30].reshape(-1)] + tables
        loss = mine[30, 0] / (valid_total * D)
    else:
        scatter = lambda v: lax.psum(
            lax.psum_scatter(v, "fsdp", scatter_dimension=0, tiled=True), "rep"
        ).astype(F32)
        d_down = scatter(weight_grad(flat(act), flat(grad_down), True))
        d_up = scatter(weight_grad(flat(second_in), flat(grad_up)))
        d_proj = scatter(weight_grad(flat(mixed), flat(grad_attn)))
        back = (grad_attn, w_proj, qkv, probs, rel_t, places_t)
        dqkv, rel_grad, qv_sum = attend_back(*back, 0, count)
        d_qkv = scatter(weight_grad(flat(first_in), flat(dqkv)))
        input_grad, sums1 = input_back(me, dqkv, w_qkv, tokens, grad_hidden, vec, 0, count)
        offsets = rel_pos_h.shape[0]
        rel_sum = rel_grad[0:64, 0:64] + rel_grad[64:128, 64:128]
        vectors = [sums1[0], sums1[1], qv_sum[0], qv_sum[1], sums2[4], sums2[2], sums2[3],
                   sums2[1], up_sum[0]]
        own = jnp.concatenate(
            [v.reshape(parts, -1) for v in vectors]
            + [
                rel_sum[at : at + offsets].reshape(offsets, parts, -1).transpose(1, 0, 2)
                .reshape(parts, -1) for at in (0, 32)
            ]
            + [jnp.broadcast_to(jnp.sum(sums2[0]), (parts, 1))],
            axis=1,
        )
        mine = lax.dynamic_index_in_dim(
            lax.psum(own, ("rep", "fsdp")), part_at, 0, keepdims=False
        )
        outs, at = [], 0
        for v in small:
            outs.append(mine[at : at + v.size].reshape(v.shape))
            at += v.size
        loss = mine[at] / (valid_total * D)
    (g_gain1, g_shift1, g_qb, g_vb, g_pb, g_gain2, g_shift2, g_db, g_ub, g_rh, g_rw) = outs
    return (
        out, loss, input_grad, g_gain1, g_shift1, d_qkv, g_qb, g_vb, g_rh, g_rw, d_proj, g_pb,
        g_gain2, g_shift2, d_up, g_ub, d_down, g_db,
    )


def solution(mesh):
    windows = P(("rep", "fsdp"), None, None)
    vector = P("fsdp")
    matrix = P("fsdp", None)
    table = P(None, "fsdp")
    in_specs = (
        windows, windows, P(("rep", "fsdp"), None), vector, vector, matrix, vector, vector, table,
        table, matrix, vector, vector, vector, matrix, vector, matrix, vector,
    )
    out_specs = (windows, P(), windows) + in_specs[3:]
    return jax.shard_map(body, mesh=mesh, in_specs=in_specs, out_specs=out_specs, check_vma=False)
```

```python
import functools
import math

import jax
import jax.numpy as jnp
import numpy as np
from jax import lax
from jax.experimental import pallas as pl
from jax.experimental.pallas import tpu as pltpu
from jax.sharding import PartitionSpec as P

D = 768
HEADS = 12
HEAD_DIM = 64
MLP = 3072
WIN = 14
MAP = 64
SLOTS = WIN * WIN
ROWS = 208
LANES = 256
PAIRS = HEADS // 2
PAIR = 2 * HEAD_DIM
SIDE = (MAP + WIN - 1) // WIN
LN_EPS = 1e-06
SQRT_HALF = 0.7071067811865476
INV_ROOT_TAU = 0.3989422804014327
F32 = jnp.float32
BF16 = jnp.bfloat16
QKV_HALF = 3 * D // 2
NOTES = 128
STEPS = (3, 4, 1)
COST = 1e8
BACK_STEPS = (2, 4, 2)


def nn(left, right):
    return jnp.dot(left, right, preferred_element_type=F32)


def nt(left, right):
    return lax.dot_general(left, right, (((1,), (1,)), ((), ())), preferred_element_type=F32)


def tn(left, right):
    return lax.dot_general(left, right, (((0,), (0,)), ((), ())), preferred_element_type=F32)


def key_places():
    table = np.zeros((ROWS, HEAD_DIM), np.float32)
    for slot in range(SLOTS):
        for base in (0, 32):
            table[slot, base + WIN - 1 - slot // WIN] = 1.0
            table[slot, base + 16 + WIN - 1 - slot % WIN] = 1.0
    return table


def keep_column(base_ref, window):
    slot = lax.broadcasted_iota(jnp.int32, (ROWS, 1), 0)
    row = lax.shift_right_logical(slot * 4682, 16)
    col = slot - row * WIN
    place = lax.rem(base_ref[2] + window, SIDE * SIDE)
    place_row = lax.div(place, SIDE)
    place_col = place - place_row * SIDE
    inside = (slot < SLOTS) & (row + place_row * WIN < MAP) & (col + place_col * WIN < MAP)
    return inside.astype(F32)


def lane_places():
    slot = lax.broadcasted_iota(jnp.int32, (1, LANES), 1)
    row = lax.shift_right_logical(slot * 4682, 16)
    return row, slot - row * WIN


def norm_parts(values):
    mean = jnp.mean(values, axis=-1, keepdims=True)
    centred = values - mean
    inv_std = lax.rsqrt(jnp.mean(centred * centred, axis=-1, keepdims=True) + LN_EPS)
    return centred * inv_std, inv_std


def norm_grad(grad, scaled, inv_std, gain):
    grad_scaled = grad * gain
    first = jnp.mean(grad_scaled, axis=-1, keepdims=True)
    second = jnp.mean(grad_scaled * scaled, axis=-1, keepdims=True)
    return inv_std * (grad_scaled - first - scaled * second)


def up_by(values, amount):
    take = lambda bit: (amount & bit) != 0
    part = jnp.where(take(8), values[8:32], values[0:24])
    part = jnp.where(take(4), pltpu.roll(part, 20, 0), part)
    part = jnp.where(take(2), pltpu.roll(part, 22, 0), part)
    part = jnp.where(take(1), pltpu.roll(part, 23, 0), part)
    return part[0:16]


def down_by(values, amount):
    take = lambda bit: (amount & bit) != 0
    zeros = jnp.zeros((8, values.shape[1]), values.dtype)
    part = jnp.concatenate([values, zeros], axis=0)
    part = jnp.where(take(1), pltpu.roll(part, 1, 0), part)
    part = jnp.where(take(2), pltpu.roll(part, 2, 0), part)
    part = jnp.where(take(4), pltpu.roll(part, 4, 0), part)
    return jnp.where(
        take(8),
        jnp.concatenate([zeros, part], axis=0),
        jnp.concatenate([part, zeros], axis=0),
    )


def fill_rows(values):
    return jnp.concatenate(
        [values, jnp.zeros((LANES - ROWS,) + values.shape[1:], values.dtype)], axis=0
    )


def chunk_place(me_ref, index, far_y, along_y):
    mid, plane = index // 2, index % 2
    dist_x, dist_y = (far_y, mid) if along_y else (mid, far_y)
    plane = plane * 2 + (0 if along_y else 4)
    return (me_ref[0] // 2) ^ dist_x, me_ref[1] ^ (plane + dist_y)


ARRIVED = tuple((half, along_y, other) for other in (0, 1) for along_y in (True, False) for half in (0, 1))


def load_first(me_ref, parts, full, sem):
    core = me_ref[0] % 2
    for at, ref in enumerate(parts):
        along_y, other = at % 2 == 0, at // 2

        def start(index, carry, ref=ref, along_y=along_y, other=other):
            far_x, owner = chunk_place(me_ref, index % 4, index // 4, along_y)
            pltpu.make_async_copy(
                ref.at[index, :, pl.ds(0, QKV_HALF)],
                full.at[
                    pl.ds(pl.multiple_of(owner * 96 + far_x * 48, 16), 48),
                    pl.ds(pl.multiple_of((core ^ other) * QKV_HALF, 128), QKV_HALF),
                ],
                sem.at[0],
            ).start()
            return carry

        lax.fori_loop(0, 8, start, 0)
    pltpu.make_async_copy(full, full, sem.at[0]).wait()


def piece_place(me_ref, index):
    group, high, mid, plane = index // 8, (index // 4) % 2, (index // 2) % 2, index % 2
    dist_x = jnp.where(group == 0, high, mid)
    dist_y = jnp.where(group == 0, mid, high)
    return (me_ref[0] // 2) ^ dist_x, me_ref[1] ^ (group * 4 + plane * 2 + dist_y)


def piece_index(me_ref, far_x, owner):
    dist = me_ref[1] ^ owner
    dist_x = (me_ref[0] // 2) ^ far_x
    dist_y, plane, group = dist % 2, (dist // 2) % 2, dist // 4
    high = jnp.where(group == 0, dist_x, dist_y)
    mid = jnp.where(group == 0, dist_y, dist_x)
    return group * 8 + high * 4 + mid * 2 + plane


def spread_rows(notes_of, owner_of, width, total):
    row = lax.broadcasted_iota(jnp.int32, (128, total), 0)
    col = lax.broadcasted_iota(jnp.int32, (128, total), 1)
    acc = None
    for at in range(8):
        put = ((row < width) & (col == row + owner_of(at) * width)).astype(BF16)
        part = nn(notes_of(at), put)
        acc = part if acc is None else acc + part
    return acc


def notes_kernel(me_ref, a_ref, b_ref, c_ref, vec_ref, rel_ref, relt_ref):
    picks = [(a_ref, at, at % 2 * 2 + at // 2) for at in range(4)]
    picks += [(b_ref, at, 4 + at * 2) for at in range(2)] + [(c_ref, at, 5 + at * 2) for at in range(2)]
    owner_of = lambda at: me_ref[1] ^ picks[at][2]
    lanes = pl.ds(QKV_HALF, NOTES)
    vec_ref[...] = spread_rows(
        lambda at: picks[at][0][picks[at][1], 0:16, lanes], owner_of, 96, D
    )[0:8]
    row = lax.broadcasted_iota(jnp.int32, (128, 128), 0)
    col = lax.broadcasted_iota(jnp.int32, (128, 128), 1)
    halves = []
    for which in range(2):
        acc = jnp.zeros((32, 128), F32)
        for at in range(8):
            lane = row - 8 * which
            place = lane + owner_of(at) * 8
            put = ((lane >= 0) & (lane < 8) & ((col == place) | (col == place + 64))).astype(BF16)
            acc = acc + nn(picks[at][0][picks[at][1], 16:48, lanes], put)
        halves.append(acc)
    table = jnp.concatenate(halves * 2, axis=0)
    table = jnp.where((row < 64) == (col < 64), table, 0.0).astype(BF16)
    rel_ref[...] = table
    relt_ref[...] = table.T


def attend_kernel(*refs, first, pieces, earlier):
    base_ref, tok_ref = refs[0:2]
    at = 2 + max(pieces, 1)
    vec_ref, rel_ref, place_ref = refs[at : at + 3]
    at += 3 + earlier
    qkv_ref, prob_ref, mix_ref, fin_ref = refs[at : at + 4]
    if pieces:
        w_ref, sem = refs[at + 4 :]

        @pl.when(pl.program_id(0) == 0)
        def _():
            load_first(base_ref, refs[2 : 2 + pieces], w_ref, sem)
    else:
        w_ref = refs[2]
    keep = keep_column(base_ref, pl.program_id(0) + first)
    scaled, _ = norm_parts(tok_ref[0].astype(F32))
    first_in = (keep * (scaled * vec_ref[0:1, :] + vec_ref[1:2, :])).astype(BF16)
    fin_ref[0] = first_in
    for part in range(3):
        cols = pl.ds(part * D, D)
        total = nn(first_in, w_ref[:, cols])
        if part != 1:
            total = total + vec_ref[2 + part // 2 : 3 + part // 2, :]
        qkv_ref[0, :, cols] = total.astype(BF16)
    lane_row, lane_col = lane_places()
    low_half = lax.broadcasted_iota(jnp.int32, (ROWS, PAIR), 1) < HEAD_DIM
    tail_rows = lax.broadcasted_iota(jnp.int32, (16, LANES), 0) + 192
    places = place_ref[...]
    place_pair = jnp.concatenate([places, places], axis=1)

    def one_pair(pair, carry):
        at = pl.multiple_of(pair * PAIR, PAIR)
        query = qkv_ref[0, :, pl.ds(at, PAIR)]
        keys = qkv_ref[0, :, pl.ds(pl.multiple_of(D + at, PAIR), PAIR)]
        values = qkv_ref[0, :, pl.ds(pl.multiple_of(2 * D + at, PAIR), PAIR)]
        query_t = fill_rows(query).T
        offsets = nn(rel_ref[...], query_t)
        mixed = []
        for head in range(2):
            mine = offsets[head * HEAD_DIM : (head + 1) * HEAD_DIM]
            along = jnp.concatenate(
                [up_by(mine[0:32], lane_row), up_by(mine[32:64], lane_col)], axis=0
            )
            high = along.astype(BF16)
            rest = (along - high.astype(F32)).astype(BF16)
            scaled_q = query_t[head * HEAD_DIM : (head + 1) * HEAD_DIM] * jnp.asarray(
                HEAD_DIM ** (-0.5), BF16
            )
            if head == 0:
                query_ext = jnp.concatenate([scaled_q, high, rest], axis=0)
                keys_ext = jnp.where(low_half, keys, place_pair)
            else:
                query_ext = jnp.concatenate([high, rest, scaled_q], axis=0)
                keys_ext = jnp.where(low_half, place_pair, keys)
            scores = nn(keys_ext, query_ext)
            scores = jnp.concatenate(
                [scores[0:192], jnp.where(tail_rows < SLOTS, scores[192:208], -1e30)], axis=0
            )
            peak = jnp.max(scores, axis=0, keepdims=True)
            expo = jnp.exp(scores - peak)
            total = jnp.sum(expo, axis=0, keepdims=True)
            probs = (expo * (1.0 / total)).astype(BF16)
            prob_ref[0, 2 * pair + head] = probs
            mixed.append(tn(probs, values)[0:ROWS].astype(BF16))
        mix_ref[0, :, pl.ds(at, PAIR)] = jnp.where(low_half, mixed[0], mixed[1])
        return carry

    lax.fori_loop(0, PAIRS, one_pair, 0, unroll=PAIRS)


def gelu_parts(pre):
    cumulative = 0.5 + 0.5 * lax.erf(pre * SQRT_HALF)
    bell = jnp.exp(pre * pre * (-0.5))
    return pre * cumulative, cumulative + pre * (bell * INV_ROOT_TAU)


def load_up(me_ref, pieces, up, proj, notes, sem):
    core = me_ref[0] % 2
    for array, (ref, (half, along_y, other)) in enumerate(zip(pieces, ARRIVED)):

        def start(index, carry, ref=ref, half=half, along_y=along_y, far_core=core ^ other, array=array):
            far_x, owner = chunk_place(me_ref, index, half, along_y)
            rows = pl.ds(pl.multiple_of(owner * 96 + far_x * 48, 16), 48)
            cols = pl.ds(pl.multiple_of(far_core * 384, 128), 384)
            pltpu.make_async_copy(
                ref.at[index, 2, :, pl.ds(0, 384)], proj.at[rows, cols], sem.at[1]
            ).start()
            pltpu.make_async_copy(
                ref.at[index, 2, pl.ds(0, 16), pl.ds(384, 384)], notes.at[array * 4 + index], sem.at[2]
            ).start()
            for block in range(2):
                cols = pl.ds(pl.multiple_of(far_core * 1536 + block * D, 128), D)
                pltpu.make_async_copy(ref.at[index, block], up.at[rows, cols], sem.at[0]).start()
            return carry

        lax.fori_loop(0, 4, start, 0)
    for at, full in ((2, notes), (1, proj), (0, up)):
        pltpu.make_async_copy(full, full, sem.at[at]).wait()


def load_down(me_ref, pieces, down, sem):
    core = me_ref[0] % 2
    for ref, (half, along_y, other) in zip(pieces, ARRIVED):

        def start(index, carry, ref=ref, half=half, along_y=along_y, far_core=core ^ other):
            far_x, owner = chunk_place(me_ref, index, half, along_y)
            place = owner * 8 + far_core * 4 + far_x * 2
            pltpu.make_async_copy(ref.at[index], down.at[pl.ds(place, 2)], sem.at[0]).start()
            return carry

        lax.fori_loop(0, 4, start, 0)
    pltpu.make_async_copy(down, down, sem.at[0]).wait()


def up_kernel(*refs, group, pieces):
    rows = group * ROWS
    me_ref, tok_ref, mix_ref, keep_ref = refs[0:4]
    at = 4 + (pieces or 4)
    hid_ref, si_ref, act_ref, slope_ref = refs[at : at + 4]
    at += 4
    if pieces:
        up_ref, wp_ref, vec_ref, ub_ref, total_ref, notes, sem = refs[at:]

        @pl.when(pl.program_id(0) == 0)
        def _():
            load_up(me_ref, refs[4 : 4 + pieces], up_ref, wp_ref, notes, sem)
            picks = [(at, at % 2 * 2 + at // 2) for at in range(4)]
            picks += [(8 + at, 4 + at * 2) for at in range(2)] + [(12 + at, 5 + at * 2) for at in range(2)]
            owner_of = lambda at: me_ref[1] ^ picks[at][1]
            vec_ref[...] = spread_rows(
                lambda at: notes[picks[at][0], :, 0:128], owner_of, 96, D
            )[0:8]
            for at in range(8):
                lanes = pl.ds(pl.multiple_of(owner_of(at) * 384, 128), 384)
                ub_ref[:, lanes] = notes[picks[at][0], 0:16, :].astype(F32)[4:5, :]
            counts = notes[0].astype(F32)
            for at in range(1, 32):
                counts = counts + notes[at].astype(F32)
            counts = counts[5:6, 0:128]
            lane = lax.broadcasted_iota(jnp.int32, (1, 128), 1)
            weight = jnp.where(lane == 0, 128.0, jnp.where(lane == 1, 1.0, 0.0))
            total_ref[...] = jnp.broadcast_to(
                jnp.sum(counts * weight, axis=1, keepdims=True), (1, 128)
            )
    else:
        wp_ref, up_ref, vec_ref, ub_ref = refs[4:8]
    pb_row, gain_row, shift_row = [vec_ref[at : at + 1, :] for at in range(3)]
    keep = keep_ref[...].reshape(rows, 2)[:, 0:1]
    attn_out = nn(mix_ref[...].reshape(rows, D), wp_ref[...]) + pb_row
    hidden = keep * (tok_ref[...].reshape(rows, D).astype(F32) + attn_out)
    hid_ref[...] = hidden.reshape(group, ROWS, D)
    scaled, _ = norm_parts(hidden)
    second_in = (scaled * gain_row + shift_row).astype(BF16)
    si_ref[...] = second_in.reshape(group, ROWS, D)
    for part in range(MLP // D):
        cols = slice(part * D, part * D + D)
        act, slope = gelu_parts(nn(second_in, up_ref[:, cols]) + ub_ref[:, cols])
        slope_ref[:, :, cols] = slope.astype(BF16).reshape(group, ROWS, D)
        act_ref[:, :, cols] = act.astype(BF16).reshape(group, ROWS, D)


def down_kernel(*refs, group, pieces, scale):
    step = pl.program_id(0)
    rows = group * ROWS
    me_ref, hid_ref, act_ref, slope_ref, teach_ref, aux_ref, up_ref, vec_ref, total_ref = refs[0:9]
    at = 9 + (pieces or 1)
    out_ref, gh_ref, ga_ref, gd_ref, gu_ref, sums_ref, usum_ref = refs[at : at + 7]
    if pieces:
        down3_ref, sem = refs[at + 7 :]

        @pl.when(step == 0)
        def _():
            load_down(me_ref, refs[9 : 9 + pieces], down3_ref, sem)

        down_rows = lambda part: down3_ref[pl.ds(part * 16, 16)].reshape(D, D)
    else:
        down_rows = lambda part: refs[9][pl.ds(part * D, D), :]

    @pl.when(step == 0)
    def _():
        sums_ref[...] = jnp.zeros_like(sums_ref)
        usum_ref[...] = jnp.zeros_like(usum_ref)

    gain_row, db_row = vec_ref[1:2, :], vec_ref[3:4, :]
    coef = scale / total_ref[:, 0:1]
    aux = aux_ref[...].reshape(rows, 2)
    keep, valid = aux[:, 0:1], aux[:, 1:2]
    hidden = hid_ref[...].reshape(rows, D)
    down = db_row
    for part in range(MLP // D):
        cols = slice(part * D, part * D + D)
        down = down + nn(act_ref[:, :, cols].reshape(rows, D), down_rows(part))
    final = keep * (hidden + down)
    for at in range(group):
        out_ref[at] = final[at * ROWS : at * ROWS + SLOTS].astype(BF16)
    error = final - teach_ref[...].reshape(rows, D).astype(F32)
    weighted = valid * error
    grad_final = coef * weighted
    grad_down = grad_final.astype(BF16)
    gd_ref[...] = grad_down.reshape(group, ROWS, D)
    sums_ref[0:1, :] += jnp.sum(weighted * error, axis=0, keepdims=True)
    sums_ref[1:2, :] += jnp.sum(grad_down.astype(F32), axis=0, keepdims=True)
    for part in range(MLP // D):
        cols = slice(part * D, part * D + D)
        slope = slope_ref[:, :, cols].reshape(rows, D).astype(F32)
        grad_up = (nt(grad_down, down_rows(part)) * slope).astype(BF16)
        gu_ref[:, :, cols] = grad_up.reshape(group, ROWS, D)
        usum_ref[:, cols] += jnp.sum(grad_up.astype(F32), axis=0, keepdims=True)
    grad_second = nt(gu_ref[...].reshape(rows, MLP), up_ref[...])
    scaled, inv_std = norm_parts(hidden)
    sums_ref[2:3, :] += jnp.sum(grad_second * scaled, axis=0, keepdims=True)
    sums_ref[3:4, :] += jnp.sum(grad_second, axis=0, keepdims=True)
    grad_hidden = keep * (grad_final + norm_grad(grad_second, scaled, inv_std, gain_row))
    gh_ref[...] = grad_hidden.reshape(group, ROWS, D)
    grad_attn = grad_hidden.astype(BF16)
    ga_ref[...] = grad_attn.reshape(group, ROWS, D)
    sums_ref[4:5, :] += jnp.sum(grad_attn.astype(F32), axis=0, keepdims=True)


def attend_back_kernel(*refs, earlier):
    ga_ref, wp_ref, qkv_ref, prob_ref, relt_ref, placet_ref = refs[0:6]
    dqkv_ref, rg_ref, qsum_ref, gm_ref = refs[6 + earlier :]

    @pl.when(pl.program_id(0) == 0)
    def _():
        rg_ref[...] = refs[7][...] if earlier else jnp.zeros_like(rg_ref)
        qsum_ref[...] = refs[8][...] if earlier else jnp.zeros_like(qsum_ref)
        gm_ref[pl.ds(ROWS, LANES - ROWS), :] = jnp.zeros((LANES - ROWS, D), BF16)

    gm_ref[pl.ds(0, ROWS), :] = nt(ga_ref[0], wp_ref[...]).astype(BF16)
    lane_row, lane_col = lane_places()
    low_half = lax.broadcasted_iota(jnp.int32, (ROWS, PAIR), 1) < HEAD_DIM
    low_full = lax.broadcasted_iota(jnp.int32, (LANES, PAIR), 1) < HEAD_DIM
    blank = jnp.zeros((), BF16)
    scale = HEAD_DIM ** (-0.5)

    def one_pair(pair, carry):
        at = pl.multiple_of(pair * PAIR, PAIR)
        q_at = pl.ds(at, PAIR)
        k_at = pl.ds(pl.multiple_of(D + at, PAIR), PAIR)
        v_at = pl.ds(pl.multiple_of(2 * D + at, PAIR), PAIR)
        query = fill_rows(qkv_ref[0, :, q_at])
        keys_t = fill_rows(qkv_ref[0, :, k_at]).T
        values = qkv_ref[0, :, v_at]
        grad_out = gm_ref[:, q_at]
        stacked = jnp.concatenate(
            [jnp.where(low_half, values, blank), jnp.where(low_half, blank, values)], axis=0
        )
        grad_probs = nt(stacked, grad_out)
        grad_values = jnp.zeros((ROWS, PAIR), F32)
        grad_keys = jnp.zeros((ROWS, PAIR), F32)
        spread, plain = [], []
        for head in range(2):
            own = (lambda full: jnp.where(low_full, full, blank)) if head == 0 else (
                lambda full: jnp.where(low_full, blank, full)
            )
            low = prob_ref[0, 2 * pair + head]
            probs = low.astype(F32)
            grad_p = grad_probs[head * ROWS : (head + 1) * ROWS]
            row_dot = jnp.sum(probs * grad_p, axis=0, keepdims=True)
            grad_score = (probs * (grad_p - row_dot)).astype(BF16)
            grad_values = grad_values + nn(low, own(grad_out))
            grad_keys = grad_keys + nn(grad_score, own(query))
            keys_ext = jnp.concatenate(
                [keys_t[head * HEAD_DIM : (head + 1) * HEAD_DIM], placet_ref[...]], axis=0
            )
            grad_ext = nn(keys_ext, fill_rows(grad_score))
            plain.append(grad_ext[0:64])
            spread.append(down_by(grad_ext[64:80], lane_row))
            spread.append(down_by(grad_ext[80:96], lane_col))
        spread = jnp.concatenate(spread, axis=0).astype(BF16)
        grad_query = jnp.concatenate(plain, axis=0) * scale + nn(relt_ref[...], spread)
        rg_ref[...] += nn(spread, query)
        grad_query = grad_query.astype(BF16).T[0:ROWS]
        grad_keys = (grad_keys * scale).astype(BF16)
        grad_values = grad_values.astype(BF16)
        dqkv_ref[0, :, q_at] = grad_query
        dqkv_ref[0, :, k_at] = grad_keys
        dqkv_ref[0, :, v_at] = grad_values
        qsum_ref[0:1, q_at] += jnp.sum(grad_query.astype(F32), axis=0, keepdims=True)
        qsum_ref[1:2, q_at] += jnp.sum(grad_values.astype(F32), axis=0, keepdims=True)
        return carry

    lax.fori_loop(0, PAIRS, one_pair, 0, unroll=PAIRS)


def input_kernel(
    base_ref, dqkv_ref, w_ref, tok_ref, gh_ref, vec_ref, *refs, group, first, earlier
):
    step = pl.program_id(0)
    out_ref, sums_ref = refs[earlier:]

    @pl.when(step == 0)
    def _():
        sums_ref[...] = refs[1][...] if earlier else jnp.zeros_like(sums_ref)

    for at in range(group):
        keep = keep_column(base_ref, first + step * group + at)
        grad_first = keep * nt(dqkv_ref[at], w_ref[...])
        scaled, inv_std = norm_parts(tok_ref[at].astype(F32))
        sums_ref[0:1, :] += jnp.sum(grad_first * scaled, axis=0, keepdims=True)
        sums_ref[1:2, :] += jnp.sum(grad_first, axis=0, keepdims=True)
        total = gh_ref[at] + norm_grad(grad_first, scaled, inv_std, vec_ref[0:1, :])
        out_ref[:, first + step * group + at, :] = total[0:SLOTS]


def weight_grad_kernel(*refs):
    left_ref, right_ref, out_ref = refs
    out_ref[...] = tn(left_ref[...], right_ref[...]).astype(BF16)


def qkv_grad_kernel(me_ref, left_ref, right_ref, notes_ref, out_ref, full, sem, *, other):
    full[...] = tn(left_ref[...], right_ref[...]).astype(BF16)
    core = (me_ref[0] % 2) ^ other

    def start(index, carry):
        far_x, owner = piece_place(me_ref, index)
        pltpu.make_async_copy(
            full.at[pl.ds(pl.multiple_of(owner * 96 + far_x * 48, 16), 48)],
            out_ref.at[index, :, pl.ds(0, QKV_HALF)],
            sem.at[0],
        ).start()
        pltpu.make_async_copy(
            notes_ref.at[core * 2 + far_x, owner],
            out_ref.at[index, :, pl.ds(QKV_HALF, NOTES)],
            sem.at[0],
        ).start()
        return carry

    lax.fori_loop(0, 16, start, 0)
    pltpu.make_async_copy(out_ref, out_ref, sem.at[0]).wait()


def up_grad_kernel(me_ref, left_ref, right_ref, out_ref, full, sem):
    step = pl.program_id(0)
    full[step] = tn(left_ref[...], right_ref[...]).astype(BF16)

    def start(index, carry):
        far_x, owner = piece_place(me_ref, index)
        rows = pl.ds(pl.multiple_of(owner * 96 + far_x * 48, 16), 48)
        pltpu.make_async_copy(full.at[step, rows], out_ref.at[index, step], sem.at[0]).start()
        return carry

    lax.fori_loop(0, 16, start, 0)

    @pl.when(step == pl.num_programs(0) - 1)
    def _():
        pltpu.make_async_copy(out_ref, out_ref, sem.at[0]).wait()


def down_grad_kernel(
    me_ref, act_ref, gd_ref, mix_any, ga_any, keep_ref, send_ref, full, half, mix_ref, ga_ref, sem
):
    step = pl.program_id(0)
    last = pl.num_programs(0) - 1
    fetches = [
        pltpu.make_async_copy(mix_any, mix_ref, sem.at[2]),
        pltpu.make_async_copy(ga_any, ga_ref, sem.at[3]),
    ]

    @pl.when(step == 0)
    def _():
        for fetch in fetches:
            fetch.start()

    @pl.when(step < last)
    def _():
        full[step] = tn(act_ref[...], gd_ref[...]).astype(BF16).reshape(16, 48, D)

    @pl.when(step == last)
    def _():
        for fetch in fetches:
            fetch.wait()
        total = tn(mix_ref[...], ga_ref[...]).astype(BF16)
        for core in range(2):
            half[core] = total[:, core * 384 : core * 384 + 384]

    core = me_ref[0] % 2
    for ref, far_core, at in ((keep_ref, core, 0), (send_ref, 1 - core, 1)):

        def start_proj(index, carry, ref=ref, far_core=far_core, at=at):
            far_x, owner = piece_place(me_ref, index)
            rows = pl.ds(pl.multiple_of(owner * 96 + far_x * 48, 16), 48)
            for col in (0, 384):
                pltpu.make_async_copy(
                    half.at[far_core, rows], ref.at[index, 2, :, pl.ds(col, 384)], sem.at[at]
                ).start()
            return carry

        @pl.when(step < last)
        def _(ref=ref, far_core=far_core, at=at):
            for place in range(4):
                which, far_x = place // 2, place % 2
                pltpu.make_async_copy(
                    full.at[step, pl.ds(which * 8 + far_core * 4 + far_x * 2, 2)],
                    ref.at[piece_index(me_ref, far_x, step * 2 + which), pl.ds(0, 2)],
                    sem.at[at],
                ).start()

        @pl.when(step == last)
        def _(start_proj=start_proj):
            lax.fori_loop(0, 16, start_proj, 0)

    @pl.when(step == last)
    def _():
        pltpu.make_async_copy(keep_ref, keep_ref, sem.at[0]).wait()
        pltpu.make_async_copy(send_ref, send_ref, sem.at[1]).wait()


def whole(shape):
    zeros = (0,) * len(shape)
    return pl.BlockSpec(shape, lambda *_: zeros, pipeline_mode=pl.Buffered(1))


def whole_out(shape):
    zeros = (0,) * len(shape)
    return pl.BlockSpec(shape, lambda *_: zeros)


def windows_from(first, shape):
    tail = (0,) * (len(shape) - 1)
    return pl.BlockSpec(shape, lambda step: (step + first,) + tail)


SMEM = pl.BlockSpec(memory_space=pltpu.SMEM)
ANY = pl.BlockSpec(memory_space=pl.ANY)


def params(mebibytes=32):
    return pltpu.CompilerParams(
        vmem_limit_bytes=mebibytes * 1024 * 1024, dimension_semantics=("arbitrary",)
    )


def shape_of(shape, dtype):
    return jax.ShapeDtypeStruct(shape, dtype)


def cost(flops, moved):
    return pl.CostEstimate(flops=int(flops), bytes_accessed=int(moved), transcendentals=0)


def notes_of(me, near, far_x, far_y):
    return pl.pallas_call(
        notes_kernel,
        in_specs=[SMEM] + [whole(v.shape) for v in (near, far_x, far_y)],
        out_specs=[whole_out((8, D)), whole_out((PAIR, PAIR)), whole_out((PAIR, PAIR))],
        out_shape=[shape_of((8, D), F32)] + [shape_of((PAIR, PAIR), BF16)] * 2,
        grid=(1,),
        compiler_params=params(),
        cost_estimate=cost(COST, 1e5),
        name="notes",
    )(me, near, far_x, far_y)


def attend(me, tokens, weight, vec, rel, places, first, number, earlier=()):
    count = tokens.shape[0]
    win = lambda shape: windows_from(first, shape)
    pieces = len(weight) if isinstance(weight, tuple) else 0
    weights = weight if pieces else (weight,)
    weight_specs = [ANY] * pieces if pieces else [whole((D, 3 * D))]
    out_specs = [win((1, ROWS, 3 * D)), win((1, HEADS, ROWS, LANES)), win((1, ROWS, D)),
                 win((1, ROWS, D))]
    out_shape = [
        shape_of((count, ROWS, 3 * D), BF16), shape_of((count, HEADS, ROWS, LANES), BF16),
        shape_of((count, ROWS, D), BF16), shape_of((count, ROWS, D), BF16),
    ]
    scratch = []
    if pieces:
        out_specs.append(whole_out((D, 3 * D)))
        out_shape.append(shape_of((D, 3 * D), BF16))
        scratch.append(pltpu.SemaphoreType.DMA((1,)))
    inputs = 5 + len(weights)
    return pl.pallas_call(
        functools.partial(attend_kernel, first=first, pieces=pieces, earlier=len(earlier)),
        grid=(number,),
        in_specs=[
            SMEM, win((1, ROWS, D)), *weight_specs, whole((8, D)),
            whole((PAIR, PAIR)), whole((ROWS, HEAD_DIM)), *([ANY] * len(earlier)),
        ],
        out_specs=out_specs,
        out_shape=out_shape,
        scratch_shapes=scratch,
        input_output_aliases={inputs + at: at for at in range(len(earlier))},
        compiler_params=params(54),
        cost_estimate=cost(COST, 1e5),
        name="attend",
    )(me, tokens, *weights, vec, rel, places, *earlier)


def mlp_up(me, tokens, mixed, aux, weights, chunked):
    count = tokens.shape[0]
    group = math.gcd(count, 2)
    win = lambda width: windows_from(0, (group, ROWS, width))
    arr = lambda width, dtype: shape_of((count, ROWS, width), dtype)
    pieces = len(weights) if chunked else 0
    out_specs = [win(D), win(D), win(MLP), win(MLP)]
    out_shape = [arr(D, F32), arr(D, BF16), arr(MLP, BF16), arr(MLP, BF16)]
    scratch = []
    if pieces:
        shapes = [((D, MLP), BF16), ((D, D), BF16), ((8, D), F32), ((1, MLP), F32), ((1, 128), F32)]
        out_specs += [whole_out(s) for s, _ in shapes]
        out_shape += [shape_of(s, t) for s, t in shapes]
        scratch += [pltpu.VMEM((32, 16, 384), BF16), pltpu.SemaphoreType.DMA((3,))]
    return pl.pallas_call(
        functools.partial(up_kernel, group=group, pieces=pieces),
        grid=(count // group,),
        in_specs=[SMEM, win(D), win(D), win(2)]
        + ([ANY] * pieces if pieces else [whole(v.shape) for v in weights]),
        out_specs=out_specs,
        out_shape=out_shape,
        scratch_shapes=scratch,
        compiler_params=params(60),
        cost_estimate=cost(COST * count, 1e5),
        name="mlp_up",
    )(me, tokens, mixed, aux, *weights)


def mlp_down(me, hidden, act, slope, teacher, aux, up, vec, total, weights, scale, chunked):
    count = hidden.shape[0]
    group = math.gcd(count, 2)
    win = lambda width: windows_from(0, (group, ROWS, width))
    plain = windows_from(0, (group, SLOTS, D))
    arr = lambda width, dtype: shape_of((count, ROWS, width), dtype)
    pieces = len(weights) if chunked else 0
    scratch = []
    if pieces:
        scratch += [pltpu.VMEM((MLP // 48, 48, D), BF16), pltpu.SemaphoreType.DMA((1,))]
    return pl.pallas_call(
        functools.partial(down_kernel, group=group, pieces=pieces, scale=scale),
        grid=(count // group,),
        in_specs=[SMEM, win(D), win(MLP), win(MLP), win(D), win(2), whole((D, MLP)), whole((8, D)),
                  whole((1, 128))]
        + ([ANY] * pieces if pieces else [whole(v.shape) for v in weights]),
        out_specs=[plain, win(D), win(D), win(D), win(MLP), whole_out((5, D)), whole_out((1, MLP))],
        out_shape=[
            shape_of((count, SLOTS, D), BF16), arr(D, F32), arr(D, BF16), arr(D, BF16),
            arr(MLP, BF16), shape_of((5, D), F32), shape_of((1, MLP), F32),
        ],
        scratch_shapes=scratch,
        compiler_params=params(60),
        cost_estimate=cost(COST * count, 1e5),
        name="mlp_down",
    )(me, hidden, act, slope, teacher, aux, up, vec, total, *weights)


def attend_back(grad_attn, proj, qkv, probs, rel_t, places_t, first, number, earlier=()):
    count = grad_attn.shape[0]
    win = lambda shape: windows_from(first, shape)
    before = [ANY, whole((PAIR, PAIR)), whole((2, D))] if earlier else []
    return pl.pallas_call(
        functools.partial(attend_back_kernel, earlier=len(earlier)),
        grid=(number,),
        in_specs=[
            win((1, ROWS, D)), whole((D, D)), win((1, ROWS, 3 * D)), win((1, HEADS, ROWS, LANES)),
            whole((PAIR, PAIR)), whole((32, LANES)), *before,
        ],
        out_specs=[win((1, ROWS, 3 * D)), whole_out((PAIR, PAIR)), whole_out((2, D))],
        out_shape=[
            shape_of((count, ROWS, 3 * D), BF16), shape_of((PAIR, PAIR), F32),
            shape_of((2, D), F32),
        ],
        scratch_shapes=[pltpu.VMEM((LANES, D), BF16)],
        input_output_aliases={6: 0} if earlier else {},
        compiler_params=params(48),
        cost_estimate=cost(COST, 1e5),
        name="attend_back",
    )(grad_attn, proj, qkv, probs, rel_t, places_t, *earlier)


def input_back(me, dqkv, weight, tokens, grad_hidden, vec, first, number, earlier=()):
    count = tokens.shape[0]
    group = math.gcd(math.gcd(first, number), 2)
    win = lambda shape: windows_from(first // group, shape)
    before = [ANY, whole((2, D))] if earlier else []
    return pl.pallas_call(
        functools.partial(input_kernel, group=group, first=first, earlier=len(earlier)),
        grid=(number // group,),
        in_specs=[
            SMEM, win((group, ROWS, 3 * D)), whole((D, 3 * D)), win((group, ROWS, D)),
            win((group, ROWS, D)), whole((8, D)), *before,
        ],
        out_specs=[whole_out((SLOTS, count, D)), whole_out((2, D))],
        out_shape=[shape_of((SLOTS, count, D), F32), shape_of((2, D), F32)],
        input_output_aliases={6: 0} if earlier else {},
        compiler_params=params(44),
        cost_estimate=cost(COST, 1e5),
        name="input_back",
    )(me, dqkv, weight, tokens, grad_hidden, vec, *earlier)


def pick(left, right):
    return jnp.dot(left, right, preferred_element_type=F32, precision=lax.Precision.HIGHEST)


def pack_kernel(me_ref, one_ref, qv_ref, two_ref, up_ref, rel_ref, out_ref):
    vectors = jnp.concatenate(
        [one_ref[0:2], qv_ref[0:2], two_ref[4:5], two_ref[2:4], two_ref[1:2]], axis=0
    )
    error = jnp.sum(two_ref[0:1, :], axis=1, keepdims=True)
    high = error.astype(BF16).astype(F32)
    middle = (error - high).astype(BF16).astype(F32)
    lane = lax.broadcasted_iota(jnp.int32, (1, 128), 1) - 3 * (me_ref[0] * 8 + me_ref[1])
    error = jnp.where(
        lane == 0, high, jnp.where(lane == 1, middle, jnp.where(lane == 2, error - high - middle, 0.0))
    )
    tables = rel_ref[0:64, 0:64] + rel_ref[64:128, 64:128]
    row = lax.broadcasted_iota(jnp.int32, (D, 128), 0)
    col = lax.broadcasted_iota(jnp.int32, (D, 128), 1)
    small_row = lax.broadcasted_iota(jnp.int32, (32, 128), 0)
    lanes_row = lax.broadcasted_iota(jnp.int32, (64, 128), 0)
    lanes_col = lax.broadcasted_iota(jnp.int32, (64, 128), 1)
    out_ref[...] = jnp.zeros_like(out_ref)
    for owner in range(8):
        own = pick(vectors, ((col < 96) & (row == col + owner * 96)).astype(F32))
        total = jnp.concatenate([own, jnp.zeros((24, 128), F32)], axis=0)
        for which in range(2):
            lane = lanes_col - 96 - 8 * which
            put = ((lane >= 0) & (lane < 8) & (lanes_row == lane + owner * 8)).astype(F32)
            total = total + pick(tables[32 * which : 32 * which + 32], put)
        for part in range(3):
            at = owner * 384 + part * 128
            total = jnp.where(small_row == 27 + part, up_ref[:, at : at + 128], total)
        total = jnp.where(small_row == 30, error, total).astype(BF16)
        for quarter in range(4):
            out_ref[quarter, owner, 0:8] = total[quarter * 8 : quarter * 8 + 8]


def pack(me, *sums):
    return pl.pallas_call(
        pack_kernel,
        grid=(1,),
        in_specs=[SMEM] + [whole(v.shape) for v in sums],
        out_specs=whole_out((4, 8, 48, NOTES)),
        out_shape=shape_of((4, 8, 48, NOTES), BF16),
        compiler_params=params(),
        cost_estimate=cost(COST, 1e5),
        name="pack",
    )(me, *sums)


def qkv_shard_kernel(me_ref, total_ref, *refs):
    quarters, out_ref, notes_ref = refs[0:4], refs[4], refs[5]
    core, far_x = me_ref[0] % 2, me_ref[0] // 2
    for at, ref in enumerate(quarters):
        this_core, this_x = core ^ (at // 2), far_x ^ (at % 2)
        rows = pl.ds(pl.multiple_of(this_x * 48, 16), 48)
        cols = pl.ds(pl.multiple_of(this_core * QKV_HALF, 128), QKV_HALF)
        out_ref[rows, cols] = ref[:, 0:QKV_HALF].astype(F32)
        here = pl.ds(pl.multiple_of((this_core * 2 + this_x) * 8, 8), 8)
        notes_ref[here, :] = ref[0:16, QKV_HALF : QKV_HALF + NOTES].astype(F32)[0:8]
    errors = jnp.sum(notes_ref[30:31, :], axis=1, keepdims=True)
    notes_ref[31:32, :] = errors / (total_ref[...] * D)


def qkv_shard(me, total, quarters):
    shapes = [(96, 3 * D), (32, 128)]
    return pl.pallas_call(
        qkv_shard_kernel,
        grid=(1,),
        in_specs=[SMEM, whole((1, 128))] + [whole(v.shape) for v in quarters],
        out_specs=[whole_out(shape) for shape in shapes],
        out_shape=[shape_of(shape, F32) for shape in shapes],
        compiler_params=params(),
        cost_estimate=cost(COST, 1e5),
        name="qkv_shard",
    )(me, total, *quarters)


def shard_kernel(me_ref, *refs):
    quarters, (up_ref, down_ref, proj_ref) = refs[0:4], refs[4:]
    core, far_x = me_ref[0] % 2, me_ref[0] // 2
    for at, ref in enumerate(quarters):
        this_core, this_x = core ^ (at // 2), far_x ^ (at % 2)
        rows = pl.ds(pl.multiple_of(this_x * 48, 16), 48)
        for block in range(2):
            cols = pl.ds(pl.multiple_of(this_core * 1536 + block * D, 128), D)
            up_ref[rows, cols] = ref[block].astype(F32)
            at_row = this_core * 192 + this_x * 96 + block * 48
            down_ref[pl.ds(pl.multiple_of(at_row, 16), 48), :] = ref[2 + block].astype(F32)
        cols = pl.ds(pl.multiple_of(this_core * 384, 128), 384)
        proj_ref[rows, cols] = ref[4, :, 0:384].astype(F32)


def shard(me, quarters):
    shapes = [(96, MLP), (384, D), (96, D)]
    return pl.pallas_call(
        shard_kernel,
        grid=(1,),
        in_specs=[SMEM] + [whole(v.shape) for v in quarters],
        out_specs=[whole_out(shape) for shape in shapes],
        out_shape=[shape_of(shape, F32) for shape in shapes],
        compiler_params=params(),
        cost_estimate=cost(COST, 1e5),
        name="shard",
    )(me, *quarters)


def column_blocks(rows):
    return pl.BlockSpec((rows, D), lambda step: (0, step))


def weight_grad(left, right, by_rows=False):
    rows = left.shape[0]
    blocks = (left if by_rows else right).shape[1] // D
    moving, still = column_blocks(rows), whole((rows, D))
    return pl.pallas_call(
        weight_grad_kernel,
        grid=(blocks,),
        in_specs=[moving, still] if by_rows else [still, moving],
        out_specs=pl.BlockSpec((D, D), (lambda s: (s, 0)) if by_rows else (lambda s: (0, s))),
        out_shape=shape_of((left.shape[1], right.shape[1]), BF16),
        compiler_params=params(44),
        name="weight_grad",
    )(left, right)


def qkv_grad(me, left, right, notes, other):
    rows = left.shape[0]
    return pl.pallas_call(
        functools.partial(qkv_grad_kernel, other=other),
        grid_spec=pltpu.PrefetchScalarGridSpec(
            num_scalar_prefetch=1,
            grid=(1,),
            in_specs=[
                whole((rows, D)),
                pl.BlockSpec((rows, QKV_HALF), lambda step, me: (0, (me[0] % 2) ^ other)),
                whole((4, 8, 48, NOTES)),
            ],
            out_specs=ANY,
            scratch_shapes=[pltpu.VMEM((D, QKV_HALF), BF16), pltpu.SemaphoreType.DMA((1,))],
        ),
        out_shape=shape_of((16, 48, QKV_HALF + NOTES), BF16),
        compiler_params=params(60),
        cost_estimate=cost(COST, 1e5),
        name="qkv_grad",
    )(me, left, right, notes)


def up_grad(me, left, right, other):
    rows = left.shape[0]
    return pl.pallas_call(
        up_grad_kernel,
        grid_spec=pltpu.PrefetchScalarGridSpec(
            num_scalar_prefetch=1,
            grid=(2,),
            in_specs=[
                whole((rows, D)),
                pl.BlockSpec((rows, D), lambda step, me: (0, ((me[0] % 2) ^ other) * 2 + step)),
            ],
            out_specs=ANY,
            scratch_shapes=[pltpu.VMEM((2, D, D), BF16), pltpu.SemaphoreType.DMA((1,))],
        ),
        out_shape=shape_of((16, 2, 48, D), BF16),
        compiler_params=params(60),
        cost_estimate=cost(COST, 1e5),
        name="up_grad",
    )(me, left, right)


def down_grad(me, act, grad_down, mixed, grad_attn):
    rows = act.shape[0]
    return pl.pallas_call(
        down_grad_kernel,
        grid=(5,),
        in_specs=[
            SMEM, pl.BlockSpec((rows, D), lambda step: (0, jnp.minimum(step, 3))),
            whole((rows, D)), ANY, ANY,
        ],
        out_specs=[ANY] * 2,
        out_shape=[shape_of((16, 3, 48, D), BF16)] * 2,
        scratch_shapes=[
            pltpu.VMEM((4, 16, 48, D), BF16), pltpu.VMEM((2, D, 384), BF16),
            pltpu.VMEM((rows, D), BF16), pltpu.VMEM((rows, D), BF16),
            pltpu.SemaphoreType.DMA((4,)),
        ],
        compiler_params=params(60),
        cost_estimate=cost(COST, 1e5),
        name="down_grad",
    )(me, act, grad_down, mixed, grad_attn)


def swap(values, axis, mask):
    size = lax.axis_size(axis)
    return lax.ppermute(values, axis, [(at, at ^ mask) for at in range(size)])


def joined(stack, axis, mask):
    return jnp.concatenate([stack, swap(stack, axis, mask)], axis=0)


def added(one, two):
    return (one.astype(F32) + two.astype(F32)).astype(BF16)


def tied(*values):
    return lax.optimization_barrier(values)


def cut(values, row, col, rows, cols):
    return lax.dynamic_slice(values, (row, col), (rows, cols))


def body(
    tokens, teacher, valid_mask, attn_gain, attn_shift, qkv_weight, query_bias, value_bias,
    rel_pos_h, rel_pos_w, proj_weight, proj_bias, mlp_gain, mlp_shift, up_weight, up_bias,
    down_weight, down_bias,
):
    count = tokens.shape[0]
    parts = lax.axis_size("fsdp")
    copies = lax.axis_size("rep")
    in_pieces = (copies, parts) == (4, 8)
    rep_at, part_at = lax.axis_index("rep"), lax.axis_index("fsdp")
    device = rep_at * parts + part_at
    core, far_x = rep_at % 2, rep_at // 2
    me = jnp.stack([rep_at, part_at, device * count]).astype(jnp.int32)
    window_ids = device * count + jnp.arange(count, dtype=jnp.int32)
    place = window_ids % (SIDE * SIDE)
    cells = jnp.arange(SLOTS, dtype=jnp.int32)
    inside = ((place // SIDE)[:, None] * WIN + (cells // WIN)[None, :] < MAP) & (
        (place % SIDE)[:, None] * WIN + (cells % WIN)[None, :] < MAP
    )
    keep = inside.astype(F32)
    valid = valid_mask.astype(F32) * keep
    counted = jnp.sum(valid_mask * inside.astype(jnp.int32))
    fill = ((0, 0), (0, ROWS - SLOTS), (0, 0))
    aux = jnp.pad(jnp.stack([keep, valid], axis=-1), fill)
    tokens, teacher = jnp.pad(tokens, fill), jnp.pad(teacher, fill)

    small = [attn_gain, attn_shift, query_bias, value_bias, proj_bias, mlp_gain, mlp_shift,
             down_bias, up_bias, rel_pos_h, rel_pos_w]
    places = jnp.asarray(key_places(), BF16)
    places_t = jnp.asarray(np.pad(key_places().T[0:32], ((0, 0), (0, LANES - ROWS))), BF16)
    counted = jnp.stack([counted // 128, counted % 128]).astype(BF16)
    loss_scale = 64.0 * D * count * copies * parts

    def noted(shape, *entries):
        total = jnp.zeros(shape, BF16)
        for values, row, col in entries:
            if values.ndim == 1:
                values = values[None]
            high, wide = values.shape
            total = total + jnp.pad(
                values, ((row, shape[0] - row - high), (col, shape[1] - col - wide))
            )
        return total

    if in_pieces:
        rect = cut(qkv_weight, far_x * 48, core * QKV_HALF, 48, QKV_HALF)
        notes = noted(
            (48, NOTES), *[(v, at, 0) for at, v in enumerate(small[0:4])],
            (rel_pos_h, 16, 0), (rel_pos_w, 16, 8),
        )
        rect = jnp.concatenate([rect, notes], axis=1)
        near = [rect] + [swap(rect, "fsdp", mask) for mask in (2, 4, 6)]
        up_rect = cut(up_weight, far_x * 48, core * 1536, 48, 1536)
        down_rect = cut(down_weight, core * 192 + far_x * 96, 0, 96, D)
        proj_rect = cut(proj_weight, far_x * 48, core * 384, 48, 384)
        notes = noted(
            (48, 384), *[(v, at, 0) for at, v in enumerate(small[4:8])], (up_bias, 4, 0),
            (counted, 5, 0),
        )
        rects = jnp.concatenate(
            [up_rect.reshape(48, 2, D).transpose(1, 0, 2),
             jnp.concatenate([proj_rect, notes], axis=1)[None]], axis=0,
        )
        down_rect = down_rect.reshape(2, 48, D)
        *near, rects, down_rect, aux = tied(*near, rects, down_rect, aux)
        planes = [rects] + [swap(rects, "fsdp", mask) for mask in (2, 4, 6)]
        near_a, near_b = jnp.stack(near[0:2]), jnp.stack(near[2:4])
        from_a, from_b = swap(near_a, "fsdp", 1), swap(near_b, "rep", 2)
        from_a, from_b, planes[1], tokens = tied(from_a, from_b, planes[1], tokens)
        near_a = jnp.concatenate([near_a, from_a])
        near_b = jnp.concatenate([near_b, from_b])
        far_a, far_b = swap(near_a, "rep", 2), swap(near_b, "fsdp", 1)
        far_a, far_b, planes[2], teacher = tied(far_a, far_b, planes[2], teacher)
        all_a, all_b = jnp.concatenate([near_a, far_a]), jnp.concatenate([near_b, far_b])
        other_a, other_b = swap(all_a, "rep", 1), swap(all_b, "rep", 1)
        vec, rel, rel_t = notes_of(me, near_a, near_b, far_b)
        vec, rel, rel_t, other_a, other_b, planes[3] = tied(
            vec, rel, rel_t, other_a, other_b, planes[3]
        )
        up_a, up_b = jnp.stack(planes[0:2]), jnp.stack(planes[2:4])
        up_a, up_b, vec = tied(up_a, up_b, vec)
        from_a, from_b = swap(up_a, "fsdp", 1), swap(up_b, "rep", 2)
        planes = [down_rect] + [swap(down_rect, "fsdp", mask) for mask in (2, 4, 6)]
        *state, w_qkv = attend(
            me, tokens, (all_a, all_b, other_a, other_b), vec, rel, places, 0, STEPS[0]
        )
        from_a, from_b, *rest = tied(from_a, from_b, *planes[1:], *state)
        planes, state = [down_rect] + rest[0:3], rest[3:]
        up_a, up_b = jnp.concatenate([up_a, from_a]), jnp.concatenate([up_b, from_b])
        down_a, down_b = jnp.stack(planes[0:2]), jnp.stack(planes[2:4])
        up_a, up_b, down_a, down_b, *state = tied(up_a, up_b, down_a, down_b, *state)
        far_up_a, far_up_b = swap(up_a, "rep", 2), swap(up_b, "fsdp", 1)
        core_up_a, core_up_b = swap(up_a, "rep", 1), swap(up_b, "rep", 1)
        state = attend(me, tokens, w_qkv, vec, rel, places, STEPS[0], STEPS[1], tuple(state))
        far_up_a, far_up_b, core_up_a, core_up_b, *state = tied(
            far_up_a, far_up_b, core_up_a, core_up_b, *state
        )
        from_a, from_b = swap(down_a, "fsdp", 1), swap(down_b, "rep", 2)
        core_far_a, core_far_b = swap(far_up_a, "rep", 1), swap(far_up_b, "rep", 1)
        state = attend(me, tokens, w_qkv, vec, rel, places, sum(STEPS[:2]), STEPS[2], tuple(state))
        from_a, from_b, core_far_a, core_far_b, *state = tied(
            from_a, from_b, core_far_a, core_far_b, *state
        )
        up_pieces = (up_a, far_up_a, up_b, far_up_b, core_up_a, core_far_a, core_up_b, core_far_b)
        down_a, down_b = jnp.concatenate([down_a, from_a]), jnp.concatenate([down_b, from_b])
        down_a, down_b, *state = tied(down_a, down_b, *state)
        far_a, far_b = swap(down_a, "rep", 2), swap(down_b, "fsdp", 1)
        core_a, core_b = swap(down_a, "rep", 1), swap(down_b, "rep", 1)
        qkv, probs, mixed, first_in = state
        hidden, second_in, act, slope, w_up, w_proj, vec2, _, total = mlp_up(
            me, tokens, mixed, aux, up_pieces, True
        )
        far_a, far_b, core_a, core_b, hidden = tied(far_a, far_b, core_a, core_b, hidden)
        down_pieces = (
            down_a, far_a, down_b, far_b,
            core_a, swap(far_a, "rep", 1), core_b, swap(far_b, "rep", 1),
        )
    else:
        gather = lambda v: lax.all_gather(v, "fsdp", axis=0, tiled=True)
        w_qkv, w_proj = gather(qkv_weight), gather(proj_weight)
        packed = gather(jnp.concatenate([v.reshape(-1) for v in small] + [counted])[None])
        pieces, at = [], 0
        for v in small:
            pieces.append(packed[:, at : at + v.size])
            at += v.size
        rows = [p.reshape(1, -1).astype(F32) for p in pieces[:9]]
        offsets = rel_pos_h.shape[0]
        tables = [
            p.reshape(parts, offsets, -1).transpose(1, 0, 2).reshape(offsets, HEAD_DIM)
            for p in pieces[9:]
        ]
        gap = jnp.zeros((32 - offsets, HEAD_DIM), BF16)
        table = jnp.concatenate([tables[0], gap, tables[1], gap], axis=0)
        hole = jnp.zeros((HEAD_DIM, HEAD_DIM), BF16)
        rel = jnp.concatenate(
            [jnp.concatenate([table, hole], axis=1), jnp.concatenate([hole, table], axis=1)],
            axis=0,
        )
        rel_t = rel.T
        fill = jnp.zeros((4, D), F32)
        vec = jnp.concatenate(rows[0:4] + [fill])
        counts = lax.psum(jnp.sum(valid), ("rep", "fsdp")).reshape(1, 1)
        vec2 = jnp.concatenate(rows[4:8] + [fill])
        total = jnp.broadcast_to(counts, (1, 128))
        w_up, down_pieces = gather(up_weight), (gather(down_weight),)
        qkv, probs, mixed, first_in = attend(me, tokens, w_qkv, vec, rel, places, 0, count)
        hidden, second_in, act, slope = mlp_up(
            me, tokens, mixed, aux, (w_proj, w_up, vec2, rows[8]), False
        )
    out, grad_hidden, grad_attn, grad_down, grad_up, sums2, up_sum = mlp_down(
        me, hidden, act, slope, teacher, aux, w_up, vec2, total, down_pieces,
        loss_scale * 2.0 / D, in_pieces,
    )
    valid_total = total[0, 0]
    flat = lambda v: v.reshape(count * ROWS, v.shape[-1])
    if in_pieces:
        back_ends = (0, BACK_STEPS[0], BACK_STEPS[0] + BACK_STEPS[1])
        parts_of = lambda keep, come: lambda at, to: added(keep[at:to], come[at:to])
        keep_d, send_d = down_grad(me, flat(act), flat(grad_down), flat(mixed), flat(grad_attn))
        send_d, second_in = tied(send_d, flat(second_in))
        from_d = swap(send_d, "rep", 1)
        send_u = up_grad(me, second_in, flat(grad_up), 1)
        from_d, send_u, second_in = tied(from_d, send_u, second_in)
        sum_d = parts_of(keep_d, from_d)
        send_a, send_b = sum_d(4, 8), sum_d(12, 16)
        send_a, send_b, send_u, second_in = tied(send_a, send_b, send_u, second_in)
        from_u = swap(send_u, "rep", 1)
        from_a, from_b = swap(send_a, "rep", 2), swap(send_b, "fsdp", 1)
        keep_u = up_grad(me, second_in, flat(grad_up), 0)
        from_u, keep_u, grad_attn = tied(from_u, keep_u, grad_attn)
        sum_u = parts_of(keep_u, from_u)
        send_ua, send_ub = sum_u(4, 8), sum_u(12, 16)
        send_ua, send_ub, grad_attn = tied(send_ua, send_ub, grad_attn)
        back = (grad_attn, w_proj, qkv, probs, rel_t, places_t)
        state = attend_back(*back, 0, BACK_STEPS[0])
        from_a, from_b, *state = tied(from_a, from_b, *state)
        d_a, d_b = added(sum_d(0, 4), from_a), added(sum_d(8, 12), from_b)
        send_a, send_b = d_a[2:4], d_b[2:4]
        send_a, send_b, *state = tied(send_a, send_b, *state)
        from_a, from_b = swap(send_a, "fsdp", 1), swap(send_b, "rep", 2)
        from_ua, from_ub = swap(send_ua, "rep", 2), swap(send_ub, "fsdp", 1)
        state = attend_back(*back, back_ends[1], BACK_STEPS[1], tuple(state))
        from_a, from_b, from_ua, from_ub, *state = tied(from_a, from_b, from_ua, from_ub, *state)
        d_a, d_b = added(d_a[0:2], from_a), added(d_b[0:2], from_b)
        u_a, u_b = added(sum_u(0, 4), from_ua), added(sum_u(8, 12), from_ub)
        sends_d = (d_a[0], d_a[1], d_b[0], d_b[1])
        send_ua, send_ub = u_a[2:4], u_b[2:4]
        *sends_d, send_ua, send_ub, s0, s1, s2 = tied(*sends_d, send_ua, send_ub, *state)
        from_z = [swap(v, "fsdp", mask) for v, mask in zip(sends_d[1:], (2, 4, 6))]
        from_ua, from_ub = swap(send_ua, "fsdp", 1), swap(send_ub, "rep", 2)
        state = attend_back(*back, back_ends[2], BACK_STEPS[2], (s0, s1, s2))
        from_ua, from_ub, from_z[0], dqkv, rel_grad, qv_sum = tied(
            from_ua, from_ub, from_z[0], *state
        )
        input_grad, sums1 = input_back(me, dqkv, w_qkv, tokens, grad_hidden, vec, 0, count)
        from_z[1], from_z[2], sums1, dqkv = tied(from_z[1], from_z[2], sums1, dqkv)
        own_d = sends_d[0].astype(F32)
        for v in from_z:
            own_d = own_d + v.astype(F32)
        u_a, u_b = added(u_a[0:2], from_ua), added(u_b[0:2], from_ub)
        notes = pack(me, sums1, qv_sum, sums2, up_sum, rel_grad)
        sends_u = (u_a[0], u_a[1], u_b[0], u_b[1])
        own_d, *sends_u, notes = tied(own_d.astype(BF16), *sends_u, notes)
        from_z = [swap(v, "fsdp", mask) for v, mask in zip(sends_u[1:], (2, 4, 6))]
        first_in, dqkv = flat(first_in), flat(dqkv)
        send = qkv_grad(me, first_in, dqkv, notes, 1)
        from_z[0], send, first_in, input_grad = tied(from_z[0], send, first_in, input_grad)
        from_core = swap(send, "rep", 1)
        keep = qkv_grad(me, first_in, dqkv, notes, 0)
        from_core, keep = tied(from_core, keep)
        both = parts_of(keep, from_core)
        send_a, send_b = both(4, 8), both(12, 16)
        send_a, send_b = tied(send_a, send_b)
        from_a, from_b = swap(send_a, "rep", 2), swap(send_b, "fsdp", 1)
        from_a, from_b, *from_z = tied(from_a, from_b, *from_z)
        sum_a, sum_b = added(both(0, 4), from_a), added(both(8, 12), from_b)
        own_u = sends_u[0].astype(F32)
        for v in from_z:
            own_u = own_u + v.astype(F32)
        own = jnp.concatenate([own_u.astype(BF16), own_d], axis=0)
        from_a, from_b = swap(sum_a[2:4], "fsdp", 1), swap(sum_b[2:4], "rep", 2)
        from_a, from_b = tied(from_a, from_b)
        sum_a, sum_b = added(sum_a[0:2], from_a), added(sum_b[0:2], from_b)
        sends = (sum_a[0], sum_a[1], sum_b[0], sum_b[1])
        *sends, own = tied(*sends, own)
        from_z = [swap(v, "fsdp", mask) for v, mask in zip(sends[1:], (2, 4, 6))]
        from_x = swap(own, "rep", 2)
        *from_z, from_x = tied(*from_z, from_x)
        own_q = sends[0].astype(F32)
        for v in from_z:
            own_q = own_q + v.astype(F32)
        own_q = own_q.astype(BF16)
        from_xq = swap(own_q, "rep", 2)
        d_up, d_down, d_proj = shard(
            me, (own, from_x, swap(own, "rep", 1), swap(from_x, "rep", 1))
        )
        from_xq, d_up = tied(from_xq, d_up)
        d_qkv, mine = qkv_shard(
            me, total, (own_q, from_xq, swap(own_q, "rep", 1), swap(from_xq, "rep", 1))
        )
        vectors = [mine[at, 0:96] for at in range(8)]
        tables = [mine[0:27, 96 + 8 * at : 104 + 8 * at] for at in range(2)]
        outs = vectors + [mine[27:30].reshape(-1)] + tables
        loss = mine[31, 0]
    else:
        scatter = lambda v: lax.psum(
            lax.psum_scatter(v, "fsdp", scatter_dimension=0, tiled=True), "rep"
        ).astype(F32)
        d_down = scatter(weight_grad(flat(act), flat(grad_down), True))
        d_up = scatter(weight_grad(flat(second_in), flat(grad_up)))
        d_proj = scatter(weight_grad(flat(mixed), flat(grad_attn)))
        back = (grad_attn, w_proj, qkv, probs, rel_t, places_t)
        dqkv, rel_grad, qv_sum = attend_back(*back, 0, count)
        d_qkv = scatter(weight_grad(flat(first_in), flat(dqkv)))
        input_grad, sums1 = input_back(me, dqkv, w_qkv, tokens, grad_hidden, vec, 0, count)
        offsets = rel_pos_h.shape[0]
        rel_sum = rel_grad[0:64, 0:64] + rel_grad[64:128, 64:128]
        vectors = [sums1[0], sums1[1], qv_sum[0], qv_sum[1], sums2[4], sums2[2], sums2[3],
                   sums2[1], up_sum[0]]
        own = jnp.concatenate(
            [v.reshape(parts, -1) for v in vectors]
            + [
                rel_sum[at : at + offsets].reshape(offsets, parts, -1).transpose(1, 0, 2)
                .reshape(parts, -1) for at in (0, 32)
            ]
            + [jnp.broadcast_to(jnp.sum(sums2[0]), (parts, 1))],
            axis=1,
        )
        mine = lax.dynamic_index_in_dim(
            lax.psum(own, ("rep", "fsdp")), part_at, 0, keepdims=False
        )
        outs, at = [], 0
        for v in small:
            outs.append(mine[at : at + v.size].reshape(v.shape))
            at += v.size
        loss = mine[at] / (valid_total * D)
    (g_gain1, g_shift1, g_qb, g_vb, g_pb, g_gain2, g_shift2, g_db, g_ub, g_rh, g_rw) = outs
    return (
        out, loss, input_grad.transpose(1, 0, 2), g_gain1, g_shift1, d_qkv, g_qb, g_vb, g_rh, g_rw, d_proj, g_pb,
        g_gain2, g_shift2, d_up, g_ub, d_down, g_db,
    )


def solution(mesh):
    windows = P(("rep", "fsdp"), None, None)
    vector = P("fsdp")
    matrix = P("fsdp", None)
    table = P(None, "fsdp")
    in_specs = (
        windows, windows, P(("rep", "fsdp"), None), vector, vector, matrix, vector, vector, table,
        table, matrix, vector, vector, vector, matrix, vector, matrix, vector,
    )
    out_specs = (windows, P(), windows) + in_specs[3:]
    return jax.shard_map(body, mesh=mesh, in_specs=in_specs, out_specs=out_specs, check_vma=False)
```

```python
import functools
import math

import jax
import jax.numpy as jnp
import numpy as np
from jax import lax
from jax.experimental import pallas as pl
from jax.experimental.pallas import tpu as pltpu
from jax.sharding import PartitionSpec as P

D = 768
HEADS = 12
HEAD_DIM = 64
MLP = 3072
WIN = 14
MAP = 64
SLOTS = WIN * WIN
ROWS = 208
LANES = 256
PAIRS = HEADS // 2
PAIR = 2 * HEAD_DIM
SIDE = (MAP + WIN - 1) // WIN
LN_EPS = 1e-06
SQRT_HALF = 0.7071067811865476
INV_ROOT_TAU = 0.3989422804014327
F32 = jnp.float32
BF16 = jnp.bfloat16
QKV_HALF = 3 * D // 2
NOTES = 128
STEPS = (3, 4, 1)
COST = 1e8
BACK_STEPS = (2, 4, 2)


def nn(left, right):
    return jnp.dot(left, right, preferred_element_type=F32)


def nt(left, right):
    return lax.dot_general(left, right, (((1,), (1,)), ((), ())), preferred_element_type=F32)


def tn(left, right):
    return lax.dot_general(left, right, (((0,), (0,)), ((), ())), preferred_element_type=F32)


def key_places():
    table = np.zeros((ROWS, HEAD_DIM), np.float32)
    for slot in range(SLOTS):
        for base in (0, 32):
            table[slot, base + WIN - 1 - slot // WIN] = 1.0
            table[slot, base + 16 + WIN - 1 - slot % WIN] = 1.0
    return table


def keep_column(base_ref, window):
    slot = lax.broadcasted_iota(jnp.int32, (ROWS, 1), 0)
    row = lax.shift_right_logical(slot * 4682, 16)
    col = slot - row * WIN
    place = lax.rem(base_ref[2] + window, SIDE * SIDE)
    place_row = lax.div(place, SIDE)
    place_col = place - place_row * SIDE
    inside = (slot < SLOTS) & (row + place_row * WIN < MAP) & (col + place_col * WIN < MAP)
    return inside.astype(F32)


def lane_places():
    slot = lax.broadcasted_iota(jnp.int32, (1, LANES), 1)
    row = lax.shift_right_logical(slot * 4682, 16)
    return row, slot - row * WIN


def norm_parts(values):
    mean = jnp.mean(values, axis=-1, keepdims=True)
    centred = values - mean
    inv_std = lax.rsqrt(jnp.mean(centred * centred, axis=-1, keepdims=True) + LN_EPS)
    return centred * inv_std, inv_std


def norm_grad(grad, scaled, inv_std, gain):
    grad_scaled = grad * gain
    first = jnp.mean(grad_scaled, axis=-1, keepdims=True)
    second = jnp.mean(grad_scaled * scaled, axis=-1, keepdims=True)
    return inv_std * (grad_scaled - first - scaled * second)


def up_by(values, amount):
    take = lambda bit: (amount & bit) != 0
    part = jnp.where(take(8), values[8:32], values[0:24])
    part = jnp.where(take(4), pltpu.roll(part, 20, 0), part)
    part = jnp.where(take(2), pltpu.roll(part, 22, 0), part)
    part = jnp.where(take(1), pltpu.roll(part, 23, 0), part)
    return part[0:16]


def down_by(values, amount):
    take = lambda bit: (amount & bit) != 0
    zeros = jnp.zeros((8, values.shape[1]), values.dtype)
    part = jnp.concatenate([values, zeros], axis=0)
    part = jnp.where(take(1), pltpu.roll(part, 1, 0), part)
    part = jnp.where(take(2), pltpu.roll(part, 2, 0), part)
    part = jnp.where(take(4), pltpu.roll(part, 4, 0), part)
    return jnp.where(
        take(8),
        jnp.concatenate([zeros, part], axis=0),
        jnp.concatenate([part, zeros], axis=0),
    )


def fill_rows(values):
    return jnp.concatenate(
        [values, jnp.zeros((LANES - ROWS,) + values.shape[1:], values.dtype)], axis=0
    )


def chunk_place(me_ref, index, far_y, along_y):
    mid, plane = index // 2, index % 2
    dist_x, dist_y = (far_y, mid) if along_y else (mid, far_y)
    plane = plane * 2 + (0 if along_y else 4)
    return (me_ref[0] // 2) ^ dist_x, me_ref[1] ^ (plane + dist_y)


ARRIVED = tuple((half, along_y, other) for other in (0, 1) for along_y in (True, False) for half in (0, 1))


def load_first(me_ref, parts, full, sem):
    core = me_ref[0] % 2
    for at, ref in enumerate(parts):
        along_y, other = at % 2 == 0, at // 2

        def start(index, carry, ref=ref, along_y=along_y, other=other):
            far_x, owner = chunk_place(me_ref, index % 4, index // 4, along_y)
            pltpu.make_async_copy(
                ref.at[index, :, pl.ds(0, QKV_HALF)],
                full.at[
                    pl.ds(pl.multiple_of(owner * 96 + far_x * 48, 16), 48),
                    pl.ds(pl.multiple_of((core ^ other) * QKV_HALF, 128), QKV_HALF),
                ],
                sem.at[0],
            ).start()
            return carry

        lax.fori_loop(0, 8, start, 0)
    pltpu.make_async_copy(full, full, sem.at[0]).wait()


def piece_place(me_ref, index):
    group, high, mid, plane = index // 8, (index // 4) % 2, (index // 2) % 2, index % 2
    dist_x = jnp.where(group == 0, high, mid)
    dist_y = jnp.where(group == 0, mid, high)
    return (me_ref[0] // 2) ^ dist_x, me_ref[1] ^ (group * 4 + plane * 2 + dist_y)


def piece_index(me_ref, far_x, owner):
    dist = me_ref[1] ^ owner
    dist_x = (me_ref[0] // 2) ^ far_x
    dist_y, plane, group = dist % 2, (dist // 2) % 2, dist // 4
    high = jnp.where(group == 0, dist_x, dist_y)
    mid = jnp.where(group == 0, dist_y, dist_x)
    return group * 8 + high * 4 + mid * 2 + plane


def spread_rows(notes_of, owner_of, width, total):
    row = lax.broadcasted_iota(jnp.int32, (128, total), 0)
    col = lax.broadcasted_iota(jnp.int32, (128, total), 1)
    acc = None
    for at in range(8):
        put = ((row < width) & (col == row + owner_of(at) * width)).astype(BF16)
        part = nn(notes_of(at), put)
        acc = part if acc is None else acc + part
    return acc


def notes_kernel(me_ref, a_ref, b_ref, c_ref, vec_ref, rel_ref, relt_ref, turn_ref):
    picks = [(a_ref, at, at % 2 * 2 + at // 2) for at in range(4)]
    picks += [(b_ref, at, 4 + at * 2) for at in range(2)] + [(c_ref, at, 5 + at * 2) for at in range(2)]
    owner_of = lambda at: me_ref[1] ^ picks[at][2]
    lanes = pl.ds(QKV_HALF, NOTES)
    vec_ref[...] = spread_rows(
        lambda at: picks[at][0][picks[at][1], 0:16, lanes], owner_of, 96, D
    )[0:8]
    for at in range(8):
        both = picks[at][0][picks[at][1], 16:32, lanes].astype(F32)
        for copy in range(2):
            place = pl.ds(pl.multiple_of(copy * 64 + owner_of(at) * 8, 8), 8)
            turn_ref[place, :] = jnp.concatenate([both[0:8, 0:32], both[8:16, 0:32]] * 2, axis=1)
    row = lax.broadcasted_iota(jnp.int32, (128, 128), 0)
    col = lax.broadcasted_iota(jnp.int32, (128, 128), 1)
    turned = jnp.where((row < 64) == (col < 64), turn_ref[...], 0.0)
    relt_ref[...] = turned.astype(BF16)
    rel_ref[...] = turned.T.astype(BF16)


def attend_kernel(*refs, first, pieces, earlier):
    base_ref, tok_ref = refs[0:2]
    at = 2 + max(pieces, 1)
    vec_ref, rel_ref, place_ref = refs[at : at + 3]
    at += 3 + earlier
    qkv_ref, prob_ref, mix_ref, fin_ref = refs[at : at + 4]
    if pieces:
        w_ref, sem, s_ref = refs[at + 4 :]

        @pl.when(pl.program_id(0) == 0)
        def _():
            load_first(base_ref, refs[2 : 2 + pieces], w_ref, sem)
    else:
        w_ref = refs[2]
        s_ref = refs[at + 4]
    keep = keep_column(base_ref, pl.program_id(0) + first)
    scaled, _ = norm_parts(tok_ref[0].astype(F32))
    first_in = (keep * (scaled * vec_ref[0:1, :] + vec_ref[1:2, :])).astype(BF16)
    fin_ref[0] = first_in
    for part in range(3):
        cols = pl.ds(part * D, D)
        total = nn(first_in, w_ref[:, cols])
        if part != 1:
            total = total + vec_ref[2 + part // 2 : 3 + part // 2, :]
        qkv_ref[0, :, cols] = total.astype(BF16)
    lane_row, lane_col = lane_places()
    low_half = lax.broadcasted_iota(jnp.int32, (ROWS, PAIR), 1) < HEAD_DIM
    tail_rows = lax.broadcasted_iota(jnp.int32, (16, LANES), 0) + 192
    places = place_ref[...]
    place_pair = jnp.concatenate([places, places], axis=1)

    def one_pair(pair, carry):
        at = pl.multiple_of(pair * PAIR, PAIR)
        query = qkv_ref[0, :, pl.ds(at, PAIR)]
        keys = qkv_ref[0, :, pl.ds(pl.multiple_of(D + at, PAIR), PAIR)]
        values = qkv_ref[0, :, pl.ds(pl.multiple_of(2 * D + at, PAIR), PAIR)]
        query_t = fill_rows(query).T
        offsets = nn(rel_ref[...], query_t)
        mixed = []
        for head in range(2):
            mine = offsets[head * HEAD_DIM : (head + 1) * HEAD_DIM]
            along = jnp.concatenate(
                [up_by(mine[0:32], lane_row), up_by(mine[32:64], lane_col)], axis=0
            )
            high = along.astype(BF16)
            rest = (along - high.astype(F32)).astype(BF16)
            scaled_q = query_t[head * HEAD_DIM : (head + 1) * HEAD_DIM] * jnp.asarray(
                HEAD_DIM ** (-0.5), BF16
            )
            if head == 0:
                query_ext = jnp.concatenate([scaled_q, high, rest], axis=0)
                keys_ext = jnp.where(low_half, keys, place_pair)
            else:
                query_ext = jnp.concatenate([high, rest, scaled_q], axis=0)
                keys_ext = jnp.where(low_half, place_pair, keys)
            s_ref[2 * pair + head] = nn(keys_ext, query_ext)
        return carry

    def soft(head, carry):
        scores = s_ref[head]
        scores = jnp.concatenate(
            [scores[0:192], jnp.where(tail_rows < SLOTS, scores[192:208], -1e30)], axis=0
        )
        peak = jnp.max(scores, axis=0, keepdims=True)
        expo = jnp.exp(scores - peak)
        total = jnp.sum(expo, axis=0, keepdims=True)
        prob_ref[0, head] = (expo * (1.0 / total)).astype(BF16)
        return carry

    def mix(pair, carry):
        at = pl.multiple_of(pair * PAIR, PAIR)
        values = qkv_ref[0, :, pl.ds(pl.multiple_of(2 * D + at, PAIR), PAIR)]
        mixed = [tn(prob_ref[0, 2 * pair + head], values)[0:ROWS].astype(BF16) for head in range(2)]
        mix_ref[0, :, pl.ds(at, PAIR)] = jnp.where(low_half, mixed[0], mixed[1])
        return carry

    lax.fori_loop(0, PAIRS, one_pair, 0, unroll=PAIRS)
    lax.fori_loop(0, HEADS, soft, 0, unroll=HEADS)
    lax.fori_loop(0, PAIRS, mix, 0, unroll=PAIRS)


def gelu_parts(pre):
    cumulative = 0.5 + 0.5 * lax.erf(pre * SQRT_HALF)
    bell = jnp.exp(pre * pre * (-0.5))
    return pre * cumulative, cumulative + pre * (bell * INV_ROOT_TAU)


def load_up(me_ref, pieces, up, proj, notes, sem):
    core = me_ref[0] % 2
    for array, (ref, (half, along_y, other)) in enumerate(zip(pieces, ARRIVED)):

        def start_small(index, carry, ref=ref, half=half, along_y=along_y, far_core=core ^ other, array=array):
            far_x, owner = chunk_place(me_ref, index, half, along_y)
            rows = pl.ds(pl.multiple_of(owner * 96 + far_x * 48, 16), 48)
            cols = pl.ds(pl.multiple_of(far_core * 384, 128), 384)
            pltpu.make_async_copy(
                ref.at[index, :, pl.ds(1536, 384)], proj.at[rows, cols], sem.at[1]
            ).start()
            pltpu.make_async_copy(
                ref.at[index, pl.ds(0, 16), pl.ds(1920, 128)], notes.at[array * 4 + index], sem.at[2]
            ).start()
            return carry

        lax.fori_loop(0, 4, start_small, 0)
    for ref, (half, along_y, other) in zip(pieces, ARRIVED):

        def start(index, carry, ref=ref, half=half, along_y=along_y, far_core=core ^ other):
            far_x, owner = chunk_place(me_ref, index, half, along_y)
            rows = pl.ds(pl.multiple_of(owner * 96 + far_x * 48, 16), 48)
            cols = pl.ds(pl.multiple_of(far_core * 1536, 128), 1536)
            pltpu.make_async_copy(
                ref.at[index, :, pl.ds(0, 1536)], up.at[rows, cols], sem.at[0]
            ).start()
            return carry

        lax.fori_loop(0, 4, start, 0)
    for at, full in ((2, notes), (1, proj)):
        pltpu.make_async_copy(full, full, sem.at[at]).wait()


def load_down(me_ref, pieces, down, sem):
    core = me_ref[0] % 2
    for ref, (half, along_y, other) in zip(pieces, ARRIVED):

        def start(index, carry, ref=ref, half=half, along_y=along_y, far_core=core ^ other):
            far_x, owner = chunk_place(me_ref, index, half, along_y)
            place = owner * 8 + far_core * 4 + far_x * 2
            pltpu.make_async_copy(ref.at[index], down.at[pl.ds(place, 2)], sem.at[0]).start()
            return carry

        lax.fori_loop(0, 4, start, 0)
    pltpu.make_async_copy(down, down, sem.at[0]).wait()


def up_kernel(*refs, group, pieces):
    rows = group * ROWS
    me_ref, tok_ref, mix_ref, keep_ref = refs[0:4]
    at = 4 + (pieces or 4)
    hid_ref, si_ref, act_ref, slope_ref = refs[at : at + 4]
    at += 4
    if pieces:
        up_ref, wp_ref, vec_ref, ub_ref, total_ref, notes, sem = refs[at:]

        @pl.when(pl.program_id(0) == 0)
        def _():
            load_up(me_ref, refs[4 : 4 + pieces], up_ref, wp_ref, notes, sem)
            picks = [(at, at % 2 * 2 + at // 2) for at in range(4)]
            picks += [(8 + at, 4 + at * 2) for at in range(2)] + [(12 + at, 5 + at * 2) for at in range(2)]
            owner_of = lambda at: me_ref[1] ^ picks[at][1]
            vec_ref[...] = spread_rows(
                lambda at: notes[picks[at][0]], owner_of, 96, D
            )[0:8]
            for at in range(8):
                lanes = pl.ds(pl.multiple_of(owner_of(at) * 384, 128), 384)
                own = notes[picks[at][0]].astype(F32)
                ub_ref[:, lanes] = jnp.concatenate([own[6:7], own[7:8], own[8:9]], axis=1)
            counts = notes[0].astype(F32)
            for at in range(1, 32):
                counts = counts + notes[at].astype(F32)
            counts = counts[5:6]
            lane = lax.broadcasted_iota(jnp.int32, (1, 128), 1)
            weight = jnp.where(lane == 0, 128.0, jnp.where(lane == 1, 1.0, 0.0))
            total_ref[...] = jnp.broadcast_to(
                jnp.sum(counts * weight, axis=1, keepdims=True), (1, 128)
            )
    else:
        wp_ref, up_ref, vec_ref, ub_ref = refs[4:8]
    pb_row, gain_row, shift_row = [vec_ref[at : at + 1, :] for at in range(3)]
    keep = keep_ref[...].reshape(rows, 2)[:, 0:1]
    attn_out = nn(mix_ref[...].reshape(rows, D), wp_ref[...]) + pb_row
    hidden = keep * (tok_ref[...].reshape(rows, D).astype(F32) + attn_out)
    hid_ref[...] = hidden.reshape(group, ROWS, D)
    scaled, _ = norm_parts(hidden)
    second_in = (scaled * gain_row + shift_row).astype(BF16)
    si_ref[...] = second_in.reshape(group, ROWS, D)
    if pieces:

        @pl.when(pl.program_id(0) == 0)
        def _():
            pltpu.make_async_copy(up_ref, up_ref, sem.at[0]).wait()

    for part in range(MLP // D):
        cols = slice(part * D, part * D + D)
        act, slope = gelu_parts(nn(second_in, up_ref[:, cols]) + ub_ref[:, cols])
        slope_ref[:, :, cols] = slope.astype(BF16).reshape(group, ROWS, D)
        act_ref[:, :, cols] = act.astype(BF16).reshape(group, ROWS, D)


def down_kernel(*refs, group, pieces, scale):
    step = pl.program_id(0)
    rows = group * ROWS
    me_ref, hid_ref, act_ref, slope_ref, teach_ref, aux_ref, up_ref, vec_ref, total_ref = refs[0:9]
    at = 9 + (pieces or 1)
    out_ref, gh_ref, ga_ref, gd_ref, gu_ref, sums_ref, usum_ref = refs[at : at + 7]
    if pieces:
        down3_ref, sem = refs[at + 7 :]

        @pl.when(step == 0)
        def _():
            load_down(me_ref, refs[9 : 9 + pieces], down3_ref, sem)

        down_rows = lambda part: down3_ref[pl.ds(part * 16, 16)].reshape(D, D)
    else:
        down_rows = lambda part: refs[9][pl.ds(part * D, D), :]

    @pl.when(step == 0)
    def _():
        sums_ref[...] = jnp.zeros_like(sums_ref)
        usum_ref[...] = jnp.zeros_like(usum_ref)

    gain_row, db_row = vec_ref[1:2, :], vec_ref[3:4, :]
    coef = scale / total_ref[:, 0:1]
    aux = aux_ref[...].reshape(rows, 2)
    keep, valid = aux[:, 0:1], aux[:, 1:2]
    hidden = hid_ref[...].reshape(rows, D)
    down = db_row
    for part in range(MLP // D):
        cols = slice(part * D, part * D + D)
        down = down + nn(act_ref[:, :, cols].reshape(rows, D), down_rows(part))
    final = keep * (hidden + down)
    for at in range(group):
        out_ref[at] = final[at * ROWS : at * ROWS + SLOTS].astype(BF16)
    error = final - teach_ref[...].reshape(rows, D).astype(F32)
    weighted = valid * error
    grad_final = coef * weighted
    grad_down = grad_final.astype(BF16)
    gd_ref[...] = grad_down.reshape(group, ROWS, D)
    sums_ref[0:1, :] += jnp.sum(weighted * error, axis=0, keepdims=True)
    sums_ref[1:2, :] += jnp.sum(grad_down.astype(F32), axis=0, keepdims=True)
    for part in range(MLP // D):
        cols = slice(part * D, part * D + D)
        slope = slope_ref[:, :, cols].reshape(rows, D).astype(F32)
        grad_up = (nt(grad_down, down_rows(part)) * slope).astype(BF16)
        gu_ref[:, :, cols] = grad_up.reshape(group, ROWS, D)
        usum_ref[:, cols] += jnp.sum(grad_up.astype(F32), axis=0, keepdims=True)
    grad_second = nt(gu_ref[...].reshape(rows, MLP), up_ref[...])
    scaled, inv_std = norm_parts(hidden)
    sums_ref[2:3, :] += jnp.sum(grad_second * scaled, axis=0, keepdims=True)
    sums_ref[3:4, :] += jnp.sum(grad_second, axis=0, keepdims=True)
    grad_hidden = keep * (grad_final + norm_grad(grad_second, scaled, inv_std, gain_row))
    gh_ref[...] = grad_hidden.reshape(group, ROWS, D)
    grad_attn = grad_hidden.astype(BF16)
    ga_ref[...] = grad_attn.reshape(group, ROWS, D)
    sums_ref[4:5, :] += jnp.sum(grad_attn.astype(F32), axis=0, keepdims=True)


def attend_back_kernel(*refs, earlier):
    ga_ref, wp_ref, qkv_ref, prob_ref, relt_ref, placet_ref = refs[0:6]
    dqkv_ref, rg_ref, qsum_ref, gm_ref, s_ref, g_ref, e_ref = refs[6 + earlier :]

    @pl.when(pl.program_id(0) == 0)
    def _():
        rg_ref[...] = refs[7][...] if earlier else jnp.zeros_like(rg_ref)
        qsum_ref[...] = refs[8][...] if earlier else jnp.zeros_like(qsum_ref)
        gm_ref[pl.ds(ROWS, LANES - ROWS), :] = jnp.zeros((LANES - ROWS, D), BF16)

    gm_ref[pl.ds(0, ROWS), :] = nt(ga_ref[0], wp_ref[...]).astype(BF16)
    lane_row, lane_col = lane_places()
    low_half = lax.broadcasted_iota(jnp.int32, (ROWS, PAIR), 1) < HEAD_DIM
    low_full = lax.broadcasted_iota(jnp.int32, (LANES, PAIR), 1) < HEAD_DIM
    blank = jnp.zeros((), BF16)
    scale = HEAD_DIM ** (-0.5)

    pair_at = lambda base, pair: pl.ds(base + pair * PAIR, PAIR)
    own = (
        lambda full: jnp.where(low_full, full, blank),
        lambda full: jnp.where(low_full, blank, full),
    )
    for pair in range(PAIRS):
        values = qkv_ref[0, :, pair_at(2 * D, pair)]
        stacked = jnp.concatenate(
            [jnp.where(low_half, values, blank), jnp.where(low_half, blank, values)], axis=0
        )
        grad_probs = nt(stacked, gm_ref[:, pair_at(0, pair)])
        s_ref[2 * pair] = grad_probs[0:ROWS]
        s_ref[2 * pair + 1] = grad_probs[ROWS : 2 * ROWS]
    for head in range(HEADS):
        probs = prob_ref[0, head].astype(F32)
        grad_p = s_ref[head]
        row_dot = jnp.sum(probs * grad_p, axis=0, keepdims=True)
        g_ref[head] = (probs * (grad_p - row_dot)).astype(BF16)
    for pair in range(PAIRS):
        query = fill_rows(qkv_ref[0, :, pair_at(0, pair)])
        grad_out = gm_ref[:, pair_at(0, pair)]
        grad_values = nn(prob_ref[0, 2 * pair], own[0](grad_out)) + nn(
            prob_ref[0, 2 * pair + 1], own[1](grad_out)
        )
        grad_keys = nn(g_ref[2 * pair], own[0](query)) + nn(g_ref[2 * pair + 1], own[1](query))
        grad_values = grad_values.astype(BF16)
        dqkv_ref[0, :, pair_at(D, pair)] = (grad_keys * scale).astype(BF16)
        dqkv_ref[0, :, pair_at(2 * D, pair)] = grad_values
        qsum_ref[1:2, pair_at(0, pair)] += jnp.sum(
            grad_values.astype(F32), axis=0, keepdims=True
        )
    for pair in range(PAIRS):
        keys_t = fill_rows(qkv_ref[0, :, pair_at(D, pair)]).T
        for head in range(2):
            keys_ext = jnp.concatenate(
                [keys_t[head * HEAD_DIM : (head + 1) * HEAD_DIM], placet_ref[...]], axis=0
            )
            e_ref[2 * pair + head] = nn(keys_ext, fill_rows(g_ref[2 * pair + head]))
    for pair in range(PAIRS):
        query = fill_rows(qkv_ref[0, :, pair_at(0, pair)])
        plain, spread = [], []
        for head in range(2):
            grad_ext = e_ref[2 * pair + head]
            plain.append(grad_ext[0:64])
            spread.append(down_by(grad_ext[64:80], lane_row))
            spread.append(down_by(grad_ext[80:96], lane_col))
        spread = jnp.concatenate(spread, axis=0).astype(BF16)
        grad_query = jnp.concatenate(plain, axis=0) * scale + nn(relt_ref[...], spread)
        rg_ref[...] += nn(spread, query)
        grad_query = grad_query.astype(BF16).T[0:ROWS]
        dqkv_ref[0, :, pair_at(0, pair)] = grad_query
        qsum_ref[0:1, pair_at(0, pair)] += jnp.sum(grad_query.astype(F32), axis=0, keepdims=True)


def input_kernel(
    base_ref, dqkv_ref, w_ref, tok_ref, gh_ref, vec_ref, *refs, group, first, earlier
):
    step = pl.program_id(0)
    out_ref, sums_ref = refs[earlier:]

    @pl.when(step == 0)
    def _():
        sums_ref[...] = refs[1][...] if earlier else jnp.zeros_like(sums_ref)

    for at in range(group):
        keep = keep_column(base_ref, first + step * group + at)
        grad_first = keep * nt(dqkv_ref[at], w_ref[...])
        scaled, inv_std = norm_parts(tok_ref[at].astype(F32))
        sums_ref[0:1, :] += jnp.sum(grad_first * scaled, axis=0, keepdims=True)
        sums_ref[1:2, :] += jnp.sum(grad_first, axis=0, keepdims=True)
        total = gh_ref[at] + norm_grad(grad_first, scaled, inv_std, vec_ref[0:1, :])
        out_ref[:, first + step * group + at, :] = total[0:SLOTS]


def weight_grad_kernel(*refs):
    left_ref, right_ref, out_ref = refs
    out_ref[...] = tn(left_ref[...], right_ref[...]).astype(BF16)


def qkv_grad_kernel(me_ref, left_ref, right_ref, notes_ref, out_ref, full, sem, *, other):
    full[...] = tn(left_ref[...], right_ref[...]).astype(BF16)
    core = (me_ref[0] % 2) ^ other

    def start(index, carry):
        far_x, owner = piece_place(me_ref, index)
        pltpu.make_async_copy(
            full.at[pl.ds(pl.multiple_of(owner * 96 + far_x * 48, 16), 48)],
            out_ref.at[index, :, pl.ds(0, QKV_HALF)],
            sem.at[0],
        ).start()
        pltpu.make_async_copy(
            notes_ref.at[core * 2 + far_x, owner],
            out_ref.at[index, :, pl.ds(QKV_HALF, NOTES)],
            sem.at[0],
        ).start()
        return carry

    lax.fori_loop(0, 16, start, 0)
    pltpu.make_async_copy(out_ref, out_ref, sem.at[0]).wait()


def up_grad_kernel(me_ref, left_ref, right_ref, out_ref, full, sem):
    step = pl.program_id(0)
    full[step] = tn(left_ref[...], right_ref[...]).astype(BF16)

    def start(index, carry):
        far_x, owner = piece_place(me_ref, index)
        rows = pl.ds(pl.multiple_of(owner * 96 + far_x * 48, 16), 48)
        pltpu.make_async_copy(full.at[step, rows], out_ref.at[index, step], sem.at[0]).start()
        return carry

    lax.fori_loop(0, 16, start, 0)

    @pl.when(step == pl.num_programs(0) - 1)
    def _():
        pltpu.make_async_copy(out_ref, out_ref, sem.at[0]).wait()


def down_grad_kernel(
    me_ref, act_ref, gd_ref, mix_any, ga_any, keep_ref, send_ref, full, half, mix_ref, ga_ref, sem
):
    step = pl.program_id(0)
    last = pl.num_programs(0) - 1
    fetches = [
        pltpu.make_async_copy(mix_any, mix_ref, sem.at[2]),
        pltpu.make_async_copy(ga_any, ga_ref, sem.at[3]),
    ]

    @pl.when(step == 0)
    def _():
        for fetch in fetches:
            fetch.start()

    @pl.when(step < last)
    def _():
        full[step] = tn(act_ref[...], gd_ref[...]).astype(BF16).reshape(16, 48, D)

    @pl.when(step == last)
    def _():
        for fetch in fetches:
            fetch.wait()
        total = tn(mix_ref[...], ga_ref[...]).astype(BF16)
        for core in range(2):
            half[core] = total[:, core * 384 : core * 384 + 384]

    core = me_ref[0] % 2
    for ref, far_core, at in ((keep_ref, core, 0), (send_ref, 1 - core, 1)):

        def start_proj(index, carry, ref=ref, far_core=far_core, at=at):
            far_x, owner = piece_place(me_ref, index)
            rows = pl.ds(pl.multiple_of(owner * 96 + far_x * 48, 16), 48)
            for col in (0, 384):
                pltpu.make_async_copy(
                    half.at[far_core, rows], ref.at[index, 2, :, pl.ds(col, 384)], sem.at[at]
                ).start()
            return carry

        @pl.when(step < last)
        def _(ref=ref, far_core=far_core, at=at):
            for place in range(4):
                which, far_x = place // 2, place % 2
                pltpu.make_async_copy(
                    full.at[step, pl.ds(which * 8 + far_core * 4 + far_x * 2, 2)],
                    ref.at[piece_index(me_ref, far_x, step * 2 + which), pl.ds(0, 2)],
                    sem.at[at],
                ).start()

        @pl.when(step == last)
        def _(start_proj=start_proj):
            lax.fori_loop(0, 16, start_proj, 0)

    @pl.when(step == last)
    def _():
        pltpu.make_async_copy(keep_ref, keep_ref, sem.at[0]).wait()
        pltpu.make_async_copy(send_ref, send_ref, sem.at[1]).wait()


def whole(shape):
    zeros = (0,) * len(shape)
    return pl.BlockSpec(shape, lambda *_: zeros, pipeline_mode=pl.Buffered(1))


def whole_out(shape):
    zeros = (0,) * len(shape)
    return pl.BlockSpec(shape, lambda *_: zeros)


def windows_from(first, shape):
    tail = (0,) * (len(shape) - 1)
    return pl.BlockSpec(shape, lambda step: (step + first,) + tail)


SMEM = pl.BlockSpec(memory_space=pltpu.SMEM)
ANY = pl.BlockSpec(memory_space=pl.ANY)


def params(mebibytes=32):
    return pltpu.CompilerParams(
        vmem_limit_bytes=mebibytes * 1024 * 1024, dimension_semantics=("arbitrary",)
    )


def shape_of(shape, dtype):
    return jax.ShapeDtypeStruct(shape, dtype)


def cost(flops, moved):
    return pl.CostEstimate(flops=int(flops), bytes_accessed=int(moved), transcendentals=0)


def notes_of(me, near, far_x, far_y):
    return pl.pallas_call(
        notes_kernel,
        in_specs=[SMEM] + [whole(v.shape) for v in (near, far_x, far_y)],
        out_specs=[whole_out((8, D)), whole_out((PAIR, PAIR)), whole_out((PAIR, PAIR))],
        out_shape=[shape_of((8, D), F32)] + [shape_of((PAIR, PAIR), BF16)] * 2,
        grid=(1,),
        scratch_shapes=[pltpu.VMEM((128, 128), F32)],
        compiler_params=params(),
        cost_estimate=cost(COST, 1e5),
        name="notes",
    )(me, near, far_x, far_y)


def attend(me, tokens, weight, vec, rel, places, first, number, earlier=()):
    count = tokens.shape[0]
    win = lambda shape: windows_from(first, shape)
    pieces = len(weight) if isinstance(weight, tuple) else 0
    weights = weight if pieces else (weight,)
    weight_specs = [ANY] * pieces if pieces else [whole((D, 3 * D))]
    out_specs = [win((1, ROWS, 3 * D)), win((1, HEADS, ROWS, LANES)), win((1, ROWS, D)),
                 win((1, ROWS, D))]
    out_shape = [
        shape_of((count, ROWS, 3 * D), BF16), shape_of((count, HEADS, ROWS, LANES), BF16),
        shape_of((count, ROWS, D), BF16), shape_of((count, ROWS, D), BF16),
    ]
    scratch = [pltpu.VMEM((HEADS, ROWS, LANES), F32)]
    if pieces:
        out_specs.append(whole_out((D, 3 * D)))
        out_shape.append(shape_of((D, 3 * D), BF16))
        scratch.insert(0, pltpu.SemaphoreType.DMA((1,)))
    inputs = 5 + len(weights)
    return pl.pallas_call(
        functools.partial(attend_kernel, first=first, pieces=pieces, earlier=len(earlier)),
        grid=(number,),
        in_specs=[
            SMEM, win((1, ROWS, D)), *weight_specs, whole((8, D)),
            whole((PAIR, PAIR)), whole((ROWS, HEAD_DIM)), *([ANY] * len(earlier)),
        ],
        out_specs=out_specs,
        out_shape=out_shape,
        scratch_shapes=scratch,
        input_output_aliases={inputs + at: at for at in range(len(earlier))},
        compiler_params=params(54),
        cost_estimate=cost(COST, 1e5),
        name="attend",
    )(me, tokens, *weights, vec, rel, places, *earlier)


def mlp_up(me, tokens, mixed, aux, weights, chunked):
    count = tokens.shape[0]
    group = math.gcd(count, 2)
    win = lambda width: windows_from(0, (group, ROWS, width))
    arr = lambda width, dtype: shape_of((count, ROWS, width), dtype)
    pieces = len(weights) if chunked else 0
    out_specs = [win(D), win(D), win(MLP), win(MLP)]
    out_shape = [arr(D, F32), arr(D, BF16), arr(MLP, BF16), arr(MLP, BF16)]
    scratch = []
    if pieces:
        shapes = [((D, MLP), BF16), ((D, D), BF16), ((8, D), F32), ((1, MLP), F32), ((1, 128), F32)]
        out_specs += [whole_out(s) for s, _ in shapes]
        out_shape += [shape_of(s, t) for s, t in shapes]
        scratch += [pltpu.VMEM((32, 16, 128), BF16), pltpu.SemaphoreType.DMA((3,))]
    return pl.pallas_call(
        functools.partial(up_kernel, group=group, pieces=pieces),
        grid=(count // group,),
        in_specs=[SMEM, win(D), win(D), win(2)]
        + ([ANY] * pieces if pieces else [whole(v.shape) for v in weights]),
        out_specs=out_specs,
        out_shape=out_shape,
        scratch_shapes=scratch,
        compiler_params=params(60),
        cost_estimate=cost(COST * count, 1e5),
        name="mlp_up",
    )(me, tokens, mixed, aux, *weights)


def mlp_down(me, hidden, act, slope, teacher, aux, up, vec, total, weights, scale, chunked):
    count = hidden.shape[0]
    group = math.gcd(count, 2)
    win = lambda width: windows_from(0, (group, ROWS, width))
    plain = windows_from(0, (group, SLOTS, D))
    arr = lambda width, dtype: shape_of((count, ROWS, width), dtype)
    pieces = len(weights) if chunked else 0
    scratch = []
    if pieces:
        scratch += [pltpu.VMEM((MLP // 48, 48, D), BF16), pltpu.SemaphoreType.DMA((1,))]
    return pl.pallas_call(
        functools.partial(down_kernel, group=group, pieces=pieces, scale=scale),
        grid=(count // group,),
        in_specs=[SMEM, win(D), win(MLP), win(MLP), win(D), win(2), whole((D, MLP)), whole((8, D)),
                  whole((1, 128))]
        + ([ANY] * pieces if pieces else [whole(v.shape) for v in weights]),
        out_specs=[plain, win(D), win(D), win(D), win(MLP), whole_out((5, D)), whole_out((1, MLP))],
        out_shape=[
            shape_of((count, SLOTS, D), BF16), arr(D, F32), arr(D, BF16), arr(D, BF16),
            arr(MLP, BF16), shape_of((5, D), F32), shape_of((1, MLP), F32),
        ],
        scratch_shapes=scratch,
        compiler_params=params(60),
        cost_estimate=cost(COST * count, 1e5),
        name="mlp_down",
    )(me, hidden, act, slope, teacher, aux, up, vec, total, *weights)


def attend_back(grad_attn, proj, qkv, probs, rel_t, places_t, first, number, earlier=()):
    count = grad_attn.shape[0]
    win = lambda shape: windows_from(first, shape)
    before = [ANY, whole((PAIR, PAIR)), whole((2, D))] if earlier else []
    return pl.pallas_call(
        functools.partial(attend_back_kernel, earlier=len(earlier)),
        grid=(number,),
        in_specs=[
            win((1, ROWS, D)), whole((D, D)), win((1, ROWS, 3 * D)), win((1, HEADS, ROWS, LANES)),
            whole((PAIR, PAIR)), whole((32, LANES)), *before,
        ],
        out_specs=[win((1, ROWS, 3 * D)), whole_out((PAIR, PAIR)), whole_out((2, D))],
        out_shape=[
            shape_of((count, ROWS, 3 * D), BF16), shape_of((PAIR, PAIR), F32),
            shape_of((2, D), F32),
        ],
        scratch_shapes=[
            pltpu.VMEM((LANES, D), BF16), pltpu.VMEM((HEADS, ROWS, LANES), F32),
            pltpu.VMEM((HEADS, ROWS, LANES), BF16), pltpu.VMEM((HEADS, 96, LANES), F32),
        ],
        input_output_aliases={6: 0} if earlier else {},
        compiler_params=params(48),
        cost_estimate=cost(COST, 1e5),
        name="attend_back",
    )(grad_attn, proj, qkv, probs, rel_t, places_t, *earlier)


def input_back(me, dqkv, weight, tokens, grad_hidden, vec, first, number, earlier=()):
    count = tokens.shape[0]
    group = math.gcd(math.gcd(first, number), 2)
    win = lambda shape: windows_from(first // group, shape)
    before = [ANY, whole((2, D))] if earlier else []
    return pl.pallas_call(
        functools.partial(input_kernel, group=group, first=first, earlier=len(earlier)),
        grid=(number // group,),
        in_specs=[
            SMEM, win((group, ROWS, 3 * D)), whole((D, 3 * D)), win((group, ROWS, D)),
            win((group, ROWS, D)), whole((8, D)), *before,
        ],
        out_specs=[whole_out((SLOTS, count, D)), whole_out((2, D))],
        out_shape=[shape_of((SLOTS, count, D), F32), shape_of((2, D), F32)],
        input_output_aliases={6: 0} if earlier else {},
        compiler_params=params(44),
        cost_estimate=cost(COST, 1e5),
        name="input_back",
    )(me, dqkv, weight, tokens, grad_hidden, vec, *earlier)


def pick(left, right):
    return jnp.dot(left, right, preferred_element_type=F32, precision=lax.Precision.HIGHEST)


def pack_kernel(me_ref, one_ref, qv_ref, two_ref, up_ref, rel_ref, out_ref):
    vectors = jnp.concatenate(
        [one_ref[0:2], qv_ref[0:2], two_ref[4:5], two_ref[2:4], two_ref[1:2]], axis=0
    )
    error = jnp.sum(two_ref[0:1, :], axis=1, keepdims=True)
    high = error.astype(BF16).astype(F32)
    middle = (error - high).astype(BF16).astype(F32)
    lane = lax.broadcasted_iota(jnp.int32, (1, 128), 1) - 3 * (me_ref[0] * 8 + me_ref[1])
    error = jnp.where(
        lane == 0, high, jnp.where(lane == 1, middle, jnp.where(lane == 2, error - high - middle, 0.0))
    )
    tables = rel_ref[0:64, 0:64] + rel_ref[64:128, 64:128]
    row = lax.broadcasted_iota(jnp.int32, (D, 128), 0)
    col = lax.broadcasted_iota(jnp.int32, (D, 128), 1)
    small_row = lax.broadcasted_iota(jnp.int32, (32, 128), 0)
    lanes_row = lax.broadcasted_iota(jnp.int32, (64, 128), 0)
    lanes_col = lax.broadcasted_iota(jnp.int32, (64, 128), 1)
    out_ref[...] = jnp.zeros_like(out_ref)
    for owner in range(8):
        own = pick(vectors, ((col < 96) & (row == col + owner * 96)).astype(F32))
        total = jnp.concatenate([own, jnp.zeros((24, 128), F32)], axis=0)
        for which in range(2):
            lane = lanes_col - 96 - 8 * which
            put = ((lane >= 0) & (lane < 8) & (lanes_row == lane + owner * 8)).astype(F32)
            total = total + pick(tables[32 * which : 32 * which + 32], put)
        for part in range(3):
            at = owner * 384 + part * 128
            total = jnp.where(small_row == 27 + part, up_ref[:, at : at + 128], total)
        total = jnp.where(small_row == 30, error, total).astype(BF16)
        for quarter in range(4):
            out_ref[quarter, owner, 0:8] = total[quarter * 8 : quarter * 8 + 8]


def pack(me, *sums):
    return pl.pallas_call(
        pack_kernel,
        grid=(1,),
        in_specs=[SMEM] + [whole(v.shape) for v in sums],
        out_specs=whole_out((4, 8, 48, NOTES)),
        out_shape=shape_of((4, 8, 48, NOTES), BF16),
        compiler_params=params(),
        cost_estimate=cost(COST, 1e5),
        name="pack",
    )(me, *sums)


def qkv_shard_kernel(me_ref, total_ref, *refs):
    quarters, out_ref, notes_ref = refs[0:4], refs[4], refs[5]
    core, far_x = me_ref[0] % 2, me_ref[0] // 2
    for at, ref in enumerate(quarters):
        this_core, this_x = core ^ (at // 2), far_x ^ (at % 2)
        rows = pl.ds(pl.multiple_of(this_x * 48, 16), 48)
        cols = pl.ds(pl.multiple_of(this_core * QKV_HALF, 128), QKV_HALF)
        out_ref[rows, cols] = ref[:, 0:QKV_HALF].astype(F32)
        here = pl.ds(pl.multiple_of((this_core * 2 + this_x) * 8, 8), 8)
        notes_ref[here, :] = ref[0:16, QKV_HALF : QKV_HALF + NOTES].astype(F32)[0:8]
    errors = jnp.sum(notes_ref[30:31, :], axis=1, keepdims=True)
    notes_ref[31:32, :] = errors / (total_ref[...] * D)


def qkv_shard(me, total, quarters):
    shapes = [(96, 3 * D), (32, 128)]
    return pl.pallas_call(
        qkv_shard_kernel,
        grid=(1,),
        in_specs=[SMEM, whole((1, 128))] + [whole(v.shape) for v in quarters],
        out_specs=[whole_out(shape) for shape in shapes],
        out_shape=[shape_of(shape, F32) for shape in shapes],
        compiler_params=params(),
        cost_estimate=cost(COST, 1e5),
        name="qkv_shard",
    )(me, total, *quarters)


def shard_kernel(me_ref, *refs):
    quarters, (up_ref, down_ref, proj_ref) = refs[0:4], refs[4:]
    core, far_x = me_ref[0] % 2, me_ref[0] // 2
    for at, ref in enumerate(quarters):
        this_core, this_x = core ^ (at // 2), far_x ^ (at % 2)
        rows = pl.ds(pl.multiple_of(this_x * 48, 16), 48)
        for block in range(2):
            cols = pl.ds(pl.multiple_of(this_core * 1536 + block * D, 128), D)
            up_ref[rows, cols] = ref[block].astype(F32)
            at_row = this_core * 192 + this_x * 96 + block * 48
            down_ref[pl.ds(pl.multiple_of(at_row, 16), 48), :] = ref[2 + block].astype(F32)
        cols = pl.ds(pl.multiple_of(this_core * 384, 128), 384)
        proj_ref[rows, cols] = ref[4, :, 0:384].astype(F32)


def shard(me, quarters):
    shapes = [(96, MLP), (384, D), (96, D)]
    return pl.pallas_call(
        shard_kernel,
        grid=(1,),
        in_specs=[SMEM] + [whole(v.shape) for v in quarters],
        out_specs=[whole_out(shape) for shape in shapes],
        out_shape=[shape_of(shape, F32) for shape in shapes],
        compiler_params=params(),
        cost_estimate=cost(COST, 1e5),
        name="shard",
    )(me, *quarters)


def column_blocks(rows):
    return pl.BlockSpec((rows, D), lambda step: (0, step))


def weight_grad(left, right, by_rows=False):
    rows = left.shape[0]
    blocks = (left if by_rows else right).shape[1] // D
    moving, still = column_blocks(rows), whole((rows, D))
    return pl.pallas_call(
        weight_grad_kernel,
        grid=(blocks,),
        in_specs=[moving, still] if by_rows else [still, moving],
        out_specs=pl.BlockSpec((D, D), (lambda s: (s, 0)) if by_rows else (lambda s: (0, s))),
        out_shape=shape_of((left.shape[1], right.shape[1]), BF16),
        compiler_params=params(44),
        name="weight_grad",
    )(left, right)


def qkv_grad(me, left, right, notes, other):
    rows = left.shape[0]
    return pl.pallas_call(
        functools.partial(qkv_grad_kernel, other=other),
        grid_spec=pltpu.PrefetchScalarGridSpec(
            num_scalar_prefetch=1,
            grid=(1,),
            in_specs=[
                whole((rows, D)),
                pl.BlockSpec((rows, QKV_HALF), lambda step, me: (0, (me[0] % 2) ^ other)),
                whole((4, 8, 48, NOTES)),
            ],
            out_specs=ANY,
            scratch_shapes=[pltpu.VMEM((D, QKV_HALF), BF16), pltpu.SemaphoreType.DMA((1,))],
        ),
        out_shape=shape_of((16, 48, QKV_HALF + NOTES), BF16),
        compiler_params=params(48),
        cost_estimate=cost(COST, 1e5),
        name="qkv_grad",
    )(me, left, right, notes)


def up_grad(me, left, right, other):
    rows = left.shape[0]
    return pl.pallas_call(
        up_grad_kernel,
        grid_spec=pltpu.PrefetchScalarGridSpec(
            num_scalar_prefetch=1,
            grid=(2,),
            in_specs=[
                whole((rows, D)),
                pl.BlockSpec((rows, D), lambda step, me: (0, ((me[0] % 2) ^ other) * 2 + step)),
            ],
            out_specs=ANY,
            scratch_shapes=[pltpu.VMEM((2, D, D), BF16), pltpu.SemaphoreType.DMA((1,))],
        ),
        out_shape=shape_of((16, 2, 48, D), BF16),
        compiler_params=params(60),
        cost_estimate=cost(COST, 1e5),
        name="up_grad",
    )(me, left, right)


def down_grad(me, act, grad_down, mixed, grad_attn):
    rows = act.shape[0]
    return pl.pallas_call(
        down_grad_kernel,
        grid=(5,),
        in_specs=[
            SMEM, pl.BlockSpec((rows, D), lambda step: (0, jnp.minimum(step, 3))),
            whole((rows, D)), ANY, ANY,
        ],
        out_specs=[ANY] * 2,
        out_shape=[shape_of((16, 3, 48, D), BF16)] * 2,
        scratch_shapes=[
            pltpu.VMEM((4, 16, 48, D), BF16), pltpu.VMEM((2, D, 384), BF16),
            pltpu.VMEM((rows, D), BF16), pltpu.VMEM((rows, D), BF16),
            pltpu.SemaphoreType.DMA((4,)),
        ],
        compiler_params=params(60),
        cost_estimate=cost(COST, 1e5),
        name="down_grad",
    )(me, act, grad_down, mixed, grad_attn)


def swap(values, axis, mask):
    size = lax.axis_size(axis)
    return lax.ppermute(values, axis, [(at, at ^ mask) for at in range(size)])


def joined(stack, axis, mask):
    return jnp.concatenate([stack, swap(stack, axis, mask)], axis=0)


def added(one, two):
    return (one.astype(F32) + two.astype(F32)).astype(BF16)


def tied(*values):
    return lax.optimization_barrier(values)


def cut(values, row, col, rows, cols):
    return lax.dynamic_slice(values, (row, col), (rows, cols))


def body(
    tokens, teacher, valid_mask, attn_gain, attn_shift, qkv_weight, query_bias, value_bias,
    rel_pos_h, rel_pos_w, proj_weight, proj_bias, mlp_gain, mlp_shift, up_weight, up_bias,
    down_weight, down_bias,
):
    count = tokens.shape[0]
    parts = lax.axis_size("fsdp")
    copies = lax.axis_size("rep")
    in_pieces = (copies, parts) == (4, 8)
    rep_at, part_at = lax.axis_index("rep"), lax.axis_index("fsdp")
    device = rep_at * parts + part_at
    core, far_x = rep_at % 2, rep_at // 2
    me = jnp.stack([rep_at, part_at, device * count]).astype(jnp.int32)
    window_ids = device * count + jnp.arange(count, dtype=jnp.int32)
    place = window_ids % (SIDE * SIDE)
    cells = jnp.arange(SLOTS, dtype=jnp.int32)
    inside = ((place // SIDE)[:, None] * WIN + (cells // WIN)[None, :] < MAP) & (
        (place % SIDE)[:, None] * WIN + (cells % WIN)[None, :] < MAP
    )
    keep = inside.astype(F32)
    valid = valid_mask.astype(F32) * keep
    counted = jnp.sum(valid_mask * inside.astype(jnp.int32))
    fill = ((0, 0), (0, ROWS - SLOTS), (0, 0))
    aux = jnp.pad(jnp.stack([keep, valid], axis=-1), fill)
    tokens, teacher = jnp.pad(tokens, fill), jnp.pad(teacher, fill)

    small = [attn_gain, attn_shift, query_bias, value_bias, proj_bias, mlp_gain, mlp_shift,
             down_bias, up_bias, rel_pos_h, rel_pos_w]
    places = jnp.asarray(key_places(), BF16)
    places_t = jnp.asarray(np.pad(key_places().T[0:32], ((0, 0), (0, LANES - ROWS))), BF16)
    counted = jnp.stack([counted // 128, counted % 128]).astype(BF16)
    loss_scale = 64.0 * D * count * copies * parts

    def noted(shape, *entries):
        total = jnp.zeros(shape, BF16)
        for values, row, col in entries:
            if values.ndim == 1:
                values = values[None]
            high, wide = values.shape
            total = total + jnp.pad(
                values, ((row, shape[0] - row - high), (col, shape[1] - col - wide))
            )
        return total

    if in_pieces:
        rect = cut(qkv_weight, far_x * 48, core * QKV_HALF, 48, QKV_HALF)
        notes = noted(
            (48, NOTES), *[(v, at, 0) for at, v in enumerate(small[0:4])],
            (rel_pos_h.T, 16, 0), (rel_pos_w.T, 24, 0),
        )
        rect = jnp.concatenate([rect, notes], axis=1)
        near = [rect] + [swap(rect, "fsdp", mask) for mask in (2, 4, 6)]
        up_rect = cut(up_weight, far_x * 48, core * 1536, 48, 1536)
        down_rect = cut(down_weight, core * 192 + far_x * 96, 0, 96, D)
        proj_rect = cut(proj_weight, far_x * 48, core * 384, 48, 384)
        notes = noted(
            (48, 128), *[(v, at, 0) for at, v in enumerate(small[4:8])],
            (up_bias.reshape(3, 128), 6, 0), (counted, 5, 0),
        )
        rects = jnp.concatenate([up_rect, proj_rect, notes], axis=1)
        down_rect = down_rect.reshape(2, 48, D)
        *near, rects, down_rect, aux = tied(*near, rects, down_rect, aux)
        planes = [rects] + [swap(rects, "fsdp", mask) for mask in (2, 4, 6)]
        near_a, near_b = jnp.stack(near[0:2]), jnp.stack(near[2:4])
        from_a, from_b = swap(near_a, "fsdp", 1), swap(near_b, "rep", 2)
        from_a, from_b, planes[1], tokens = tied(from_a, from_b, planes[1], tokens)
        near_a = jnp.concatenate([near_a, from_a])
        near_b = jnp.concatenate([near_b, from_b])
        far_a, far_b = swap(near_a, "rep", 2), swap(near_b, "fsdp", 1)
        far_a, far_b, planes[2], teacher = tied(far_a, far_b, planes[2], teacher)
        all_a, all_b = jnp.concatenate([near_a, far_a]), jnp.concatenate([near_b, far_b])
        other_a, other_b = swap(all_a, "rep", 1), swap(all_b, "rep", 1)
        vec, rel, rel_t = notes_of(me, near_a, near_b, far_b)
        vec, rel, rel_t, other_a, other_b, planes[3] = tied(
            vec, rel, rel_t, other_a, other_b, planes[3]
        )
        up_a, up_b = jnp.stack(planes[0:2]), jnp.stack(planes[2:4])
        up_a, up_b, vec = tied(up_a, up_b, vec)
        from_a, from_b = swap(up_a, "fsdp", 1), swap(up_b, "rep", 2)
        planes = [down_rect] + [swap(down_rect, "fsdp", mask) for mask in (2, 4, 6)]
        *state, w_qkv = attend(
            me, tokens, (all_a, all_b, other_a, other_b), vec, rel, places, 0, STEPS[0]
        )
        from_a, from_b, *rest = tied(from_a, from_b, *planes[1:], *state)
        planes, state = [down_rect] + rest[0:3], rest[3:]
        up_a, up_b = jnp.concatenate([up_a, from_a]), jnp.concatenate([up_b, from_b])
        down_a, down_b = jnp.stack(planes[0:2]), jnp.stack(planes[2:4])
        up_a, up_b, down_a, down_b, *state = tied(up_a, up_b, down_a, down_b, *state)
        far_up_a, far_up_b = swap(up_a, "rep", 2), swap(up_b, "fsdp", 1)
        core_up_a, core_up_b = swap(up_a, "rep", 1), swap(up_b, "rep", 1)
        state = attend(me, tokens, w_qkv, vec, rel, places, STEPS[0], STEPS[1], tuple(state))
        far_up_a, far_up_b, core_up_a, core_up_b, *state = tied(
            far_up_a, far_up_b, core_up_a, core_up_b, *state
        )
        from_a, from_b = swap(down_a, "fsdp", 1), swap(down_b, "rep", 2)
        core_far_a, core_far_b = swap(far_up_a, "rep", 1), swap(far_up_b, "rep", 1)
        state = attend(me, tokens, w_qkv, vec, rel, places, sum(STEPS[:2]), STEPS[2], tuple(state))
        from_a, from_b, core_far_a, core_far_b, *state = tied(
            from_a, from_b, core_far_a, core_far_b, *state
        )
        up_pieces = (up_a, far_up_a, up_b, far_up_b, core_up_a, core_far_a, core_up_b, core_far_b)
        down_a, down_b = jnp.concatenate([down_a, from_a]), jnp.concatenate([down_b, from_b])
        down_a, down_b, *state = tied(down_a, down_b, *state)
        far_a, far_b = swap(down_a, "rep", 2), swap(down_b, "fsdp", 1)
        core_a, core_b = swap(down_a, "rep", 1), swap(down_b, "rep", 1)
        qkv, probs, mixed, first_in = state
        hidden, second_in, act, slope, w_up, w_proj, vec2, _, total = mlp_up(
            me, tokens, mixed, aux, up_pieces, True
        )
        far_a, far_b, core_a, core_b, hidden = tied(far_a, far_b, core_a, core_b, hidden)
        down_pieces = (
            down_a, far_a, down_b, far_b,
            core_a, swap(far_a, "rep", 1), core_b, swap(far_b, "rep", 1),
        )
    else:
        gather = lambda v: lax.all_gather(v, "fsdp", axis=0, tiled=True)
        w_qkv, w_proj = gather(qkv_weight), gather(proj_weight)
        packed = gather(jnp.concatenate([v.reshape(-1) for v in small] + [counted])[None])
        pieces, at = [], 0
        for v in small:
            pieces.append(packed[:, at : at + v.size])
            at += v.size
        rows = [p.reshape(1, -1).astype(F32) for p in pieces[:9]]
        offsets = rel_pos_h.shape[0]
        tables = [
            p.reshape(parts, offsets, -1).transpose(1, 0, 2).reshape(offsets, HEAD_DIM)
            for p in pieces[9:]
        ]
        gap = jnp.zeros((32 - offsets, HEAD_DIM), BF16)
        table = jnp.concatenate([tables[0], gap, tables[1], gap], axis=0)
        hole = jnp.zeros((HEAD_DIM, HEAD_DIM), BF16)
        rel = jnp.concatenate(
            [jnp.concatenate([table, hole], axis=1), jnp.concatenate([hole, table], axis=1)],
            axis=0,
        )
        rel_t = rel.T
        fill = jnp.zeros((4, D), F32)
        vec = jnp.concatenate(rows[0:4] + [fill])
        counts = lax.psum(jnp.sum(valid), ("rep", "fsdp")).reshape(1, 1)
        vec2 = jnp.concatenate(rows[4:8] + [fill])
        total = jnp.broadcast_to(counts, (1, 128))
        w_up, down_pieces = gather(up_weight), (gather(down_weight),)
        qkv, probs, mixed, first_in = attend(me, tokens, w_qkv, vec, rel, places, 0, count)
        hidden, second_in, act, slope = mlp_up(
            me, tokens, mixed, aux, (w_proj, w_up, vec2, rows[8]), False
        )
    out, grad_hidden, grad_attn, grad_down, grad_up, sums2, up_sum = mlp_down(
        me, hidden, act, slope, teacher, aux, w_up, vec2, total, down_pieces,
        loss_scale * 2.0 / D, in_pieces,
    )
    valid_total = total[0, 0]
    flat = lambda v: v.reshape(count * ROWS, v.shape[-1])
    if in_pieces:
        back_ends = (0, BACK_STEPS[0], BACK_STEPS[0] + BACK_STEPS[1])
        parts_of = lambda keep, come: lambda at, to: added(keep[at:to], come[at:to])
        keep_d, send_d = down_grad(me, flat(act), flat(grad_down), flat(mixed), flat(grad_attn))
        send_d, second_in = tied(send_d, flat(second_in))
        from_d = swap(send_d, "rep", 1)
        send_u = up_grad(me, second_in, flat(grad_up), 1)
        from_d, send_u, second_in = tied(from_d, send_u, second_in)
        sum_d = parts_of(keep_d, from_d)
        send_a, send_b = sum_d(4, 8), sum_d(12, 16)
        send_a, send_b, send_u, second_in = tied(send_a, send_b, send_u, second_in)
        from_u = swap(send_u, "rep", 1)
        from_a, from_b = swap(send_a, "rep", 2), swap(send_b, "fsdp", 1)
        keep_u = up_grad(me, second_in, flat(grad_up), 0)
        from_u, keep_u, grad_attn = tied(from_u, keep_u, grad_attn)
        sum_u = parts_of(keep_u, from_u)
        send_ua, send_ub = sum_u(4, 8), sum_u(12, 16)
        send_ua, send_ub, grad_attn = tied(send_ua, send_ub, grad_attn)
        back = (grad_attn, w_proj, qkv, probs, rel_t, places_t)
        state = attend_back(*back, 0, BACK_STEPS[0])
        from_a, from_b, *state = tied(from_a, from_b, *state)
        d_a, d_b = added(sum_d(0, 4), from_a), added(sum_d(8, 12), from_b)
        send_a, send_b = d_a[2:4], d_b[2:4]
        send_a, send_b, *state = tied(send_a, send_b, *state)
        from_a, from_b = swap(send_a, "fsdp", 1), swap(send_b, "rep", 2)
        from_ua, from_ub = swap(send_ua, "rep", 2), swap(send_ub, "fsdp", 1)
        state = attend_back(*back, back_ends[1], BACK_STEPS[1], tuple(state))
        from_a, from_b, from_ua, from_ub, *state = tied(from_a, from_b, from_ua, from_ub, *state)
        d_a, d_b = added(d_a[0:2], from_a), added(d_b[0:2], from_b)
        u_a, u_b = added(sum_u(0, 4), from_ua), added(sum_u(8, 12), from_ub)
        sends_d = (d_a[0], d_a[1], d_b[0], d_b[1])
        send_ua, send_ub = u_a[2:4], u_b[2:4]
        *sends_d, send_ua, send_ub, s0, s1, s2 = tied(*sends_d, send_ua, send_ub, *state)
        from_z = [swap(v, "fsdp", mask) for v, mask in zip(sends_d[1:], (2, 4, 6))]
        from_ua, from_ub = swap(send_ua, "fsdp", 1), swap(send_ub, "rep", 2)
        state = attend_back(*back, back_ends[2], BACK_STEPS[2], (s0, s1, s2))
        from_ua, from_ub, from_z[0], dqkv, rel_grad, qv_sum = tied(
            from_ua, from_ub, from_z[0], *state
        )
        input_grad, sums1 = input_back(me, dqkv, w_qkv, tokens, grad_hidden, vec, 0, count)
        from_z[1], from_z[2], sums1, dqkv = tied(from_z[1], from_z[2], sums1, dqkv)
        own_d = sends_d[0].astype(F32)
        for v in from_z:
            own_d = own_d + v.astype(F32)
        u_a, u_b = added(u_a[0:2], from_ua), added(u_b[0:2], from_ub)
        notes = pack(me, sums1, qv_sum, sums2, up_sum, rel_grad)
        sends_u = (u_a[0], u_a[1], u_b[0], u_b[1])
        own_d, *sends_u, notes = tied(own_d.astype(BF16), *sends_u, notes)
        from_z = [swap(v, "fsdp", mask) for v, mask in zip(sends_u[1:], (2, 4, 6))]
        first_in, dqkv = flat(first_in), flat(dqkv)
        send = qkv_grad(me, first_in, dqkv, notes, 1)
        from_z[0], send, first_in, input_grad = tied(from_z[0], send, first_in, input_grad)
        from_core = swap(send, "rep", 1)
        keep = qkv_grad(me, first_in, dqkv, notes, 0)
        from_core, keep = tied(from_core, keep)
        both = parts_of(keep, from_core)
        send_a, send_b = both(4, 8), both(12, 16)
        send_a, send_b = tied(send_a, send_b)
        from_a, from_b = swap(send_a, "rep", 2), swap(send_b, "fsdp", 1)
        from_a, from_b, *from_z = tied(from_a, from_b, *from_z)
        sum_a, sum_b = added(both(0, 4), from_a), added(both(8, 12), from_b)
        own_u = sends_u[0].astype(F32)
        for v in from_z:
            own_u = own_u + v.astype(F32)
        own = jnp.concatenate([own_u.astype(BF16), own_d], axis=0)
        from_a, from_b = swap(sum_a[2:4], "fsdp", 1), swap(sum_b[2:4], "rep", 2)
        from_a, from_b = tied(from_a, from_b)
        sum_a, sum_b = added(sum_a[0:2], from_a), added(sum_b[0:2], from_b)
        sends = (sum_a[0], sum_a[1], sum_b[0], sum_b[1])
        *sends, own = tied(*sends, own)
        from_z = [swap(v, "fsdp", mask) for v, mask in zip(sends[1:], (2, 4, 6))]
        from_x = swap(own, "rep", 2)
        *from_z, from_x = tied(*from_z, from_x)
        own_q = sends[0].astype(F32)
        for v in from_z:
            own_q = own_q + v.astype(F32)
        own_q = own_q.astype(BF16)
        from_xq = swap(own_q, "rep", 2)
        d_up, d_down, d_proj = shard(
            me, (own, from_x, swap(own, "rep", 1), swap(from_x, "rep", 1))
        )
        from_xq, d_up = tied(from_xq, d_up)
        d_qkv, mine = qkv_shard(
            me, total, (own_q, from_xq, swap(own_q, "rep", 1), swap(from_xq, "rep", 1))
        )
        vectors = [mine[at, 0:96] for at in range(8)]
        tables = [mine[0:27, 96 + 8 * at : 104 + 8 * at] for at in range(2)]
        outs = vectors + [mine[27:30].reshape(-1)] + tables
        loss = mine[31, 0]
    else:
        scatter = lambda v: lax.psum(
            lax.psum_scatter(v, "fsdp", scatter_dimension=0, tiled=True), "rep"
        ).astype(F32)
        d_down = scatter(weight_grad(flat(act), flat(grad_down), True))
        d_up = scatter(weight_grad(flat(second_in), flat(grad_up)))
        d_proj = scatter(weight_grad(flat(mixed), flat(grad_attn)))
        back = (grad_attn, w_proj, qkv, probs, rel_t, places_t)
        dqkv, rel_grad, qv_sum = attend_back(*back, 0, count)
        d_qkv = scatter(weight_grad(flat(first_in), flat(dqkv)))
        input_grad, sums1 = input_back(me, dqkv, w_qkv, tokens, grad_hidden, vec, 0, count)
        offsets = rel_pos_h.shape[0]
        rel_sum = rel_grad[0:64, 0:64] + rel_grad[64:128, 64:128]
        vectors = [sums1[0], sums1[1], qv_sum[0], qv_sum[1], sums2[4], sums2[2], sums2[3],
                   sums2[1], up_sum[0]]
        own = jnp.concatenate(
            [v.reshape(parts, -1) for v in vectors]
            + [
                rel_sum[at : at + offsets].reshape(offsets, parts, -1).transpose(1, 0, 2)
                .reshape(parts, -1) for at in (0, 32)
            ]
            + [jnp.broadcast_to(jnp.sum(sums2[0]), (parts, 1))],
            axis=1,
        )
        mine = lax.dynamic_index_in_dim(
            lax.psum(own, ("rep", "fsdp")), part_at, 0, keepdims=False
        )
        outs, at = [], 0
        for v in small:
            outs.append(mine[at : at + v.size].reshape(v.shape))
            at += v.size
        loss = mine[at] / (valid_total * D)
    (g_gain1, g_shift1, g_qb, g_vb, g_pb, g_gain2, g_shift2, g_db, g_ub, g_rh, g_rw) = outs
    return (
        out, loss, input_grad.transpose(1, 0, 2), g_gain1, g_shift1, d_qkv, g_qb, g_vb, g_rh, g_rw, d_proj, g_pb,
        g_gain2, g_shift2, d_up, g_ub, d_down, g_db,
    )


def solution(mesh):
    windows = P(("rep", "fsdp"), None, None)
    vector = P("fsdp")
    matrix = P("fsdp", None)
    table = P(None, "fsdp")
    in_specs = (
        windows, windows, P(("rep", "fsdp"), None), vector, vector, matrix, vector, vector, table,
        table, matrix, vector, vector, vector, matrix, vector, matrix, vector,
    )
    out_specs = (windows, P(), windows) + in_specs[3:]
    return jax.shard_map(body, mesh=mesh, in_specs=in_specs, out_specs=out_specs, check_vma=False)
```

```python
import functools
import math

import jax
import jax.numpy as jnp
import numpy as np
from jax import lax
from jax.experimental import pallas as pl
from jax.experimental.pallas import tpu as pltpu
from jax.sharding import PartitionSpec as P

D = 768
HEADS = 12
HEAD_DIM = 64
MLP = 3072
WIN = 14
MAP = 64
SLOTS = WIN * WIN
ROWS = 208
LANES = 256
PAIRS = HEADS // 2
PAIR = 2 * HEAD_DIM
SIDE = (MAP + WIN - 1) // WIN
LN_EPS = 1e-06
SQRT_HALF = 0.7071067811865476
INV_ROOT_TAU = 0.3989422804014327
F32 = jnp.float32
BF16 = jnp.bfloat16
QKV_HALF = 3 * D // 2
NOTES = 128
STEPS = (3, 4, 1)
COST = 1e8
BACK_STEPS = (2, 5, 1)


def nn(left, right):
    return jnp.dot(left, right, preferred_element_type=F32)


def nt(left, right):
    return lax.dot_general(left, right, (((1,), (1,)), ((), ())), preferred_element_type=F32)


def tn(left, right):
    return lax.dot_general(left, right, (((0,), (0,)), ((), ())), preferred_element_type=F32)


def key_places():
    table = np.zeros((ROWS, HEAD_DIM), np.float32)
    for slot in range(SLOTS):
        for base in (0, 32):
            table[slot, base + WIN - 1 - slot // WIN] = 1.0
            table[slot, base + 16 + WIN - 1 - slot % WIN] = 1.0
    return table


def keep_column(base_ref, window):
    slot = lax.broadcasted_iota(jnp.int32, (ROWS, 1), 0)
    row = lax.shift_right_logical(slot * 4682, 16)
    col = slot - row * WIN
    place = lax.rem(base_ref[2] + window, SIDE * SIDE)
    place_row = lax.div(place, SIDE)
    place_col = place - place_row * SIDE
    inside = (slot < SLOTS) & (row + place_row * WIN < MAP) & (col + place_col * WIN < MAP)
    return inside.astype(F32)


def lane_places():
    slot = lax.broadcasted_iota(jnp.int32, (1, LANES), 1)
    row = lax.shift_right_logical(slot * 4682, 16)
    return row, slot - row * WIN


def norm_parts(values):
    mean = jnp.mean(values, axis=-1, keepdims=True)
    centred = values - mean
    inv_std = lax.rsqrt(jnp.mean(centred * centred, axis=-1, keepdims=True) + LN_EPS)
    return centred * inv_std, inv_std


def norm_grad(grad, scaled, inv_std, gain):
    grad_scaled = grad * gain
    first = jnp.mean(grad_scaled, axis=-1, keepdims=True)
    second = jnp.mean(grad_scaled * scaled, axis=-1, keepdims=True)
    return inv_std * (grad_scaled - first - scaled * second)


def up_by(values, amount):
    take = lambda bit: (amount & bit) != 0
    part = jnp.where(take(8), values[8:32], values[0:24])
    part = jnp.where(take(4), pltpu.roll(part, 20, 0), part)
    part = jnp.where(take(2), pltpu.roll(part, 22, 0), part)
    part = jnp.where(take(1), pltpu.roll(part, 23, 0), part)
    return part[0:16]


def down_by(values, amount):
    take = lambda bit: (amount & bit) != 0
    zeros = jnp.zeros((8, values.shape[1]), values.dtype)
    part = jnp.concatenate([values, zeros], axis=0)
    part = jnp.where(take(1), pltpu.roll(part, 1, 0), part)
    part = jnp.where(take(2), pltpu.roll(part, 2, 0), part)
    part = jnp.where(take(4), pltpu.roll(part, 4, 0), part)
    return jnp.where(
        take(8),
        jnp.concatenate([zeros, part], axis=0),
        jnp.concatenate([part, zeros], axis=0),
    )


def fill_rows(values):
    return jnp.concatenate(
        [values, jnp.zeros((LANES - ROWS,) + values.shape[1:], values.dtype)], axis=0
    )


def chunk_place(me_ref, index, far_y, along_y):
    mid, plane = index // 2, index % 2
    dist_x, dist_y = (far_y, mid) if along_y else (mid, far_y)
    plane = plane * 2 + (0 if along_y else 4)
    return (me_ref[0] // 2) ^ dist_x, me_ref[1] ^ (plane + dist_y)


ARRIVED = tuple((half, along_y, other) for other in (0, 1) for along_y in (True, False) for half in (0, 1))


def load_first(me_ref, parts, full, sem):
    core = me_ref[0] % 2
    for at, ref in enumerate(parts):
        along_y, other = at % 2 == 0, at // 2

        def start(index, carry, ref=ref, along_y=along_y, other=other):
            far_x, owner = chunk_place(me_ref, index % 4, index // 4, along_y)
            pltpu.make_async_copy(
                ref.at[index, :, pl.ds(0, QKV_HALF)],
                full.at[
                    pl.ds(pl.multiple_of(owner * 96 + far_x * 48, 16), 48),
                    pl.ds(pl.multiple_of((core ^ other) * QKV_HALF, 128), QKV_HALF),
                ],
                sem.at[0],
            ).start()
            return carry

        lax.fori_loop(0, 8, start, 0)
    pltpu.make_async_copy(full, full, sem.at[0]).wait()


def piece_place(me_ref, index):
    group, high, mid, plane = index // 8, (index // 4) % 2, (index // 2) % 2, index % 2
    dist_x = jnp.where(group == 0, high, mid)
    dist_y = jnp.where(group == 0, mid, high)
    return (me_ref[0] // 2) ^ dist_x, me_ref[1] ^ (group * 4 + plane * 2 + dist_y)


def piece_index(me_ref, far_x, owner):
    dist = me_ref[1] ^ owner
    dist_x = (me_ref[0] // 2) ^ far_x
    dist_y, plane, group = dist % 2, (dist // 2) % 2, dist // 4
    high = jnp.where(group == 0, dist_x, dist_y)
    mid = jnp.where(group == 0, dist_y, dist_x)
    return group * 8 + high * 4 + mid * 2 + plane


def spread_rows(notes_of, owner_of, width, total):
    row = lax.broadcasted_iota(jnp.int32, (128, total), 0)
    col = lax.broadcasted_iota(jnp.int32, (128, total), 1)
    acc = None
    for at in range(8):
        put = ((row < width) & (col == row + owner_of(at) * width)).astype(BF16)
        part = nn(notes_of(at), put)
        acc = part if acc is None else acc + part
    return acc


def notes_kernel(me_ref, a_ref, b_ref, c_ref, vec_ref, rel_ref, relt_ref, turn_ref):
    picks = [(a_ref, at, at % 2 * 2 + at // 2) for at in range(4)]
    picks += [(b_ref, at, 4 + at * 2) for at in range(2)] + [(c_ref, at, 5 + at * 2) for at in range(2)]
    owner_of = lambda at: me_ref[1] ^ picks[at][2]
    lanes = pl.ds(QKV_HALF, NOTES)
    vec_ref[...] = spread_rows(
        lambda at: picks[at][0][picks[at][1], 0:16, lanes], owner_of, 96, D
    )[0:8]
    for at in range(8):
        both = picks[at][0][picks[at][1], 16:32, lanes].astype(F32)
        for copy in range(2):
            place = pl.ds(pl.multiple_of(copy * 64 + owner_of(at) * 8, 8), 8)
            turn_ref[place, :] = jnp.concatenate([both[0:8, 0:32], both[8:16, 0:32]] * 2, axis=1)
    row = lax.broadcasted_iota(jnp.int32, (128, 128), 0)
    col = lax.broadcasted_iota(jnp.int32, (128, 128), 1)
    turned = jnp.where((row < 64) == (col < 64), turn_ref[...], 0.0)
    relt_ref[...] = turned.astype(BF16)
    rel_ref[...] = turned.T.astype(BF16)


def attend_kernel(*refs, first, pieces, earlier):
    base_ref, tok_ref = refs[0:2]
    at = 2 + max(pieces, 1)
    vec_ref, rel_ref, place_ref = refs[at : at + 3]
    at += 3 + earlier
    qkv_ref, prob_ref, mix_ref, fin_ref = refs[at : at + 4]
    if pieces:
        w_ref, sem, s_ref = refs[at + 4 :]

        @pl.when(pl.program_id(0) == 0)
        def _():
            load_first(base_ref, refs[2 : 2 + pieces], w_ref, sem)
    else:
        w_ref = refs[2]
        s_ref = refs[at + 4]
    keep = keep_column(base_ref, pl.program_id(0) + first)
    scaled, _ = norm_parts(tok_ref[0].astype(F32))
    first_in = (keep * (scaled * vec_ref[0:1, :] + vec_ref[1:2, :])).astype(BF16)
    fin_ref[0] = first_in
    for part in range(3):
        cols = pl.ds(part * D, D)
        total = nn(first_in, w_ref[:, cols])
        if part != 1:
            total = total + vec_ref[2 + part // 2 : 3 + part // 2, :]
        qkv_ref[0, :, cols] = total.astype(BF16)
    lane_row, lane_col = lane_places()
    low_half = lax.broadcasted_iota(jnp.int32, (ROWS, PAIR), 1) < HEAD_DIM
    tail_rows = lax.broadcasted_iota(jnp.int32, (16, LANES), 0) + 192
    places = place_ref[...]
    place_pair = jnp.concatenate([places, places], axis=1)

    def one_pair(pair, carry):
        at = pl.multiple_of(pair * PAIR, PAIR)
        query = qkv_ref[0, :, pl.ds(at, PAIR)]
        keys = qkv_ref[0, :, pl.ds(pl.multiple_of(D + at, PAIR), PAIR)]
        values = qkv_ref[0, :, pl.ds(pl.multiple_of(2 * D + at, PAIR), PAIR)]
        query_t = fill_rows(query).T
        offsets = nn(rel_ref[...], query_t)
        mixed = []
        for head in range(2):
            mine = offsets[head * HEAD_DIM : (head + 1) * HEAD_DIM]
            along = jnp.concatenate(
                [up_by(mine[0:32], lane_row), up_by(mine[32:64], lane_col)], axis=0
            )
            high = along.astype(BF16)
            rest = (along - high.astype(F32)).astype(BF16)
            scaled_q = query_t[head * HEAD_DIM : (head + 1) * HEAD_DIM] * jnp.asarray(
                HEAD_DIM ** (-0.5), BF16
            )
            if head == 0:
                query_ext = jnp.concatenate([scaled_q, high, rest], axis=0)
                keys_ext = jnp.where(low_half, keys, place_pair)
            else:
                query_ext = jnp.concatenate([high, rest, scaled_q], axis=0)
                keys_ext = jnp.where(low_half, place_pair, keys)
            s_ref[2 * pair + head] = nn(keys_ext, query_ext)
        return carry

    def soft(head, carry):
        scores = s_ref[head]
        scores = jnp.concatenate(
            [scores[0:192], jnp.where(tail_rows < SLOTS, scores[192:208], -1e30)], axis=0
        )
        peak = jnp.max(scores, axis=0, keepdims=True)
        expo = jnp.exp(scores - peak)
        total = jnp.sum(expo, axis=0, keepdims=True)
        prob_ref[0, head] = (expo * (1.0 / total)).astype(BF16)
        return carry

    def mix(pair, carry):
        at = pl.multiple_of(pair * PAIR, PAIR)
        values = qkv_ref[0, :, pl.ds(pl.multiple_of(2 * D + at, PAIR), PAIR)]
        mixed = [tn(prob_ref[0, 2 * pair + head], values)[0:ROWS].astype(BF16) for head in range(2)]
        mix_ref[0, :, pl.ds(at, PAIR)] = jnp.where(low_half, mixed[0], mixed[1])
        return carry

    lax.fori_loop(0, PAIRS, one_pair, 0, unroll=PAIRS)
    lax.fori_loop(0, HEADS, soft, 0, unroll=HEADS)
    lax.fori_loop(0, PAIRS, mix, 0, unroll=PAIRS)


def gelu_parts(pre):
    cumulative = 0.5 + 0.5 * lax.erf(pre * SQRT_HALF)
    bell = jnp.exp(pre * pre * (-0.5))
    return pre * cumulative, cumulative + pre * (bell * INV_ROOT_TAU)


def load_up(me_ref, pieces, up, proj, notes, sem):
    core = me_ref[0] % 2
    for array, (ref, (half, along_y, other)) in enumerate(zip(pieces, ARRIVED)):

        def start_small(index, carry, ref=ref, half=half, along_y=along_y, far_core=core ^ other, array=array):
            far_x, owner = chunk_place(me_ref, index, half, along_y)
            rows = pl.ds(pl.multiple_of(owner * 96 + far_x * 48, 16), 48)
            cols = pl.ds(pl.multiple_of(far_core * 384, 128), 384)
            pltpu.make_async_copy(
                ref.at[index, :, pl.ds(1536, 384)], proj.at[rows, cols], sem.at[1]
            ).start()
            pltpu.make_async_copy(
                ref.at[index, pl.ds(0, 16), pl.ds(1920, 128)], notes.at[array * 4 + index], sem.at[2]
            ).start()
            return carry

        lax.fori_loop(0, 4, start_small, 0)
    for ref, (half, along_y, other) in zip(pieces, ARRIVED):

        def start(index, carry, ref=ref, half=half, along_y=along_y, far_core=core ^ other):
            far_x, owner = chunk_place(me_ref, index, half, along_y)
            rows = pl.ds(pl.multiple_of(owner * 96 + far_x * 48, 16), 48)
            cols = pl.ds(pl.multiple_of(far_core * 1536, 128), 1536)
            pltpu.make_async_copy(
                ref.at[index, :, pl.ds(0, 1536)], up.at[rows, cols], sem.at[0]
            ).start()
            return carry

        lax.fori_loop(0, 4, start, 0)
    for at, full in ((2, notes), (1, proj)):
        pltpu.make_async_copy(full, full, sem.at[at]).wait()


def load_down(me_ref, pieces, down, sem):
    core = me_ref[0] % 2
    for ref, (half, along_y, other) in zip(pieces, ARRIVED):

        def start(index, carry, ref=ref, half=half, along_y=along_y, far_core=core ^ other):
            far_x, owner = chunk_place(me_ref, index, half, along_y)
            place = owner * 8 + far_core * 4 + far_x * 2
            pltpu.make_async_copy(ref.at[index], down.at[pl.ds(place, 2)], sem.at[0]).start()
            return carry

        lax.fori_loop(0, 4, start, 0)
    pltpu.make_async_copy(down, down, sem.at[0]).wait()


def up_kernel(*refs, group, pieces):
    rows = group * ROWS
    me_ref, tok_ref, mix_ref, keep_ref = refs[0:4]
    at = 4 + (pieces or 4)
    hid_ref, si_ref, act_ref, slope_ref = refs[at : at + 4]
    at += 4
    if pieces:
        up_ref, wp_ref, vec_ref, ub_ref, total_ref, notes, sem = refs[at:]

        @pl.when(pl.program_id(0) == 0)
        def _():
            load_up(me_ref, refs[4 : 4 + pieces], up_ref, wp_ref, notes, sem)
            picks = [(at, at % 2 * 2 + at // 2) for at in range(4)]
            picks += [(8 + at, 4 + at * 2) for at in range(2)] + [(12 + at, 5 + at * 2) for at in range(2)]
            owner_of = lambda at: me_ref[1] ^ picks[at][1]
            vec_ref[...] = spread_rows(
                lambda at: notes[picks[at][0]], owner_of, 96, D
            )[0:8]
            for at in range(8):
                lanes = pl.ds(pl.multiple_of(owner_of(at) * 384, 128), 384)
                own = notes[picks[at][0]].astype(F32)
                ub_ref[:, lanes] = jnp.concatenate([own[6:7], own[7:8], own[8:9]], axis=1)
            counts = notes[0].astype(F32)
            for at in range(1, 32):
                counts = counts + notes[at].astype(F32)
            counts = counts[5:6]
            lane = lax.broadcasted_iota(jnp.int32, (1, 128), 1)
            weight = jnp.where(lane == 0, 128.0, jnp.where(lane == 1, 1.0, 0.0))
            total_ref[...] = jnp.broadcast_to(
                jnp.sum(counts * weight, axis=1, keepdims=True), (1, 128)
            )
    else:
        wp_ref, up_ref, vec_ref, ub_ref = refs[4:8]
    pb_row, gain_row, shift_row = [vec_ref[at : at + 1, :] for at in range(3)]
    keep = keep_ref[...].reshape(rows, 2)[:, 0:1]
    attn_out = nn(mix_ref[...].reshape(rows, D), wp_ref[...]) + pb_row
    hidden = keep * (tok_ref[...].reshape(rows, D).astype(F32) + attn_out)
    hid_ref[...] = hidden.reshape(group, ROWS, D)
    scaled, _ = norm_parts(hidden)
    second_in = (scaled * gain_row + shift_row).astype(BF16)
    si_ref[...] = second_in.reshape(group, ROWS, D)
    if pieces:

        @pl.when(pl.program_id(0) == 0)
        def _():
            pltpu.make_async_copy(up_ref, up_ref, sem.at[0]).wait()

    for part in range(MLP // D):
        cols = slice(part * D, part * D + D)
        act, slope = gelu_parts(nn(second_in, up_ref[:, cols]) + ub_ref[:, cols])
        slope_ref[:, :, cols] = slope.astype(BF16).reshape(group, ROWS, D)
        act_ref[:, :, cols] = act.astype(BF16).reshape(group, ROWS, D)


def down_kernel(*refs, group, pieces, scale):
    step = pl.program_id(0)
    rows = group * ROWS
    me_ref, hid_ref, act_ref, slope_ref, teach_ref, aux_ref, up_ref, vec_ref, total_ref = refs[0:9]
    at = 9 + (pieces or 1)
    out_ref, gh_ref, ga_ref, gd_ref, gu_ref, sums_ref, usum_ref = refs[at : at + 7]
    if pieces:
        down3_ref, sem = refs[at + 7 :]

        @pl.when(step == 0)
        def _():
            load_down(me_ref, refs[9 : 9 + pieces], down3_ref, sem)

        down_rows = lambda part: down3_ref[pl.ds(part * 16, 16)].reshape(D, D)
    else:
        down_rows = lambda part: refs[9][pl.ds(part * D, D), :]

    @pl.when(step == 0)
    def _():
        sums_ref[...] = jnp.zeros_like(sums_ref)
        usum_ref[...] = jnp.zeros_like(usum_ref)

    gain_row, db_row = vec_ref[1:2, :], vec_ref[3:4, :]
    coef = scale / total_ref[:, 0:1]
    aux = aux_ref[...].reshape(rows, 2)
    keep, valid = aux[:, 0:1], aux[:, 1:2]
    hidden = hid_ref[...].reshape(rows, D)
    down = db_row
    for part in range(MLP // D):
        cols = slice(part * D, part * D + D)
        down = down + nn(act_ref[:, :, cols].reshape(rows, D), down_rows(part))
    final = keep * (hidden + down)
    for at in range(group):
        out_ref[at] = final[at * ROWS : at * ROWS + SLOTS].astype(BF16)
    error = final - teach_ref[...].reshape(rows, D).astype(F32)
    weighted = valid * error
    grad_final = coef * weighted
    grad_down = grad_final.astype(BF16)
    gd_ref[...] = grad_down.reshape(group, ROWS, D)
    sums_ref[0:1, :] += jnp.sum(weighted * error, axis=0, keepdims=True)
    sums_ref[1:2, :] += jnp.sum(grad_down.astype(F32), axis=0, keepdims=True)
    for part in range(MLP // D):
        cols = slice(part * D, part * D + D)
        slope = slope_ref[:, :, cols].reshape(rows, D).astype(F32)
        grad_up = (nt(grad_down, down_rows(part)) * slope).astype(BF16)
        gu_ref[:, :, cols] = grad_up.reshape(group, ROWS, D)
        usum_ref[:, cols] += jnp.sum(grad_up.astype(F32), axis=0, keepdims=True)
    grad_second = nt(gu_ref[...].reshape(rows, MLP), up_ref[...])
    scaled, inv_std = norm_parts(hidden)
    sums_ref[2:3, :] += jnp.sum(grad_second * scaled, axis=0, keepdims=True)
    sums_ref[3:4, :] += jnp.sum(grad_second, axis=0, keepdims=True)
    grad_hidden = keep * (grad_final + norm_grad(grad_second, scaled, inv_std, gain_row))
    gh_ref[...] = grad_hidden.reshape(group, ROWS, D)
    grad_attn = grad_hidden.astype(BF16)
    ga_ref[...] = grad_attn.reshape(group, ROWS, D)
    sums_ref[4:5, :] += jnp.sum(grad_attn.astype(F32), axis=0, keepdims=True)


def attend_back_kernel(*refs, earlier):
    ga_ref, wp_ref, qkv_ref, prob_ref, relt_ref, placet_ref = refs[0:6]
    dqkv_ref, rg_ref, qsum_ref, gm_ref, s_ref, g_ref, e_ref = refs[6 + earlier :]

    @pl.when(pl.program_id(0) == 0)
    def _():
        rg_ref[...] = refs[7][...] if earlier else jnp.zeros_like(rg_ref)
        qsum_ref[...] = refs[8][...] if earlier else jnp.zeros_like(qsum_ref)
        gm_ref[pl.ds(ROWS, LANES - ROWS), :] = jnp.zeros((LANES - ROWS, D), BF16)

    gm_ref[pl.ds(0, ROWS), :] = nt(ga_ref[0], wp_ref[...]).astype(BF16)
    lane_row, lane_col = lane_places()
    low_half = lax.broadcasted_iota(jnp.int32, (ROWS, PAIR), 1) < HEAD_DIM
    low_full = lax.broadcasted_iota(jnp.int32, (LANES, PAIR), 1) < HEAD_DIM
    blank = jnp.zeros((), BF16)
    scale = HEAD_DIM ** (-0.5)

    pair_at = lambda base, pair: pl.ds(base + pair * PAIR, PAIR)
    own = (
        lambda full: jnp.where(low_full, full, blank),
        lambda full: jnp.where(low_full, blank, full),
    )
    for pair in range(PAIRS):
        values = qkv_ref[0, :, pair_at(2 * D, pair)]
        stacked = jnp.concatenate(
            [jnp.where(low_half, values, blank), jnp.where(low_half, blank, values)], axis=0
        )
        grad_probs = nt(stacked, gm_ref[:, pair_at(0, pair)])
        s_ref[2 * pair] = grad_probs[0:ROWS]
        s_ref[2 * pair + 1] = grad_probs[ROWS : 2 * ROWS]
    for head in range(HEADS):
        probs = prob_ref[0, head].astype(F32)
        grad_p = s_ref[head]
        row_dot = jnp.sum(probs * grad_p, axis=0, keepdims=True)
        g_ref[head] = (probs * (grad_p - row_dot)).astype(BF16)
    for pair in range(PAIRS):
        query = fill_rows(qkv_ref[0, :, pair_at(0, pair)])
        grad_out = gm_ref[:, pair_at(0, pair)]
        grad_values = nn(prob_ref[0, 2 * pair], own[0](grad_out)) + nn(
            prob_ref[0, 2 * pair + 1], own[1](grad_out)
        )
        grad_keys = nn(g_ref[2 * pair], own[0](query)) + nn(g_ref[2 * pair + 1], own[1](query))
        grad_values = grad_values.astype(BF16)
        dqkv_ref[0, :, pair_at(D, pair)] = (grad_keys * scale).astype(BF16)
        dqkv_ref[0, :, pair_at(2 * D, pair)] = grad_values
        qsum_ref[1:2, pair_at(0, pair)] += jnp.sum(
            grad_values.astype(F32), axis=0, keepdims=True
        )
    for pair in range(PAIRS):
        keys_t = fill_rows(qkv_ref[0, :, pair_at(D, pair)]).T
        for head in range(2):
            keys_ext = jnp.concatenate(
                [keys_t[head * HEAD_DIM : (head + 1) * HEAD_DIM], placet_ref[...]], axis=0
            )
            e_ref[2 * pair + head] = nn(keys_ext, fill_rows(g_ref[2 * pair + head]))
    for pair in range(PAIRS):
        query = fill_rows(qkv_ref[0, :, pair_at(0, pair)])
        plain, spread = [], []
        for head in range(2):
            grad_ext = e_ref[2 * pair + head]
            plain.append(grad_ext[0:64])
            spread.append(down_by(grad_ext[64:80], lane_row))
            spread.append(down_by(grad_ext[80:96], lane_col))
        spread = jnp.concatenate(spread, axis=0).astype(BF16)
        grad_query = jnp.concatenate(plain, axis=0) * scale + nn(relt_ref[...], spread)
        rg_ref[...] += nn(spread, query)
        grad_query = grad_query.astype(BF16).T[0:ROWS]
        dqkv_ref[0, :, pair_at(0, pair)] = grad_query
        qsum_ref[0:1, pair_at(0, pair)] += jnp.sum(grad_query.astype(F32), axis=0, keepdims=True)


def input_kernel(
    base_ref, dqkv_ref, w_ref, tok_ref, gh_ref, vec_ref, *refs, group, first, earlier
):
    step = pl.program_id(0)
    out_ref, sums_ref = refs[earlier:]

    @pl.when(step == 0)
    def _():
        sums_ref[...] = refs[1][...] if earlier else jnp.zeros_like(sums_ref)

    keep = jnp.concatenate(
        [keep_column(base_ref, first + step * group + at) for at in range(group)], axis=0
    )
    rows = group * ROWS
    grad_first = keep * nt(dqkv_ref[...].reshape(rows, 3 * D), w_ref[...])
    scaled, inv_std = norm_parts(tok_ref[...].reshape(rows, D).astype(F32))
    sums_ref[0:1, :] += jnp.sum(grad_first * scaled, axis=0, keepdims=True)
    sums_ref[1:2, :] += jnp.sum(grad_first, axis=0, keepdims=True)
    total = gh_ref[...].reshape(rows, D) + norm_grad(grad_first, scaled, inv_std, vec_ref[0:1, :])
    for at in range(group):
        out_ref[:, first + step * group + at, :] = total[at * ROWS : at * ROWS + SLOTS]


def weight_grad_kernel(*refs):
    left_ref, right_ref, out_ref = refs
    out_ref[...] = tn(left_ref[...], right_ref[...]).astype(BF16)


def qkv_grad_kernel(me_ref, left_ref, right_ref, notes_ref, out_ref, full, sem, *, other):
    full[...] = tn(left_ref[...], right_ref[...]).astype(BF16)
    core = (me_ref[0] % 2) ^ other

    def start(index, carry):
        far_x, owner = piece_place(me_ref, index)
        pltpu.make_async_copy(
            full.at[pl.ds(pl.multiple_of(owner * 96 + far_x * 48, 16), 48)],
            out_ref.at[index, :, pl.ds(0, QKV_HALF)],
            sem.at[0],
        ).start()
        pltpu.make_async_copy(
            notes_ref.at[core * 2 + far_x, owner],
            out_ref.at[index, :, pl.ds(QKV_HALF, NOTES)],
            sem.at[0],
        ).start()
        return carry

    lax.fori_loop(0, 16, start, 0)
    pltpu.make_async_copy(out_ref, out_ref, sem.at[0]).wait()


def up_grad_kernel(me_ref, left_ref, right_ref, out_ref, full, sem):
    step = pl.program_id(0)
    full[step] = tn(left_ref[...], right_ref[...]).astype(BF16)

    def start(index, carry):
        far_x, owner = piece_place(me_ref, index)
        rows = pl.ds(pl.multiple_of(owner * 96 + far_x * 48, 16), 48)
        pltpu.make_async_copy(full.at[step, rows], out_ref.at[index, step], sem.at[0]).start()
        return carry

    lax.fori_loop(0, 16, start, 0)

    @pl.when(step == pl.num_programs(0) - 1)
    def _():
        pltpu.make_async_copy(out_ref, out_ref, sem.at[0]).wait()


def down_grad_kernel(
    me_ref, act_ref, gd_ref, mix_any, ga_any, keep_ref, send_ref, full, half, mix_ref, ga_ref, sem
):
    step = pl.program_id(0)
    last = pl.num_programs(0) - 1
    fetches = [
        pltpu.make_async_copy(mix_any, mix_ref, sem.at[2]),
        pltpu.make_async_copy(ga_any, ga_ref, sem.at[3]),
    ]

    @pl.when(step == 0)
    def _():
        for fetch in fetches:
            fetch.start()

    @pl.when(step < last)
    def _():
        full[step] = tn(act_ref[...], gd_ref[...]).astype(BF16).reshape(16, 48, D)

    @pl.when(step == last)
    def _():
        for fetch in fetches:
            fetch.wait()
        total = tn(mix_ref[...], ga_ref[...]).astype(BF16)
        for core in range(2):
            half[core] = total[:, core * 384 : core * 384 + 384]

    core = me_ref[0] % 2
    for ref, far_core, at in ((keep_ref, core, 0), (send_ref, 1 - core, 1)):

        def start_proj(index, carry, ref=ref, far_core=far_core, at=at):
            far_x, owner = piece_place(me_ref, index)
            rows = pl.ds(pl.multiple_of(owner * 96 + far_x * 48, 16), 48)
            for col in (0, 384):
                pltpu.make_async_copy(
                    half.at[far_core, rows], ref.at[index, 2, :, pl.ds(col, 384)], sem.at[at]
                ).start()
            return carry

        @pl.when(step < last)
        def _(ref=ref, far_core=far_core, at=at):
            for place in range(4):
                which, far_x = place // 2, place % 2
                pltpu.make_async_copy(
                    full.at[step, pl.ds(which * 8 + far_core * 4 + far_x * 2, 2)],
                    ref.at[piece_index(me_ref, far_x, step * 2 + which), pl.ds(0, 2)],
                    sem.at[at],
                ).start()

        @pl.when(step == last)
        def _(start_proj=start_proj):
            lax.fori_loop(0, 16, start_proj, 0)

    @pl.when(step == last)
    def _():
        pltpu.make_async_copy(keep_ref, keep_ref, sem.at[0]).wait()
        pltpu.make_async_copy(send_ref, send_ref, sem.at[1]).wait()


def whole(shape):
    zeros = (0,) * len(shape)
    return pl.BlockSpec(shape, lambda *_: zeros, pipeline_mode=pl.Buffered(1))


def whole_out(shape):
    zeros = (0,) * len(shape)
    return pl.BlockSpec(shape, lambda *_: zeros)


def windows_from(first, shape):
    tail = (0,) * (len(shape) - 1)
    return pl.BlockSpec(shape, lambda step: (step + first,) + tail)


SMEM = pl.BlockSpec(memory_space=pltpu.SMEM)
ANY = pl.BlockSpec(memory_space=pl.ANY)


def params(mebibytes=32):
    return pltpu.CompilerParams(
        vmem_limit_bytes=mebibytes * 1024 * 1024, dimension_semantics=("arbitrary",)
    )


def shape_of(shape, dtype):
    return jax.ShapeDtypeStruct(shape, dtype)


def cost(flops, moved):
    return pl.CostEstimate(flops=int(flops), bytes_accessed=int(moved), transcendentals=0)


def notes_of(me, near, far_x, far_y):
    return pl.pallas_call(
        notes_kernel,
        in_specs=[SMEM] + [whole(v.shape) for v in (near, far_x, far_y)],
        out_specs=[whole_out((8, D)), whole_out((PAIR, PAIR)), whole_out((PAIR, PAIR))],
        out_shape=[shape_of((8, D), F32)] + [shape_of((PAIR, PAIR), BF16)] * 2,
        grid=(1,),
        scratch_shapes=[pltpu.VMEM((128, 128), F32)],
        compiler_params=params(),
        cost_estimate=cost(COST, 1e5),
        name="notes",
    )(me, near, far_x, far_y)


def attend(me, tokens, weight, vec, rel, places, first, number, earlier=()):
    count = tokens.shape[0]
    win = lambda shape: windows_from(first, shape)
    pieces = len(weight) if isinstance(weight, tuple) else 0
    weights = weight if pieces else (weight,)
    weight_specs = [ANY] * pieces if pieces else [whole((D, 3 * D))]
    out_specs = [win((1, ROWS, 3 * D)), win((1, HEADS, ROWS, LANES)), win((1, ROWS, D)),
                 win((1, ROWS, D))]
    out_shape = [
        shape_of((count, ROWS, 3 * D), BF16), shape_of((count, HEADS, ROWS, LANES), BF16),
        shape_of((count, ROWS, D), BF16), shape_of((count, ROWS, D), BF16),
    ]
    scratch = [pltpu.VMEM((HEADS, ROWS, LANES), F32)]
    if pieces:
        out_specs.append(whole_out((D, 3 * D)))
        out_shape.append(shape_of((D, 3 * D), BF16))
        scratch.insert(0, pltpu.SemaphoreType.DMA((1,)))
    inputs = 5 + len(weights)
    return pl.pallas_call(
        functools.partial(attend_kernel, first=first, pieces=pieces, earlier=len(earlier)),
        grid=(number,),
        in_specs=[
            SMEM, win((1, ROWS, D)), *weight_specs, whole((8, D)),
            whole((PAIR, PAIR)), whole((ROWS, HEAD_DIM)), *([ANY] * len(earlier)),
        ],
        out_specs=out_specs,
        out_shape=out_shape,
        scratch_shapes=scratch,
        input_output_aliases={inputs + at: at for at in range(len(earlier))},
        compiler_params=params(54),
        cost_estimate=cost(COST, 1e5),
        name="attend",
    )(me, tokens, *weights, vec, rel, places, *earlier)


def mlp_up(me, tokens, mixed, aux, weights, chunked):
    count = tokens.shape[0]
    group = math.gcd(count, 2)
    win = lambda width: windows_from(0, (group, ROWS, width))
    arr = lambda width, dtype: shape_of((count, ROWS, width), dtype)
    pieces = len(weights) if chunked else 0
    out_specs = [win(D), win(D), win(MLP), win(MLP)]
    out_shape = [arr(D, F32), arr(D, BF16), arr(MLP, BF16), arr(MLP, BF16)]
    scratch = []
    if pieces:
        shapes = [((D, MLP), BF16), ((D, D), BF16), ((8, D), F32), ((1, MLP), F32), ((1, 128), F32)]
        out_specs += [whole_out(s) for s, _ in shapes]
        out_shape += [shape_of(s, t) for s, t in shapes]
        scratch += [pltpu.VMEM((32, 16, 128), BF16), pltpu.SemaphoreType.DMA((3,))]
    return pl.pallas_call(
        functools.partial(up_kernel, group=group, pieces=pieces),
        grid=(count // group,),
        in_specs=[SMEM, win(D), win(D), win(2)]
        + ([ANY] * pieces if pieces else [whole(v.shape) for v in weights]),
        out_specs=out_specs,
        out_shape=out_shape,
        scratch_shapes=scratch,
        compiler_params=params(60),
        cost_estimate=cost(COST * count, 1e5),
        name="mlp_up",
    )(me, tokens, mixed, aux, *weights)


def mlp_down(me, hidden, act, slope, teacher, aux, up, vec, total, weights, scale, chunked):
    count = hidden.shape[0]
    group = math.gcd(count, 2)
    win = lambda width: windows_from(0, (group, ROWS, width))
    plain = windows_from(0, (group, SLOTS, D))
    arr = lambda width, dtype: shape_of((count, ROWS, width), dtype)
    pieces = len(weights) if chunked else 0
    scratch = []
    if pieces:
        scratch += [pltpu.VMEM((MLP // 48, 48, D), BF16), pltpu.SemaphoreType.DMA((1,))]
    return pl.pallas_call(
        functools.partial(down_kernel, group=group, pieces=pieces, scale=scale),
        grid=(count // group,),
        in_specs=[SMEM, win(D), win(MLP), win(MLP), win(D), win(2), whole((D, MLP)), whole((8, D)),
                  whole((1, 128))]
        + ([ANY] * pieces if pieces else [whole(v.shape) for v in weights]),
        out_specs=[plain, win(D), win(D), win(D), win(MLP), whole_out((5, D)), whole_out((1, MLP))],
        out_shape=[
            shape_of((count, SLOTS, D), BF16), arr(D, F32), arr(D, BF16), arr(D, BF16),
            arr(MLP, BF16), shape_of((5, D), F32), shape_of((1, MLP), F32),
        ],
        scratch_shapes=scratch,
        compiler_params=params(60),
        cost_estimate=cost(COST * count, 1e5),
        name="mlp_down",
    )(me, hidden, act, slope, teacher, aux, up, vec, total, *weights)


def attend_back(grad_attn, proj, qkv, probs, rel_t, places_t, first, number, earlier=()):
    count = grad_attn.shape[0]
    win = lambda shape: windows_from(first, shape)
    before = [ANY, whole((PAIR, PAIR)), whole((2, D))] if earlier else []
    return pl.pallas_call(
        functools.partial(attend_back_kernel, earlier=len(earlier)),
        grid=(number,),
        in_specs=[
            win((1, ROWS, D)), whole((D, D)), win((1, ROWS, 3 * D)), win((1, HEADS, ROWS, LANES)),
            whole((PAIR, PAIR)), whole((32, LANES)), *before,
        ],
        out_specs=[win((1, ROWS, 3 * D)), whole_out((PAIR, PAIR)), whole_out((2, D))],
        out_shape=[
            shape_of((count, ROWS, 3 * D), BF16), shape_of((PAIR, PAIR), F32),
            shape_of((2, D), F32),
        ],
        scratch_shapes=[
            pltpu.VMEM((LANES, D), BF16), pltpu.VMEM((HEADS, ROWS, LANES), F32),
            pltpu.VMEM((HEADS, ROWS, LANES), BF16), pltpu.VMEM((HEADS, 96, LANES), F32),
        ],
        input_output_aliases={6: 0} if earlier else {},
        compiler_params=params(48),
        cost_estimate=cost(COST, 1e5),
        name="attend_back",
    )(grad_attn, proj, qkv, probs, rel_t, places_t, *earlier)


def input_back(me, dqkv, weight, tokens, grad_hidden, vec, first, number, earlier=()):
    count = tokens.shape[0]
    group = math.gcd(math.gcd(first, number), 2)
    win = lambda shape: windows_from(first // group, shape)
    before = [ANY, whole((2, D))] if earlier else []
    return pl.pallas_call(
        functools.partial(input_kernel, group=group, first=first, earlier=len(earlier)),
        grid=(number // group,),
        in_specs=[
            SMEM, win((group, ROWS, 3 * D)), whole((D, 3 * D)), win((group, ROWS, D)),
            win((group, ROWS, D)), whole((8, D)), *before,
        ],
        out_specs=[whole_out((SLOTS, count, D)), whole_out((2, D))],
        out_shape=[shape_of((SLOTS, count, D), F32), shape_of((2, D), F32)],
        input_output_aliases={6: 0} if earlier else {},
        compiler_params=params(44),
        cost_estimate=cost(COST, 1e5),
        name="input_back",
    )(me, dqkv, weight, tokens, grad_hidden, vec, *earlier)


def pick(left, right):
    return jnp.dot(left, right, preferred_element_type=F32, precision=lax.Precision.HIGHEST)


def pack_kernel(me_ref, one_ref, qv_ref, two_ref, up_ref, rel_ref, out_ref):
    vectors = jnp.concatenate(
        [one_ref[0:2], qv_ref[0:2], two_ref[4:5], two_ref[2:4], two_ref[1:2]], axis=0
    )
    error = jnp.sum(two_ref[0:1, :], axis=1, keepdims=True)
    high = error.astype(BF16).astype(F32)
    middle = (error - high).astype(BF16).astype(F32)
    lane = lax.broadcasted_iota(jnp.int32, (1, 128), 1) - 3 * (me_ref[0] * 8 + me_ref[1])
    error = jnp.where(
        lane == 0, high, jnp.where(lane == 1, middle, jnp.where(lane == 2, error - high - middle, 0.0))
    )
    tables = rel_ref[0:64, 0:64] + rel_ref[64:128, 64:128]
    row = lax.broadcasted_iota(jnp.int32, (D, 128), 0)
    col = lax.broadcasted_iota(jnp.int32, (D, 128), 1)
    small_row = lax.broadcasted_iota(jnp.int32, (32, 128), 0)
    lanes_row = lax.broadcasted_iota(jnp.int32, (64, 128), 0)
    lanes_col = lax.broadcasted_iota(jnp.int32, (64, 128), 1)
    out_ref[...] = jnp.zeros_like(out_ref)
    for owner in range(8):
        own = pick(vectors, ((col < 96) & (row == col + owner * 96)).astype(F32))
        total = jnp.concatenate([own, jnp.zeros((24, 128), F32)], axis=0)
        for which in range(2):
            lane = lanes_col - 96 - 8 * which
            put = ((lane >= 0) & (lane < 8) & (lanes_row == lane + owner * 8)).astype(F32)
            total = total + pick(tables[32 * which : 32 * which + 32], put)
        for part in range(3):
            at = owner * 384 + part * 128
            total = jnp.where(small_row == 27 + part, up_ref[:, at : at + 128], total)
        total = jnp.where(small_row == 30, error, total).astype(BF16)
        for quarter in range(4):
            out_ref[quarter, owner, 0:8] = total[quarter * 8 : quarter * 8 + 8]


def pack(me, *sums):
    return pl.pallas_call(
        pack_kernel,
        grid=(1,),
        in_specs=[SMEM] + [whole(v.shape) for v in sums],
        out_specs=whole_out((4, 8, 48, NOTES)),
        out_shape=shape_of((4, 8, 48, NOTES), BF16),
        compiler_params=params(),
        cost_estimate=cost(COST, 1e5),
        name="pack",
    )(me, *sums)


def qkv_shard_kernel(me_ref, total_ref, *refs):
    quarters, out_ref, notes_ref = refs[0:4], refs[4], refs[5]
    core, far_x = me_ref[0] % 2, me_ref[0] // 2
    for at, ref in enumerate(quarters):
        this_core, this_x = core ^ (at // 2), far_x ^ (at % 2)
        rows = pl.ds(pl.multiple_of(this_x * 48, 16), 48)
        cols = pl.ds(pl.multiple_of(this_core * QKV_HALF, 128), QKV_HALF)
        out_ref[rows, cols] = ref[:, 0:QKV_HALF].astype(F32)
        here = pl.ds(pl.multiple_of((this_core * 2 + this_x) * 8, 8), 8)
        notes_ref[here, :] = ref[0:16, QKV_HALF : QKV_HALF + NOTES].astype(F32)[0:8]
    errors = jnp.sum(notes_ref[30:31, :], axis=1, keepdims=True)
    notes_ref[31:32, :] = errors / (total_ref[...] * D)


def qkv_shard(me, total, quarters):
    shapes = [(96, 3 * D), (32, 128)]
    return pl.pallas_call(
        qkv_shard_kernel,
        grid=(1,),
        in_specs=[SMEM, whole((1, 128))] + [whole(v.shape) for v in quarters],
        out_specs=[whole_out(shape) for shape in shapes],
        out_shape=[shape_of(shape, F32) for shape in shapes],
        compiler_params=params(),
        cost_estimate=cost(COST, 1e5),
        name="qkv_shard",
    )(me, total, *quarters)


def shard_kernel(me_ref, *refs):
    quarters, (up_ref, down_ref, proj_ref) = refs[0:4], refs[4:]
    core, far_x = me_ref[0] % 2, me_ref[0] // 2
    for at, ref in enumerate(quarters):
        this_core, this_x = core ^ (at // 2), far_x ^ (at % 2)
        rows = pl.ds(pl.multiple_of(this_x * 48, 16), 48)
        for block in range(2):
            cols = pl.ds(pl.multiple_of(this_core * 1536 + block * D, 128), D)
            up_ref[rows, cols] = ref[block].astype(F32)
            at_row = this_core * 192 + this_x * 96 + block * 48
            down_ref[pl.ds(pl.multiple_of(at_row, 16), 48), :] = ref[2 + block].astype(F32)
        cols = pl.ds(pl.multiple_of(this_core * 384, 128), 384)
        proj_ref[rows, cols] = ref[4, :, 0:384].astype(F32)


def shard(me, quarters):
    shapes = [(96, MLP), (384, D), (96, D)]
    return pl.pallas_call(
        shard_kernel,
        grid=(1,),
        in_specs=[SMEM] + [whole(v.shape) for v in quarters],
        out_specs=[whole_out(shape) for shape in shapes],
        out_shape=[shape_of(shape, F32) for shape in shapes],
        compiler_params=params(),
        cost_estimate=cost(COST, 1e5),
        name="shard",
    )(me, *quarters)


def column_blocks(rows):
    return pl.BlockSpec((rows, D), lambda step: (0, step))


def weight_grad(left, right, by_rows=False):
    rows = left.shape[0]
    blocks = (left if by_rows else right).shape[1] // D
    moving, still = column_blocks(rows), whole((rows, D))
    return pl.pallas_call(
        weight_grad_kernel,
        grid=(blocks,),
        in_specs=[moving, still] if by_rows else [still, moving],
        out_specs=pl.BlockSpec((D, D), (lambda s: (s, 0)) if by_rows else (lambda s: (0, s))),
        out_shape=shape_of((left.shape[1], right.shape[1]), BF16),
        compiler_params=params(44),
        name="weight_grad",
    )(left, right)


def qkv_grad(me, left, right, notes, other):
    rows = left.shape[0]
    return pl.pallas_call(
        functools.partial(qkv_grad_kernel, other=other),
        grid_spec=pltpu.PrefetchScalarGridSpec(
            num_scalar_prefetch=1,
            grid=(1,),
            in_specs=[
                whole((rows, D)),
                pl.BlockSpec((rows, QKV_HALF), lambda step, me: (0, (me[0] % 2) ^ other)),
                whole((4, 8, 48, NOTES)),
            ],
            out_specs=ANY,
            scratch_shapes=[pltpu.VMEM((D, QKV_HALF), BF16), pltpu.SemaphoreType.DMA((1,))],
        ),
        out_shape=shape_of((16, 48, QKV_HALF + NOTES), BF16),
        compiler_params=params(48),
        cost_estimate=cost(COST, 1e5),
        name="qkv_grad",
    )(me, left, right, notes)


def up_grad(me, left, right, other):
    rows = left.shape[0]
    return pl.pallas_call(
        up_grad_kernel,
        grid_spec=pltpu.PrefetchScalarGridSpec(
            num_scalar_prefetch=1,
            grid=(2,),
            in_specs=[
                whole((rows, D)),
                pl.BlockSpec((rows, D), lambda step, me: (0, ((me[0] % 2) ^ other) * 2 + step)),
            ],
            out_specs=ANY,
            scratch_shapes=[pltpu.VMEM((2, D, D), BF16), pltpu.SemaphoreType.DMA((1,))],
        ),
        out_shape=shape_of((16, 2, 48, D), BF16),
        compiler_params=params(60),
        cost_estimate=cost(COST, 1e5),
        name="up_grad",
    )(me, left, right)


def down_grad(me, act, grad_down, mixed, grad_attn):
    rows = act.shape[0]
    return pl.pallas_call(
        down_grad_kernel,
        grid=(5,),
        in_specs=[
            SMEM, pl.BlockSpec((rows, D), lambda step: (0, jnp.minimum(step, 3))),
            whole((rows, D)), ANY, ANY,
        ],
        out_specs=[ANY] * 2,
        out_shape=[shape_of((16, 3, 48, D), BF16)] * 2,
        scratch_shapes=[
            pltpu.VMEM((4, 16, 48, D), BF16), pltpu.VMEM((2, D, 384), BF16),
            pltpu.VMEM((rows, D), BF16), pltpu.VMEM((rows, D), BF16),
            pltpu.SemaphoreType.DMA((4,)),
        ],
        compiler_params=params(60),
        cost_estimate=cost(COST, 1e5),
        name="down_grad",
    )(me, act, grad_down, mixed, grad_attn)


def swap(values, axis, mask):
    size = lax.axis_size(axis)
    return lax.ppermute(values, axis, [(at, at ^ mask) for at in range(size)])


def joined(stack, axis, mask):
    return jnp.concatenate([stack, swap(stack, axis, mask)], axis=0)


def added(one, two):
    return (one.astype(F32) + two.astype(F32)).astype(BF16)


def tied(*values):
    return lax.optimization_barrier(values)


def cut(values, row, col, rows, cols):
    return lax.dynamic_slice(values, (row, col), (rows, cols))


def body(
    tokens, teacher, valid_mask, attn_gain, attn_shift, qkv_weight, query_bias, value_bias,
    rel_pos_h, rel_pos_w, proj_weight, proj_bias, mlp_gain, mlp_shift, up_weight, up_bias,
    down_weight, down_bias,
):
    count = tokens.shape[0]
    parts = lax.axis_size("fsdp")
    copies = lax.axis_size("rep")
    in_pieces = (copies, parts) == (4, 8)
    rep_at, part_at = lax.axis_index("rep"), lax.axis_index("fsdp")
    device = rep_at * parts + part_at
    core, far_x = rep_at % 2, rep_at // 2
    me = jnp.stack([rep_at, part_at, device * count]).astype(jnp.int32)
    window_ids = device * count + jnp.arange(count, dtype=jnp.int32)
    place = window_ids % (SIDE * SIDE)
    cells = jnp.arange(SLOTS, dtype=jnp.int32)
    inside = ((place // SIDE)[:, None] * WIN + (cells // WIN)[None, :] < MAP) & (
        (place % SIDE)[:, None] * WIN + (cells % WIN)[None, :] < MAP
    )
    keep = inside.astype(F32)
    valid = valid_mask.astype(F32) * keep
    counted = jnp.sum(valid_mask * inside.astype(jnp.int32))
    fill = ((0, 0), (0, ROWS - SLOTS), (0, 0))
    aux = jnp.pad(jnp.stack([keep, valid], axis=-1), fill)
    tokens, teacher = jnp.pad(tokens, fill), jnp.pad(teacher, fill)

    small = [attn_gain, attn_shift, query_bias, value_bias, proj_bias, mlp_gain, mlp_shift,
             down_bias, up_bias, rel_pos_h, rel_pos_w]
    places = jnp.asarray(key_places(), BF16)
    places_t = jnp.asarray(np.pad(key_places().T[0:32], ((0, 0), (0, LANES - ROWS))), BF16)
    counted = jnp.stack([counted // 128, counted % 128]).astype(BF16)
    loss_scale = 64.0 * D * count * copies * parts

    def noted(shape, *entries):
        total = jnp.zeros(shape, BF16)
        for values, row, col in entries:
            if values.ndim == 1:
                values = values[None]
            high, wide = values.shape
            total = total + jnp.pad(
                values, ((row, shape[0] - row - high), (col, shape[1] - col - wide))
            )
        return total

    if in_pieces:
        rect = cut(qkv_weight, far_x * 48, core * QKV_HALF, 48, QKV_HALF)
        notes = noted(
            (48, NOTES), *[(v, at, 0) for at, v in enumerate(small[0:4])],
            (rel_pos_h.T, 16, 0), (rel_pos_w.T, 24, 0),
        )
        rect = jnp.concatenate([rect, notes], axis=1)
        near = [rect] + [swap(rect, "fsdp", mask) for mask in (2, 4, 6)]
        up_rect = cut(up_weight, far_x * 48, core * 1536, 48, 1536)
        down_rect = cut(down_weight, core * 192 + far_x * 96, 0, 96, D)
        proj_rect = cut(proj_weight, far_x * 48, core * 384, 48, 384)
        notes = noted(
            (48, 128), *[(v, at, 0) for at, v in enumerate(small[4:8])],
            (up_bias.reshape(3, 128), 6, 0), (counted, 5, 0),
        )
        rects = jnp.concatenate([up_rect, proj_rect, notes], axis=1)
        down_rect = down_rect.reshape(2, 48, D)
        *near, rects, down_rect, aux = tied(*near, rects, down_rect, aux)
        planes = [rects] + [swap(rects, "fsdp", mask) for mask in (2, 4, 6)]
        near_a, near_b = jnp.stack(near[0:2]), jnp.stack(near[2:4])
        from_a, from_b = swap(near_a, "fsdp", 1), swap(near_b, "rep", 2)
        from_a, from_b, planes[1], tokens = tied(from_a, from_b, planes[1], tokens)
        near_a = jnp.concatenate([near_a, from_a])
        near_b = jnp.concatenate([near_b, from_b])
        far_a, far_b = swap(near_a, "rep", 2), swap(near_b, "fsdp", 1)
        far_a, far_b, planes[2], teacher = tied(far_a, far_b, planes[2], teacher)
        all_a, all_b = jnp.concatenate([near_a, far_a]), jnp.concatenate([near_b, far_b])
        other_a, other_b = swap(all_a, "rep", 1), swap(all_b, "rep", 1)
        vec, rel, rel_t = notes_of(me, near_a, near_b, far_b)
        vec, rel, rel_t, other_a, other_b, planes[3] = tied(
            vec, rel, rel_t, other_a, other_b, planes[3]
        )
        up_a, up_b = jnp.stack(planes[0:2]), jnp.stack(planes[2:4])
        up_a, up_b, vec = tied(up_a, up_b, vec)
        from_a, from_b = swap(up_a, "fsdp", 1), swap(up_b, "rep", 2)
        planes = [down_rect] + [swap(down_rect, "fsdp", mask) for mask in (2, 4, 6)]
        *state, w_qkv = attend(
            me, tokens, (all_a, all_b, other_a, other_b), vec, rel, places, 0, STEPS[0]
        )
        from_a, from_b, *rest = tied(from_a, from_b, *planes[1:], *state)
        planes, state = [down_rect] + rest[0:3], rest[3:]
        up_a, up_b = jnp.concatenate([up_a, from_a]), jnp.concatenate([up_b, from_b])
        down_a, down_b = jnp.stack(planes[0:2]), jnp.stack(planes[2:4])
        up_a, up_b, down_a, down_b, *state = tied(up_a, up_b, down_a, down_b, *state)
        far_up_a, far_up_b = swap(up_a, "rep", 2), swap(up_b, "fsdp", 1)
        core_up_a, core_up_b = swap(up_a, "rep", 1), swap(up_b, "rep", 1)
        state = attend(me, tokens, w_qkv, vec, rel, places, STEPS[0], STEPS[1], tuple(state))
        far_up_a, far_up_b, core_up_a, core_up_b, *state = tied(
            far_up_a, far_up_b, core_up_a, core_up_b, *state
        )
        from_a, from_b = swap(down_a, "fsdp", 1), swap(down_b, "rep", 2)
        core_far_a, core_far_b = swap(far_up_a, "rep", 1), swap(far_up_b, "rep", 1)
        state = attend(me, tokens, w_qkv, vec, rel, places, sum(STEPS[:2]), STEPS[2], tuple(state))
        from_a, from_b, core_far_a, core_far_b, *state = tied(
            from_a, from_b, core_far_a, core_far_b, *state
        )
        up_pieces = (up_a, far_up_a, up_b, far_up_b, core_up_a, core_far_a, core_up_b, core_far_b)
        down_a, down_b = jnp.concatenate([down_a, from_a]), jnp.concatenate([down_b, from_b])
        down_a, down_b, *state = tied(down_a, down_b, *state)
        far_a, far_b = swap(down_a, "rep", 2), swap(down_b, "fsdp", 1)
        core_a, core_b = swap(down_a, "rep", 1), swap(down_b, "rep", 1)
        qkv, probs, mixed, first_in = state
        hidden, second_in, act, slope, w_up, w_proj, vec2, _, total = mlp_up(
            me, tokens, mixed, aux, up_pieces, True
        )
        far_a, far_b, core_a, core_b, hidden = tied(far_a, far_b, core_a, core_b, hidden)
        down_pieces = (
            down_a, far_a, down_b, far_b,
            core_a, swap(far_a, "rep", 1), core_b, swap(far_b, "rep", 1),
        )
    else:
        gather = lambda v: lax.all_gather(v, "fsdp", axis=0, tiled=True)
        w_qkv, w_proj = gather(qkv_weight), gather(proj_weight)
        packed = gather(jnp.concatenate([v.reshape(-1) for v in small] + [counted])[None])
        pieces, at = [], 0
        for v in small:
            pieces.append(packed[:, at : at + v.size])
            at += v.size
        rows = [p.reshape(1, -1).astype(F32) for p in pieces[:9]]
        offsets = rel_pos_h.shape[0]
        tables = [
            p.reshape(parts, offsets, -1).transpose(1, 0, 2).reshape(offsets, HEAD_DIM)
            for p in pieces[9:]
        ]
        gap = jnp.zeros((32 - offsets, HEAD_DIM), BF16)
        table = jnp.concatenate([tables[0], gap, tables[1], gap], axis=0)
        hole = jnp.zeros((HEAD_DIM, HEAD_DIM), BF16)
        rel = jnp.concatenate(
            [jnp.concatenate([table, hole], axis=1), jnp.concatenate([hole, table], axis=1)],
            axis=0,
        )
        rel_t = rel.T
        fill = jnp.zeros((4, D), F32)
        vec = jnp.concatenate(rows[0:4] + [fill])
        counts = lax.psum(jnp.sum(valid), ("rep", "fsdp")).reshape(1, 1)
        vec2 = jnp.concatenate(rows[4:8] + [fill])
        total = jnp.broadcast_to(counts, (1, 128))
        w_up, down_pieces = gather(up_weight), (gather(down_weight),)
        qkv, probs, mixed, first_in = attend(me, tokens, w_qkv, vec, rel, places, 0, count)
        hidden, second_in, act, slope = mlp_up(
            me, tokens, mixed, aux, (w_proj, w_up, vec2, rows[8]), False
        )
    out, grad_hidden, grad_attn, grad_down, grad_up, sums2, up_sum = mlp_down(
        me, hidden, act, slope, teacher, aux, w_up, vec2, total, down_pieces,
        loss_scale * 2.0 / D, in_pieces,
    )
    valid_total = total[0, 0]
    flat = lambda v: v.reshape(count * ROWS, v.shape[-1])
    if in_pieces:
        back_ends = (0, BACK_STEPS[0], BACK_STEPS[0] + BACK_STEPS[1])
        parts_of = lambda keep, come: lambda at, to: added(keep[at:to], come[at:to])
        keep_d, send_d = down_grad(me, flat(act), flat(grad_down), flat(mixed), flat(grad_attn))
        send_d, second_in = tied(send_d, flat(second_in))
        from_d = swap(send_d, "rep", 1)
        send_u = up_grad(me, second_in, flat(grad_up), 1)
        from_d, send_u, second_in = tied(from_d, send_u, second_in)
        sum_d = parts_of(keep_d, from_d)
        send_a, send_b = sum_d(4, 8), sum_d(12, 16)
        send_a, send_b, send_u, second_in = tied(send_a, send_b, send_u, second_in)
        from_u = swap(send_u, "rep", 1)
        from_a, from_b = swap(send_a, "rep", 2), swap(send_b, "fsdp", 1)
        keep_u = up_grad(me, second_in, flat(grad_up), 0)
        from_u, keep_u, grad_attn = tied(from_u, keep_u, grad_attn)
        sum_u = parts_of(keep_u, from_u)
        send_ua, send_ub = sum_u(4, 8), sum_u(12, 16)
        send_ua, send_ub, grad_attn = tied(send_ua, send_ub, grad_attn)
        back = (grad_attn, w_proj, qkv, probs, rel_t, places_t)
        state = attend_back(*back, 0, BACK_STEPS[0])
        from_a, from_b, *state = tied(from_a, from_b, *state)
        d_a, d_b = added(sum_d(0, 4), from_a), added(sum_d(8, 12), from_b)
        send_a, send_b = d_a[2:4], d_b[2:4]
        send_a, send_b, *state = tied(send_a, send_b, *state)
        from_a, from_b = swap(send_a, "fsdp", 1), swap(send_b, "rep", 2)
        from_ua, from_ub = swap(send_ua, "rep", 2), swap(send_ub, "fsdp", 1)
        state = attend_back(*back, back_ends[1], BACK_STEPS[1], tuple(state))
        from_a, from_b, from_ua, from_ub, *state = tied(from_a, from_b, from_ua, from_ub, *state)
        d_a, d_b = added(d_a[0:2], from_a), added(d_b[0:2], from_b)
        u_a, u_b = added(sum_u(0, 4), from_ua), added(sum_u(8, 12), from_ub)
        sends_d = (d_a[0], d_a[1], d_b[0], d_b[1])
        send_ua, send_ub = u_a[2:4], u_b[2:4]
        *sends_d, send_ua, send_ub, s0, s1, s2 = tied(*sends_d, send_ua, send_ub, *state)
        from_z = [swap(v, "fsdp", mask) for v, mask in zip(sends_d[1:], (2, 4, 6))]
        from_ua, from_ub = swap(send_ua, "fsdp", 1), swap(send_ub, "rep", 2)
        state = attend_back(*back, back_ends[2], BACK_STEPS[2], (s0, s1, s2))
        from_ua, from_ub, from_z[0], dqkv, rel_grad, qv_sum = tied(
            from_ua, from_ub, from_z[0], *state
        )
        input_grad, sums1 = input_back(me, dqkv, w_qkv, tokens, grad_hidden, vec, 0, count)
        from_z[1], from_z[2], sums1, dqkv = tied(from_z[1], from_z[2], sums1, dqkv)
        own_d = sends_d[0].astype(F32)
        for v in from_z:
            own_d = own_d + v.astype(F32)
        u_a, u_b = added(u_a[0:2], from_ua), added(u_b[0:2], from_ub)
        notes = pack(me, sums1, qv_sum, sums2, up_sum, rel_grad)
        sends_u = (u_a[0], u_a[1], u_b[0], u_b[1])
        own_d, *sends_u, notes = tied(own_d.astype(BF16), *sends_u, notes)
        from_z = [swap(v, "fsdp", mask) for v, mask in zip(sends_u[1:], (2, 4, 6))]
        first_in, dqkv = flat(first_in), flat(dqkv)
        send = qkv_grad(me, first_in, dqkv, notes, 1)
        from_z[0], send, first_in, input_grad = tied(from_z[0], send, first_in, input_grad)
        from_core = swap(send, "rep", 1)
        keep = qkv_grad(me, first_in, dqkv, notes, 0)
        from_core, keep = tied(from_core, keep)
        both = parts_of(keep, from_core)
        send_a, send_b = both(4, 8), both(12, 16)
        send_a, send_b = tied(send_a, send_b)
        from_a, from_b = swap(send_a, "rep", 2), swap(send_b, "fsdp", 1)
        from_a, from_b, *from_z = tied(from_a, from_b, *from_z)
        sum_a, sum_b = added(both(0, 4), from_a), added(both(8, 12), from_b)
        own_u = sends_u[0].astype(F32)
        for v in from_z:
            own_u = own_u + v.astype(F32)
        own = jnp.concatenate([own_u.astype(BF16), own_d], axis=0)
        from_a, from_b = swap(sum_a[2:4], "fsdp", 1), swap(sum_b[2:4], "rep", 2)
        from_a, from_b = tied(from_a, from_b)
        sum_a, sum_b = added(sum_a[0:2], from_a), added(sum_b[0:2], from_b)
        sends = (sum_a[0], sum_a[1], sum_b[0], sum_b[1])
        *sends, own = tied(*sends, own)
        from_z = [swap(v, "fsdp", mask) for v, mask in zip(sends[1:], (2, 4, 6))]
        from_x = swap(own, "rep", 2)
        *from_z, from_x = tied(*from_z, from_x)
        own_q = sends[0].astype(F32)
        for v in from_z:
            own_q = own_q + v.astype(F32)
        own_q = own_q.astype(BF16)
        from_xq = swap(own_q, "rep", 2)
        d_up, d_down, d_proj = shard(
            me, (own, from_x, swap(own, "rep", 1), swap(from_x, "rep", 1))
        )
        from_xq, d_up = tied(from_xq, d_up)
        d_qkv, mine = qkv_shard(
            me, total, (own_q, from_xq, swap(own_q, "rep", 1), swap(from_xq, "rep", 1))
        )
        vectors = [mine[at, 0:96] for at in range(8)]
        tables = [mine[0:27, 96 + 8 * at : 104 + 8 * at] for at in range(2)]
        outs = vectors + [mine[27:30].reshape(-1)] + tables
        loss = mine[31, 0]
    else:
        scatter = lambda v: lax.psum(
            lax.psum_scatter(v, "fsdp", scatter_dimension=0, tiled=True), "rep"
        ).astype(F32)
        d_down = scatter(weight_grad(flat(act), flat(grad_down), True))
        d_up = scatter(weight_grad(flat(second_in), flat(grad_up)))
        d_proj = scatter(weight_grad(flat(mixed), flat(grad_attn)))
        back = (grad_attn, w_proj, qkv, probs, rel_t, places_t)
        dqkv, rel_grad, qv_sum = attend_back(*back, 0, count)
        d_qkv = scatter(weight_grad(flat(first_in), flat(dqkv)))
        input_grad, sums1 = input_back(me, dqkv, w_qkv, tokens, grad_hidden, vec, 0, count)
        offsets = rel_pos_h.shape[0]
        rel_sum = rel_grad[0:64, 0:64] + rel_grad[64:128, 64:128]
        vectors = [sums1[0], sums1[1], qv_sum[0], qv_sum[1], sums2[4], sums2[2], sums2[3],
                   sums2[1], up_sum[0]]
        own = jnp.concatenate(
            [v.reshape(parts, -1) for v in vectors]
            + [
                rel_sum[at : at + offsets].reshape(offsets, parts, -1).transpose(1, 0, 2)
                .reshape(parts, -1) for at in (0, 32)
            ]
            + [jnp.broadcast_to(jnp.sum(sums2[0]), (parts, 1))],
            axis=1,
        )
        mine = lax.dynamic_index_in_dim(
            lax.psum(own, ("rep", "fsdp")), part_at, 0, keepdims=False
        )
        outs, at = [], 0
        for v in small:
            outs.append(mine[at : at + v.size].reshape(v.shape))
            at += v.size
        loss = mine[at] / (valid_total * D)
    (g_gain1, g_shift1, g_qb, g_vb, g_pb, g_gain2, g_shift2, g_db, g_ub, g_rh, g_rw) = outs
    return (
        out, loss, input_grad.transpose(1, 0, 2), g_gain1, g_shift1, d_qkv, g_qb, g_vb, g_rh, g_rw, d_proj, g_pb,
        g_gain2, g_shift2, d_up, g_ub, d_down, g_db,
    )


def solution(mesh):
    windows = P(("rep", "fsdp"), None, None)
    vector = P("fsdp")
    matrix = P("fsdp", None)
    table = P(None, "fsdp")
    in_specs = (
        windows, windows, P(("rep", "fsdp"), None), vector, vector, matrix, vector, vector, table,
        table, matrix, vector, vector, vector, matrix, vector, matrix, vector,
    )
    out_specs = (windows, P(), windows) + in_specs[3:]
    return jax.shard_map(body, mesh=mesh, in_specs=in_specs, out_specs=out_specs, check_vma=False)
```

```python
import functools
import math

import jax
import jax.numpy as jnp
import numpy as np
from jax import lax
from jax.experimental import pallas as pl
from jax.experimental.pallas import tpu as pltpu
from jax.sharding import PartitionSpec as P

D = 768
HEADS = 12
HEAD_DIM = 64
MLP = 3072
WIN = 14
MAP = 64
SLOTS = WIN * WIN
ROWS = 208
LANES = 256
PAIRS = HEADS // 2
PAIR = 2 * HEAD_DIM
SIDE = (MAP + WIN - 1) // WIN
LN_EPS = 1e-06
SQRT_HALF = 0.7071067811865476
INV_ROOT_TAU = 0.3989422804014327
F32 = jnp.float32
BF16 = jnp.bfloat16
QKV_HALF = 3 * D // 2
NOTES = 128
STEPS = (3, 4, 1)
COST = 1e8
BACK_STEPS = (2, 5, 1)


def nn(left, right):
    return jnp.dot(left, right, preferred_element_type=F32)


def nt(left, right):
    return lax.dot_general(left, right, (((1,), (1,)), ((), ())), preferred_element_type=F32)


def tn(left, right):
    return lax.dot_general(left, right, (((0,), (0,)), ((), ())), preferred_element_type=F32)


def key_places():
    table = np.zeros((ROWS, HEAD_DIM), np.float32)
    for slot in range(SLOTS):
        for base in (0, 32):
            table[slot, base + WIN - 1 - slot // WIN] = 1.0
            table[slot, base + 16 + WIN - 1 - slot % WIN] = 1.0
    return table


def keep_column(base_ref, window):
    slot = lax.broadcasted_iota(jnp.int32, (ROWS, 1), 0)
    row = lax.shift_right_logical(slot * 4682, 16)
    col = slot - row * WIN
    place = lax.rem(base_ref[2] + window, SIDE * SIDE)
    place_row = lax.div(place, SIDE)
    place_col = place - place_row * SIDE
    inside = (slot < SLOTS) & (row + place_row * WIN < MAP) & (col + place_col * WIN < MAP)
    return inside.astype(F32)


def lane_places():
    slot = lax.broadcasted_iota(jnp.int32, (1, LANES), 1)
    row = lax.shift_right_logical(slot * 4682, 16)
    return row, slot - row * WIN


def norm_parts(values):
    mean = jnp.mean(values, axis=-1, keepdims=True)
    centred = values - mean
    inv_std = lax.rsqrt(jnp.mean(centred * centred, axis=-1, keepdims=True) + LN_EPS)
    return centred * inv_std, inv_std


def norm_grad(grad, scaled, inv_std, gain):
    grad_scaled = grad * gain
    first = jnp.mean(grad_scaled, axis=-1, keepdims=True)
    second = jnp.mean(grad_scaled * scaled, axis=-1, keepdims=True)
    return inv_std * (grad_scaled - first - scaled * second)


def up_by(values, amount):
    take = lambda bit: (amount & bit) != 0
    part = jnp.where(take(8), values[8:32], values[0:24])
    part = jnp.where(take(4), pltpu.roll(part, 20, 0), part)
    part = jnp.where(take(2), pltpu.roll(part, 22, 0), part)
    part = jnp.where(take(1), pltpu.roll(part, 23, 0), part)
    return part[0:16]


def down_by(values, amount):
    take = lambda bit: (amount & bit) != 0
    zeros = jnp.zeros((8, values.shape[1]), values.dtype)
    part = jnp.concatenate([values, zeros], axis=0)
    part = jnp.where(take(1), pltpu.roll(part, 1, 0), part)
    part = jnp.where(take(2), pltpu.roll(part, 2, 0), part)
    part = jnp.where(take(4), pltpu.roll(part, 4, 0), part)
    return jnp.where(
        take(8),
        jnp.concatenate([zeros, part], axis=0),
        jnp.concatenate([part, zeros], axis=0),
    )


def fill_rows(values):
    return jnp.concatenate(
        [values, jnp.zeros((LANES - ROWS,) + values.shape[1:], values.dtype)], axis=0
    )


def chunk_place(me_ref, index, far_y, along_y):
    mid, plane = index // 2, index % 2
    dist_x, dist_y = (far_y, mid) if along_y else (mid, far_y)
    plane = plane * 2 + (0 if along_y else 4)
    return (me_ref[0] // 2) ^ dist_x, me_ref[1] ^ (plane + dist_y)


ARRIVED = tuple((half, along_y, other) for other in (0, 1) for along_y in (True, False) for half in (0, 1))


def load_first(me_ref, parts, full, sem):
    core = me_ref[0] % 2
    for at, ref in enumerate(parts):
        along_y, other = at % 2 == 0, at // 2

        def start(index, carry, ref=ref, along_y=along_y, other=other):
            far_x, owner = chunk_place(me_ref, index % 4, index // 4, along_y)
            pltpu.make_async_copy(
                ref.at[index, :, pl.ds(0, QKV_HALF)],
                full.at[
                    pl.ds(pl.multiple_of(owner * 96 + far_x * 48, 16), 48),
                    pl.ds(pl.multiple_of((core ^ other) * QKV_HALF, 128), QKV_HALF),
                ],
                sem.at[0],
            ).start()
            return carry

        lax.fori_loop(0, 8, start, 0)
    pltpu.make_async_copy(full, full, sem.at[0]).wait()


def piece_place(me_ref, index):
    group, high, mid, plane = index // 8, (index // 4) % 2, (index // 2) % 2, index % 2
    dist_x = jnp.where(group == 0, high, mid)
    dist_y = jnp.where(group == 0, mid, high)
    return (me_ref[0] // 2) ^ dist_x, me_ref[1] ^ (group * 4 + plane * 2 + dist_y)


def piece_index(me_ref, far_x, owner):
    dist = me_ref[1] ^ owner
    dist_x = (me_ref[0] // 2) ^ far_x
    dist_y, plane, group = dist % 2, (dist // 2) % 2, dist // 4
    high = jnp.where(group == 0, dist_x, dist_y)
    mid = jnp.where(group == 0, dist_y, dist_x)
    return group * 8 + high * 4 + mid * 2 + plane


def spread_rows(notes_of, owner_of, width, total):
    row = lax.broadcasted_iota(jnp.int32, (128, total), 0)
    col = lax.broadcasted_iota(jnp.int32, (128, total), 1)
    acc = None
    for at in range(8):
        put = ((row < width) & (col == row + owner_of(at) * width)).astype(BF16)
        part = nn(notes_of(at), put)
        acc = part if acc is None else acc + part
    return acc


def notes_kernel(me_ref, a_ref, b_ref, c_ref, vec_ref, rel_ref, relt_ref, turn_ref):
    picks = [(a_ref, at, at % 2 * 2 + at // 2) for at in range(4)]
    picks += [(b_ref, at, 4 + at * 2) for at in range(2)] + [(c_ref, at, 5 + at * 2) for at in range(2)]
    owner_of = lambda at: me_ref[1] ^ picks[at][2]
    lanes = pl.ds(QKV_HALF, NOTES)
    vec_ref[...] = spread_rows(
        lambda at: picks[at][0][picks[at][1], 0:16, lanes], owner_of, 96, D
    )[0:8]
    for at in range(8):
        both = picks[at][0][picks[at][1], 16:32, lanes].astype(F32)
        for copy in range(2):
            place = pl.ds(pl.multiple_of(copy * 64 + owner_of(at) * 8, 8), 8)
            turn_ref[place, :] = jnp.concatenate([both[0:8, 0:32], both[8:16, 0:32]] * 2, axis=1)
    row = lax.broadcasted_iota(jnp.int32, (128, 128), 0)
    col = lax.broadcasted_iota(jnp.int32, (128, 128), 1)
    turned = jnp.where((row < 64) == (col < 64), turn_ref[...], 0.0)
    relt_ref[...] = turned.astype(BF16)
    rel_ref[...] = turned.T.astype(BF16)


def attend_kernel(*refs, first, pieces, earlier):
    base_ref, tok_ref = refs[0:2]
    at = 2 + max(pieces, 1)
    vec_ref, rel_ref, place_ref = refs[at : at + 3]
    at += 3 + earlier
    qkv_ref, prob_ref, mix_ref, fin_ref = refs[at : at + 4]
    if pieces:
        w_ref, sem, s_ref = refs[at + 4 :]

        @pl.when(pl.program_id(0) == 0)
        def _():
            load_first(base_ref, refs[2 : 2 + pieces], w_ref, sem)
    else:
        w_ref = refs[2]
        s_ref = refs[at + 4]
    keep = keep_column(base_ref, pl.program_id(0) + first)
    scaled, _ = norm_parts(tok_ref[0].astype(F32))
    first_in = (keep * (scaled * vec_ref[0:1, :] + vec_ref[1:2, :])).astype(BF16)
    fin_ref[0] = first_in
    for part in range(3):
        cols = pl.ds(part * D, D)
        total = nn(first_in, w_ref[:, cols])
        if part != 1:
            total = total + vec_ref[2 + part // 2 : 3 + part // 2, :]
        qkv_ref[0, :, cols] = total.astype(BF16)
    lane_row, lane_col = lane_places()
    low_half = lax.broadcasted_iota(jnp.int32, (ROWS, PAIR), 1) < HEAD_DIM
    tail_rows = lax.broadcasted_iota(jnp.int32, (16, LANES), 0) + 192
    places = place_ref[...]
    place_pair = jnp.concatenate([places, places], axis=1)

    def one_pair(pair, carry):
        at = pl.multiple_of(pair * PAIR, PAIR)
        query = qkv_ref[0, :, pl.ds(at, PAIR)]
        keys = qkv_ref[0, :, pl.ds(pl.multiple_of(D + at, PAIR), PAIR)]
        values = qkv_ref[0, :, pl.ds(pl.multiple_of(2 * D + at, PAIR), PAIR)]
        query_t = fill_rows(query).T
        offsets = nn(rel_ref[...], query_t)
        mixed = []
        for head in range(2):
            mine = offsets[head * HEAD_DIM : (head + 1) * HEAD_DIM]
            along = jnp.concatenate(
                [up_by(mine[0:32], lane_row), up_by(mine[32:64], lane_col)], axis=0
            )
            high = along.astype(BF16)
            rest = (along - high.astype(F32)).astype(BF16)
            scaled_q = query_t[head * HEAD_DIM : (head + 1) * HEAD_DIM] * jnp.asarray(
                HEAD_DIM ** (-0.5), BF16
            )
            if head == 0:
                query_ext = jnp.concatenate([scaled_q, high, rest], axis=0)
                keys_ext = jnp.where(low_half, keys, place_pair)
            else:
                query_ext = jnp.concatenate([high, rest, scaled_q], axis=0)
                keys_ext = jnp.where(low_half, place_pair, keys)
            s_ref[2 * pair + head] = nn(keys_ext, query_ext)
        return carry

    def soft(head, carry):
        scores = s_ref[head]
        scores = jnp.concatenate(
            [scores[0:192], jnp.where(tail_rows < SLOTS, scores[192:208], -1e30)], axis=0
        )
        peak = jnp.max(scores, axis=0, keepdims=True)
        expo = jnp.exp(scores - peak)
        total = jnp.sum(expo, axis=0, keepdims=True)
        prob_ref[0, head] = (expo * (1.0 / total)).astype(BF16)
        return carry

    def mix(pair, carry):
        at = pl.multiple_of(pair * PAIR, PAIR)
        values = qkv_ref[0, :, pl.ds(pl.multiple_of(2 * D + at, PAIR), PAIR)]
        mixed = [tn(prob_ref[0, 2 * pair + head], values)[0:ROWS].astype(BF16) for head in range(2)]
        mix_ref[0, :, pl.ds(at, PAIR)] = jnp.where(low_half, mixed[0], mixed[1])
        return carry

    lax.fori_loop(0, PAIRS, one_pair, 0, unroll=PAIRS)
    lax.fori_loop(0, HEADS, soft, 0, unroll=HEADS)
    lax.fori_loop(0, PAIRS, mix, 0, unroll=PAIRS)


def gelu_parts(pre):
    cumulative = 0.5 + 0.5 * lax.erf(pre * SQRT_HALF)
    bell = jnp.exp(pre * pre * (-0.5))
    return pre * cumulative, cumulative + pre * (bell * INV_ROOT_TAU)


def load_up(me_ref, pieces, up, proj, notes, sem):
    core = me_ref[0] % 2
    for array, (ref, (half, along_y, other)) in enumerate(zip(pieces, ARRIVED)):

        def start_small(index, carry, ref=ref, half=half, along_y=along_y, far_core=core ^ other, array=array):
            far_x, owner = chunk_place(me_ref, index, half, along_y)
            rows = pl.ds(pl.multiple_of(owner * 96 + far_x * 48, 16), 48)
            cols = pl.ds(pl.multiple_of(far_core * 384, 128), 384)
            pltpu.make_async_copy(
                ref.at[index, :, pl.ds(1536, 384)], proj.at[rows, cols], sem.at[1]
            ).start()
            pltpu.make_async_copy(
                ref.at[index, pl.ds(0, 16), pl.ds(1920, 128)], notes.at[array * 4 + index], sem.at[2]
            ).start()
            return carry

        lax.fori_loop(0, 4, start_small, 0)
    for ref, (half, along_y, other) in zip(pieces, ARRIVED):

        def start(index, carry, ref=ref, half=half, along_y=along_y, far_core=core ^ other):
            far_x, owner = chunk_place(me_ref, index, half, along_y)
            rows = pl.ds(pl.multiple_of(owner * 96 + far_x * 48, 16), 48)
            cols = pl.ds(pl.multiple_of(far_core * 1536, 128), 1536)
            pltpu.make_async_copy(
                ref.at[index, :, pl.ds(0, 1536)], up.at[rows, cols], sem.at[0]
            ).start()
            return carry

        lax.fori_loop(0, 4, start, 0)
    for at, full in ((2, notes), (1, proj)):
        pltpu.make_async_copy(full, full, sem.at[at]).wait()


def load_down(me_ref, pieces, down, sem):
    core = me_ref[0] % 2
    for ref, (half, along_y, other) in zip(pieces, ARRIVED):

        def start(index, carry, ref=ref, half=half, along_y=along_y, far_core=core ^ other):
            far_x, owner = chunk_place(me_ref, index, half, along_y)
            place = owner * 8 + far_core * 4 + far_x * 2
            pltpu.make_async_copy(ref.at[index], down.at[pl.ds(place, 2)], sem.at[0]).start()
            return carry

        lax.fori_loop(0, 4, start, 0)
    pltpu.make_async_copy(down, down, sem.at[0]).wait()


def up_kernel(*refs, group, pieces):
    rows = group * ROWS
    me_ref, tok_ref, mix_ref, keep_ref = refs[0:4]
    at = 4 + (pieces or 4)
    hid_ref, si_ref, act_ref, slope_ref = refs[at : at + 4]
    at += 4
    if pieces:
        up_ref, wp_ref, vec_ref, ub_ref, total_ref, notes, sem = refs[at:]

        @pl.when(pl.program_id(0) == 0)
        def _():
            load_up(me_ref, refs[4 : 4 + pieces], up_ref, wp_ref, notes, sem)
            picks = [(at, at % 2 * 2 + at // 2) for at in range(4)]
            picks += [(8 + at, 4 + at * 2) for at in range(2)] + [(12 + at, 5 + at * 2) for at in range(2)]
            owner_of = lambda at: me_ref[1] ^ picks[at][1]
            vec_ref[...] = spread_rows(
                lambda at: notes[picks[at][0]], owner_of, 96, D
            )[0:8]
            for at in range(8):
                lanes = pl.ds(pl.multiple_of(owner_of(at) * 384, 128), 384)
                own = notes[picks[at][0]].astype(F32)
                ub_ref[:, lanes] = jnp.concatenate([own[6:7], own[7:8], own[8:9]], axis=1)
            counts = notes[0].astype(F32)
            for at in range(1, 32):
                counts = counts + notes[at].astype(F32)
            counts = counts[5:6]
            lane = lax.broadcasted_iota(jnp.int32, (1, 128), 1)
            weight = jnp.where(lane == 0, 128.0, jnp.where(lane == 1, 1.0, 0.0))
            total_ref[...] = jnp.broadcast_to(
                jnp.sum(counts * weight, axis=1, keepdims=True), (1, 128)
            )
    else:
        wp_ref, up_ref, vec_ref, ub_ref = refs[4:8]
    pb_row, gain_row, shift_row = [vec_ref[at : at + 1, :] for at in range(3)]
    keep = keep_ref[...].reshape(rows, 2)[:, 0:1]
    attn_out = nn(mix_ref[...].reshape(rows, D), wp_ref[...]) + pb_row
    hidden = keep * (tok_ref[...].reshape(rows, D).astype(F32) + attn_out)
    hid_ref[...] = hidden.reshape(group, ROWS, D)
    scaled, _ = norm_parts(hidden)
    second_in = (scaled * gain_row + shift_row).astype(BF16)
    si_ref[...] = second_in.reshape(group, ROWS, D)
    if pieces:

        @pl.when(pl.program_id(0) == 0)
        def _():
            pltpu.make_async_copy(up_ref, up_ref, sem.at[0]).wait()

    for part in range(MLP // D):
        cols = slice(part * D, part * D + D)
        act, slope = gelu_parts(nn(second_in, up_ref[:, cols]) + ub_ref[:, cols])
        slope_ref[:, :, cols] = slope.astype(BF16).reshape(group, ROWS, D)
        act_ref[:, :, cols] = act.astype(BF16).reshape(group, ROWS, D)


def down_kernel(*refs, group, pieces, scale):
    step = pl.program_id(0)
    rows = group * ROWS
    me_ref, hid_ref, act_ref, slope_ref, teach_ref, aux_ref, up_ref, vec_ref, total_ref = refs[0:9]
    at = 9 + (pieces or 1)
    out_ref, gh_ref, ga_ref, gd_ref, gu_ref, sums_ref, usum_ref = refs[at : at + 7]
    final_ref = refs[at + 7]
    if pieces:
        down3_ref, sem = refs[at + 8 :]

        @pl.when(step == 0)
        def _():
            load_down(me_ref, refs[9 : 9 + pieces], down3_ref, sem)

        down_rows = lambda part: down3_ref[pl.ds(part * 16, 16)].reshape(D, D)
    else:
        down_rows = lambda part: refs[9][pl.ds(part * D, D), :]

    @pl.when(step == 0)
    def _():
        sums_ref[...] = jnp.zeros_like(sums_ref)
        usum_ref[...] = jnp.zeros_like(usum_ref)

    gain_row, db_row = vec_ref[1:2, :], vec_ref[3:4, :]
    coef = scale / total_ref[:, 0:1]
    aux = aux_ref[...].reshape(rows, 2)
    keep, valid = aux[:, 0:1], aux[:, 1:2]
    hidden = hid_ref[...].reshape(rows, D)
    down = db_row
    for part in range(MLP // D):
        cols = slice(part * D, part * D + D)
        down = down + nn(act_ref[:, :, cols].reshape(rows, D), down_rows(part))
    final = keep * (hidden + down)
    for at in range(group):
        final_ref[:, step * group + at, :] = final[at * ROWS : at * ROWS + SLOTS]

    @pl.when(step == pl.num_programs(0) - 1)
    def _():
        out_ref[...] = final_ref[...].astype(BF16)

    error = final - teach_ref[...].reshape(rows, D).astype(F32)
    weighted = valid * error
    grad_final = coef * weighted
    grad_down = grad_final.astype(BF16)
    gd_ref[...] = grad_down.reshape(group, ROWS, D)
    sums_ref[0:1, :] += jnp.sum(weighted * error, axis=0, keepdims=True)
    sums_ref[1:2, :] += jnp.sum(grad_down.astype(F32), axis=0, keepdims=True)
    for part in range(MLP // D):
        cols = slice(part * D, part * D + D)
        slope = slope_ref[:, :, cols].reshape(rows, D).astype(F32)
        grad_up = (nt(grad_down, down_rows(part)) * slope).astype(BF16)
        gu_ref[:, :, cols] = grad_up.reshape(group, ROWS, D)
        usum_ref[:, cols] += jnp.sum(grad_up.astype(F32), axis=0, keepdims=True)
    grad_second = nt(gu_ref[...].reshape(rows, MLP), up_ref[...])
    scaled, inv_std = norm_parts(hidden)
    sums_ref[2:3, :] += jnp.sum(grad_second * scaled, axis=0, keepdims=True)
    sums_ref[3:4, :] += jnp.sum(grad_second, axis=0, keepdims=True)
    grad_hidden = keep * (grad_final + norm_grad(grad_second, scaled, inv_std, gain_row))
    gh_ref[...] = grad_hidden.reshape(group, ROWS, D)
    grad_attn = grad_hidden.astype(BF16)
    ga_ref[...] = grad_attn.reshape(group, ROWS, D)
    sums_ref[4:5, :] += jnp.sum(grad_attn.astype(F32), axis=0, keepdims=True)


def attend_back_kernel(*refs, earlier):
    ga_ref, wp_ref, qkv_ref, prob_ref, relt_ref, placet_ref = refs[0:6]
    dqkv_ref, rg_ref, qsum_ref, gm_ref, s_ref, g_ref, e_ref = refs[6 + earlier :]

    @pl.when(pl.program_id(0) == 0)
    def _():
        rg_ref[...] = refs[7][...] if earlier else jnp.zeros_like(rg_ref)
        qsum_ref[...] = refs[8][...] if earlier else jnp.zeros_like(qsum_ref)
        gm_ref[pl.ds(ROWS, LANES - ROWS), :] = jnp.zeros((LANES - ROWS, D), BF16)

    gm_ref[pl.ds(0, ROWS), :] = nt(ga_ref[0], wp_ref[...]).astype(BF16)
    lane_row, lane_col = lane_places()
    low_half = lax.broadcasted_iota(jnp.int32, (ROWS, PAIR), 1) < HEAD_DIM
    low_full = lax.broadcasted_iota(jnp.int32, (LANES, PAIR), 1) < HEAD_DIM
    blank = jnp.zeros((), BF16)
    scale = HEAD_DIM ** (-0.5)

    pair_at = lambda base, pair: pl.ds(base + pair * PAIR, PAIR)
    own = (
        lambda full: jnp.where(low_full, full, blank),
        lambda full: jnp.where(low_full, blank, full),
    )
    for pair in range(PAIRS):
        values = qkv_ref[0, :, pair_at(2 * D, pair)]
        stacked = jnp.concatenate(
            [jnp.where(low_half, values, blank), jnp.where(low_half, blank, values)], axis=0
        )
        grad_probs = nt(stacked, gm_ref[:, pair_at(0, pair)])
        s_ref[2 * pair] = grad_probs[0:ROWS]
        s_ref[2 * pair + 1] = grad_probs[ROWS : 2 * ROWS]
    for head in range(HEADS):
        probs = prob_ref[0, head].astype(F32)
        grad_p = s_ref[head]
        row_dot = jnp.sum(probs * grad_p, axis=0, keepdims=True)
        g_ref[head] = (probs * (grad_p - row_dot)).astype(BF16)
    for pair in range(PAIRS):
        query = fill_rows(qkv_ref[0, :, pair_at(0, pair)])
        grad_out = gm_ref[:, pair_at(0, pair)]
        grad_values = nn(prob_ref[0, 2 * pair], own[0](grad_out)) + nn(
            prob_ref[0, 2 * pair + 1], own[1](grad_out)
        )
        grad_keys = nn(g_ref[2 * pair], own[0](query)) + nn(g_ref[2 * pair + 1], own[1](query))
        grad_values = grad_values.astype(BF16)
        dqkv_ref[0, :, pair_at(D, pair)] = (grad_keys * scale).astype(BF16)
        dqkv_ref[0, :, pair_at(2 * D, pair)] = grad_values
        qsum_ref[1:2, pair_at(0, pair)] += jnp.sum(
            grad_values.astype(F32), axis=0, keepdims=True
        )
    for pair in range(PAIRS):
        keys_t = fill_rows(qkv_ref[0, :, pair_at(D, pair)]).T
        for head in range(2):
            keys_ext = jnp.concatenate(
                [keys_t[head * HEAD_DIM : (head + 1) * HEAD_DIM], placet_ref[...]], axis=0
            )
            e_ref[2 * pair + head] = nn(keys_ext, fill_rows(g_ref[2 * pair + head]))
    for pair in range(PAIRS):
        query = fill_rows(qkv_ref[0, :, pair_at(0, pair)])
        plain, spread = [], []
        for head in range(2):
            grad_ext = e_ref[2 * pair + head]
            plain.append(grad_ext[0:64])
            spread.append(down_by(grad_ext[64:80], lane_row))
            spread.append(down_by(grad_ext[80:96], lane_col))
        spread = jnp.concatenate(spread, axis=0).astype(BF16)
        grad_query = jnp.concatenate(plain, axis=0) * scale + nn(relt_ref[...], spread)
        rg_ref[...] += nn(spread, query)
        grad_query = grad_query.astype(BF16).T[0:ROWS]
        dqkv_ref[0, :, pair_at(0, pair)] = grad_query
        qsum_ref[0:1, pair_at(0, pair)] += jnp.sum(grad_query.astype(F32), axis=0, keepdims=True)


def input_kernel(
    base_ref, dqkv_ref, w_ref, tok_ref, gh_ref, vec_ref, *refs, group, first, earlier
):
    step = pl.program_id(0)
    out_ref, sums_ref = refs[earlier:]

    @pl.when(step == 0)
    def _():
        sums_ref[...] = refs[1][...] if earlier else jnp.zeros_like(sums_ref)

    keep = jnp.concatenate(
        [keep_column(base_ref, first + step * group + at) for at in range(group)], axis=0
    )
    rows = group * ROWS
    grad_first = keep * nt(dqkv_ref[...].reshape(rows, 3 * D), w_ref[...])
    scaled, inv_std = norm_parts(tok_ref[...].reshape(rows, D).astype(F32))
    sums_ref[0:1, :] += jnp.sum(grad_first * scaled, axis=0, keepdims=True)
    sums_ref[1:2, :] += jnp.sum(grad_first, axis=0, keepdims=True)
    total = gh_ref[...].reshape(rows, D) + norm_grad(grad_first, scaled, inv_std, vec_ref[0:1, :])
    for at in range(group):
        out_ref[:, first + step * group + at, :] = total[at * ROWS : at * ROWS + SLOTS]


def weight_grad_kernel(*refs):
    left_ref, right_ref, out_ref = refs
    out_ref[...] = tn(left_ref[...], right_ref[...]).astype(BF16)


def qkv_grad_kernel(me_ref, left_ref, right_ref, notes_ref, out_ref, full, sem, *, other):
    full[...] = tn(left_ref[...], right_ref[...]).astype(BF16)
    core = (me_ref[0] % 2) ^ other

    def start(index, carry):
        far_x, owner = piece_place(me_ref, index)
        pltpu.make_async_copy(
            full.at[pl.ds(pl.multiple_of(owner * 96 + far_x * 48, 16), 48)],
            out_ref.at[index, :, pl.ds(0, QKV_HALF)],
            sem.at[0],
        ).start()
        pltpu.make_async_copy(
            notes_ref.at[core * 2 + far_x, owner],
            out_ref.at[index, :, pl.ds(QKV_HALF, NOTES)],
            sem.at[0],
        ).start()
        return carry

    lax.fori_loop(0, 16, start, 0)
    pltpu.make_async_copy(out_ref, out_ref, sem.at[0]).wait()


def up_grad_kernel(me_ref, left_ref, right_ref, out_ref, full, sem):
    step = pl.program_id(0)
    full[step] = tn(left_ref[...], right_ref[...]).astype(BF16)

    def start(index, carry):
        far_x, owner = piece_place(me_ref, index)
        rows = pl.ds(pl.multiple_of(owner * 96 + far_x * 48, 16), 48)
        pltpu.make_async_copy(full.at[step, rows], out_ref.at[index, step], sem.at[0]).start()
        return carry

    lax.fori_loop(0, 16, start, 0)

    @pl.when(step == pl.num_programs(0) - 1)
    def _():
        pltpu.make_async_copy(out_ref, out_ref, sem.at[0]).wait()


def down_grad_kernel(
    me_ref, act_ref, gd_ref, mix_any, ga_any, keep_ref, send_ref, full, half, mix_ref, ga_ref, sem
):
    step = pl.program_id(0)
    last = pl.num_programs(0) - 1
    fetches = [
        pltpu.make_async_copy(mix_any, mix_ref, sem.at[2]),
        pltpu.make_async_copy(ga_any, ga_ref, sem.at[3]),
    ]

    @pl.when(step == 0)
    def _():
        for fetch in fetches:
            fetch.start()

    @pl.when(step < last)
    def _():
        full[step] = tn(act_ref[...], gd_ref[...]).astype(BF16).reshape(16, 48, D)

    @pl.when(step == last)
    def _():
        for fetch in fetches:
            fetch.wait()
        total = tn(mix_ref[...], ga_ref[...]).astype(BF16)
        for core in range(2):
            half[core] = total[:, core * 384 : core * 384 + 384]

    core = me_ref[0] % 2
    for ref, far_core, at in ((keep_ref, core, 0), (send_ref, 1 - core, 1)):

        def start_proj(index, carry, ref=ref, far_core=far_core, at=at):
            far_x, owner = piece_place(me_ref, index)
            rows = pl.ds(pl.multiple_of(owner * 96 + far_x * 48, 16), 48)
            for col in (0, 384):
                pltpu.make_async_copy(
                    half.at[far_core, rows], ref.at[index, 2, :, pl.ds(col, 384)], sem.at[at]
                ).start()
            return carry

        @pl.when(step < last)
        def _(ref=ref, far_core=far_core, at=at):
            for place in range(4):
                which, far_x = place // 2, place % 2
                pltpu.make_async_copy(
                    full.at[step, pl.ds(which * 8 + far_core * 4 + far_x * 2, 2)],
                    ref.at[piece_index(me_ref, far_x, step * 2 + which), pl.ds(0, 2)],
                    sem.at[at],
                ).start()

        @pl.when(step == last)
        def _(start_proj=start_proj):
            lax.fori_loop(0, 16, start_proj, 0)

    @pl.when(step == last)
    def _():
        pltpu.make_async_copy(keep_ref, keep_ref, sem.at[0]).wait()
        pltpu.make_async_copy(send_ref, send_ref, sem.at[1]).wait()


def whole(shape):
    zeros = (0,) * len(shape)
    return pl.BlockSpec(shape, lambda *_: zeros, pipeline_mode=pl.Buffered(1))


def whole_out(shape):
    zeros = (0,) * len(shape)
    return pl.BlockSpec(shape, lambda *_: zeros)


def windows_from(first, shape):
    tail = (0,) * (len(shape) - 1)
    return pl.BlockSpec(shape, lambda step: (step + first,) + tail)


SMEM = pl.BlockSpec(memory_space=pltpu.SMEM)
ANY = pl.BlockSpec(memory_space=pl.ANY)


def params(mebibytes=32):
    return pltpu.CompilerParams(
        vmem_limit_bytes=mebibytes * 1024 * 1024, dimension_semantics=("arbitrary",)
    )


def shape_of(shape, dtype):
    return jax.ShapeDtypeStruct(shape, dtype)


def cost(flops, moved):
    return pl.CostEstimate(flops=int(flops), bytes_accessed=int(moved), transcendentals=0)


def notes_of(me, near, far_x, far_y):
    return pl.pallas_call(
        notes_kernel,
        in_specs=[SMEM] + [whole(v.shape) for v in (near, far_x, far_y)],
        out_specs=[whole_out((8, D)), whole_out((PAIR, PAIR)), whole_out((PAIR, PAIR))],
        out_shape=[shape_of((8, D), F32)] + [shape_of((PAIR, PAIR), BF16)] * 2,
        grid=(1,),
        scratch_shapes=[pltpu.VMEM((128, 128), F32)],
        compiler_params=params(),
        cost_estimate=cost(COST, 1e5),
        name="notes",
    )(me, near, far_x, far_y)


def attend(me, tokens, weight, vec, rel, places, first, number, earlier=()):
    count = tokens.shape[0]
    win = lambda shape: windows_from(first, shape)
    pieces = len(weight) if isinstance(weight, tuple) else 0
    weights = weight if pieces else (weight,)
    weight_specs = [ANY] * pieces if pieces else [whole((D, 3 * D))]
    out_specs = [win((1, ROWS, 3 * D)), win((1, HEADS, ROWS, LANES)), win((1, ROWS, D)),
                 win((1, ROWS, D))]
    out_shape = [
        shape_of((count, ROWS, 3 * D), BF16), shape_of((count, HEADS, ROWS, LANES), BF16),
        shape_of((count, ROWS, D), BF16), shape_of((count, ROWS, D), BF16),
    ]
    scratch = [pltpu.VMEM((HEADS, ROWS, LANES), F32)]
    if pieces:
        out_specs.append(whole_out((D, 3 * D)))
        out_shape.append(shape_of((D, 3 * D), BF16))
        scratch.insert(0, pltpu.SemaphoreType.DMA((1,)))
    inputs = 5 + len(weights)
    return pl.pallas_call(
        functools.partial(attend_kernel, first=first, pieces=pieces, earlier=len(earlier)),
        grid=(number,),
        in_specs=[
            SMEM, win((1, ROWS, D)), *weight_specs, whole((8, D)),
            whole((PAIR, PAIR)), whole((ROWS, HEAD_DIM)), *([ANY] * len(earlier)),
        ],
        out_specs=out_specs,
        out_shape=out_shape,
        scratch_shapes=scratch,
        input_output_aliases={inputs + at: at for at in range(len(earlier))},
        compiler_params=params(54),
        cost_estimate=cost(COST, 1e5),
        name="attend",
    )(me, tokens, *weights, vec, rel, places, *earlier)


def mlp_up(me, tokens, mixed, aux, weights, chunked):
    count = tokens.shape[0]
    group = math.gcd(count, 2)
    win = lambda width: windows_from(0, (group, ROWS, width))
    arr = lambda width, dtype: shape_of((count, ROWS, width), dtype)
    pieces = len(weights) if chunked else 0
    out_specs = [win(D), win(D), win(MLP), win(MLP)]
    out_shape = [arr(D, F32), arr(D, BF16), arr(MLP, BF16), arr(MLP, BF16)]
    scratch = []
    if pieces:
        shapes = [((D, MLP), BF16), ((D, D), BF16), ((8, D), F32), ((1, MLP), F32), ((1, 128), F32)]
        out_specs += [whole_out(s) for s, _ in shapes]
        out_shape += [shape_of(s, t) for s, t in shapes]
        scratch += [pltpu.VMEM((32, 16, 128), BF16), pltpu.SemaphoreType.DMA((3,))]
    return pl.pallas_call(
        functools.partial(up_kernel, group=group, pieces=pieces),
        grid=(count // group,),
        in_specs=[SMEM, win(D), win(D), win(2)]
        + ([ANY] * pieces if pieces else [whole(v.shape) for v in weights]),
        out_specs=out_specs,
        out_shape=out_shape,
        scratch_shapes=scratch,
        compiler_params=params(60),
        cost_estimate=cost(COST * count, 1e5),
        name="mlp_up",
    )(me, tokens, mixed, aux, *weights)


def mlp_down(me, hidden, act, slope, teacher, aux, up, vec, total, weights, scale, chunked):
    count = hidden.shape[0]
    group = math.gcd(count, 2)
    win = lambda width: windows_from(0, (group, ROWS, width))
    arr = lambda width, dtype: shape_of((count, ROWS, width), dtype)
    pieces = len(weights) if chunked else 0
    scratch = [pltpu.VMEM((SLOTS, count, D), F32)]
    if pieces:
        scratch += [pltpu.VMEM((MLP // 48, 48, D), BF16), pltpu.SemaphoreType.DMA((1,))]
    return pl.pallas_call(
        functools.partial(down_kernel, group=group, pieces=pieces, scale=scale),
        grid=(count // group,),
        in_specs=[SMEM, win(D), win(MLP), win(MLP), win(D), win(2), whole((D, MLP)), whole((8, D)),
                  whole((1, 128))]
        + ([ANY] * pieces if pieces else [whole(v.shape) for v in weights]),
        out_specs=[whole_out((SLOTS, count, D)), win(D), win(D), win(D), win(MLP), whole_out((5, D)), whole_out((1, MLP))],
        out_shape=[
            shape_of((SLOTS, count, D), BF16), arr(D, F32), arr(D, BF16), arr(D, BF16),
            arr(MLP, BF16), shape_of((5, D), F32), shape_of((1, MLP), F32),
        ],
        scratch_shapes=scratch,
        compiler_params=params(60),
        cost_estimate=cost(COST * count, 1e5),
        name="mlp_down",
    )(me, hidden, act, slope, teacher, aux, up, vec, total, *weights)


def attend_back(grad_attn, proj, qkv, probs, rel_t, places_t, first, number, earlier=()):
    count = grad_attn.shape[0]
    win = lambda shape: windows_from(first, shape)
    before = [ANY, whole((PAIR, PAIR)), whole((2, D))] if earlier else []
    return pl.pallas_call(
        functools.partial(attend_back_kernel, earlier=len(earlier)),
        grid=(number,),
        in_specs=[
            win((1, ROWS, D)), whole((D, D)), win((1, ROWS, 3 * D)), win((1, HEADS, ROWS, LANES)),
            whole((PAIR, PAIR)), whole((32, LANES)), *before,
        ],
        out_specs=[win((1, ROWS, 3 * D)), whole_out((PAIR, PAIR)), whole_out((2, D))],
        out_shape=[
            shape_of((count, ROWS, 3 * D), BF16), shape_of((PAIR, PAIR), F32),
            shape_of((2, D), F32),
        ],
        scratch_shapes=[
            pltpu.VMEM((LANES, D), BF16), pltpu.VMEM((HEADS, ROWS, LANES), F32),
            pltpu.VMEM((HEADS, ROWS, LANES), BF16), pltpu.VMEM((HEADS, 96, LANES), F32),
        ],
        input_output_aliases={6: 0} if earlier else {},
        compiler_params=params(48),
        cost_estimate=cost(COST, 1e5),
        name="attend_back",
    )(grad_attn, proj, qkv, probs, rel_t, places_t, *earlier)


def input_back(me, dqkv, weight, tokens, grad_hidden, vec, first, number, earlier=()):
    count = tokens.shape[0]
    group = math.gcd(math.gcd(first, number), 2)
    win = lambda shape: windows_from(first // group, shape)
    before = [ANY, whole((2, D))] if earlier else []
    return pl.pallas_call(
        functools.partial(input_kernel, group=group, first=first, earlier=len(earlier)),
        grid=(number // group,),
        in_specs=[
            SMEM, win((group, ROWS, 3 * D)), whole((D, 3 * D)), win((group, ROWS, D)),
            win((group, ROWS, D)), whole((8, D)), *before,
        ],
        out_specs=[whole_out((SLOTS, count, D)), whole_out((2, D))],
        out_shape=[shape_of((SLOTS, count, D), F32), shape_of((2, D), F32)],
        input_output_aliases={6: 0} if earlier else {},
        compiler_params=params(44),
        cost_estimate=cost(COST, 1e5),
        name="input_back",
    )(me, dqkv, weight, tokens, grad_hidden, vec, *earlier)


def pick(left, right):
    return jnp.dot(left, right, preferred_element_type=F32, precision=lax.Precision.HIGHEST)


def pack_kernel(me_ref, one_ref, qv_ref, two_ref, up_ref, rel_ref, out_ref):
    vectors = jnp.concatenate(
        [one_ref[0:2], qv_ref[0:2], two_ref[4:5], two_ref[2:4], two_ref[1:2]], axis=0
    )
    error = jnp.sum(two_ref[0:1, :], axis=1, keepdims=True)
    high = error.astype(BF16).astype(F32)
    middle = (error - high).astype(BF16).astype(F32)
    lane = lax.broadcasted_iota(jnp.int32, (1, 128), 1) - 3 * (me_ref[0] * 8 + me_ref[1])
    error = jnp.where(
        lane == 0, high, jnp.where(lane == 1, middle, jnp.where(lane == 2, error - high - middle, 0.0))
    )
    tables = rel_ref[0:64, 0:64] + rel_ref[64:128, 64:128]
    row = lax.broadcasted_iota(jnp.int32, (D, 128), 0)
    col = lax.broadcasted_iota(jnp.int32, (D, 128), 1)
    small_row = lax.broadcasted_iota(jnp.int32, (32, 128), 0)
    lanes_row = lax.broadcasted_iota(jnp.int32, (64, 128), 0)
    lanes_col = lax.broadcasted_iota(jnp.int32, (64, 128), 1)
    out_ref[...] = jnp.zeros_like(out_ref)
    for owner in range(8):
        own = pick(vectors, ((col < 96) & (row == col + owner * 96)).astype(F32))
        total = jnp.concatenate([own, jnp.zeros((24, 128), F32)], axis=0)
        for which in range(2):
            lane = lanes_col - 96 - 8 * which
            put = ((lane >= 0) & (lane < 8) & (lanes_row == lane + owner * 8)).astype(F32)
            total = total + pick(tables[32 * which : 32 * which + 32], put)
        for part in range(3):
            at = owner * 384 + part * 128
            total = jnp.where(small_row == 27 + part, up_ref[:, at : at + 128], total)
        total = jnp.where(small_row == 30, error, total).astype(BF16)
        for quarter in range(4):
            out_ref[quarter, owner, 0:8] = total[quarter * 8 : quarter * 8 + 8]


def pack(me, *sums):
    return pl.pallas_call(
        pack_kernel,
        grid=(1,),
        in_specs=[SMEM] + [whole(v.shape) for v in sums],
        out_specs=whole_out((4, 8, 48, NOTES)),
        out_shape=shape_of((4, 8, 48, NOTES), BF16),
        compiler_params=params(),
        cost_estimate=cost(COST, 1e5),
        name="pack",
    )(me, *sums)


def qkv_shard_kernel(me_ref, total_ref, *refs):
    quarters, out_ref, notes_ref, turned_ref = refs[0:4], refs[4], refs[5], refs[6]
    core, far_x = me_ref[0] % 2, me_ref[0] // 2
    for at, ref in enumerate(quarters):
        this_core, this_x = core ^ (at // 2), far_x ^ (at % 2)
        rows = pl.ds(pl.multiple_of(this_x * 48, 16), 48)
        cols = pl.ds(pl.multiple_of(this_core * QKV_HALF, 128), QKV_HALF)
        out_ref[rows, cols] = ref[:, 0:QKV_HALF].astype(F32)
        here = pl.ds(pl.multiple_of((this_core * 2 + this_x) * 8, 8), 8)
        notes_ref[here, :] = ref[0:16, QKV_HALF : QKV_HALF + NOTES].astype(F32)[0:8]
    errors = jnp.sum(notes_ref[30:31, :], axis=1, keepdims=True)
    turned_ref[...] = notes_ref[...].T[96:112]
    notes_ref[31:32, :] = errors / (total_ref[...] * D)


def qkv_shard(me, total, quarters):
    shapes = [(96, 3 * D), (32, 128), (16, 32)]
    return pl.pallas_call(
        qkv_shard_kernel,
        grid=(1,),
        in_specs=[SMEM, whole((1, 128))] + [whole(v.shape) for v in quarters],
        out_specs=[whole_out(shape) for shape in shapes],
        out_shape=[shape_of(shape, F32) for shape in shapes],
        compiler_params=params(),
        cost_estimate=cost(COST, 1e5),
        name="qkv_shard",
    )(me, total, *quarters)


def shard_kernel(me_ref, *refs):
    quarters, (up_ref, down_ref, proj_ref) = refs[0:4], refs[4:]
    core, far_x = me_ref[0] % 2, me_ref[0] // 2
    for at, ref in enumerate(quarters):
        this_core, this_x = core ^ (at // 2), far_x ^ (at % 2)
        rows = pl.ds(pl.multiple_of(this_x * 48, 16), 48)
        for block in range(2):
            cols = pl.ds(pl.multiple_of(this_core * 1536 + block * D, 128), D)
            up_ref[rows, cols] = ref[block].astype(F32)
            at_row = this_core * 192 + this_x * 96 + block * 48
            down_ref[pl.ds(pl.multiple_of(at_row, 16), 48), :] = ref[2 + block].astype(F32)
        cols = pl.ds(pl.multiple_of(this_core * 384, 128), 384)
        proj_ref[rows, cols] = ref[4, :, 0:384].astype(F32)


def shard(me, quarters):
    shapes = [(96, MLP), (384, D), (96, D)]
    return pl.pallas_call(
        shard_kernel,
        grid=(1,),
        in_specs=[SMEM] + [whole(v.shape) for v in quarters],
        out_specs=[whole_out(shape) for shape in shapes],
        out_shape=[shape_of(shape, F32) for shape in shapes],
        compiler_params=params(),
        cost_estimate=cost(COST, 1e5),
        name="shard",
    )(me, *quarters)


def column_blocks(rows):
    return pl.BlockSpec((rows, D), lambda step: (0, step))


def weight_grad(left, right, by_rows=False):
    rows = left.shape[0]
    blocks = (left if by_rows else right).shape[1] // D
    moving, still = column_blocks(rows), whole((rows, D))
    return pl.pallas_call(
        weight_grad_kernel,
        grid=(blocks,),
        in_specs=[moving, still] if by_rows else [still, moving],
        out_specs=pl.BlockSpec((D, D), (lambda s: (s, 0)) if by_rows else (lambda s: (0, s))),
        out_shape=shape_of((left.shape[1], right.shape[1]), BF16),
        compiler_params=params(44),
        name="weight_grad",
    )(left, right)


def qkv_grad(me, left, right, notes, other):
    rows = left.shape[0]
    return pl.pallas_call(
        functools.partial(qkv_grad_kernel, other=other),
        grid_spec=pltpu.PrefetchScalarGridSpec(
            num_scalar_prefetch=1,
            grid=(1,),
            in_specs=[
                whole((rows, D)),
                pl.BlockSpec((rows, QKV_HALF), lambda step, me: (0, (me[0] % 2) ^ other)),
                whole((4, 8, 48, NOTES)),
            ],
            out_specs=ANY,
            scratch_shapes=[pltpu.VMEM((D, QKV_HALF), BF16), pltpu.SemaphoreType.DMA((1,))],
        ),
        out_shape=shape_of((16, 48, QKV_HALF + NOTES), BF16),
        compiler_params=params(48),
        cost_estimate=cost(COST, 1e5),
        name="qkv_grad",
    )(me, left, right, notes)


def up_grad(me, left, right, other):
    rows = left.shape[0]
    return pl.pallas_call(
        up_grad_kernel,
        grid_spec=pltpu.PrefetchScalarGridSpec(
            num_scalar_prefetch=1,
            grid=(2,),
            in_specs=[
                whole((rows, D)),
                pl.BlockSpec((rows, D), lambda step, me: (0, ((me[0] % 2) ^ other) * 2 + step)),
            ],
            out_specs=ANY,
            scratch_shapes=[pltpu.VMEM((2, D, D), BF16), pltpu.SemaphoreType.DMA((1,))],
        ),
        out_shape=shape_of((16, 2, 48, D), BF16),
        compiler_params=params(60),
        cost_estimate=cost(COST, 1e5),
        name="up_grad",
    )(me, left, right)


def down_grad(me, act, grad_down, mixed, grad_attn):
    rows = act.shape[0]
    return pl.pallas_call(
        down_grad_kernel,
        grid=(5,),
        in_specs=[
            SMEM, pl.BlockSpec((rows, D), lambda step: (0, jnp.minimum(step, 3))),
            whole((rows, D)), ANY, ANY,
        ],
        out_specs=[ANY] * 2,
        out_shape=[shape_of((16, 3, 48, D), BF16)] * 2,
        scratch_shapes=[
            pltpu.VMEM((4, 16, 48, D), BF16), pltpu.VMEM((2, D, 384), BF16),
            pltpu.VMEM((rows, D), BF16), pltpu.VMEM((rows, D), BF16),
            pltpu.SemaphoreType.DMA((4,)),
        ],
        compiler_params=params(60),
        cost_estimate=cost(COST, 1e5),
        name="down_grad",
    )(me, act, grad_down, mixed, grad_attn)


def swap(values, axis, mask):
    size = lax.axis_size(axis)
    return lax.ppermute(values, axis, [(at, at ^ mask) for at in range(size)])


def joined(stack, axis, mask):
    return jnp.concatenate([stack, swap(stack, axis, mask)], axis=0)


def added(one, two):
    return (one.astype(F32) + two.astype(F32)).astype(BF16)


def tied(*values):
    return lax.optimization_barrier(values)


def cut(values, row, col, rows, cols):
    return lax.dynamic_slice(values, (row, col), (rows, cols))


def body(
    tokens, teacher, valid_mask, attn_gain, attn_shift, qkv_weight, query_bias, value_bias,
    rel_pos_h, rel_pos_w, proj_weight, proj_bias, mlp_gain, mlp_shift, up_weight, up_bias,
    down_weight, down_bias,
):
    count = tokens.shape[0]
    parts = lax.axis_size("fsdp")
    copies = lax.axis_size("rep")
    in_pieces = (copies, parts) == (4, 8)
    rep_at, part_at = lax.axis_index("rep"), lax.axis_index("fsdp")
    device = rep_at * parts + part_at
    core, far_x = rep_at % 2, rep_at // 2
    me = jnp.stack([rep_at, part_at, device * count]).astype(jnp.int32)
    window_ids = device * count + jnp.arange(count, dtype=jnp.int32)
    place = window_ids % (SIDE * SIDE)
    cells = jnp.arange(SLOTS, dtype=jnp.int32)
    inside = ((place // SIDE)[:, None] * WIN + (cells // WIN)[None, :] < MAP) & (
        (place % SIDE)[:, None] * WIN + (cells % WIN)[None, :] < MAP
    )
    keep = inside.astype(F32)
    valid = valid_mask.astype(F32) * keep
    counted = jnp.sum(valid_mask * inside.astype(jnp.int32))
    fill = ((0, 0), (0, ROWS - SLOTS), (0, 0))
    aux = jnp.pad(jnp.stack([keep, valid], axis=-1), fill)
    tokens, teacher = jnp.pad(tokens, fill), jnp.pad(teacher, fill)

    small = [attn_gain, attn_shift, query_bias, value_bias, proj_bias, mlp_gain, mlp_shift,
             down_bias, up_bias, rel_pos_h, rel_pos_w]
    places = jnp.asarray(key_places(), BF16)
    places_t = jnp.asarray(np.pad(key_places().T[0:32], ((0, 0), (0, LANES - ROWS))), BF16)
    counted = jnp.stack([counted // 128, counted % 128]).astype(BF16)
    loss_scale = 64.0 * D * count * copies * parts

    def noted(shape, *entries):
        total = jnp.zeros(shape, BF16)
        for values, row, col in entries:
            if values.ndim == 1:
                values = values[None]
            high, wide = values.shape
            total = total + jnp.pad(
                values, ((row, shape[0] - row - high), (col, shape[1] - col - wide))
            )
        return total

    if in_pieces:
        rect = cut(qkv_weight, far_x * 48, core * QKV_HALF, 48, QKV_HALF)
        notes = noted(
            (48, NOTES), *[(v, at, 0) for at, v in enumerate(small[0:4])],
            (rel_pos_h.T, 16, 0), (rel_pos_w.T, 24, 0),
        )
        rect = jnp.concatenate([rect, notes], axis=1)
        near = [rect] + [swap(rect, "fsdp", mask) for mask in (2, 4, 6)]
        up_rect = cut(up_weight, far_x * 48, core * 1536, 48, 1536)
        down_rect = cut(down_weight, core * 192 + far_x * 96, 0, 96, D)
        proj_rect = cut(proj_weight, far_x * 48, core * 384, 48, 384)
        notes = noted(
            (48, 128), *[(v, at, 0) for at, v in enumerate(small[4:8])],
            (up_bias.reshape(3, 128), 6, 0), (counted, 5, 0),
        )
        rects = jnp.concatenate([up_rect, proj_rect, notes], axis=1)
        down_rect = down_rect.reshape(2, 48, D)
        *near, rects, down_rect, aux = tied(*near, rects, down_rect, aux)
        planes = [rects] + [swap(rects, "fsdp", mask) for mask in (2, 4, 6)]
        near_a, near_b = jnp.stack(near[0:2]), jnp.stack(near[2:4])
        from_a, from_b = swap(near_a, "fsdp", 1), swap(near_b, "rep", 2)
        from_a, from_b, planes[1], tokens = tied(from_a, from_b, planes[1], tokens)
        near_a = jnp.concatenate([near_a, from_a])
        near_b = jnp.concatenate([near_b, from_b])
        far_a, far_b = swap(near_a, "rep", 2), swap(near_b, "fsdp", 1)
        far_a, far_b, planes[2], teacher = tied(far_a, far_b, planes[2], teacher)
        all_a, all_b = jnp.concatenate([near_a, far_a]), jnp.concatenate([near_b, far_b])
        other_a, other_b = swap(all_a, "rep", 1), swap(all_b, "rep", 1)
        vec, rel, rel_t = notes_of(me, near_a, near_b, far_b)
        vec, rel, rel_t, other_a, other_b, planes[3] = tied(
            vec, rel, rel_t, other_a, other_b, planes[3]
        )
        up_a, up_b = jnp.stack(planes[0:2]), jnp.stack(planes[2:4])
        up_a, up_b, vec = tied(up_a, up_b, vec)
        from_a, from_b = swap(up_a, "fsdp", 1), swap(up_b, "rep", 2)
        planes = [down_rect] + [swap(down_rect, "fsdp", mask) for mask in (2, 4, 6)]
        *state, w_qkv = attend(
            me, tokens, (all_a, all_b, other_a, other_b), vec, rel, places, 0, STEPS[0]
        )
        from_a, from_b, *rest = tied(from_a, from_b, *planes[1:], *state)
        planes, state = [down_rect] + rest[0:3], rest[3:]
        up_a, up_b = jnp.concatenate([up_a, from_a]), jnp.concatenate([up_b, from_b])
        down_a, down_b = jnp.stack(planes[0:2]), jnp.stack(planes[2:4])
        up_a, up_b, down_a, down_b, *state = tied(up_a, up_b, down_a, down_b, *state)
        far_up_a, far_up_b = swap(up_a, "rep", 2), swap(up_b, "fsdp", 1)
        core_up_a, core_up_b = swap(up_a, "rep", 1), swap(up_b, "rep", 1)
        state = attend(me, tokens, w_qkv, vec, rel, places, STEPS[0], STEPS[1], tuple(state))
        far_up_a, far_up_b, core_up_a, core_up_b, *state = tied(
            far_up_a, far_up_b, core_up_a, core_up_b, *state
        )
        from_a, from_b = swap(down_a, "fsdp", 1), swap(down_b, "rep", 2)
        core_far_a, core_far_b = swap(far_up_a, "rep", 1), swap(far_up_b, "rep", 1)
        state = attend(me, tokens, w_qkv, vec, rel, places, sum(STEPS[:2]), STEPS[2], tuple(state))
        from_a, from_b, core_far_a, core_far_b, *state = tied(
            from_a, from_b, core_far_a, core_far_b, *state
        )
        up_pieces = (up_a, far_up_a, up_b, far_up_b, core_up_a, core_far_a, core_up_b, core_far_b)
        down_a, down_b = jnp.concatenate([down_a, from_a]), jnp.concatenate([down_b, from_b])
        down_a, down_b, *state = tied(down_a, down_b, *state)
        far_a, far_b = swap(down_a, "rep", 2), swap(down_b, "fsdp", 1)
        core_a, core_b = swap(down_a, "rep", 1), swap(down_b, "rep", 1)
        qkv, probs, mixed, first_in = state
        hidden, second_in, act, slope, w_up, w_proj, vec2, _, total = mlp_up(
            me, tokens, mixed, aux, up_pieces, True
        )
        far_a, far_b, core_a, core_b, hidden = tied(far_a, far_b, core_a, core_b, hidden)
        down_pieces = (
            down_a, far_a, down_b, far_b,
            core_a, swap(far_a, "rep", 1), core_b, swap(far_b, "rep", 1),
        )
    else:
        gather = lambda v: lax.all_gather(v, "fsdp", axis=0, tiled=True)
        w_qkv, w_proj = gather(qkv_weight), gather(proj_weight)
        packed = gather(jnp.concatenate([v.reshape(-1) for v in small] + [counted])[None])
        pieces, at = [], 0
        for v in small:
            pieces.append(packed[:, at : at + v.size])
            at += v.size
        rows = [p.reshape(1, -1).astype(F32) for p in pieces[:9]]
        offsets = rel_pos_h.shape[0]
        tables = [
            p.reshape(parts, offsets, -1).transpose(1, 0, 2).reshape(offsets, HEAD_DIM)
            for p in pieces[9:]
        ]
        gap = jnp.zeros((32 - offsets, HEAD_DIM), BF16)
        table = jnp.concatenate([tables[0], gap, tables[1], gap], axis=0)
        hole = jnp.zeros((HEAD_DIM, HEAD_DIM), BF16)
        rel = jnp.concatenate(
            [jnp.concatenate([table, hole], axis=1), jnp.concatenate([hole, table], axis=1)],
            axis=0,
        )
        rel_t = rel.T
        fill = jnp.zeros((4, D), F32)
        vec = jnp.concatenate(rows[0:4] + [fill])
        counts = lax.psum(jnp.sum(valid), ("rep", "fsdp")).reshape(1, 1)
        vec2 = jnp.concatenate(rows[4:8] + [fill])
        total = jnp.broadcast_to(counts, (1, 128))
        w_up, down_pieces = gather(up_weight), (gather(down_weight),)
        qkv, probs, mixed, first_in = attend(me, tokens, w_qkv, vec, rel, places, 0, count)
        hidden, second_in, act, slope = mlp_up(
            me, tokens, mixed, aux, (w_proj, w_up, vec2, rows[8]), False
        )
    out, grad_hidden, grad_attn, grad_down, grad_up, sums2, up_sum = mlp_down(
        me, hidden, act, slope, teacher, aux, w_up, vec2, total, down_pieces,
        loss_scale * 2.0 / D, in_pieces,
    )
    valid_total = total[0, 0]
    flat = lambda v: v.reshape(count * ROWS, v.shape[-1])
    if in_pieces:
        back_ends = (0, BACK_STEPS[0], BACK_STEPS[0] + BACK_STEPS[1])
        parts_of = lambda keep, come: lambda at, to: added(keep[at:to], come[at:to])
        keep_d, send_d = down_grad(me, flat(act), flat(grad_down), flat(mixed), flat(grad_attn))
        send_d, second_in = tied(send_d, flat(second_in))
        from_d = swap(send_d, "rep", 1)
        send_u = up_grad(me, second_in, flat(grad_up), 1)
        from_d, send_u, second_in = tied(from_d, send_u, second_in)
        sum_d = parts_of(keep_d, from_d)
        send_a, send_b = sum_d(4, 8), sum_d(12, 16)
        send_a, send_b, send_u, second_in = tied(send_a, send_b, send_u, second_in)
        from_u = swap(send_u, "rep", 1)
        from_a, from_b = swap(send_a, "rep", 2), swap(send_b, "fsdp", 1)
        keep_u = up_grad(me, second_in, flat(grad_up), 0)
        from_u, keep_u, grad_attn = tied(from_u, keep_u, grad_attn)
        sum_u = parts_of(keep_u, from_u)
        send_ua, send_ub = sum_u(4, 8), sum_u(12, 16)
        send_ua, send_ub, grad_attn = tied(send_ua, send_ub, grad_attn)
        back = (grad_attn, w_proj, qkv, probs, rel_t, places_t)
        state = attend_back(*back, 0, BACK_STEPS[0])
        from_a, from_b, *state = tied(from_a, from_b, *state)
        d_a, d_b = added(sum_d(0, 4), from_a), added(sum_d(8, 12), from_b)
        send_a, send_b = d_a[2:4], d_b[2:4]
        send_a, send_b, *state = tied(send_a, send_b, *state)
        from_a, from_b = swap(send_a, "fsdp", 1), swap(send_b, "rep", 2)
        from_ua, from_ub = swap(send_ua, "rep", 2), swap(send_ub, "fsdp", 1)
        state = attend_back(*back, back_ends[1], BACK_STEPS[1], tuple(state))
        from_a, from_b, from_ua, from_ub, *state = tied(from_a, from_b, from_ua, from_ub, *state)
        d_a, d_b = added(d_a[0:2], from_a), added(d_b[0:2], from_b)
        u_a, u_b = added(sum_u(0, 4), from_ua), added(sum_u(8, 12), from_ub)
        sends_d = (d_a[0], d_a[1], d_b[0], d_b[1])
        send_ua, send_ub = u_a[2:4], u_b[2:4]
        *sends_d, send_ua, send_ub, s0, s1, s2 = tied(*sends_d, send_ua, send_ub, *state)
        from_z = [swap(v, "fsdp", mask) for v, mask in zip(sends_d[1:], (2, 4, 6))]
        from_ua, from_ub = swap(send_ua, "fsdp", 1), swap(send_ub, "rep", 2)
        state = attend_back(*back, back_ends[2], BACK_STEPS[2], (s0, s1, s2))
        from_ua, from_ub, from_z[0], dqkv, rel_grad, qv_sum = tied(
            from_ua, from_ub, from_z[0], *state
        )
        input_grad, sums1 = input_back(me, dqkv, w_qkv, tokens, grad_hidden, vec, 0, count)
        from_z[1], from_z[2], sums1, dqkv = tied(from_z[1], from_z[2], sums1, dqkv)
        own_d = sends_d[0].astype(F32)
        for v in from_z:
            own_d = own_d + v.astype(F32)
        u_a, u_b = added(u_a[0:2], from_ua), added(u_b[0:2], from_ub)
        notes = pack(me, sums1, qv_sum, sums2, up_sum, rel_grad)
        sends_u = (u_a[0], u_a[1], u_b[0], u_b[1])
        own_d, *sends_u, notes = tied(own_d.astype(BF16), *sends_u, notes)
        from_z = [swap(v, "fsdp", mask) for v, mask in zip(sends_u[1:], (2, 4, 6))]
        first_in, dqkv = flat(first_in), flat(dqkv)
        send = qkv_grad(me, first_in, dqkv, notes, 1)
        from_z[0], send, first_in, input_grad = tied(from_z[0], send, first_in, input_grad)
        from_core = swap(send, "rep", 1)
        keep = qkv_grad(me, first_in, dqkv, notes, 0)
        from_core, keep = tied(from_core, keep)
        both = parts_of(keep, from_core)
        send_a, send_b = both(4, 8), both(12, 16)
        send_a, send_b = tied(send_a, send_b)
        from_a, from_b = swap(send_a, "rep", 2), swap(send_b, "fsdp", 1)
        from_a, from_b, *from_z = tied(from_a, from_b, *from_z)
        sum_a, sum_b = added(both(0, 4), from_a), added(both(8, 12), from_b)
        own_u = sends_u[0].astype(F32)
        for v in from_z:
            own_u = own_u + v.astype(F32)
        own = jnp.concatenate([own_u.astype(BF16), own_d], axis=0)
        from_a, from_b = swap(sum_a[2:4], "fsdp", 1), swap(sum_b[2:4], "rep", 2)
        from_a, from_b = tied(from_a, from_b)
        sum_a, sum_b = added(sum_a[0:2], from_a), added(sum_b[0:2], from_b)
        sends = (sum_a[0], sum_a[1], sum_b[0], sum_b[1])
        *sends, own = tied(*sends, own)
        from_z = [swap(v, "fsdp", mask) for v, mask in zip(sends[1:], (2, 4, 6))]
        from_x = swap(own, "rep", 2)
        *from_z, from_x = tied(*from_z, from_x)
        own_q = sends[0].astype(F32)
        for v in from_z:
            own_q = own_q + v.astype(F32)
        own_q = own_q.astype(BF16)
        from_xq = swap(own_q, "rep", 2)
        d_up, d_down, d_proj = shard(
            me, (own, from_x, swap(own, "rep", 1), swap(from_x, "rep", 1))
        )
        from_xq, d_up = tied(from_xq, d_up)
        d_qkv, mine, turned = qkv_shard(
            me, total, (own_q, from_xq, swap(own_q, "rep", 1), swap(from_xq, "rep", 1))
        )
        vectors = [mine[at, 0:96] for at in range(8)]
        tables = [turned[8 * at : 8 * at + 8, 0:27].T for at in range(2)]
        outs = vectors + [mine[27:30].reshape(-1)] + tables
        loss = mine[31, 0]
    else:
        scatter = lambda v: lax.psum(
            lax.psum_scatter(v, "fsdp", scatter_dimension=0, tiled=True), "rep"
        ).astype(F32)
        d_down = scatter(weight_grad(flat(act), flat(grad_down), True))
        d_up = scatter(weight_grad(flat(second_in), flat(grad_up)))
        d_proj = scatter(weight_grad(flat(mixed), flat(grad_attn)))
        back = (grad_attn, w_proj, qkv, probs, rel_t, places_t)
        dqkv, rel_grad, qv_sum = attend_back(*back, 0, count)
        d_qkv = scatter(weight_grad(flat(first_in), flat(dqkv)))
        input_grad, sums1 = input_back(me, dqkv, w_qkv, tokens, grad_hidden, vec, 0, count)
        offsets = rel_pos_h.shape[0]
        rel_sum = rel_grad[0:64, 0:64] + rel_grad[64:128, 64:128]
        vectors = [sums1[0], sums1[1], qv_sum[0], qv_sum[1], sums2[4], sums2[2], sums2[3],
                   sums2[1], up_sum[0]]
        own = jnp.concatenate(
            [v.reshape(parts, -1) for v in vectors]
            + [
                rel_sum[at : at + offsets].reshape(offsets, parts, -1).transpose(1, 0, 2)
                .reshape(parts, -1) for at in (0, 32)
            ]
            + [jnp.broadcast_to(jnp.sum(sums2[0]), (parts, 1))],
            axis=1,
        )
        mine = lax.dynamic_index_in_dim(
            lax.psum(own, ("rep", "fsdp")), part_at, 0, keepdims=False
        )
        outs, at = [], 0
        for v in small:
            outs.append(mine[at : at + v.size].reshape(v.shape))
            at += v.size
        loss = mine[at] / (valid_total * D)
    (g_gain1, g_shift1, g_qb, g_vb, g_pb, g_gain2, g_shift2, g_db, g_ub, g_rh, g_rw) = outs
    return (
        out.transpose(1, 0, 2), loss, input_grad.transpose(1, 0, 2), g_gain1, g_shift1, d_qkv, g_qb, g_vb, g_rh, g_rw, d_proj, g_pb,
        g_gain2, g_shift2, d_up, g_ub, d_down, g_db,
    )


def solution(mesh):
    windows = P(("rep", "fsdp"), None, None)
    vector = P("fsdp")
    matrix = P("fsdp", None)
    table = P(None, "fsdp")
    in_specs = (
        windows, windows, P(("rep", "fsdp"), None), vector, vector, matrix, vector, vector, table,
        table, matrix, vector, vector, vector, matrix, vector, matrix, vector,
    )
    out_specs = (windows, P(), windows) + in_specs[3:]
    return jax.shard_map(body, mesh=mesh, in_specs=in_specs, out_specs=out_specs, check_vma=False)
```
